32 devices in a mesh: clip: 4 (over y, x), frame: 8 (over z, core).
Axes of the slice: x: 2, y: 2, z: 4, core: 2. Of those that a mesh axis runs over, the one named last changes fastest.
Arguments:
- hidden_in: bfloat16 [8, 1024, 1024], P('clip', 'frame'), may hold values from -6 to 6
- text_states: bfloat16 [8, 128, 1024], P('clip'), may hold values from -6 to 6
- out_grad: bfloat16 [8, 1024, 1024], P('clip', 'frame'), may hold values from -6 to 6
- self_qkv: bfloat16 [1024, 3, 1024], P(('clip', 'frame')), may hold values from -0.1875 to 0.1875
- self_out: bfloat16 [1024, 1024], P(('clip', 'frame')), may hold values from -1 to 1
- cross_qkv: bfloat16 [1024, 3, 1024], P(('clip', 'frame')), may hold values from -0.1875 to 0.1875
- cross_out: bfloat16 [1024, 1024], P(('clip', 'frame')), may hold values from -0.5 to 0.5
- ffn_in: bfloat16 [1024, 4096], P(('clip', 'frame')), may hold values from -0.1875 to 0.1875
- ffn_out: bfloat16 [4096, 1024], P(('clip', 'frame')), may hold values from -0.09375 to 0.09375
- ln_gain: bfloat16 [3, 1024], P(None, ('clip', 'frame')), may hold values from 0.5 to 1.5
- ln_bias: bfloat16 [3, 1024], P(None, ('clip', 'frame')), may hold values from -3 to 3
- clip_len: int32 [8], P('clip'), may hold values from 170 to 1024, as said below
- frame_mask: int32 [8, 1024], P('clip'), may hold values 0 or 1
- text_len: int32 [8], P('clip'), may hold values from 5 to 120
- text_mask: int32 [8, 128], P('clip'), may hold values 0 or 1
Outputs:
- output: bfloat16 [8, 1024, 1024], P('clip', 'frame')
- grad_hidden: bfloat16 [8, 1024, 1024], P('clip', 'frame')
- grad_text: bfloat16 [8, 128, 1024], P('clip', 'frame')
- grad_self_qkv: float32 [1024, 3, 1024], P(('clip', 'frame'))
- grad_self_out: float32 [1024, 1024], P(('clip', 'frame'))
- grad_cross_qkv: float32 [1024, 3, 1024], P(('clip', 'frame'))
- grad_cross_out: float32 [1024, 1024], P(('clip', 'frame'))
- grad_ffn_in: float32 [1024, 4096], P(('clip', 'frame'))
- grad_ffn_out: float32 [4096, 1024], P(('clip', 'frame'))
- grad_ln_gain: float32 [3, 1024], P(None, ('clip', 'frame'))
- grad_ln_bias: float32 [3, 1024], P(None, ('clip', 'frame'))
The draws below stay inside these ranges and needn't reach their ends.
Inputs may be any that keep to these rules, and one draw needn't show every extreme that they name: `clip_len`: in every aligned group of 2 clips at least one has the full length 1024.
All inputs are finite; a program needn't handle non-finite values. No bound on the sum of `frame_mask` or of `text_mask` on one device may be relied on, other than what follows from the above.
Results may differ from the reference program's by a relative error of at most 0.019.
Values may be sent and summed in bfloat16 or wider, within the bound.
A program may use at most 320 MiB of HBM per device.

```python
import math
import jax
import jax.numpy as jnp
from jax import lax

D = 1024
H = 16
HD = 64
FF = 4096
TXT = 128
CLIP_DEV = 2
CLIPS = 8
LEN = 1024


def draw_clip_len(key, part):
    key = jax.random.fold_in(key, 11)
    base = jax.random.randint(jax.random.fold_in(key, 1), (CLIPS,), LEN // 6, LEN + 1)
    chosen = jax.random.randint(jax.random.fold_in(key, 2), (CLIPS // CLIP_DEV, 1), 0, CLIP_DEV)
    slot_index = jnp.arange(CLIP_DEV, dtype=jnp.int32)[None, :]
    full = (slot_index == chosen).reshape(CLIPS)
    return jnp.where(full, LEN, base).astype(jnp.int32)


def place_ends(values, key, low, largest):
    place = [jax.random.randint(jax.random.fold_in(key, axis), (), 0, length) for axis, length in enumerate(values.shape)]
    longest = values.shape.index(max(values.shape))
    beside = place[:longest] + [(place[longest] + 1) % values.shape[longest]] + place[longest + 1:]
    return values.at[tuple(place)].set(low).at[tuple(beside)].set(largest)


def block_scale(rng, extent, shards, smallest, largest):
    def one(axis_at, shards_of):
        heights = jax.random.uniform(jax.random.fold_in(jax.random.fold_in(rng, 6), axis_at), (shards_of,), jnp.float32, smallest / len(shards), largest / len(shards))
        return jnp.repeat(jnp.exp(heights), extent[axis_at] // shards_of).reshape((-1,) + (1,) * (len(extent) - axis_at - 1))

    level = one(*shards[0])
    for cut in shards[1:]:
        level = level * one(*cut)
    return level


def bell_draw(own_key, extent, width, bound, cuts=(), kind=jnp.bfloat16):
    values = width * jax.random.normal(own_key, extent, jnp.float32)
    if cuts:
        values = values * block_scale(own_key, extent, cuts, -0.22, 0.18)
    return jnp.clip(values, -bound, bound).astype(kind)


def setup_inputs(seed: int = 0) -> dict:
    arg_keys = jax.random.split(jax.random.key(seed), 16)
    return {
        "hidden_in": bell_draw(arg_keys[0], (CLIPS, LEN, D), 1.0, 6.0, ((0, 4), (1, 8))),
        "text_states": bell_draw(arg_keys[1], (CLIPS, TXT, D), 1.0, 6.0, ((0, 4),)),
        "out_grad": bell_draw(arg_keys[2], (CLIPS, LEN, D), 1.0, 6.0, ((0, 4), (1, 8))),
        "self_qkv": bell_draw(arg_keys[3], (D, 3, D), D ** -0.5, 0.1875, ((0, 32),)),
        "self_out": bell_draw(arg_keys[4], (D, D), (D // 32) ** -0.5, 1.0, ((0, 32),)),
        "cross_qkv": bell_draw(arg_keys[5], (D, 3, D), D ** -0.5, 0.1875, ((0, 32),)),
        "cross_out": bell_draw(arg_keys[6], (D, D), (D // 8) ** -0.5, 0.5, ((0, 32),)),
        "ffn_in": bell_draw(arg_keys[7], (D, FF), D ** -0.5, 0.1875, ((0, 32),)),
        "ffn_out": bell_draw(arg_keys[8], (FF, D), FF ** -0.5, 0.09375, ((0, 32),)),
        "ln_gain": jnp.clip(1.0 + 0.1 * jax.random.normal(arg_keys[9], (3, D), jnp.float32), 0.5, 1.5).astype(jnp.bfloat16),
        "ln_bias": bell_draw(arg_keys[10], (3, D), 0.5, 3.0, ((1, 32),)),
        "clip_len": draw_clip_len(jax.random.fold_in(arg_keys[15], 71), 0),
        "frame_mask": place_ends((jax.random.randint(arg_keys[12], (CLIPS, LEN), 0, 8) < 7).astype(jnp.int32), jax.random.fold_in(arg_keys[12], 1), 0, 1),
        "text_len": place_ends(jax.random.randint(arg_keys[13], (CLIPS,), 5, TXT - 7), jax.random.fold_in(arg_keys[13], 1), 5, (TXT - 7) - 1).astype(jnp.int32),
        "text_mask": place_ends((jax.random.randint(arg_keys[14], (CLIPS, TXT), 0, 8) < 7).astype(jnp.int32), jax.random.fold_in(arg_keys[14], 1), 0, 1),
    }


PRECISE = lax.Precision.HIGHEST
MASKED = -1000000000.0
EPSILON = 1e-05

@jax.custom_vjp
def low(v):
    return lax.optimization_barrier(v.astype(jnp.bfloat16)).astype(jnp.float32)

@jax.custom_vjp
def low_back(v):
    return v

def low_keep(v):
    return (low(v), None)

def low_pass(kept, grad):
    return (grad,)

def back_keep(v):
    return (v, None)

def back_low(kept, grad):
    return (low(grad),)
low.defvjp(low_keep, low_pass)
low_back.defvjp(back_keep, back_low)

def round_both(value):
    return low(low_back(value))

def layer_norm(value, gain, shift):
    average = lax.optimization_barrier(jnp.mean(value, axis=-1, keepdims=True))
    centered = value - average
    variance = lax.optimization_barrier(jnp.mean(centered * centered, axis=-1, keepdims=True))
    return centered * lax.rsqrt(variance + EPSILON) * gain + shift

def project(left, right):
    return jnp.einsum('gnd,de->gne', left, right, precision=PRECISE)

def softmax_rows(logits):
    row_max = lax.optimization_barrier(jnp.max(logits, axis=-1, keepdims=True))
    exponent = jnp.exp(logits - row_max)
    row_sum = lax.optimization_barrier(jnp.sum(exponent, axis=-1, keepdims=True))
    return exponent / row_sum

def self_attention(query_rows, key_rows, value_rows, clip_len, frame_mask):
    length = query_rows.shape[1]
    block_rows = min(512, length)
    score_scale = HD ** (-0.5)
    columns = jnp.arange(length, dtype=jnp.int32)
    key_valid = (columns[None, :] < clip_len[:, None]) & (frame_mask > 0)

    def one_block(block_index):
        first_row = block_index * block_rows
        row_ids = first_row + jnp.arange(block_rows, dtype=jnp.int32)
        query_block = lax.dynamic_slice_in_dim(query_rows, first_row, block_rows, 1)
        raw_scores = low_back(jnp.einsum('gqhd,gkhd->ghqk', query_block, key_rows, precision=PRECISE))
        diagonal = columns[None, :] == row_ids[:, None]
        allowed = (columns[None, :] <= row_ids[:, None])[None] & (key_valid[:, None, :] | diagonal[None])
        logits = jnp.where(allowed[:, None], raw_scores * score_scale, MASKED)
        live_rows = (row_ids[None, :] < clip_len[:, None]).astype(jnp.float32)
        weights = low(softmax_rows(logits) * live_rows[:, None, :, None])
        return jnp.einsum('ghqk,gkhd->gqhd', weights, value_rows, precision=PRECISE)
    blocks = lax.map(jax.checkpoint(one_block), jnp.arange(length // block_rows, dtype=jnp.int32))
    return jnp.moveaxis(blocks, 0, 1).reshape(query_rows.shape)

def cross_attention(query_rows, key_rows, value_rows, text_len, text_mask):
    slots = jnp.arange(text_mask.shape[1], dtype=jnp.int32)
    allowed = (slots[None, :] < text_len[:, None]) & ((text_mask > 0) | (slots[None, :] == 0))
    raw_scores = low_back(jnp.einsum('gqhd,gkhd->ghqk', query_rows, key_rows, precision=PRECISE))
    logits = jnp.where(allowed[:, None, None, :], raw_scores * HD ** (-0.5), MASKED)
    weights = low(softmax_rows(logits))
    return jnp.einsum('ghqk,gkhd->gqhd', weights, value_rows, precision=PRECISE)

def layer(hidden, text, weights, clip_len, frame_mask, text_len, text_mask):
    self_qkv, self_out, cross_qkv, cross_out, ffn_in, ffn_out, ln_gain, ln_bias = weights
    group_size, length, model_width = hidden.shape
    text_slots = text.shape[1]
    first_low = low(layer_norm(hidden, ln_gain[0], ln_bias[0]))
    query_rows = round_both(project(first_low, self_qkv[:, 0])).reshape(group_size, length, H, HD)
    key_rows = round_both(project(first_low, self_qkv[:, 1])).reshape(group_size, length, H, HD)
    value_rows = round_both(project(first_low, self_qkv[:, 2])).reshape(group_size, length, H, HD)
    attended = self_attention(query_rows, key_rows, value_rows, clip_len, frame_mask)
    attended = round_both(attended).reshape(group_size, length, model_width)
    after_self = hidden + low_back(project(attended, self_out))
    second = low(layer_norm(after_self, ln_gain[1], ln_bias[1]))
    cross_query = round_both(project(second, cross_qkv[:, 0])).reshape(group_size, length, H, HD)
    text_keys = round_both(project(text, cross_qkv[:, 1])).reshape(group_size, text_slots, H, HD)
    text_values = round_both(project(text, cross_qkv[:, 2])).reshape(group_size, text_slots, H, HD)
    crossed = cross_attention(cross_query, text_keys, text_values, text_len, text_mask)
    crossed = round_both(crossed).reshape(group_size, length, model_width)
    after_cross = after_self + low_back(project(crossed, cross_out))
    third_low = low(layer_norm(after_cross, ln_gain[2], ln_bias[2]))
    inner = low(jax.nn.gelu(low_back(project(third_low, ffn_in)), approximate=False))
    return after_cross + low_back(project(inner, ffn_out))

def reference(hidden_in, text_states, out_grad, self_qkv, self_out, cross_qkv, cross_out, ffn_in, ffn_out, ln_gain, ln_bias, clip_len, frame_mask, text_len, text_mask):
    weights = (self_qkv.astype(jnp.float32), self_out.astype(jnp.float32), cross_qkv.astype(jnp.float32), cross_out.astype(jnp.float32), ffn_in.astype(jnp.float32), ffn_out.astype(jnp.float32), ln_gain.astype(jnp.float32), ln_bias.astype(jnp.float32))
    group_size = math.gcd(CLIPS, max(1, 4096 // LEN))
    step_count = CLIPS // group_size

    def split(array):
        return array.reshape((step_count, group_size) + array.shape[1:])

    def one_step(totals, step_items):
        hidden, text, cotangent, lengths, fmask, tlengths, tmask = step_items

        def forward(hidden_value, text_value, weight_values):
            return layer(hidden_value, text_value, weight_values, lengths, fmask, tlengths, tmask)
        result, pullback = jax.vjp(forward, hidden.astype(jnp.float32), text.astype(jnp.float32), weights)
        grad_hidden, grad_text, grad_weights = pullback(cotangent.astype(jnp.float32))
        totals = jax.tree.map(jnp.add, totals, grad_weights)
        return (totals, (result.astype(jnp.bfloat16), grad_hidden.astype(jnp.bfloat16), grad_text.astype(jnp.bfloat16)))
    zeros = jax.tree.map(jnp.zeros_like, weights)
    inputs = (split(hidden_in), split(text_states), split(out_grad), split(clip_len), split(frame_mask), split(text_len), split(text_mask))
    totals, (output, grad_hidden, grad_text) = lax.scan(one_step, zeros, inputs)
    output = output.reshape(hidden_in.shape)
    grad_hidden = grad_hidden.reshape(hidden_in.shape)
    grad_text = grad_text.reshape(text_states.shape)
    return (output, grad_hidden, grad_text, totals[0], totals[1], totals[2], totals[3], totals[4], totals[5], totals[6], totals[7])
```

```python
import functools

import jax
import jax.numpy as jnp
from jax import lax
from jax.experimental import pallas as pl
from jax.experimental.pallas import tpu as pltpu
from jax.sharding import PartitionSpec as P

HD = 64


MASKED = -1000000000.0
EPSILON = 1e-05


def layer_norm(value, gain, shift):
    average = jnp.mean(value, axis=-1, keepdims=True)
    centered = value - average
    variance = jnp.mean(centered * centered, axis=-1, keepdims=True)
    return centered * lax.rsqrt(variance + EPSILON) * gain + shift


def activate(value):
    return jax.nn.gelu(value, approximate=False)


def project(left, right):
    return jnp.einsum("cnd,de->cne", left, right, preferred_element_type=jnp.float32)


def project_back(grad_rows, weight):
    return jnp.einsum("cne,de->cnd", grad_rows, weight, preferred_element_type=jnp.float32)


def weight_grad(left, right):
    return jnp.einsum("cnd,cne->de", left, right, preferred_element_type=jnp.float32)


def fetch_attention(self_qkv, self_out, cross_qkv, cross_out, ln_gain, ln_bias):
    return (
        lax.all_gather(self_qkv, ("clip", "frame"), axis=0, tiled=True),
        lax.all_gather(self_out, ("clip", "frame"), axis=0, tiled=True),
        lax.all_gather(cross_qkv, ("clip", "frame"), axis=0, tiled=True),
        lax.all_gather(cross_out, ("clip", "frame"), axis=0, tiled=True),
        lax.all_gather(ln_gain, ("clip", "frame"), axis=1, tiled=True),
        lax.all_gather(ln_bias, ("clip", "frame"), axis=1, tiled=True),
    )


def fetch_ffn(ffn_in, ffn_out):
    return (
        lax.all_gather(ffn_in, ("clip", "frame"), axis=0, tiled=True),
        lax.all_gather(ffn_out, ("clip", "frame"), axis=0, tiled=True),
    )


def self_masks(first_row, block_rows, clip_len, key_valid):
    columns = jnp.arange(key_valid.shape[1], dtype=jnp.int32)
    row_ids = first_row + jnp.arange(block_rows, dtype=jnp.int32)
    diagonal = columns[None, :] == row_ids[:, None]
    allowed = (columns[None, :] <= row_ids[:, None])[None] & (
        key_valid[:, None, :] | diagonal[None]
    )
    live_rows = (row_ids[None, :] < clip_len[:, None]).astype(jnp.float32)
    return (allowed[:, None], live_rows[:, None, :, None])


def self_forward(query_rows, key_rows, value_rows, clip_len, key_valid):
    length = query_rows.shape[1]
    block_rows = min(512, length)
    score_scale = query_rows.shape[3] ** (-0.5)

    def one_block(block_index):
        first_row = block_index * block_rows
        query_block = lax.dynamic_slice_in_dim(query_rows, first_row, block_rows, 1)
        raw_scores = jnp.einsum(
            "cqhd,ckhd->chqk", query_block, key_rows, preferred_element_type=jnp.float32
        )
        allowed, live_rows = self_masks(first_row, block_rows, clip_len, key_valid)
        logits = jnp.where(allowed, raw_scores * score_scale, MASKED)
        row_max = jnp.max(logits, axis=-1, keepdims=True)
        exponent = jnp.exp(logits - row_max)
        row_sum = jnp.sum(exponent, axis=-1, keepdims=True)
        weights = (exponent / row_sum * live_rows).astype(jnp.bfloat16)
        attended = jnp.einsum(
            "chqk,ckhd->cqhd", weights, value_rows, preferred_element_type=jnp.float32
        )
        return (attended.astype(jnp.bfloat16), row_max + jnp.log(row_sum))

    blocks, log_sums = lax.map(one_block, jnp.arange(length // block_rows, dtype=jnp.int32))
    return (jnp.moveaxis(blocks, 0, 1).reshape(query_rows.shape), log_sums)


def self_backward(query_rows, key_rows, value_rows, grad_rows, log_sums, clip_len, key_valid):
    length = query_rows.shape[1]
    block_rows = min(512, length)
    score_scale = query_rows.shape[3] ** (-0.5)

    def one_block(totals, block_index):
        grad_keys, grad_values = totals
        first_row = block_index * block_rows
        query_block = lax.dynamic_slice_in_dim(query_rows, first_row, block_rows, 1)
        grad_block = lax.dynamic_slice_in_dim(grad_rows, first_row, block_rows, 1)
        raw_scores = jnp.einsum(
            "cqhd,ckhd->chqk", query_block, key_rows, preferred_element_type=jnp.float32
        )
        allowed, live_rows = self_masks(first_row, block_rows, clip_len, key_valid)
        logits = jnp.where(allowed, raw_scores * score_scale, MASKED)
        probs = jnp.exp(logits - log_sums[block_index])
        weights = (probs * live_rows).astype(jnp.bfloat16)
        grad_probs = (
            jnp.einsum(
                "cqhd,ckhd->chqk", grad_block, value_rows, preferred_element_type=jnp.float32
            )
            * live_rows
        )
        row_dot = jnp.sum(probs * grad_probs, axis=-1, keepdims=True)
        grad_scores = (probs * (grad_probs - row_dot)).astype(jnp.bfloat16)
        grad_query = (
            jnp.einsum("chqk,ckhd->cqhd", grad_scores, key_rows, preferred_element_type=jnp.float32)
            * score_scale
        )
        grad_keys = (
            grad_keys
            + jnp.einsum(
                "chqk,cqhd->ckhd", grad_scores, query_block, preferred_element_type=jnp.float32
            )
            * score_scale
        )
        grad_values = grad_values + jnp.einsum(
            "chqk,cqhd->ckhd", weights, grad_block, preferred_element_type=jnp.float32
        )
        return ((grad_keys, grad_values), grad_query)

    zeros = jnp.zeros(key_rows.shape, jnp.float32)
    (grad_keys, grad_values), grad_blocks = lax.scan(
        one_block, (zeros, zeros), jnp.arange(length // block_rows, dtype=jnp.int32)
    )
    grad_query = jnp.moveaxis(grad_blocks, 0, 1).reshape(query_rows.shape)
    return (grad_query, grad_keys, grad_values)


def text_allowed(text_len, text_mask):
    slots = jnp.arange(text_mask.shape[1], dtype=jnp.int32)
    allowed = (slots[None, :] < text_len[:, None]) & ((text_mask > 0) | (slots[None, :] == 0))
    return allowed[:, None, None, :]


def cross_forward(query_rows, key_rows, value_rows, allowed):
    score_scale = query_rows.shape[3] ** (-0.5)
    raw_scores = jnp.einsum(
        "cqhd,ckhd->chqk", query_rows, key_rows, preferred_element_type=jnp.float32
    )
    logits = jnp.where(allowed, raw_scores * score_scale, MASKED)
    row_max = jnp.max(logits, axis=-1, keepdims=True)
    exponent = jnp.exp(logits - row_max)
    row_sum = jnp.sum(exponent, axis=-1, keepdims=True)
    weights = (exponent / row_sum).astype(jnp.bfloat16)
    crossed = jnp.einsum("chqk,ckhd->cqhd", weights, value_rows, preferred_element_type=jnp.float32)
    return (crossed.astype(jnp.bfloat16), row_max + jnp.log(row_sum))


def cross_backward(query_rows, key_rows, value_rows, grad_rows, log_sums, allowed):
    score_scale = query_rows.shape[3] ** (-0.5)
    raw_scores = jnp.einsum(
        "cqhd,ckhd->chqk", query_rows, key_rows, preferred_element_type=jnp.float32
    )
    logits = jnp.where(allowed, raw_scores * score_scale, MASKED)
    probs = jnp.exp(logits - log_sums)
    weights = probs.astype(jnp.bfloat16)
    grad_probs = jnp.einsum(
        "cqhd,ckhd->chqk", grad_rows, value_rows, preferred_element_type=jnp.float32
    )
    row_dot = jnp.sum(probs * grad_probs, axis=-1, keepdims=True)
    grad_scores = (probs * (grad_probs - row_dot)).astype(jnp.bfloat16)
    grad_query = (
        jnp.einsum("chqk,ckhd->cqhd", grad_scores, key_rows, preferred_element_type=jnp.float32)
        * score_scale
    )
    grad_keys = (
        jnp.einsum("chqk,cqhd->ckhd", grad_scores, query_rows, preferred_element_type=jnp.float32)
        * score_scale
    )
    grad_values = jnp.einsum(
        "chqk,cqhd->ckhd", weights, grad_rows, preferred_element_type=jnp.float32
    )
    return (grad_query, grad_keys, grad_values)


def sum_ffn(grad_ffn_in, grad_ffn_out):
    return (
        lax.psum_scatter(grad_ffn_in, ("clip", "frame"), scatter_dimension=0, tiled=True),
        lax.psum_scatter(grad_ffn_out, ("clip", "frame"), scatter_dimension=0, tiled=True),
    )


def sum_attention(
    grad_self_qkv, grad_self_out, grad_cross_qkv, grad_cross_out, grad_gains, grad_shifts
):
    return (
        lax.psum_scatter(grad_self_qkv, ("clip", "frame"), scatter_dimension=0, tiled=True),
        lax.psum_scatter(grad_self_out, ("clip", "frame"), scatter_dimension=0, tiled=True),
        lax.psum_scatter(grad_cross_qkv, ("clip", "frame"), scatter_dimension=0, tiled=True),
        lax.psum_scatter(grad_cross_out, ("clip", "frame"), scatter_dimension=0, tiled=True),
        lax.psum_scatter(grad_gains, ("clip", "frame"), scatter_dimension=1, tiled=True),
        lax.psum_scatter(grad_shifts, ("clip", "frame"), scatter_dimension=1, tiled=True),
    )


def on_device_any(
    hidden_in,
    text_states,
    out_grad,
    self_qkv,
    self_out,
    cross_qkv,
    cross_out,
    ffn_in,
    ffn_out,
    ln_gain,
    ln_bias,
    clip_len,
    frame_mask,
    text_len,
    text_mask,
):
    clip_count, frames, model_width = hidden_in.shape
    text_slots = text_states.shape[1]
    group_count = lax.axis_size("frame")
    columns_here = model_width // group_count
    heads_here = columns_here // HD
    length = frames * group_count
    frame_index = lax.axis_index("frame")
    full_qkv, full_out, full_cross, full_cross_out, gains_low, shifts_low = fetch_attention(
        self_qkv, self_out, cross_qkv, cross_out, ln_gain, ln_bias
    )
    gains = gains_low.astype(jnp.float32)
    shifts = shifts_low.astype(jnp.float32)
    hidden = hidden_in.astype(jnp.float32)
    first_norm, first_pull = jax.vjp(layer_norm, hidden, gains[0], shifts[0])
    first_low = first_norm.astype(jnp.bfloat16)
    query_low = project(first_low, full_qkv[:, 0]).astype(jnp.bfloat16)
    key_low = project(first_low, full_qkv[:, 1]).astype(jnp.bfloat16)
    value_low = project(first_low, full_qkv[:, 2]).astype(jnp.bfloat16)
    query_heads, key_heads, value_heads = (
        lax.all_to_all(query_low, "frame", split_axis=2, concat_axis=1, tiled=True),
        lax.all_to_all(key_low, "frame", split_axis=2, concat_axis=1, tiled=True),
        lax.all_to_all(value_low, "frame", split_axis=2, concat_axis=1, tiled=True),
    )
    head_shape = (clip_count, length, heads_here, HD)
    query_heads = query_heads.reshape(head_shape)
    key_heads = key_heads.reshape(head_shape)
    value_heads = value_heads.reshape(head_shape)
    columns = jnp.arange(length, dtype=jnp.int32)
    key_valid = (columns[None, :] < clip_len[:, None]) & (frame_mask > 0)
    attended_heads, self_sums = self_forward(
        query_heads, key_heads, value_heads, clip_len, key_valid
    )
    attended = lax.all_to_all(
        attended_heads.reshape(clip_count, length, columns_here),
        "frame",
        split_axis=1,
        concat_axis=2,
        tiled=True,
    )
    after_self = hidden + project(attended, full_out)
    second_norm, second_pull = jax.vjp(layer_norm, after_self, gains[1], shifts[1])
    second_low = second_norm.astype(jnp.bfloat16)
    cross_query = project(second_low, full_cross[:, 0]).astype(jnp.bfloat16)
    cross_query_heads = lax.all_to_all(
        cross_query, "frame", split_axis=2, concat_axis=1, tiled=True
    ).reshape(head_shape)
    key_columns = lax.dynamic_slice_in_dim(
        full_cross[:, 1], frame_index * columns_here, columns_here, 1
    )
    value_columns = lax.dynamic_slice_in_dim(
        full_cross[:, 2], frame_index * columns_here, columns_here, 1
    )
    text_shape = (clip_count, text_slots, heads_here, HD)
    text_keys = project(text_states, key_columns).astype(jnp.bfloat16).reshape(text_shape)
    text_values = project(text_states, value_columns).astype(jnp.bfloat16).reshape(text_shape)
    allowed_text = text_allowed(text_len, text_mask)
    crossed_heads, cross_sums = cross_forward(
        cross_query_heads, text_keys, text_values, allowed_text
    )
    crossed = lax.all_to_all(
        crossed_heads.reshape(clip_count, length, columns_here),
        "frame",
        split_axis=1,
        concat_axis=2,
        tiled=True,
    )
    after_cross = after_self + project(crossed, full_cross_out)
    ffn_weight_in, ffn_weight_out = fetch_ffn(ffn_in, ffn_out)
    third_norm, third_pull = jax.vjp(layer_norm, after_cross, gains[2], shifts[2])
    third_low = third_norm.astype(jnp.bfloat16)
    pre_act = project(third_low, ffn_weight_in)
    activated, gelu_pull = jax.vjp(activate, pre_act)
    inner_low = activated.astype(jnp.bfloat16)
    output = (after_cross + project(inner_low, ffn_weight_out)).astype(jnp.bfloat16)
    ffn_weight_in, ffn_weight_out = fetch_ffn(ffn_in, ffn_out)
    grad_ffn_out = weight_grad(inner_low, out_grad)
    (grad_pre,) = gelu_pull(project_back(out_grad, ffn_weight_out))
    grad_pre_low = grad_pre.astype(jnp.bfloat16)
    grad_ffn_in = weight_grad(third_low, grad_pre_low)
    ffn_sums = sum_ffn(grad_ffn_in, grad_ffn_out)
    grad_third, gain_third, shift_third = third_pull(project_back(grad_pre_low, ffn_weight_in))
    grad_after_cross = out_grad.astype(jnp.float32) + grad_third
    full_qkv, full_out, full_cross, full_cross_out, gains_low, shifts_low = fetch_attention(
        self_qkv, self_out, cross_qkv, cross_out, ln_gain, ln_bias
    )
    key_columns = lax.dynamic_slice_in_dim(
        full_cross[:, 1], frame_index * columns_here, columns_here, 1
    )
    value_columns = lax.dynamic_slice_in_dim(
        full_cross[:, 2], frame_index * columns_here, columns_here, 1
    )
    cross_branch = grad_after_cross.astype(jnp.bfloat16)
    grad_cross_out = weight_grad(crossed, cross_branch)
    grad_crossed = project_back(cross_branch, full_cross_out).astype(jnp.bfloat16)
    grad_crossed_heads = lax.all_to_all(
        grad_crossed, "frame", split_axis=2, concat_axis=1, tiled=True
    ).reshape(head_shape)
    grad_cq, grad_tk, grad_tv = cross_backward(
        cross_query_heads, text_keys, text_values, grad_crossed_heads, cross_sums, allowed_text
    )
    grad_tk_low = grad_tk.astype(jnp.bfloat16).reshape(clip_count, text_slots, columns_here)
    grad_tv_low = grad_tv.astype(jnp.bfloat16).reshape(clip_count, text_slots, columns_here)
    text_terms = project_back(grad_tk_low, key_columns) + project_back(grad_tv_low, value_columns)
    grad_text = lax.psum_scatter(
        text_terms.astype(jnp.bfloat16), "frame", scatter_dimension=1, tiled=True
    )
    empty_square = jnp.zeros((model_width, model_width), jnp.float32)
    grad_cross_key = lax.dynamic_update_slice_in_dim(
        empty_square, weight_grad(text_states, grad_tk_low), frame_index * columns_here, 1
    )
    grad_cross_value = lax.dynamic_update_slice_in_dim(
        empty_square, weight_grad(text_states, grad_tv_low), frame_index * columns_here, 1
    )
    grad_cq_low = grad_cq.astype(jnp.bfloat16).reshape(clip_count, length, columns_here)
    grad_cross_query = lax.all_to_all(grad_cq_low, "frame", split_axis=1, concat_axis=2, tiled=True)
    grad_cross_qw = weight_grad(second_low, grad_cross_query)
    grad_second, gain_second, shift_second = second_pull(
        project_back(grad_cross_query, full_cross[:, 0])
    )
    grad_after_self = grad_after_cross + grad_second
    self_branch = grad_after_self.astype(jnp.bfloat16)
    grad_self_out = weight_grad(attended, self_branch)
    grad_attended = project_back(self_branch, full_out).astype(jnp.bfloat16)
    grad_attended_heads = lax.all_to_all(
        grad_attended, "frame", split_axis=2, concat_axis=1, tiled=True
    ).reshape(head_shape)
    grad_query, grad_keys, grad_values = self_backward(
        query_heads, key_heads, value_heads, grad_attended_heads, self_sums, clip_len, key_valid
    )
    flat_shape = (clip_count, length, columns_here)
    grad_query, grad_keys, grad_values = (
        lax.all_to_all(
            grad_query.astype(jnp.bfloat16).reshape(flat_shape),
            "frame",
            split_axis=1,
            concat_axis=2,
            tiled=True,
        ),
        lax.all_to_all(
            grad_keys.astype(jnp.bfloat16).reshape(flat_shape),
            "frame",
            split_axis=1,
            concat_axis=2,
            tiled=True,
        ),
        lax.all_to_all(
            grad_values.astype(jnp.bfloat16).reshape(flat_shape),
            "frame",
            split_axis=1,
            concat_axis=2,
            tiled=True,
        ),
    )
    grad_self_qkv = jnp.stack(
        [
            weight_grad(first_low, grad_query),
            weight_grad(first_low, grad_keys),
            weight_grad(first_low, grad_values),
        ],
        axis=1,
    )
    grad_first_norm = (
        project_back(grad_query, full_qkv[:, 0])
        + project_back(grad_keys, full_qkv[:, 1])
        + project_back(grad_values, full_qkv[:, 2])
    )
    grad_first, gain_first, shift_first = first_pull(grad_first_norm)
    grad_hidden = (grad_after_self + grad_first).astype(jnp.bfloat16)
    grad_cross_qkv = jnp.stack([grad_cross_qw, grad_cross_key, grad_cross_value], axis=1)
    grad_gains = jnp.stack([gain_first, gain_second, gain_third])
    grad_shifts = jnp.stack([shift_first, shift_second, shift_third])
    attn_sums = sum_attention(
        grad_self_qkv, grad_self_out, grad_cross_qkv, grad_cross_out, grad_gains, grad_shifts
    )
    return (
        output,
        grad_hidden,
        grad_text,
        attn_sums[0],
        attn_sums[1],
        attn_sums[2],
        attn_sums[3],
        ffn_sums[0],
        ffn_sums[1],
        attn_sums[4],
        attn_sums[5],
    )


MESH = pl.DeviceIdType.MESH
HBM = pl.BlockSpec(memory_space=pl.ANY)
VMEM = pl.BlockSpec(memory_space=pltpu.VMEM)
SMEM = pl.BlockSpec(memory_space=pltpu.SMEM)
NEG = -1e30
F32 = jnp.float32
BF16 = jnp.bfloat16


def fits(mesh):
    return mesh.shape["clip"] == 4 and mesh.shape["frame"] == 8


class Here:
    def __init__(self):
        self.c = lax.axis_index("clip")
        self.f = lax.axis_index("frame")
        self.core = lax.rem(self.f, 2)
        self.z = lax.div(self.f, 2)
        self.pair = lax.div(self.z, 2)
        self.role = lax.rem(self.z, 2)
        self.group = lax.rem(self.f, 4)
        self.cx = self.c + 1 - 2 * lax.rem(self.c, 2)
        self.cy = lax.rem(self.c + 2, 4)
        self.cd = 3 - self.c
        self.sib = self.f + 1 - 2 * self.core
        self.partner = self.f + 2 - 4 * self.role
        self.far_gate = 2 * (2 - self.pair) + self.core
        self.is_gate = self.role + self.pair == 1
        self.far = [2 * (2 * (1 - self.pair) + j) + self.core for j in range(2)]

    def step(self, d):
        return lax.rem(self.f + d, 8)

    def zstep(self, d):
        return lax.rem(self.f + 2 * d, 8)


class Wire:
    def __init__(self, here, send_sem, recv_sem):
        self.here, self.send_sem, self.recv_sem = here, send_sem, recv_sem
        self.used = 0
        self.open = []

    def copy(self, src, dst, tag, c, f):
        self.used += 1
        return pltpu.make_async_remote_copy(
            src_ref=src,
            dst_ref=dst,
            send_sem=self.send_sem.at[self.used - 1],
            recv_sem=self.recv_sem.at[tag],
            device_id=(c, f),
            device_id_type=MESH,
        )

    def send(self, src, dst, tag, c, f):
        copy = self.copy(src, dst, tag, c, f)
        copy.start()
        self.open.append(copy)

    def arrived(self, dst, tag):
        pltpu.make_async_remote_copy(
            src_ref=dst,
            dst_ref=dst,
            send_sem=self.send_sem.at[0],
            recv_sem=self.recv_sem.at[tag],
            device_id=(self.here.c, self.here.sib),
            device_id_type=MESH,
        ).wait_recv()

    def drain(self):
        for copy in self.open:
            copy.wait_send()
        self.open = []


def greet(devices):
    barrier = pltpu.get_barrier_semaphore()
    for device in devices:
        pl.semaphore_signal(barrier, inc=1, device_id=device, device_id_type=MESH)
    pl.semaphore_wait(barrier, len(devices))


def frame_others(here):
    return [(here.c, here.step(d)) for d in range(1, 8)]


def clip_others(here):
    return [(here.cx, here.f), (here.cy, here.f), (here.cd, here.f)]


class ClipGather:
    def __init__(self, wire, block, tag):
        self.wire, self.block, self.tag = wire, block, tag

    def begin(self):
        h, w, b, t = self.wire.here, self.wire, self.block, self.tag
        w.send(b(h.c, 0), b(h.c, 0), t, h.cx, h.f)
        w.send(b(h.c, 1), b(h.c, 1), t + 2, h.cy, h.f)
        w.send(b(h.c, 1), b(h.c, 1), t + 1, h.cx, h.f)
        w.send(b(h.c, 0), b(h.c, 0), t + 3, h.cy, h.f)

    def middle(self):
        h, w, b, t = self.wire.here, self.wire, self.block, self.tag
        w.arrived(b(h.cx, 0), t)
        w.send(b(h.cx, 0), b(h.cx, 0), t + 4, h.cy, h.f)
        w.arrived(b(h.cy, 1), t + 2)
        w.send(b(h.cy, 1), b(h.cy, 1), t + 5, h.cx, h.f)

    def near(self):
        h, w, b, t = self.wire.here, self.wire, self.block, self.tag
        w.arrived(b(h.cx, 1), t + 1)
        w.arrived(b(h.cy, 0), t + 3)

    def end(self):
        h, w, b, t = self.wire.here, self.wire, self.block, self.tag
        w.arrived(b(h.cd, 0), t + 4)
        w.arrived(b(h.cd, 1), t + 5)


class ClipScatter:
    def __init__(self, wire, parts, slots, tag):
        self.wire, self.parts, self.slots, self.tag = wire, parts, slots, tag

    def begin(self):
        h, w, p, s, t = self.wire.here, self.wire, self.parts, self.slots, self.tag
        w.send(p(h.cd, 0), s[0], t, h.cx, h.f)
        w.send(p(h.cd, 1), s[1], t + 1, h.cy, h.f)
        w.send(p(h.cx, 0), s[2], t + 2, h.cx, h.f)
        w.send(p(h.cy, 1), s[3], t + 3, h.cy, h.f)

    def middle(self):
        h, w, p, s, t = self.wire.here, self.wire, self.parts, self.slots, self.tag
        w.arrived(s[0], t)
        add_into(s[0], p(h.cy, 0))
        w.send(s[0], s[4], t + 4, h.cy, h.f)
        w.arrived(s[1], t + 1)
        add_into(s[1], p(h.cx, 1))
        w.send(s[1], s[5], t + 5, h.cx, h.f)

    def end(self):
        w, s, t = self.wire, self.slots, self.tag
        for i in range(2, 6):
            w.arrived(s[i], t + i)

    def total(self, half):
        s = self.slots
        first, second = (s[2], s[4]) if half == 0 else (s[5], s[3])
        own = self.parts(self.wire.here.c, half)
        return own[...].astype(F32) + first[...].astype(F32) + second[...].astype(F32)


def add_into(into, other):
    into[...] = (into[...].astype(F32) + other[...].astype(F32)).astype(BF16)


def comm_call(body, out_shape, in_specs, out_specs, scratch, copies, tags, collective_id, cost=None):
    return pl.pallas_call(
        body,
        out_shape=out_shape,
        in_specs=in_specs,
        out_specs=out_specs,
        scratch_shapes=list(scratch)
        + [pltpu.SemaphoreType.DMA((copies,)), pltpu.SemaphoreType.DMA((tags,))],
        compiler_params=pltpu.CompilerParams(
            collective_id=collective_id, has_side_effects=True, vmem_limit_bytes=60 * 2**20
        ),
    )


def shape(dims, dtype=BF16):
    return jax.ShapeDtypeStruct(dims, dtype)


def fetch_body(hid, w5, square, grad, fin, o_hid, o_w5, o_square, o_grad, o_fin, local, send_sem, recv_sem):
    h = Here()
    w = Wire(h, send_sem, recv_sem)
    greet(frame_others(h) + clip_others(h))
    T_HID, T_W, T_FIN, T_ZL, T_ZR = 0, 7, 14, 17, 20
    T_WXY, T_GXY, T_SXY, T_SIB = 23, 29, 35, 59

    def my_columns(f):
        return pl.ds(pl.multiple_of(lax.rem(f, 4) * 256, 256), 256)

    def my_rows(f):
        return pl.ds(pl.multiple_of(f * 32, 32), 32)

    here_copies = [
        pltpu.make_async_copy(hid.at[h.pair], o_hid.at[h.f], local.at[0]),
        pltpu.make_async_copy(
            w5.at[:, :, my_columns(h.f)], o_w5.at[:, h.c, my_rows(h.f), :], local.at[1]
        ),
        pltpu.make_async_copy(square, o_square.at[h.c, h.f], local.at[2]),
        pltpu.make_async_copy(grad, o_grad.at[h.c], local.at[3]),
        pltpu.make_async_copy(
            fin.at[:, pl.ds(pl.multiple_of(h.c * 1024, 1024), 1024)], o_fin.at[h.c], local.at[4]
        ),
    ]
    w.send(hid.at[h.pair], o_hid.at[h.f], T_HID + 1, h.c, h.partner)
    far_tag = T_HID + 2 + h.role
    w.send(hid.at[1 - h.pair], o_hid.at[h.f], far_tag, h.c, h.far_gate)
    w.send(hid.at[h.pair], o_hid.at[h.f], T_HID, h.c, h.sib)
    for d in range(1, 8):
        f = h.step(d)
        w.send(w5.at[:, :, my_columns(f)], o_w5.at[:, h.c, my_rows(h.f), :], T_W + d - 1, h.c, f)
    for copy in here_copies:
        copy.start()
    for i, (c, f) in enumerate(clip_others(h)):
        w.send(
            fin.at[:, pl.ds(pl.multiple_of(c * 1024, 1024), 1024)], o_fin.at[h.c], T_FIN + i, c, f
        )
    for copy in here_copies:
        copy.wait()
    def square_slot(c, f):
        return o_square.at[c, f]

    z_copies = []

    def z_step(s):
        if s > 1:
            @pl.when(h.z - (s - 1) >= 0)
            def _():
                w.arrived(square_slot(h.c, h.f - 2 * (s - 1)), T_ZL + s - 2)

            @pl.when(h.z + (s - 1) <= 3)
            def _():
                w.arrived(square_slot(h.c, h.f + 2 * (s - 1)), T_ZR + s - 2)

        if s > 3:
            return
        right_block = h.f - 2 * (s - 1)
        left_block = h.f + 2 * (s - 1)
        go_right = (right_block >= 0) & (h.z <= 2)
        go_left = (left_block <= 7) & (h.z >= 1)
        right = w.copy(
            square_slot(h.c, right_block), square_slot(h.c, right_block), T_ZL + s - 1, h.c, h.f + 2
        )
        left = w.copy(
            square_slot(h.c, left_block), square_slot(h.c, left_block), T_ZR + s - 1, h.c, h.f - 2
        )
        for go, copy in ((go_right, right), (go_left, left)):
            pl.when(go)(copy.start)
            z_copies.append((go, copy))

    z_step(1)
    for d in range(1, 8):
        f = lax.rem(h.f + 8 - d, 8)
        w.arrived(o_w5.at[:, h.c, my_rows(f), :], T_W + d - 1)
    w5_gather = ClipGather(w, lambda c, half: o_w5.at[:, c, pl.ds(128 * half, 128), :], T_WXY)
    w5_gather.begin()
    w.arrived(o_hid.at[h.partner], T_HID + 1)
    w.send(o_hid.at[h.partner], o_hid.at[h.partner], T_HID + 4, h.c, h.sib)
    forwards = []
    for j in range(2):
        block = o_hid.at[h.far[j]]
        w.arrived(block, T_HID + 2 + j)
        forward = w.copy(block, block, T_HID + 2 + j, h.c, h.partner)
        pl.when(h.is_gate)(forward.start)
        forwards.append(forward)
        w.send(block, block, T_HID + 5 + j, h.c, h.sib)
    w5_gather.middle()
    z_step(2)

    def square_gather(d):
        f = h.zstep(d)
        return ClipGather(
            w,
            lambda c, half: o_square.at[c, f, pl.ds(64 * half, 64 - 16 * half), :],
            T_SXY + 6 * d,
        )

    gathers = [square_gather(d) for d in range(4)]
    gathers[0].begin()
    grad_gather = ClipGather(w, lambda c, half: o_grad.at[c, pl.ds(128 * half, 128), :], T_GXY)
    grad_gather.begin()
    z_step(3)
    z_step(4)
    for d in range(1, 4):
        gathers[d].begin()
    grad_gather.middle()
    for d in range(4):
        f = h.zstep(d)
        w.send(square_slot(h.c, f), square_slot(h.c, f), T_SIB + 4 * d, h.c, h.sib)
        gathers[d].middle()
        gathers[d].near()
        w.send(square_slot(h.cx, f), square_slot(h.cx, f), T_SIB + 4 * d + 1, h.c, h.sib)
        w.send(square_slot(h.cy, f), square_slot(h.cy, f), T_SIB + 4 * d + 2, h.c, h.sib)
    for d in range(4):
        f = h.zstep(d)
        gathers[d].end()
        w.send(square_slot(h.cd, f), square_slot(h.cd, f), T_SIB + 4 * d + 3, h.c, h.sib)
    w5_gather.near()
    w5_gather.end()
    grad_gather.near()
    grad_gather.end()
    for i, (c, f) in enumerate(clip_others(h)):
        w.arrived(o_fin.at[c], T_FIN + i)
    w.arrived(o_hid.at[h.sib], T_HID)
    w.arrived(o_hid.at[h.partner + h.sib - h.f], T_HID + 4)
    for j in range(2):
        w.arrived(o_hid.at[h.far[j] + h.sib - h.f], T_HID + 5 + j)
    for d in range(4):
        f = h.zstep(d) + h.sib - h.f
        for i, c in enumerate((h.c, h.cx, h.cy, h.cd)):
            w.arrived(square_slot(c, f), T_SIB + 4 * d + i)
    w.drain()
    for go, copy in z_copies:
        pl.when(go)(copy.wait_send)
    for copy in forwards:
        pl.when(h.is_gate)(copy.wait_send)


def fetch(hid, w5, square, grad, fin):
    return comm_call(
        fetch_body,
        (
            shape((8, 128, 1024)),
            shape((5, 4, 256, 256)),
            shape((4, 8, 112, 1024)),
            shape((4, 256, 1024)),
            shape((4, 32, 1024)),
        ),
        [HBM] * 5,
        (HBM,) * 5,
        [pltpu.SemaphoreType.DMA((5,))],
        96,
        80,
        1,
    )(hid, w5, square, grad, fin)


ROWS = 256


def dot(left, right, contract):
    return lax.dot_general(left, right, ((contract[:1], contract[1:]), ((), ())), preferred_element_type=F32)


def mask_scores(scores, bias_ref, first, rows):
    low = scores[first:] + bias_ref[first : first + rows, 0:1]
    key = lax.broadcasted_iota(jnp.int32, (rows, rows), 0)
    query = lax.broadcasted_iota(jnp.int32, (rows, rows), 1)
    low = jnp.where(key < query, low, jnp.where(key == query, scores[first:], NEG))
    if first == 0:
        return low
    return jnp.concatenate([scores[:first] + bias_ref[0:first, 0:1], low], axis=0)


def attend_body(length, bias, q_ref, k_ref, v_ref, o_ref, lse_ref, out_t, v_t):
    v_t[...] = v_ref[...].T
    lane_head = lax.broadcasted_iota(jnp.int32, (ROWS, 256), 1) // HD
    for i in range(1024 // ROWS):
        first, n = i * ROWS, (i + 1) * ROWS
        q = q_ref[first:n, :]

        def head(j, _):
            q_head = jnp.where(lane_head == j, q, 0) * jnp.asarray(HD**-0.5, BF16)
            scores = mask_scores(dot(k_ref[0:n, :], q_head, (1, 1)), bias, first, ROWS)
            top = jnp.max(scores, axis=0, keepdims=True)
            weight = jnp.exp(scores - top)
            total = jnp.sum(weight, axis=0, keepdims=True)
            at = pl.ds(pl.multiple_of(j * HD, HD), HD)
            part = dot(v_t[at, 0:n], weight.astype(BF16), (1, 0))
            out_t[at, :] = part / total
            lse_ref[pl.ds(j, 1), first:n] = top + jnp.log(total)
            return 0

        lax.fori_loop(0, 4, head, 0)
        live = first + lax.broadcasted_iota(jnp.int32, (ROWS, 256), 0) < length[0]
        o_ref[first:n, :] = jnp.where(live, out_t[...].T, 0).astype(BF16)


def attend(length, bias, q, k, v):
    return pl.pallas_call(
        attend_body,
        out_shape=(shape((1024, 256)), shape((8, 1024), F32)),
        in_specs=[SMEM] + [VMEM] * 4,
        out_specs=(VMEM, VMEM),
        scratch_shapes=[pltpu.VMEM((256, ROWS), F32), pltpu.VMEM((256, 1024), BF16)],
        compiler_params=pltpu.CompilerParams(vmem_limit_bytes=56 * 2**20),
    )(length, bias, q, k, v)


def attend_back_body(
    length, bias, q_ref, k_ref, v_ref, o_ref, lse_ref, g_ref, dq_ref, dk_ref, dv_ref, dq_t, k_t, dk, dv
):
    k_t[...] = k_ref[...].T
    lane_head = lax.broadcasted_iota(jnp.int32, (ROWS, 256), 1) // HD
    dk[...] = jnp.zeros_like(dk)
    dv[...] = jnp.zeros_like(dv)
    for i in range(1024 // ROWS):
        first, n = i * ROWS, (i + 1) * ROWS
        q = q_ref[first:n, :] * jnp.asarray(HD**-0.5, BF16)
        live = first + lax.broadcasted_iota(jnp.int32, (ROWS, 256), 0) < length[0]
        g = jnp.where(live, g_ref[first:n, :], 0)
        both = (g.astype(F32) * o_ref[first:n, :].astype(F32)).T
        row_dots = jnp.concatenate(
            [jnp.sum(both[HD * j : HD * j + HD], axis=0, keepdims=True) for j in range(4)], axis=0
        )
        lse = lse_ref[0:4, first:n]

        def pick(rows, j):
            at = lax.broadcasted_iota(jnp.int32, rows.shape, 0) == j
            return jnp.sum(jnp.where(at, rows, 0), axis=0, keepdims=True)

        def head(j, _):
            q_head = jnp.where(lane_head == j, q, 0)
            g_head = jnp.where(lane_head == j, g, 0)
            scores = mask_scores(dot(k_ref[0:n, :], q_head, (1, 1)), bias, first, ROWS)
            probs = jnp.exp(scores - pick(lse, j))
            grads = dot(v_ref[0:n, :], g_head, (1, 1))
            dlogits = (probs * (grads - pick(row_dots, j))).astype(BF16)
            dv[0:n, :] += dot(probs.astype(BF16), g_head, (1, 0))
            dk[0:n, :] += dot(dlogits, q_head, (1, 0))
            at = pl.ds(pl.multiple_of(j * HD, HD), HD)
            dq_t[at, :] = dot(k_t[at, 0:n], dlogits, (1, 0))
            return 0

        lax.fori_loop(0, 4, head, 0)
        dq_ref[first:n, :] = (dq_t[...].T * (HD**-0.5)).astype(BF16)
    dk_ref[...] = dk[...].astype(BF16)
    dv_ref[...] = dv[...].astype(BF16)


def attend_back(length, bias, q, k, v, o, lse, g):
    return pl.pallas_call(
        attend_back_body,
        out_shape=(shape((1024, 256)),) * 3,
        in_specs=[SMEM] + [VMEM] * 7,
        out_specs=(VMEM,) * 3,
        scratch_shapes=[
            pltpu.VMEM((256, ROWS), F32),
            pltpu.VMEM((256, 1024), BF16),
            pltpu.VMEM((1024, 256), F32),
            pltpu.VMEM((1024, 256), F32),
        ],
        compiler_params=pltpu.CompilerParams(vmem_limit_bytes=56 * 2**20),
    )(length, bias, q, k, v, o, lse, g)


def return_body(att, tkv, o_att, o_tkv, local, send_sem, recv_sem):
    h = Here()
    w = Wire(h, send_sem, recv_sem)
    greet(frame_others(h))

    def slot(f):
        return o_att.at[lax.div(f, 4), :, pl.ds(pl.multiple_of(lax.rem(f, 4) * 256, 256), 256)]

    def text_slot(f):
        return o_tkv.at[lax.div(f, 4), :, :, pl.ds(pl.multiple_of(lax.rem(f, 4) * 256, 256), 256)]

    for d in range(1, 8):
        f = h.step(d)
        w.send(att.at[f], slot(h.f), d - 1, h.c, f)
    copies = [
        pltpu.make_async_copy(att.at[h.f], slot(h.f), local.at[0]),
        pltpu.make_async_copy(tkv, text_slot(h.f), local.at[1]),
    ]
    for copy in copies:
        copy.start()
    for d in range(1, 4):
        w.send(tkv, text_slot(h.f), 7 + d, h.c, h.zstep(d))
    w.send(tkv, text_slot(h.f), 11, h.c, h.sib)
    for d in range(1, 4):
        f = lax.rem(h.f + 8 - 2 * d, 8)
        w.arrived(text_slot(f), 7 + d)
        w.send(text_slot(f), text_slot(f), 11 + d, h.c, h.sib)
    for d in range(1, 8):
        w.arrived(slot(lax.rem(h.f + 8 - d, 8)), d - 1)
    w.arrived(text_slot(h.sib), 11)
    for d in range(1, 4):
        w.arrived(text_slot(lax.rem(h.sib + 8 - 2 * d, 8)), 11 + d)
    for copy in copies:
        copy.wait()
    w.drain()


def give_back(att, tkv):
    return comm_call(
        return_body,
        (shape((2, 128, 1024)), shape((2, 2, 128, 1024))),
        [HBM] * 2,
        (HBM,) * 2,
        [pltpu.SemaphoreType.DMA((2,))],
        16,
        16,
        2,
    )(att, tkv)


def norm_parts(value):
    centered = value - jnp.mean(value, axis=-1, keepdims=True)
    scale = lax.rsqrt(jnp.mean(centered * centered, axis=-1, keepdims=True) + EPSILON)
    return centered * scale, scale


def square_of(square, which):
    return square[:, 32 * which : 32 * which + 32, :].reshape(1024, 1024)


def text_probs(query, keys, bias, lane_head):
    heads = [jnp.where(lane_head == j, query, 0) for j in range(4)]
    stacked = jnp.concatenate(heads, axis=0)
    scores = dot(stacked, keys, (1, 1)) + bias
    weight = jnp.exp(scores - jnp.max(scores, axis=1, keepdims=True))
    return weight / jnp.sum(weight, axis=1, keepdims=True), stacked


def pick_heads(stacked, lane_head):
    return sum(jnp.where(lane_head == j, stacked[128 * j : 128 * j + 128], 0) for j in range(4))


def middle_body(
    hid, att, square, tkv, text_bias, params, o_self, second_ref, query_ref, crossed_ref, o_cross, third_ref
):
    att_value = att[...].reshape(256, 1024)
    after_self = hid[...].reshape(256, 1024).astype(F32) + dot(att_value, square_of(square, 0), (1, 0))
    o_self[...] = after_self
    xhat, _ = norm_parts(after_self)
    second_ref[...] = (xhat * params[1:2, :] + params[4:5, :]).astype(BF16)
    query_ref[...] = dot(second_ref[...], square_of(square, 1), (1, 0)).astype(BF16)
    lane_head = lax.broadcasted_iota(jnp.int32, (128, 256), 1) // HD
    for clip in range(2):
        for group in range(4):
            rows, columns = pl.ds(128 * clip, 128), pl.ds(256 * group, 256)
            query = query_ref[rows, columns] * jnp.asarray(HD**-0.5, BF16)
            probs, _ = text_probs(query, tkv[clip, 0, :, columns], text_bias[clip : clip + 1, :], lane_head)
            part = dot(probs.astype(BF16), tkv[clip, 1, :, columns], (1, 0))
            crossed_ref[rows, columns] = pick_heads(part, lane_head).astype(BF16)
    after_cross = after_self + dot(crossed_ref[...], square_of(square, 2), (1, 0))
    o_cross[...] = after_cross
    xhat, _ = norm_parts(after_cross)
    third_ref[...] = (xhat * params[2:3, :] + params[5:6, :]).astype(BF16)


def middle(hid, att, square, tkv, text_bias, params):
    rows = (256, 1024)
    return pl.pallas_call(
        middle_body,
        out_shape=(shape(rows, F32), shape(rows), shape(rows), shape(rows), shape(rows, F32), shape(rows)),
        in_specs=[VMEM] * 6,
        out_specs=(VMEM,) * 6,
        compiler_params=pltpu.CompilerParams(vmem_limit_bytes=56 * 2**20),
    )(hid, att, square, tkv, text_bias, params)


def norm_back(xhat, scale, grad, gain):
    h = grad * gain
    return scale * (
        h
        - jnp.mean(h, axis=-1, keepdims=True)
        - xhat * jnp.mean(h * xhat, axis=-1, keepdims=True)
    )


def middle_back_body(
    g_third, g_out, after_cross, after_self, second, query_ref, crossed, att, square, tkv, text_bias, params,
    o_after_self, o_square, o_att, o_text, o_norm, g_crossed, g_query,
):
    def put(which, value):
        o_square[:, 32 * which : 32 * which + 32, :] = value.astype(BF16).reshape(32, 32, 1024)

    xhat, scale = norm_parts(after_cross[...])
    grad = g_third[...]
    o_norm[0:1, :] = jnp.sum(grad * xhat, axis=0, keepdims=True)
    o_norm[1:2, :] = jnp.sum(grad, axis=0, keepdims=True)
    g_after_cross = g_out[...].reshape(256, 1024).astype(F32) + norm_back(xhat, scale, grad, params[2:3, :])
    branch = g_after_cross.astype(BF16)
    put(2, dot(crossed[...], branch, (0, 0)))
    g_crossed[...] = dot(branch, square_of(square, 2), (1, 1)).astype(BF16)
    lane_head = lax.broadcasted_iota(jnp.int32, (128, 256), 1) // HD
    for clip in range(2):
        for group in range(4):
            rows, columns = pl.ds(128 * clip, 128), pl.ds(256 * group, 256)
            keys, values = tkv[clip, 0, :, columns], tkv[clip, 1, :, columns]
            query = query_ref[rows, columns] * jnp.asarray(HD**-0.5, BF16)
            probs, stacked = text_probs(query, keys, text_bias[clip : clip + 1, :], lane_head)
            grads = g_crossed[rows, columns]
            g_stacked = jnp.concatenate([jnp.where(lane_head == j, grads, 0) for j in range(4)], axis=0)
            g_probs = dot(g_stacked, values, (1, 1))
            row_dot = jnp.sum(probs * g_probs, axis=1, keepdims=True)
            g_logits = (probs * (g_probs - row_dot)).astype(BF16)
            part = dot(g_logits, keys, (1, 0))
            g_query[rows, columns] = (pick_heads(part, lane_head) * (HD**-0.5)).astype(BF16)
            o_text[clip, 0, :, columns] = dot(g_logits, stacked, (0, 0)).astype(BF16)
            o_text[clip, 1, :, columns] = dot(probs.astype(BF16), g_stacked, (0, 0)).astype(BF16)
    put(1, dot(second[...], g_query[...], (0, 0)))
    grad = dot(g_query[...], square_of(square, 1), (1, 1))
    xhat, scale = norm_parts(after_self[...])
    o_norm[2:3, :] = jnp.sum(grad * xhat, axis=0, keepdims=True)
    o_norm[3:4, :] = jnp.sum(grad, axis=0, keepdims=True)
    g_after_self = g_after_cross + norm_back(xhat, scale, grad, params[1:2, :])
    o_after_self[...] = g_after_self
    branch = g_after_self.astype(BF16)
    put(0, dot(att[...].reshape(256, 1024), branch, (0, 0)))
    o_att[...] = dot(branch, square_of(square, 0), (1, 1)).astype(BF16).reshape(2, 128, 1024)


def middle_back(*args):
    return pl.pallas_call(
        middle_back_body,
        out_shape=(
            shape((256, 1024), F32),
            shape((32, 96, 1024)),
            shape((2, 128, 1024)),
            shape((2, 2, 128, 1024)),
            shape((8, 1024), F32),
        ),
        in_specs=[VMEM] * 12,
        out_specs=(VMEM,) * 5,
        scratch_shapes=[pltpu.VMEM((256, 1024), BF16)] * 2,
        compiler_params=pltpu.CompilerParams(vmem_limit_bytes=60 * 2**20),
    )(*args)


def clip_gather_body(block, out, local, send_sem, recv_sem):
    h = Here()
    w = Wire(h, send_sem, recv_sem)
    greet(clip_others(h)[:2])
    copy = pltpu.make_async_copy(block, out.at[h.c], local.at[0])
    copy.start()
    copy.wait()
    gather = ClipGather(w, lambda c, half: out.at[c, pl.ds(128 * half, 128), :], 0)
    gather.begin()
    gather.middle()
    gather.near()
    gather.end()
    w.drain()


def clip_gather(block):
    return comm_call(
        clip_gather_body,
        shape((4, 256, 1024)),
        [HBM],
        HBM,
        [pltpu.SemaphoreType.DMA((1,))],
        6,
        6,
        3,
    )(block)


def clip_scatter_body(first, second, o_first, o_second, slots, send_sem, recv_sem):
    h = Here()
    w = Wire(h, send_sem, recv_sem)
    greet(clip_others(h)[:2])
    scatters = []
    for i, terms in enumerate((first, second)):
        scatters.append(
            ClipScatter(
                w,
                lambda c, half, terms=terms: terms.at[c, pl.ds(128 * half, 128), :],
                [slots.at[i, j] for j in range(6)],
                6 * i,
            )
        )
    for one in scatters:
        one.begin()
    for one in scatters:
        one.middle()
    for one, out in zip(scatters, (o_first, o_second)):
        one.end()
        for half in range(2):
            out[128 * half : 128 * half + 128, :] = one.total(half)
    w.drain()


def clip_scatter(first, second):
    return comm_call(
        clip_scatter_body,
        (shape((256, 1024), F32),) * 2,
        [VMEM] * 2,
        (VMEM,) * 2,
        [pltpu.VMEM((2, 6, 128, 1024), BF16)],
        12,
        12,
        4,
    )(first, second)


def forth_body(g_att, text, o_att, o_text, sums, from_sib, from_z, local, send_sem, recv_sem):
    h = Here()
    w = Wire(h, send_sem, recv_sem)
    greet(frame_others(h))

    def columns(f):
        return pl.ds(pl.multiple_of(lax.rem(f, 4) * 256, 256), 256)

    def part(f):
        return g_att.at[lax.div(f, 4), :, columns(f)]

    def text_part(f):
        return text.at[lax.div(f, 4), :, :, columns(f)]

    for z in range(4):
        w.send(text_part(2 * z + 1 - h.core), from_sib.at[z], 8 + z, h.c, h.sib)
    for d in range(1, 8):
        f = h.step(d)
        w.send(part(f), o_att.at[h.f], d - 1, h.c, f)
    copy = pltpu.make_async_copy(part(h.f), o_att.at[h.f], local.at[0])
    copy.start()
    for z in range(4):
        w.arrived(from_sib.at[z], 8 + z)
        mine = text_part(2 * z + h.core)
        sums[z] = (mine[...].astype(F32) + from_sib[z].astype(F32)).astype(BF16)
    for d in range(1, 4):
        w.send(sums.at[lax.rem(h.z + d, 4)], from_z.at[d - 1], 11 + d, h.c, h.zstep(d))
    for d in range(1, 4):
        w.arrived(from_z.at[d - 1], 11 + d)
    total = sums[h.z].astype(F32)
    for d in range(3):
        total = total + from_z[d].astype(F32)
    o_text[...] = total.astype(BF16)
    for d in range(1, 8):
        w.arrived(o_att.at[lax.rem(h.f + 8 - d, 8)], d - 1)
    copy.wait()
    w.drain()


def give_forth(g_att, text):
    block = (2, 128, 256)
    return comm_call(
        forth_body,
        (shape((8, 128, 256)), shape(block)),
        [VMEM] * 2,
        (VMEM,) * 2,
        [
            pltpu.VMEM((4,) + block, BF16),
            pltpu.VMEM((4,) + block, BF16),
            pltpu.VMEM((3,) + block, BF16),
            pltpu.SemaphoreType.DMA((1,)),
        ],
        16,
        16,
        5,
    )(g_att, text)


def last_body(
    first, square, cols, text, o_first, o_square, o_cols, o_norm, o_text,
    f_sib, f_sum, f_in, s_sib, s_sum, s_slots, s_z, s_zin, c_slots, c_sum, c_in, t_in,
    send_sem, recv_sem,
):
    h = Here()
    w = Wire(h, send_sem, recv_sem)
    greet(frame_others(h) + clip_others(h)[:2])
    T_F, T_S, T_C, T_T = 0, 12, 24, 40
    for z in range(4):
        w.send(first.at[2 * z + 1 - h.core], f_sib.at[z], T_F + z, h.c, h.sib)
    for z in range(4):
        w.send(square.at[:, 2 * z + 1 - h.core], s_sib.at[:, z], T_S + z, h.c, h.sib)
    cols_scatter = ClipScatter(
        w,
        lambda c, half: cols.at[c, pl.ds(4 * half, 4)],
        [c_slots.at[i] for i in range(6)],
        T_C,
    )
    cols_scatter.begin()
    for d in range(1, 8):
        f = h.step(d)
        w.send(text.at[pl.ds(pl.multiple_of(f * 16, 16), 16), :], t_in.at[h.f], T_T + d - 1, h.c, f)
    t_in[h.f] = text[pl.ds(pl.multiple_of(h.f * 16, 16), 16), :]
    for z in range(4):
        w.arrived(f_sib.at[z], T_F + z)
        f_sum[z] = (first[2 * z + h.core].astype(F32) + f_sib[z].astype(F32)).astype(BF16)
    other = 2 * (1 - h.pair)
    is_end = jnp.logical_not(h.is_gate)
    w.send(f_sum.at[lax.div(h.partner, 2)], f_in.at[0], T_F + 4, h.c, h.partner)
    to_gate, to_far = [], []
    for j in range(2):
        to_gate.append(w.copy(f_sum.at[other + j], f_in.at[1 + j], T_F + 5 + j, h.c, h.partner))
        pl.when(is_end)(to_gate[j].start)
    for z in range(4):
        w.arrived(s_sib.at[:, z], T_S + z)

    def add_square(i, _):
        c, z = lax.div(i, 4), lax.rem(i, 4)
        s_sum[c, z] = (square[c, 2 * z + h.core].astype(F32) + s_sib[c, z].astype(F32)).astype(BF16)
        return 0

    lax.fori_loop(0, 16, add_square, 0)
    square_scatter = ClipScatter(
        w,
        lambda c, half: s_sum.at[c, :, pl.ds(48 * half, 48), :],
        [s_slots.at[i] for i in range(6)],
        T_S + 4,
    )
    square_scatter.begin()
    for j in range(2):
        @pl.when(h.is_gate)
        def _():
            w.arrived(f_in.at[1 + j], T_F + 5 + j)
            f_sum[other + j] = (f_sum[other + j].astype(F32) + f_in[1 + j].astype(F32)).astype(BF16)

        to_far.append(w.copy(f_sum.at[other + j], f_in.at[3], T_F + 7, h.c, h.far[j]))
        pl.when(h.is_gate)(to_far[j].start)
    cols_scatter.middle()
    square_scatter.middle()
    cols_scatter.end()
    for half in range(2):
        c_sum[4 * half : 4 * half + 4] = cols_scatter.total(half).astype(BF16)
    for d in range(1, 8):
        f = h.step(d)
        w.send(c_sum.at[f], c_in.at[h.f], T_C + 6 + d - 1, h.c, f)
    c_in[h.f] = c_sum[h.f]
    square_scatter.end()
    for half in range(2):
        s_z[:, 48 * half : 48 * half + 48, :] = square_scatter.total(half).astype(BF16)
    for d in range(1, 4):
        w.send(s_z.at[lax.rem(h.z + d, 4)], s_zin.at[d - 1], T_S + 10 + d - 1 if d < 3 else 47, h.c, h.zstep(d))
    w.arrived(f_in.at[0], T_F + 4)
    w.arrived(f_in.at[3], T_F + 7)
    o_first[h.pair] = f_sum[h.z].astype(F32) + f_in[0].astype(F32)
    o_first[1 - h.pair] = f_in[3].astype(F32)
    for d in range(1, 8):
        w.arrived(t_in.at[lax.rem(h.f + 8 - d, 8)], T_T + d - 1)
    for p in range(2):
        o_text[p] = sum(t_in[4 * p + q].astype(F32) for q in range(4)).astype(BF16)
    for d in range(1, 8):
        w.arrived(c_in.at[lax.rem(h.f + 8 - d, 8)], T_C + 6 + d - 1)
    for q in range(4):
        o_cols[:, 256 * q : 256 * q + 256] = c_in[q, 0:160, :].astype(F32) + c_in[4 + q, 0:160, :].astype(F32)
    o_norm[...] = sum(c_in[f, 160:176, 0:128].astype(F32) for f in range(8))
    for d in range(1, 4):
        w.arrived(s_zin.at[d - 1], T_S + 10 + d - 1 if d < 3 else 47)
    o_square[...] = s_z[h.z].astype(F32) + sum(s_zin[d].astype(F32) for d in range(3))
    w.drain()
    for j in range(2):
        pl.when(is_end)(to_gate[j].wait_send)
        pl.when(h.is_gate)(to_far[j].wait_send)


def last_sums(first, square, cols, text):
    def buffer(*dims):
        return pltpu.VMEM(dims, BF16)

    return comm_call(
        last_body,
        (
            shape((2, 128, 1024), F32),
            shape((96, 1024), F32),
            shape((160, 1024), F32),
            shape((16, 128), F32),
            shape((2, 16, 1024)),
        ),
        [VMEM] * 4,
        (VMEM,) * 5,
        [
            buffer(4, 128, 1024),
            buffer(4, 128, 1024),
            buffer(4, 128, 1024),
            buffer(4, 4, 96, 1024),
            buffer(4, 4, 96, 1024),
            buffer(6, 4, 48, 1024),
            buffer(4, 96, 1024),
            buffer(3, 96, 1024),
            buffer(6, 4, 176, 256),
            buffer(8, 176, 256),
            buffer(8, 176, 256),
            buffer(8, 16, 1024),
        ],
        64,
        48,
        6,
    )(first, square, cols, text)


def matmul(left, right):
    return jnp.dot(left, right, preferred_element_type=F32)


def on_device_fast(
    hidden_in,
    text_states,
    out_grad,
    self_qkv,
    self_out,
    cross_qkv,
    cross_out,
    ffn_in,
    ffn_out,
    ln_gain,
    ln_bias,
    clip_len,
    frame_mask,
    text_len,
    text_mask,
):
    frame = lax.axis_index("frame")
    pair = frame // 4
    w5 = jnp.concatenate([jnp.moveaxis(self_qkv, 1, 0), jnp.moveaxis(cross_qkv, 1, 0)[1:]], axis=0)
    norms = jnp.concatenate([ln_gain, ln_bias], axis=0).reshape(1, 192)
    square_here = jnp.concatenate(
        [self_out, cross_qkv[:, 0], cross_out, jnp.pad(norms, ((0, 15), (0, 832)))], axis=0
    )
    hid_all, w_all, square_all, grad_all, fin_all = fetch(
        hidden_in, w5, square_here, out_grad.reshape(256, 1024), ffn_in
    )
    square = square_all.reshape(32, 112, 1024)
    params = square[:, 96, :192].reshape(32, 6, 32).transpose(1, 0, 2).reshape(6, 1024).astype(F32)
    params = jnp.pad(params, ((0, 2), (0, 0)))
    weights = w_all.reshape(5, 1024, 256)
    ffn_w_out = lax.all_gather(ffn_out, "frame", axis=0, tiled=True)
    ffn_w_in = (
        lax.all_gather(fin_all, "frame", axis=0).transpose(1, 0, 2, 3).reshape(1024, 1024)
    )
    clip_x = hid_all.reshape(1024, 1024).astype(F32)
    first_hat, first_scale = norm_parts(clip_x)
    first_low = (first_hat * params[0:1] + params[3:4]).astype(BF16)
    query, key, value = (matmul(first_low, weights[i]).astype(BF16) for i in range(3))
    columns = jnp.arange(1024, dtype=jnp.int32)
    my_len = lax.dynamic_slice_in_dim(clip_len, pair, 1, 0)
    my_mask = lax.dynamic_slice_in_dim(frame_mask, pair, 1, 0)[0]
    bias = jnp.where((columns < my_len) & (my_mask > 0), 0.0, NEG).astype(F32)
    bias = jnp.broadcast_to(bias[:, None], (1024, 128))
    att_heads, lse = attend(my_len, bias, query, key, value)
    my_text = lax.dynamic_slice_in_dim(text_states, pair, 1, 0)[0]
    text_kv = jnp.stack([matmul(my_text, weights[3]), matmul(my_text, weights[4])]).astype(BF16)
    att, tkv = give_back(att_heads.reshape(8, 128, 256), text_kv)
    slots = jnp.arange(128, dtype=jnp.int32)
    text_ok = (slots[None] < text_len[:, None]) & ((text_mask > 0) | (slots[None] == 0))
    text_bias = jnp.where(text_ok, 0.0, NEG).astype(F32)
    after_self, second, cross_query, crossed, after_cross, third = middle(
        hidden_in, att, square, tkv, text_bias, params
    )
    third_all = clip_gather(third).reshape(1024, 1024)
    grad_tokens = grad_all.reshape(1024, 1024)
    pre_act = matmul(third_all, ffn_w_in)
    activated, gelu_pull = jax.vjp(activate, pre_act)
    inner = activated.astype(BF16)
    out_terms = matmul(inner, ffn_w_out).astype(BF16)
    (grad_pre,) = gelu_pull(lax.dot_general(grad_tokens, ffn_w_out, (((1,), (1,)), ((), ())), preferred_element_type=F32))
    grad_pre = grad_pre.astype(BF16)
    third_terms = lax.dot_general(grad_pre, ffn_w_in, (((1,), (1,)), ((), ())), preferred_element_type=F32).astype(BF16)
    out_sum, third_sum = clip_scatter(out_terms.reshape(4, 256, 1024), third_terms.reshape(4, 256, 1024))
    output = (after_cross + out_sum).astype(BF16).reshape(2, 128, 1024)
    g_ffn_out = lax.dot_general(inner, grad_tokens, (((0,), (0,)), ((), ())), preferred_element_type=F32).astype(BF16)
    g_ffn_in = lax.dot_general(third_all, grad_pre, (((0,), (0,)), ((), ())), preferred_element_type=F32).astype(BF16)
    ffn_terms = jnp.concatenate(
        [
            g_ffn_out.reshape(8, 128, 1024),
            g_ffn_in.reshape(4, 8, 32, 1024).transpose(1, 0, 2, 3).reshape(8, 128, 1024),
        ],
        axis=1,
    )
    ffn_sum = lax.psum_scatter(ffn_terms, "frame", scatter_dimension=0, tiled=True)[0]
    grad_ffn_out = ffn_sum[:128].astype(F32)
    grad_ffn_in = lax.all_to_all(
        ffn_sum[128:].reshape(4, 32, 1024), "clip", split_axis=0, concat_axis=2, tiled=True
    )[0].astype(F32)
    g_after_self, g_square, g_att, g_text, g_norms = middle_back(
        third_sum, out_grad, after_cross, after_self, second, cross_query, crossed, att, square, tkv,
        text_bias, params,
    )
    g_heads, g_tkv = give_forth(g_att, g_text)
    g_query, g_key, g_value = attend_back(
        my_len, bias, query, key, value, att_heads, lse, g_heads.reshape(1024, 256)
    )

    def back(grad, weight):
        return lax.dot_general(grad, weight, (((1,), (1,)), ((), ())), preferred_element_type=F32)

    def weight_term(left, grad):
        return lax.dot_general(left, grad, (((0,), (0,)), ((), ())), preferred_element_type=F32)

    g_first = back(g_query, weights[0]) + back(g_key, weights[1]) + back(g_value, weights[2])
    gain_first = jnp.sum(g_first * first_hat, axis=0)
    shift_first = jnp.sum(g_first, axis=0)
    text_terms = (back(g_tkv[0], weights[3]) + back(g_tkv[1], weights[4])).astype(BF16)
    terms = jnp.stack(
        [weight_term(first_low, g) for g in (g_query, g_key, g_value)]
        + [weight_term(my_text, g_tkv[i]) for i in range(2)]
    )
    terms = terms.astype(BF16).reshape(5, 4, 8, 32, 256).transpose(1, 2, 0, 3, 4).reshape(4, 8, 160, 256)
    norm_terms = jnp.stack([gain_first, g_norms[2], g_norms[0], shift_first, g_norms[3], g_norms[1]])
    norm_terms = norm_terms.astype(BF16).reshape(6, 4, 8, 32).transpose(1, 2, 0, 3)
    norm_terms = jnp.pad(norm_terms, ((0, 0), (0, 0), (0, 10), (0, 224)))
    cols = jnp.concatenate([terms, norm_terms], axis=2)
    first_sum, square_sum, cols_sum, norm_sum, grad_text = last_sums(
        g_first.astype(BF16).reshape(8, 128, 1024), g_square.reshape(4, 8, 96, 1024), cols, text_terms
    )
    own_hat, own_scale = norm_parts(hidden_in.astype(F32))
    grad_hidden = (
        g_after_self.reshape(2, 128, 1024) + norm_back(own_hat, own_scale, first_sum, params[0])
    ).astype(BF16)
    cols_sum = cols_sum.reshape(5, 32, 1024)
    return (
        output,
        grad_hidden,
        grad_text,
        jnp.stack([cols_sum[0], cols_sum[1], cols_sum[2]], axis=1),
        square_sum[0:32],
        jnp.stack([square_sum[32:64], cols_sum[3], cols_sum[4]], axis=1),
        square_sum[64:96],
        grad_ffn_in,
        grad_ffn_out,
        norm_sum[0:3, 0:32],
        norm_sum[3:6, 0:32],
    )

def solution(mesh):
    return jax.shard_map(
        on_device_fast if fits(mesh) else on_device_any,
        mesh=mesh,
        in_specs=(
            P("clip", "frame", None),
            P("clip", None, None),
            P("clip", "frame", None),
            P(("clip", "frame"), None, None),
            P(("clip", "frame"), None),
            P(("clip", "frame"), None, None),
            P(("clip", "frame"), None),
            P(("clip", "frame"), None),
            P(("clip", "frame"), None),
            P(None, ("clip", "frame")),
            P(None, ("clip", "frame")),
            P("clip"),
            P("clip", None),
            P("clip"),
            P("clip", None),
        ),
        out_specs=(
            P("clip", "frame", None),
            P("clip", "frame", None),
            P("clip", "frame", None),
            P(("clip", "frame"), None, None),
            P(("clip", "frame"), None),
            P(("clip", "frame"), None, None),
            P(("clip", "frame"), None),
            P(("clip", "frame"), None),
            P(("clip", "frame"), None),
            P(None, ("clip", "frame")),
            P(None, ("clip", "frame")),
        ),
        check_vma=False,
    )
```

```python
import functools

import jax
import jax.numpy as jnp
from jax import lax
from jax.experimental import pallas as pl
from jax.experimental.pallas import tpu as pltpu
from jax.sharding import PartitionSpec as P

HD = 64


MASKED = -1000000000.0
EPSILON = 1e-05


def layer_norm(value, gain, shift):
    average = jnp.mean(value, axis=-1, keepdims=True)
    centered = value - average
    variance = jnp.mean(centered * centered, axis=-1, keepdims=True)
    return centered * lax.rsqrt(variance + EPSILON) * gain + shift


def activate(value):
    return jax.nn.gelu(value, approximate=False)


def project(left, right):
    return jnp.einsum("cnd,de->cne", left, right, preferred_element_type=jnp.float32)


def project_back(grad_rows, weight):
    return jnp.einsum("cne,de->cnd", grad_rows, weight, preferred_element_type=jnp.float32)


def weight_grad(left, right):
    return jnp.einsum("cnd,cne->de", left, right, preferred_element_type=jnp.float32)


def fetch_attention(self_qkv, self_out, cross_qkv, cross_out, ln_gain, ln_bias):
    return (
        lax.all_gather(self_qkv, ("clip", "frame"), axis=0, tiled=True),
        lax.all_gather(self_out, ("clip", "frame"), axis=0, tiled=True),
        lax.all_gather(cross_qkv, ("clip", "frame"), axis=0, tiled=True),
        lax.all_gather(cross_out, ("clip", "frame"), axis=0, tiled=True),
        lax.all_gather(ln_gain, ("clip", "frame"), axis=1, tiled=True),
        lax.all_gather(ln_bias, ("clip", "frame"), axis=1, tiled=True),
    )


def fetch_ffn(ffn_in, ffn_out):
    return (
        lax.all_gather(ffn_in, ("clip", "frame"), axis=0, tiled=True),
        lax.all_gather(ffn_out, ("clip", "frame"), axis=0, tiled=True),
    )


def self_masks(first_row, block_rows, clip_len, key_valid):
    columns = jnp.arange(key_valid.shape[1], dtype=jnp.int32)
    row_ids = first_row + jnp.arange(block_rows, dtype=jnp.int32)
    diagonal = columns[None, :] == row_ids[:, None]
    allowed = (columns[None, :] <= row_ids[:, None])[None] & (
        key_valid[:, None, :] | diagonal[None]
    )
    live_rows = (row_ids[None, :] < clip_len[:, None]).astype(jnp.float32)
    return (allowed[:, None], live_rows[:, None, :, None])


def self_forward(query_rows, key_rows, value_rows, clip_len, key_valid):
    length = query_rows.shape[1]
    block_rows = min(512, length)
    score_scale = query_rows.shape[3] ** (-0.5)

    def one_block(block_index):
        first_row = block_index * block_rows
        query_block = lax.dynamic_slice_in_dim(query_rows, first_row, block_rows, 1)
        raw_scores = jnp.einsum(
            "cqhd,ckhd->chqk", query_block, key_rows, preferred_element_type=jnp.float32
        )
        allowed, live_rows = self_masks(first_row, block_rows, clip_len, key_valid)
        logits = jnp.where(allowed, raw_scores * score_scale, MASKED)
        row_max = jnp.max(logits, axis=-1, keepdims=True)
        exponent = jnp.exp(logits - row_max)
        row_sum = jnp.sum(exponent, axis=-1, keepdims=True)
        weights = (exponent / row_sum * live_rows).astype(jnp.bfloat16)
        attended = jnp.einsum(
            "chqk,ckhd->cqhd", weights, value_rows, preferred_element_type=jnp.float32
        )
        return (attended.astype(jnp.bfloat16), row_max + jnp.log(row_sum))

    blocks, log_sums = lax.map(one_block, jnp.arange(length // block_rows, dtype=jnp.int32))
    return (jnp.moveaxis(blocks, 0, 1).reshape(query_rows.shape), log_sums)


def self_backward(query_rows, key_rows, value_rows, grad_rows, log_sums, clip_len, key_valid):
    length = query_rows.shape[1]
    block_rows = min(512, length)
    score_scale = query_rows.shape[3] ** (-0.5)

    def one_block(totals, block_index):
        grad_keys, grad_values = totals
        first_row = block_index * block_rows
        query_block = lax.dynamic_slice_in_dim(query_rows, first_row, block_rows, 1)
        grad_block = lax.dynamic_slice_in_dim(grad_rows, first_row, block_rows, 1)
        raw_scores = jnp.einsum(
            "cqhd,ckhd->chqk", query_block, key_rows, preferred_element_type=jnp.float32
        )
        allowed, live_rows = self_masks(first_row, block_rows, clip_len, key_valid)
        logits = jnp.where(allowed, raw_scores * score_scale, MASKED)
        probs = jnp.exp(logits - log_sums[block_index])
        weights = (probs * live_rows).astype(jnp.bfloat16)
        grad_probs = (
            jnp.einsum(
                "cqhd,ckhd->chqk", grad_block, value_rows, preferred_element_type=jnp.float32
            )
            * live_rows
        )
        row_dot = jnp.sum(probs * grad_probs, axis=-1, keepdims=True)
        grad_scores = (probs * (grad_probs - row_dot)).astype(jnp.bfloat16)
        grad_query = (
            jnp.einsum("chqk,ckhd->cqhd", grad_scores, key_rows, preferred_element_type=jnp.float32)
            * score_scale
        )
        grad_keys = (
            grad_keys
            + jnp.einsum(
                "chqk,cqhd->ckhd", grad_scores, query_block, preferred_element_type=jnp.float32
            )
            * score_scale
        )
        grad_values = grad_values + jnp.einsum(
            "chqk,cqhd->ckhd", weights, grad_block, preferred_element_type=jnp.float32
        )
        return ((grad_keys, grad_values), grad_query)

    zeros = jnp.zeros(key_rows.shape, jnp.float32)
    (grad_keys, grad_values), grad_blocks = lax.scan(
        one_block, (zeros, zeros), jnp.arange(length // block_rows, dtype=jnp.int32)
    )
    grad_query = jnp.moveaxis(grad_blocks, 0, 1).reshape(query_rows.shape)
    return (grad_query, grad_keys, grad_values)


def text_allowed(text_len, text_mask):
    slots = jnp.arange(text_mask.shape[1], dtype=jnp.int32)
    allowed = (slots[None, :] < text_len[:, None]) & ((text_mask > 0) | (slots[None, :] == 0))
    return allowed[:, None, None, :]


def cross_forward(query_rows, key_rows, value_rows, allowed):
    score_scale = query_rows.shape[3] ** (-0.5)
    raw_scores = jnp.einsum(
        "cqhd,ckhd->chqk", query_rows, key_rows, preferred_element_type=jnp.float32
    )
    logits = jnp.where(allowed, raw_scores * score_scale, MASKED)
    row_max = jnp.max(logits, axis=-1, keepdims=True)
    exponent = jnp.exp(logits - row_max)
    row_sum = jnp.sum(exponent, axis=-1, keepdims=True)
    weights = (exponent / row_sum).astype(jnp.bfloat16)
    crossed = jnp.einsum("chqk,ckhd->cqhd", weights, value_rows, preferred_element_type=jnp.float32)
    return (crossed.astype(jnp.bfloat16), row_max + jnp.log(row_sum))


def cross_backward(query_rows, key_rows, value_rows, grad_rows, log_sums, allowed):
    score_scale = query_rows.shape[3] ** (-0.5)
    raw_scores = jnp.einsum(
        "cqhd,ckhd->chqk", query_rows, key_rows, preferred_element_type=jnp.float32
    )
    logits = jnp.where(allowed, raw_scores * score_scale, MASKED)
    probs = jnp.exp(logits - log_sums)
    weights = probs.astype(jnp.bfloat16)
    grad_probs = jnp.einsum(
        "cqhd,ckhd->chqk", grad_rows, value_rows, preferred_element_type=jnp.float32
    )
    row_dot = jnp.sum(probs * grad_probs, axis=-1, keepdims=True)
    grad_scores = (probs * (grad_probs - row_dot)).astype(jnp.bfloat16)
    grad_query = (
        jnp.einsum("chqk,ckhd->cqhd", grad_scores, key_rows, preferred_element_type=jnp.float32)
        * score_scale
    )
    grad_keys = (
        jnp.einsum("chqk,cqhd->ckhd", grad_scores, query_rows, preferred_element_type=jnp.float32)
        * score_scale
    )
    grad_values = jnp.einsum(
        "chqk,cqhd->ckhd", weights, grad_rows, preferred_element_type=jnp.float32
    )
    return (grad_query, grad_keys, grad_values)


def sum_ffn(grad_ffn_in, grad_ffn_out):
    return (
        lax.psum_scatter(grad_ffn_in, ("clip", "frame"), scatter_dimension=0, tiled=True),
        lax.psum_scatter(grad_ffn_out, ("clip", "frame"), scatter_dimension=0, tiled=True),
    )


def sum_attention(
    grad_self_qkv, grad_self_out, grad_cross_qkv, grad_cross_out, grad_gains, grad_shifts
):
    return (
        lax.psum_scatter(grad_self_qkv, ("clip", "frame"), scatter_dimension=0, tiled=True),
        lax.psum_scatter(grad_self_out, ("clip", "frame"), scatter_dimension=0, tiled=True),
        lax.psum_scatter(grad_cross_qkv, ("clip", "frame"), scatter_dimension=0, tiled=True),
        lax.psum_scatter(grad_cross_out, ("clip", "frame"), scatter_dimension=0, tiled=True),
        lax.psum_scatter(grad_gains, ("clip", "frame"), scatter_dimension=1, tiled=True),
        lax.psum_scatter(grad_shifts, ("clip", "frame"), scatter_dimension=1, tiled=True),
    )


def on_device_any(
    hidden_in,
    text_states,
    out_grad,
    self_qkv,
    self_out,
    cross_qkv,
    cross_out,
    ffn_in,
    ffn_out,
    ln_gain,
    ln_bias,
    clip_len,
    frame_mask,
    text_len,
    text_mask,
):
    clip_count, frames, model_width = hidden_in.shape
    text_slots = text_states.shape[1]
    group_count = lax.axis_size("frame")
    columns_here = model_width // group_count
    heads_here = columns_here // HD
    length = frames * group_count
    frame_index = lax.axis_index("frame")
    full_qkv, full_out, full_cross, full_cross_out, gains_low, shifts_low = fetch_attention(
        self_qkv, self_out, cross_qkv, cross_out, ln_gain, ln_bias
    )
    gains = gains_low.astype(jnp.float32)
    shifts = shifts_low.astype(jnp.float32)
    hidden = hidden_in.astype(jnp.float32)
    first_norm, first_pull = jax.vjp(layer_norm, hidden, gains[0], shifts[0])
    first_low = first_norm.astype(jnp.bfloat16)
    query_low = project(first_low, full_qkv[:, 0]).astype(jnp.bfloat16)
    key_low = project(first_low, full_qkv[:, 1]).astype(jnp.bfloat16)
    value_low = project(first_low, full_qkv[:, 2]).astype(jnp.bfloat16)
    query_heads, key_heads, value_heads = (
        lax.all_to_all(query_low, "frame", split_axis=2, concat_axis=1, tiled=True),
        lax.all_to_all(key_low, "frame", split_axis=2, concat_axis=1, tiled=True),
        lax.all_to_all(value_low, "frame", split_axis=2, concat_axis=1, tiled=True),
    )
    head_shape = (clip_count, length, heads_here, HD)
    query_heads = query_heads.reshape(head_shape)
    key_heads = key_heads.reshape(head_shape)
    value_heads = value_heads.reshape(head_shape)
    columns = jnp.arange(length, dtype=jnp.int32)
    key_valid = (columns[None, :] < clip_len[:, None]) & (frame_mask > 0)
    attended_heads, self_sums = self_forward(
        query_heads, key_heads, value_heads, clip_len, key_valid
    )
    attended = lax.all_to_all(
        attended_heads.reshape(clip_count, length, columns_here),
        "frame",
        split_axis=1,
        concat_axis=2,
        tiled=True,
    )
    after_self = hidden + project(attended, full_out)
    second_norm, second_pull = jax.vjp(layer_norm, after_self, gains[1], shifts[1])
    second_low = second_norm.astype(jnp.bfloat16)
    cross_query = project(second_low, full_cross[:, 0]).astype(jnp.bfloat16)
    cross_query_heads = lax.all_to_all(
        cross_query, "frame", split_axis=2, concat_axis=1, tiled=True
    ).reshape(head_shape)
    key_columns = lax.dynamic_slice_in_dim(
        full_cross[:, 1], frame_index * columns_here, columns_here, 1
    )
    value_columns = lax.dynamic_slice_in_dim(
        full_cross[:, 2], frame_index * columns_here, columns_here, 1
    )
    text_shape = (clip_count, text_slots, heads_here, HD)
    text_keys = project(text_states, key_columns).astype(jnp.bfloat16).reshape(text_shape)
    text_values = project(text_states, value_columns).astype(jnp.bfloat16).reshape(text_shape)
    allowed_text = text_allowed(text_len, text_mask)
    crossed_heads, cross_sums = cross_forward(
        cross_query_heads, text_keys, text_values, allowed_text
    )
    crossed = lax.all_to_all(
        crossed_heads.reshape(clip_count, length, columns_here),
        "frame",
        split_axis=1,
        concat_axis=2,
        tiled=True,
    )
    after_cross = after_self + project(crossed, full_cross_out)
    ffn_weight_in, ffn_weight_out = fetch_ffn(ffn_in, ffn_out)
    third_norm, third_pull = jax.vjp(layer_norm, after_cross, gains[2], shifts[2])
    third_low = third_norm.astype(jnp.bfloat16)
    pre_act = project(third_low, ffn_weight_in)
    activated, gelu_pull = jax.vjp(activate, pre_act)
    inner_low = activated.astype(jnp.bfloat16)
    output = (after_cross + project(inner_low, ffn_weight_out)).astype(jnp.bfloat16)
    ffn_weight_in, ffn_weight_out = fetch_ffn(ffn_in, ffn_out)
    grad_ffn_out = weight_grad(inner_low, out_grad)
    (grad_pre,) = gelu_pull(project_back(out_grad, ffn_weight_out))
    grad_pre_low = grad_pre.astype(jnp.bfloat16)
    grad_ffn_in = weight_grad(third_low, grad_pre_low)
    ffn_sums = sum_ffn(grad_ffn_in, grad_ffn_out)
    grad_third, gain_third, shift_third = third_pull(project_back(grad_pre_low, ffn_weight_in))
    grad_after_cross = out_grad.astype(jnp.float32) + grad_third
    full_qkv, full_out, full_cross, full_cross_out, gains_low, shifts_low = fetch_attention(
        self_qkv, self_out, cross_qkv, cross_out, ln_gain, ln_bias
    )
    key_columns = lax.dynamic_slice_in_dim(
        full_cross[:, 1], frame_index * columns_here, columns_here, 1
    )
    value_columns = lax.dynamic_slice_in_dim(
        full_cross[:, 2], frame_index * columns_here, columns_here, 1
    )
    cross_branch = grad_after_cross.astype(jnp.bfloat16)
    grad_cross_out = weight_grad(crossed, cross_branch)
    grad_crossed = project_back(cross_branch, full_cross_out).astype(jnp.bfloat16)
    grad_crossed_heads = lax.all_to_all(
        grad_crossed, "frame", split_axis=2, concat_axis=1, tiled=True
    ).reshape(head_shape)
    grad_cq, grad_tk, grad_tv = cross_backward(
        cross_query_heads, text_keys, text_values, grad_crossed_heads, cross_sums, allowed_text
    )
    grad_tk_low = grad_tk.astype(jnp.bfloat16).reshape(clip_count, text_slots, columns_here)
    grad_tv_low = grad_tv.astype(jnp.bfloat16).reshape(clip_count, text_slots, columns_here)
    text_terms = project_back(grad_tk_low, key_columns) + project_back(grad_tv_low, value_columns)
    grad_text = lax.psum_scatter(
        text_terms.astype(jnp.bfloat16), "frame", scatter_dimension=1, tiled=True
    )
    empty_square = jnp.zeros((model_width, model_width), jnp.float32)
    grad_cross_key = lax.dynamic_update_slice_in_dim(
        empty_square, weight_grad(text_states, grad_tk_low), frame_index * columns_here, 1
    )
    grad_cross_value = lax.dynamic_update_slice_in_dim(
        empty_square, weight_grad(text_states, grad_tv_low), frame_index * columns_here, 1
    )
    grad_cq_low = grad_cq.astype(jnp.bfloat16).reshape(clip_count, length, columns_here)
    grad_cross_query = lax.all_to_all(grad_cq_low, "frame", split_axis=1, concat_axis=2, tiled=True)
    grad_cross_qw = weight_grad(second_low, grad_cross_query)
    grad_second, gain_second, shift_second = second_pull(
        project_back(grad_cross_query, full_cross[:, 0])
    )
    grad_after_self = grad_after_cross + grad_second
    self_branch = grad_after_self.astype(jnp.bfloat16)
    grad_self_out = weight_grad(attended, self_branch)
    grad_attended = project_back(self_branch, full_out).astype(jnp.bfloat16)
    grad_attended_heads = lax.all_to_all(
        grad_attended, "frame", split_axis=2, concat_axis=1, tiled=True
    ).reshape(head_shape)
    grad_query, grad_keys, grad_values = self_backward(
        query_heads, key_heads, value_heads, grad_attended_heads, self_sums, clip_len, key_valid
    )
    flat_shape = (clip_count, length, columns_here)
    grad_query, grad_keys, grad_values = (
        lax.all_to_all(
            grad_query.astype(jnp.bfloat16).reshape(flat_shape),
            "frame",
            split_axis=1,
            concat_axis=2,
            tiled=True,
        ),
        lax.all_to_all(
            grad_keys.astype(jnp.bfloat16).reshape(flat_shape),
            "frame",
            split_axis=1,
            concat_axis=2,
            tiled=True,
        ),
        lax.all_to_all(
            grad_values.astype(jnp.bfloat16).reshape(flat_shape),
            "frame",
            split_axis=1,
            concat_axis=2,
            tiled=True,
        ),
    )
    grad_self_qkv = jnp.stack(
        [
            weight_grad(first_low, grad_query),
            weight_grad(first_low, grad_keys),
            weight_grad(first_low, grad_values),
        ],
        axis=1,
    )
    grad_first_norm = (
        project_back(grad_query, full_qkv[:, 0])
        + project_back(grad_keys, full_qkv[:, 1])
        + project_back(grad_values, full_qkv[:, 2])
    )
    grad_first, gain_first, shift_first = first_pull(grad_first_norm)
    grad_hidden = (grad_after_self + grad_first).astype(jnp.bfloat16)
    grad_cross_qkv = jnp.stack([grad_cross_qw, grad_cross_key, grad_cross_value], axis=1)
    grad_gains = jnp.stack([gain_first, gain_second, gain_third])
    grad_shifts = jnp.stack([shift_first, shift_second, shift_third])
    attn_sums = sum_attention(
        grad_self_qkv, grad_self_out, grad_cross_qkv, grad_cross_out, grad_gains, grad_shifts
    )
    return (
        output,
        grad_hidden,
        grad_text,
        attn_sums[0],
        attn_sums[1],
        attn_sums[2],
        attn_sums[3],
        ffn_sums[0],
        ffn_sums[1],
        attn_sums[4],
        attn_sums[5],
    )


MESH = pl.DeviceIdType.MESH
HBM = pl.BlockSpec(memory_space=pl.ANY)
VMEM = pl.BlockSpec(memory_space=pltpu.VMEM)
SMEM = pl.BlockSpec(memory_space=pltpu.SMEM)
NEG = -1e30
F32 = jnp.float32
BF16 = jnp.bfloat16


def fits(mesh):
    return mesh.shape["clip"] == 4 and mesh.shape["frame"] == 8


class Here:
    def __init__(self):
        self.c = lax.axis_index("clip")
        self.f = lax.axis_index("frame")
        self.core = lax.rem(self.f, 2)
        self.z = lax.div(self.f, 2)
        self.pair = lax.div(self.z, 2)
        self.role = lax.rem(self.z, 2)
        self.group = lax.rem(self.f, 4)
        self.cx = self.c + 1 - 2 * lax.rem(self.c, 2)
        self.cy = lax.rem(self.c + 2, 4)
        self.cd = 3 - self.c
        self.sib = self.f + 1 - 2 * self.core
        self.partner = self.f + 2 - 4 * self.role
        self.far_gate = 2 * (2 - self.pair) + self.core
        self.is_gate = self.role + self.pair == 1
        self.far = [2 * (2 * (1 - self.pair) + j) + self.core for j in range(2)]

    def step(self, d):
        return lax.rem(self.f + d, 8)

    def zstep(self, d):
        return lax.rem(self.f + 2 * d, 8)


class Wire:
    def __init__(self, here, send_sem, recv_sem):
        self.here, self.send_sem, self.recv_sem = here, send_sem, recv_sem
        self.used = 0
        self.open = []

    def copy(self, src, dst, tag, c, f):
        self.used += 1
        return pltpu.make_async_remote_copy(
            src_ref=src,
            dst_ref=dst,
            send_sem=self.send_sem.at[self.used - 1],
            recv_sem=self.recv_sem.at[tag],
            device_id=(c, f),
            device_id_type=MESH,
        )

    def send(self, src, dst, tag, c, f):
        copy = self.copy(src, dst, tag, c, f)
        copy.start()
        self.open.append(copy)

    def arrived(self, dst, tag):
        pltpu.make_async_remote_copy(
            src_ref=dst,
            dst_ref=dst,
            send_sem=self.send_sem.at[0],
            recv_sem=self.recv_sem.at[tag],
            device_id=(self.here.c, self.here.sib),
            device_id_type=MESH,
        ).wait_recv()

    def drain(self):
        for copy in self.open:
            copy.wait_send()
        self.open = []


def greet(devices):
    barrier = pltpu.get_barrier_semaphore()
    for device in devices:
        pl.semaphore_signal(barrier, inc=1, device_id=device, device_id_type=MESH)
    pl.semaphore_wait(barrier, len(devices))


def frame_others(here):
    return [(here.c, here.step(d)) for d in range(1, 8)]


def clip_others(here):
    return [(here.cx, here.f), (here.cy, here.f), (here.cd, here.f)]


class ClipGather:
    def __init__(self, wire, block, tag, own=None):
        self.wire, self.block, self.tag = wire, block, tag
        self.own = own or (lambda half: block(wire.here.c, half))

    def begin(self):
        h, w, b, t, own = self.wire.here, self.wire, self.block, self.tag, self.own
        w.send(own(0), b(h.c, 0), t, h.cx, h.f)
        w.send(own(1), b(h.c, 1), t + 2, h.cy, h.f)
        w.send(own(1), b(h.c, 1), t + 1, h.cx, h.f)
        w.send(own(0), b(h.c, 0), t + 3, h.cy, h.f)

    def middle(self):
        h, w, b, t = self.wire.here, self.wire, self.block, self.tag
        w.arrived(b(h.cx, 0), t)
        w.send(b(h.cx, 0), b(h.cx, 0), t + 4, h.cy, h.f)
        w.arrived(b(h.cy, 1), t + 2)
        w.send(b(h.cy, 1), b(h.cy, 1), t + 5, h.cx, h.f)

    def near(self):
        h, w, b, t = self.wire.here, self.wire, self.block, self.tag
        w.arrived(b(h.cx, 1), t + 1)
        w.arrived(b(h.cy, 0), t + 3)

    def end(self):
        h, w, b, t = self.wire.here, self.wire, self.block, self.tag
        w.arrived(b(h.cd, 0), t + 4)
        w.arrived(b(h.cd, 1), t + 5)


class ZGather:
    def __init__(self, wire, slot, tag, own=None):
        self.wire, self.slot, self.tag = wire, slot, tag
        self.own = own if own is not None else slot(wire.here.f)
        self.open = []

    def step(self, s):
        h, w = self.wire.here, self.wire
        left, right = h.f - 2 * (s - 1), h.f + 2 * (s - 1)
        if s > 1:

            @pl.when(left >= 0)
            def _():
                w.arrived(self.slot(left), self.tag + s - 2)

            @pl.when(right <= 7)
            def _():
                w.arrived(self.slot(right), self.tag + 3 + s - 2)

        if s > 3:
            return
        for block, tag, go, to in (
            (left, self.tag, (left >= 0) & (h.z <= 2), h.f + 2),
            (right, self.tag + 3, (right <= 7) & (h.z >= 1), h.f - 2),
        ):
            src = self.own if s == 1 else self.slot(block)
            copy = w.copy(src, self.slot(block), tag + s - 1, h.c, to)
            pl.when(go)(copy.start)
            self.open.append((go, copy))

    def relay(self, d):
        h, w = self.wire.here, self.wire
        f = h.zstep(d)
        w.send(self.own if d == 0 else self.slot(f), self.slot(f), self.tag + 6 + d, h.c, h.sib)

    def end(self):
        h, w = self.wire.here, self.wire
        for d in range(4):
            w.arrived(self.slot(h.zstep(d) + h.sib - h.f), self.tag + 6 + d)
        for go, copy in self.open:
            pl.when(go)(copy.wait_send)


class ClipScatter:
    def __init__(self, wire, parts, slots, tag):
        self.wire, self.parts, self.slots, self.tag = wire, parts, slots, tag

    def begin(self, which=None):
        h, w, p, s, t = self.wire.here, self.wire, self.parts, self.slots, self.tag
        if which != 1:
            w.send(p(h.cd, 0), s[0], t, h.cx, h.f)
            w.send(p(h.cd, 1), s[1], t + 1, h.cy, h.f)
        if which != 0:
            w.send(p(h.cx, 0), s[2], t + 2, h.cx, h.f)
            w.send(p(h.cy, 1), s[3], t + 3, h.cy, h.f)

    def middle(self):
        h, w, p, s, t = self.wire.here, self.wire, self.parts, self.slots, self.tag
        w.arrived(s[0], t)
        add_into(s[0], p(h.cy, 0))
        w.send(s[0], s[4], t + 4, h.cy, h.f)
        w.arrived(s[1], t + 1)
        add_into(s[1], p(h.cx, 1))
        w.send(s[1], s[5], t + 5, h.cx, h.f)

    def end(self):
        w, s, t = self.wire, self.slots, self.tag
        for i in range(2, 6):
            w.arrived(s[i], t + i)

    def total(self, half):
        s = self.slots
        first, second = (s[2], s[4]) if half == 0 else (s[5], s[3])
        own = self.parts(self.wire.here.c, half)
        return own[...].astype(F32) + first[...].astype(F32) + second[...].astype(F32)


def add_into(into, other):
    into[...] = (into[...].astype(F32) + other[...].astype(F32)).astype(BF16)


class LocalCopy:
    def __init__(self, src, through, dst, sem):
        self.a = pltpu.make_async_copy(src, through, sem)
        self.b = pltpu.make_async_copy(through, dst, sem)
        self.a.start()

    def turn(self):
        self.a.wait()
        self.b.start()

    def wait(self):
        self.b.wait()


def comm_call(body, out_shape, in_specs, out_specs, scratch, copies, tags, collective_id, cost=None):
    return pl.pallas_call(
        body,
        out_shape=out_shape,
        in_specs=in_specs,
        out_specs=out_specs,
        scratch_shapes=list(scratch)
        + [pltpu.SemaphoreType.DMA((copies,)), pltpu.SemaphoreType.DMA((tags,))],
        compiler_params=pltpu.CompilerParams(
            collective_id=collective_id, has_side_effects=True, vmem_limit_bytes=60 * 2**20
        ),
    )


def shape(dims, dtype=BF16):
    return jax.ShapeDtypeStruct(dims, dtype)


ROWS = 256


def dot(left, right, contract):
    return lax.dot_general(left, right, ((contract[:1], contract[1:]), ((), ())), preferred_element_type=F32)


def mask_scores(scores, bias_ref, first, rows):
    low = scores[first:] + bias_ref[first : first + rows, 0:1]
    key = lax.broadcasted_iota(jnp.int32, (rows, rows), 0)
    query = lax.broadcasted_iota(jnp.int32, (rows, rows), 1)
    low = jnp.where(key < query, low, jnp.where(key == query, scores[first:], NEG))
    if first == 0:
        return low
    return jnp.concatenate([scores[:first] + bias_ref[0:first, 0:1], low], axis=0)


def norm_parts(value):
    centered = value - jnp.mean(value, axis=-1, keepdims=True)
    scale = lax.rsqrt(jnp.mean(centered * centered, axis=-1, keepdims=True) + EPSILON)
    return centered * scale, scale


def column_weight(cols, j):
    return cols[:, :, 32 * j : 32 * j + 32, :].reshape(1024, 256)


def attend_rows(i, length, bias, q_ref, k_ref, v_t, o_ref, lse_ref, out_t):
    lane_head = lax.broadcasted_iota(jnp.int32, (ROWS, 256), 1) // HD
    first, n = i * ROWS, (i + 1) * ROWS
    q = q_ref[first:n, :]

    def head(j, _):
        q_head = jnp.where(lane_head == j, q, 0) * jnp.asarray(HD**-0.5, BF16)
        scores = mask_scores(dot(k_ref[0:n, :], q_head, (1, 1)), bias, first, ROWS)
        top = jnp.max(scores, axis=0, keepdims=True)
        weight = jnp.exp(scores - top)
        total = jnp.sum(weight, axis=0, keepdims=True)
        at = pl.ds(pl.multiple_of(j * HD, HD), HD)
        out_t[at, :] = dot(v_t[at, 0:n], weight.astype(BF16), (1, 0)) / total
        lse_ref[pl.ds(j, 1), first:n] = top + jnp.log(total)
        return 0

    lax.fori_loop(0, 4, head, 0)
    live = first + lax.broadcasted_iota(jnp.int32, (ROWS, 256), 0) < length[0]
    o_ref[first:n, :] = jnp.where(live, out_t[...].T, 0).astype(BF16)


def front_body(
    length, bias, text, hid, cols_a, cols_b, square, fin,
    o_hid, o_first, o_q, o_k, o_v, o_heads, o_lse, o_cols_a, o_cols_b, o_params, o_att, o_tkv, o_square, o_fin,
    out_t, v_t, tkv, v_square, v_fin, local, send_sem, recv_sem,
):
    h = Here()
    w = Wire(h, send_sem, recv_sem)
    T_HID, T_A, T_B, T_FIN, T_AXY, T_BXY = 0, 10, 17, 24, 27, 33
    T_Z, T_SXY, T_SIB, T_ATT, T_TKV = 39, 49, 73, 85, 93

    def my_columns(f):
        return pl.ds(pl.multiple_of(lax.rem(f, 4) * 256, 256), 256)

    def fin_part(c):
        return fin.at[:, pl.ds(pl.multiple_of(c * 1024, 1024), 1024)]

    plain = [
        pltpu.make_async_copy(cols_a.at[:, my_columns(h.f)], o_cols_a.at[h.c, h.f], local.at[0]),
        pltpu.make_async_copy(cols_b.at[:, my_columns(h.f)], o_cols_b.at[h.c, h.f], local.at[1]),
        pltpu.make_async_copy(hid.at[h.pair], o_hid.at[h.f], local.at[2]),
    ]
    for copy in plain:
        copy.start()
    turned = [
        LocalCopy(square, v_square, o_square.at[h.c, h.f], local.at[3]),
        LocalCopy(fin_part(h.c), v_fin, o_fin.at[h.c], local.at[4]),
    ]
    greet(frame_others(h) + clip_others(h))

    for d in (2, 6, 4, 3, 5, 1, 7):
        f = h.step(d)
        w.send(cols_a.at[:, my_columns(f)], o_cols_a.at[h.c, h.f], T_A + d - 1, h.c, f)

    def half_of(ref, part):
        return ref.at[pl.ds(64 * part, 64), :]

    for part in range(2):
        w.send(half_of(hid.at[h.pair], part), half_of(o_hid.at[h.f], part), T_HID + 1 + part, h.c, h.partner)
        w.send(
            half_of(hid.at[1 - h.pair], part),
            half_of(o_hid.at[h.f], part),
            T_HID + 3 + 2 * h.role + part,
            h.c,
            h.far_gate,
        )
    w.send(hid.at[h.pair], o_hid.at[h.f], T_HID, h.c, h.sib)

    def square_slot(f):
        return o_square.at[h.c, f]

    z_gather = ZGather(w, square_slot, T_Z, square)

    def square_gather(d):
        f = h.zstep(d)
        return ClipGather(
            w,
            lambda c, half: o_square.at[c, f, pl.ds(48 * half, 48), :],
            T_SXY + 6 * d,
            (lambda half: square.at[pl.ds(48 * half, 48), :]) if d == 0 else None,
        )

    gathers = [square_gather(d) for d in range(4)]
    gathers[0].begin()
    for i, (c, f) in enumerate(clip_others(h)):
        w.send(fin_part(c), o_fin.at[h.c], T_FIN + i, c, f)
    for copy in turned:
        copy.turn()
    plain[0].wait()
    for d in range(1, 8):
        w.arrived(o_cols_a.at[h.c, lax.rem(h.f + 8 - d, 8)], T_A + d - 1)
    a_gather = ClipGather(w, lambda c, half: o_cols_a.at[c, pl.ds(4 * half, 4)], T_AXY)
    a_gather.begin()
    forwards = []
    for part in range(2):
        for j in range(2):
            block = half_of(o_hid.at[h.far[j]], part)
            w.arrived(block, T_HID + 3 + 2 * j + part)
            forward = w.copy(block, block, T_HID + 3 + 2 * j + part, h.c, h.partner)
            pl.when(h.is_gate)(forward.start)
            forwards.append(forward)
    for d in (2, 6, 4, 3, 5, 1, 7):
        f = h.step(d)
        w.send(cols_b.at[:, my_columns(f)], o_cols_b.at[h.c, h.f], T_B + d - 1, h.c, f)
    for part in range(2):
        w.arrived(half_of(o_hid.at[h.partner], part), T_HID + 1 + part)
    w.send(o_hid.at[h.partner], o_hid.at[h.partner], T_HID + 7, h.c, h.sib)
    for j in range(2):
        w.send(o_hid.at[h.far[j]], o_hid.at[h.far[j]], T_HID + 8 + j, h.c, h.sib)
    a_gather.middle()
    z_gather.step(1)
    z_gather.relay(0)
    plain[1].wait()
    for d in range(1, 8):
        w.arrived(o_cols_b.at[h.c, lax.rem(h.f + 8 - d, 8)], T_B + d - 1)
    b_gather = ClipGather(w, lambda c, half: o_cols_b.at[c, pl.ds(4 * half, 4)], T_BXY)
    b_gather.begin()
    gathers[0].middle()
    a_gather.near()
    a_gather.end()
    for g in range(8):
        group = sum(o_cols_a[g // 2, 4 * (g % 2) + i, 96:104, 0:128].astype(F32) for i in range(4))
        o_params[:, 128 * g : 128 * g + 128] = group
    plain[2].wait()
    w.arrived(o_hid.at[h.sib], T_HID)
    w.arrived(o_hid.at[h.partner + h.sib - h.f], T_HID + 7)
    for j in range(2):
        w.arrived(o_hid.at[h.far[j] + h.sib - h.f], T_HID + 8 + j)
    z_gather.step(2)

    def project_rows(i, _):
        at = pl.ds(pl.multiple_of(i * 256, 256), 256)
        rows = o_hid[pl.ds(2 * i, 2)].reshape(256, 1024).astype(F32)
        xhat, _ = norm_parts(rows)
        low = (xhat * o_params[0:1, :] + o_params[3:4, :]).astype(BF16)
        o_first[at, :] = low
        for j, out in enumerate((o_q, o_k, o_v)):
            out[at, :] = dot(low, column_weight(o_cols_a, j), (1, 0)).astype(BF16)
        return 0

    lax.fori_loop(0, 2, project_rows, 0)
    z_gather.step(3)
    gathers[2].begin()
    z_gather.relay(2)
    b_gather.middle()
    lax.fori_loop(2, 4, project_rows, 0)
    v_t[...] = o_v[...].T
    b_gather.near()
    b_gather.end()
    z_gather.step(4)
    for d in (1, 3):
        gathers[d].begin()
        z_gather.relay(d)

    def text_slot(f):
        return o_tkv.at[lax.div(f, 4), :, :, my_columns(f)]

    for j in range(2):
        tkv[j] = dot(text[h.pair], column_weight(o_cols_b, j), (1, 0)).astype(BF16)
    for d in range(1, 4):
        w.send(tkv, text_slot(h.f), T_TKV + d, h.c, h.zstep(d))
    w.send(tkv, text_slot(h.f), T_TKV, h.c, h.sib)
    text_copy = pltpu.make_async_copy(tkv, text_slot(h.f), local.at[5])
    text_copy.start()

    def att_slot(f):
        return o_att.at[lax.div(f, 4), :, my_columns(f)]

    att_sends = []

    def attend_and_send(i):
        attend_rows(i, length, bias, o_q, o_k, v_t, o_heads, o_lse, out_t)
        for f in (2 * i, 2 * i + 1):
            block = o_heads.at[pl.ds(128 * f, 128), :]
            away = h.f != f
            copy = w.copy(block, att_slot(h.f), T_ATT + h.f, h.c, f)
            stay = pltpu.make_async_copy(block, att_slot(h.f), local.at[6])
            pl.when(away)(copy.start)
            pl.when(jnp.logical_not(away))(stay.start)
            att_sends.append((away, copy, stay))

    def square_steps(d):
        f = h.zstep(d)
        if d > 0:
            gathers[d].middle()
        gathers[d].near()
        for i, c in enumerate((h.cx, h.cy)):
            w.send(o_square.at[c, f], o_square.at[c, f], T_SIB + 3 * d + i, h.c, h.sib)

    def square_last(d):
        f = h.zstep(d)
        gathers[d].end()
        w.send(o_square.at[h.cd, f], o_square.at[h.cd, f], T_SIB + 3 * d + 2, h.c, h.sib)

    attend_and_send(3)
    square_steps(0)
    square_steps(2)
    square_last(0)
    attend_and_send(2)
    square_steps(1)
    square_last(2)
    for d in range(1, 4):
        f = lax.rem(h.f + 8 - 2 * d, 8)
        w.arrived(text_slot(f), T_TKV + d)
        w.send(text_slot(f), text_slot(f), T_TKV + 3 + d, h.c, h.sib)
    attend_and_send(1)
    square_steps(3)
    attend_and_send(0)
    square_last(1)
    square_last(3)
    z_gather.end()
    for d in range(4):
        f = h.zstep(d) + h.sib - h.f
        for i, c in enumerate((h.cx, h.cy, h.cd)):
            w.arrived(o_square.at[c, f], T_SIB + 3 * d + i)
    for d in range(1, 8):
        f = lax.rem(h.f + 8 - d, 8)
        w.arrived(att_slot(f), T_ATT + f)
    w.arrived(text_slot(h.sib), T_TKV)
    for d in range(1, 4):
        w.arrived(text_slot(lax.rem(h.sib + 8 - 2 * d, 8)), T_TKV + 3 + d)
    for i, (c, f) in enumerate(clip_others(h)):
        w.arrived(o_fin.at[c], T_FIN + i)
    for copy in turned:
        copy.wait()
    text_copy.wait()
    w.drain()
    for copy in forwards:
        pl.when(h.is_gate)(copy.wait_send)
    for away, copy, stay in att_sends:
        pl.when(away)(copy.wait_send)
        pl.when(jnp.logical_not(away))(stay.wait)


def front(length, bias, text, hid, cols_a, cols_b, square, fin):
    column = (1024, 256)
    return comm_call(
        front_body,
        (
            shape((8, 128, 1024)),
            shape((1024, 1024)),
            shape(column),
            shape(column),
            shape(column),
            shape(column),
            shape((8, 1024), F32),
            shape((4, 8, 112, 256)),
            shape((4, 8, 64, 256)),
            shape((8, 1024), F32),
            shape((2, 128, 1024)),
            shape((2, 2, 128, 1024)),
            shape((4, 8, 96, 1024)),
            shape((4, 32, 1024)),
        ),
        [SMEM, VMEM, VMEM] + [HBM] * 5,
        (VMEM,) * 10 + (HBM,) * 4,
        [
            pltpu.VMEM((256, ROWS), F32),
            pltpu.VMEM((256, 1024), BF16),
            pltpu.VMEM((2, 128, 256), BF16),
            pltpu.VMEM((96, 1024), BF16),
            pltpu.VMEM((32, 1024), BF16),
            pltpu.SemaphoreType.DMA((7,)),
        ],
        128,
        100,
        1,
    )(length, bias, text, hid, cols_a, cols_b, square, fin)


def attend_back_body(
    length, bias, q_ref, k_ref, v_ref, o_ref, lse_ref, g_ref, dq_ref, dk_ref, dv_ref, dq_t, k_t, dk, dv
):
    k_t[...] = k_ref[...].T
    lane_head = lax.broadcasted_iota(jnp.int32, (ROWS, 256), 1) // HD
    dk[...] = jnp.zeros_like(dk)
    dv[...] = jnp.zeros_like(dv)
    for i in range(1024 // ROWS):
        first, n = i * ROWS, (i + 1) * ROWS
        q = q_ref[first:n, :] * jnp.asarray(HD**-0.5, BF16)
        live = first + lax.broadcasted_iota(jnp.int32, (ROWS, 256), 0) < length[0]
        g = jnp.where(live, g_ref[first:n, :], 0)
        both = (g.astype(F32) * o_ref[first:n, :].astype(F32)).T
        row_dots = jnp.concatenate(
            [jnp.sum(both[HD * j : HD * j + HD], axis=0, keepdims=True) for j in range(4)], axis=0
        )
        lse = lse_ref[0:4, first:n]

        def pick(rows, j):
            at = lax.broadcasted_iota(jnp.int32, rows.shape, 0) == j
            return jnp.sum(jnp.where(at, rows, 0), axis=0, keepdims=True)

        def head(j, _):
            q_head = jnp.where(lane_head == j, q, 0)
            g_head = jnp.where(lane_head == j, g, 0)
            scores = mask_scores(dot(k_ref[0:n, :], q_head, (1, 1)), bias, first, ROWS)
            probs = jnp.exp(scores - pick(lse, j))
            grads = dot(v_ref[0:n, :], g_head, (1, 1))
            dlogits = (probs * (grads - pick(row_dots, j))).astype(BF16)
            dv[0:n, :] += dot(probs.astype(BF16), g_head, (1, 0))
            dk[0:n, :] += dot(dlogits, q_head, (1, 0))
            at = pl.ds(pl.multiple_of(j * HD, HD), HD)
            dq_t[at, :] = dot(k_t[at, 0:n], dlogits, (1, 0))
            return 0

        lax.fori_loop(0, 4, head, 0)
        dq_ref[first:n, :] = (dq_t[...].T * (HD**-0.5)).astype(BF16)
    dk_ref[...] = dk[...].astype(BF16)
    dv_ref[...] = dv[...].astype(BF16)


def attend_back(length, bias, q, k, v, o, lse, g):
    return pl.pallas_call(
        attend_back_body,
        out_shape=(shape((1024, 256)),) * 3,
        in_specs=[SMEM] + [VMEM] * 7,
        out_specs=(VMEM,) * 3,
        scratch_shapes=[
            pltpu.VMEM((256, ROWS), F32),
            pltpu.VMEM((256, 1024), BF16),
            pltpu.VMEM((1024, 256), F32),
            pltpu.VMEM((1024, 256), F32),
        ],
        compiler_params=pltpu.CompilerParams(vmem_limit_bytes=56 * 2**20),
    )(length, bias, q, k, v, o, lse, g)


def square_of(square, which):
    return square[:, 32 * which : 32 * which + 32, :].reshape(1024, 1024)


def text_probs(query, keys, bias, lane_head):
    heads = [jnp.where(lane_head == j, query, 0) for j in range(4)]
    stacked = jnp.concatenate(heads, axis=0)
    scores = dot(stacked, keys, (1, 1)) + bias
    weight = jnp.exp(scores - jnp.max(scores, axis=1, keepdims=True))
    return weight / jnp.sum(weight, axis=1, keepdims=True), stacked


def pick_heads(stacked, lane_head):
    return sum(jnp.where(lane_head == j, stacked[128 * j : 128 * j + 128], 0) for j in range(4))


def near_devices(here):
    return [(here.c, here.sib)] + [(here.c, here.zstep(d)) for d in range(1, 4)] + clip_others(here)[:2]


def middle_body(
    hid, att, square, tkv, text_bias, params, grad, fin,
    o_self, second_ref, query_ref, crossed_ref, o_cross, third_ref, o_grad, o_win,
    v_grad, v_fin, local, send_sem, recv_sem,
):
    h = Here()
    w = Wire(h, send_sem, recv_sem)

    def win_slot(f):
        return o_win.at[:, f]

    own = [
        LocalCopy(grad, v_grad, o_grad.at[h.c], local.at[0]),
        LocalCopy(fin, v_fin, win_slot(h.f), local.at[1]),
    ]
    greet(near_devices(h))
    z_gather = ZGather(w, win_slot, 0, fin)
    grad_gather = ClipGather(
        w,
        lambda c, half: o_grad.at[c, pl.ds(128 * half, 128), :],
        10,
        lambda half: grad.at[pl.ds(128 * half, 128), :],
    )
    z_gather.step(1)
    grad_gather.begin()
    z_gather.relay(0)
    for copy in own:
        copy.turn()
    att_value = att[...].reshape(256, 1024)
    after_self = hid[...].reshape(256, 1024).astype(F32) + dot(att_value, square_of(square, 0), (1, 0))
    o_self[...] = after_self
    xhat, _ = norm_parts(after_self)
    second_ref[...] = (xhat * params[1:2, :] + params[4:5, :]).astype(BF16)
    z_gather.step(2)
    query_ref[...] = dot(second_ref[...], square_of(square, 1), (1, 0)).astype(BF16)
    grad_gather.middle()
    lane_head = lax.broadcasted_iota(jnp.int32, (128, 256), 1) // HD
    for clip in range(2):
        for group in range(4):
            rows, columns = pl.ds(128 * clip, 128), pl.ds(256 * group, 256)
            query = query_ref[rows, columns] * jnp.asarray(HD**-0.5, BF16)
            probs, _ = text_probs(query, tkv[clip, 0, :, columns], text_bias[clip : clip + 1, :], lane_head)
            part = dot(probs.astype(BF16), tkv[clip, 1, :, columns], (1, 0))
            crossed_ref[rows, columns] = pick_heads(part, lane_head).astype(BF16)
        z_gather.step(3 + clip)
    for d in range(1, 4):
        z_gather.relay(d)
    after_cross = o_self[...] + dot(crossed_ref[...], square_of(square, 2), (1, 0))
    o_cross[...] = after_cross
    xhat, _ = norm_parts(after_cross)
    third_ref[...] = (xhat * params[2:3, :] + params[5:6, :]).astype(BF16)
    grad_gather.near()
    grad_gather.end()
    z_gather.end()
    for copy in own:
        copy.wait()
    w.drain()


def middle(hid, att, square, tkv, text_bias, params, grad, fin):
    rows = (256, 1024)
    return comm_call(
        middle_body,
        (
            shape(rows, F32),
            shape(rows),
            shape(rows),
            shape(rows),
            shape(rows, F32),
            shape(rows),
            shape((4, 256, 1024)),
            shape((4, 8, 32, 1024)),
        ),
        [VMEM] * 6 + [HBM] * 2,
        (VMEM,) * 6 + (HBM,) * 2,
        [
            pltpu.VMEM((256, 1024), BF16),
            pltpu.VMEM((4, 32, 1024), BF16),
            pltpu.SemaphoreType.DMA((2,)),
        ],
        20,
        16,
        2,
    )(hid, att, square, tkv, text_bias, params, grad, fin)


def feed_body(
    third, grad, win, fout, o_third, o_out, o_terms,
    tokens, wout, inner, slope, g_pre, terms, slots, local, send_sem, recv_sem,
):
    h = Here()
    w = Wire(h, send_sem, recv_sem)
    own = [
        pltpu.make_async_copy(third, tokens.at[h.c], local.at[0]),
        pltpu.make_async_copy(fout, wout.at[h.f], local.at[1]),
    ]
    for copy in own:
        copy.start()
    greet(near_devices(h))
    gather = ClipGather(
        w,
        lambda c, half: tokens.at[c, pl.ds(128 * half, 128), :],
        0,
        lambda half: third.at[pl.ds(128 * half, 128), :],
    )
    gather.begin()
    z_gather = ZGather(w, lambda f: wout.at[f], 6, fout)
    z_gather.step(1)
    z_gather.relay(0)
    for copy in own:
        copy.wait()

    def hidden(c):
        for part in range(2):
            rows = pl.ds(128 * part, 128)
            pre = dot(tokens[c, rows, :], win[...].reshape(1024, 1024), (1, 0))
            cdf = 0.5 * (1.0 + lax.erf(pre * (0.5**0.5)))
            inner[c, rows, :] = (pre * cdf).astype(BF16)
            slope[c, rows, :] = cdf + pre * jnp.exp(-0.5 * pre * pre) * 0.3989422804014327

    def hidden_back(c):
        g_inner = dot(grad[c], wout[...].reshape(1024, 1024), (1, 1))
        g_pre[c] = (g_inner * slope[c]).astype(BF16)
        terms[c] = dot(g_pre[c], win[...].reshape(1024, 1024), (1, 1)).astype(BF16)

    def out_terms(c):
        o_out[c] = dot(inner[c], wout[...].reshape(1024, 1024), (1, 0)).astype(BF16)

    hidden(h.c)
    z_gather.step(2)
    gather.middle()
    gather.near()
    z_gather.step(3)
    hidden(h.cx)
    z_gather.step(4)
    for d in range(1, 4):
        z_gather.relay(d)
    hidden(h.cy)
    gather.end()
    hidden(h.cd)
    z_gather.end()
    scatter = ClipScatter(
        w,
        lambda c, half: terms.at[c, pl.ds(128 * half, 128), :],
        [slots.at[i] for i in range(6)],
        16,
    )
    hidden_back(h.cd)
    scatter.begin(0)
    hidden_back(h.cx)
    hidden_back(h.cy)
    scatter.begin(1)
    scatter.middle()
    hidden_back(h.c)

    def weight_terms(i, _):
        columns = pl.ds(pl.multiple_of(i * 256, 256), 256)
        tall = (1024, 1024)
        out = dot(inner[:, :, columns].reshape(1024, 256), grad[...].reshape(tall), (0, 0))
        o_terms[pl.ds(2 * i, 2), 0:128, :] = out.astype(BF16).reshape(2, 128, 1024)
        out = dot(tokens[:, :, columns].reshape(1024, 256), g_pre[...].reshape(tall), (0, 0))
        o_terms[:, pl.ds(pl.multiple_of(128 + 32 * i, 32), 32), :] = out.astype(BF16).reshape(8, 32, 1024)
        return 0

    lax.fori_loop(0, 4, weight_terms, 0)
    for c in range(4):
        out_terms(c)
    scatter.end()
    for half in range(2):
        o_third[128 * half : 128 * half + 128, :] = scatter.total(half)
    w.drain()


def feed(third, grad, win, fout):
    full = (4, 256, 1024)
    return comm_call(
        feed_body,
        (shape((256, 1024), F32), shape(full), shape((8, 256, 1024))),
        [HBM, VMEM, VMEM, HBM],
        (VMEM,) * 3,
        [
            pltpu.VMEM(full, BF16),
            pltpu.VMEM((8, 128, 1024), BF16),
            pltpu.VMEM(full, BF16),
            pltpu.VMEM(full, F32),
            pltpu.VMEM(full, BF16),
            pltpu.VMEM(full, BF16),
            pltpu.VMEM((6, 128, 1024), BF16),
            pltpu.SemaphoreType.DMA((2,)),
        ],
        32,
        22,
        3,
    )(third, grad, win, fout)


def norm_back(xhat, scale, grad, gain):
    h = grad * gain
    return scale * (
        h
        - jnp.mean(h, axis=-1, keepdims=True)
        - xhat * jnp.mean(h * xhat, axis=-1, keepdims=True)
    )


def middle_back_body(
    g_third, g_out, after_cross, after_self, second, query_ref, crossed, att, square, tkv, text_bias, params, out_terms,
    o_after_self, o_square, o_heads, o_text, o_norm, o_output,
    g_crossed, g_query, g_att, g_text, slots, sums, from_sib, from_z, local, send_sem, recv_sem,
):
    h = Here()
    w = Wire(h, send_sem, recv_sem)
    greet(frame_others(h) + clip_others(h)[:2])
    scatter = ClipScatter(
        w,
        lambda c, half: out_terms.at[c, pl.ds(128 * half, 128), :],
        [slots.at[i] for i in range(6)],
        16,
    )
    scatter.begin()

    def columns_of(f):
        return pl.ds(pl.multiple_of(lax.rem(f, 4) * 256, 256), 256)

    def part_of(f):
        return g_att.at[lax.div(f, 4), :, columns_of(f)]

    def text_part(f):
        return g_text.at[lax.div(f, 4), :, :, columns_of(f)]

    def put(which, value):
        o_square[:, 32 * which : 32 * which + 32, :] = value.astype(BF16).reshape(32, 32, 1024)

    xhat, scale = norm_parts(after_cross[...])
    grad = g_third[...]
    o_norm[0:1, :] = jnp.sum(grad * xhat, axis=0, keepdims=True)
    o_norm[1:2, :] = jnp.sum(grad, axis=0, keepdims=True)
    g_after_cross = g_out[...].reshape(256, 1024).astype(F32) + norm_back(xhat, scale, grad, params[2:3, :])
    branch = g_after_cross.astype(BF16)
    put(2, dot(crossed[...], branch, (0, 0)))
    g_crossed[...] = dot(branch, square_of(square, 2), (1, 1)).astype(BF16)
    lane_head = lax.broadcasted_iota(jnp.int32, (128, 256), 1) // HD
    for clip in range(2):
        for group in range(4):
            rows, columns = pl.ds(128 * clip, 128), pl.ds(256 * group, 256)
            keys, values = tkv[clip, 0, :, columns], tkv[clip, 1, :, columns]
            query = query_ref[rows, columns] * jnp.asarray(HD**-0.5, BF16)
            probs, stacked = text_probs(query, keys, text_bias[clip : clip + 1, :], lane_head)
            grads = g_crossed[rows, columns]
            g_stacked = jnp.concatenate([jnp.where(lane_head == j, grads, 0) for j in range(4)], axis=0)
            g_probs = dot(g_stacked, values, (1, 1))
            row_dot = jnp.sum(probs * g_probs, axis=1, keepdims=True)
            g_logits = (probs * (g_probs - row_dot)).astype(BF16)
            part = dot(g_logits, keys, (1, 0))
            g_query[rows, columns] = (pick_heads(part, lane_head) * (HD**-0.5)).astype(BF16)
            g_text[clip, 0, :, columns] = dot(g_logits, stacked, (0, 0)).astype(BF16)
            g_text[clip, 1, :, columns] = dot(probs.astype(BF16), g_stacked, (0, 0)).astype(BF16)
        if clip == 0:
            scatter.middle()
    for z in range(4):
        w.send(text_part(2 * z + 1 - h.core), from_sib.at[z], 8 + z, h.c, h.sib)
    put(1, dot(second[...], g_query[...], (0, 0)))
    grad = dot(g_query[...], square_of(square, 1), (1, 1))
    xhat, scale = norm_parts(after_self[...])
    o_norm[2:3, :] = jnp.sum(grad * xhat, axis=0, keepdims=True)
    o_norm[3:4, :] = jnp.sum(grad, axis=0, keepdims=True)
    g_after_self = g_after_cross + norm_back(xhat, scale, grad, params[1:2, :])
    o_after_self[...] = g_after_self
    branch = g_after_self.astype(BF16)
    g_att[...] = dot(branch, square_of(square, 0), (1, 1)).astype(BF16).reshape(2, 128, 1024)
    for d in range(1, 8):
        f = h.step(d)
        w.send(part_of(f), o_heads.at[h.f], d - 1, h.c, f)
    copy = pltpu.make_async_copy(part_of(h.f), o_heads.at[h.f], local.at[0])
    copy.start()
    for z in range(4):
        w.arrived(from_sib.at[z], 8 + z)
        mine = text_part(2 * z + h.core)
        sums[z] = (mine[...].astype(F32) + from_sib[z].astype(F32)).astype(BF16)
    for d in range(1, 4):
        w.send(sums.at[lax.rem(h.z + d, 4)], from_z.at[d - 1], 11 + d, h.c, h.zstep(d))
    put(0, dot(att[...].reshape(256, 1024), branch, (0, 0)))
    scatter.end()
    for half in range(2):
        rows = pl.ds(128 * half, 128)
        o_output[rows, :] = (after_cross[rows, :] + scatter.total(half)).astype(BF16)
    for d in range(1, 4):
        w.arrived(from_z.at[d - 1], 11 + d)
    total = sums[h.z].astype(F32)
    for d in range(3):
        total = total + from_z[d].astype(F32)
    o_text[...] = total.astype(BF16)
    for d in range(1, 8):
        w.arrived(o_heads.at[lax.rem(h.f + 8 - d, 8)], d - 1)
    copy.wait()
    w.drain()


def middle_back(*args):
    rows, block = (256, 1024), (2, 128, 256)
    return comm_call(
        middle_back_body,
        (
            shape(rows, F32),
            shape((32, 96, 1024)),
            shape((8, 128, 256)),
            shape(block),
            shape((8, 1024), F32),
            shape(rows),
        ),
        [VMEM] * 13,
        (VMEM,) * 6,
        [
            pltpu.VMEM(rows, BF16),
            pltpu.VMEM(rows, BF16),
            pltpu.VMEM((2, 128, 1024), BF16),
            pltpu.VMEM((2, 2, 128, 1024), BF16),
            pltpu.VMEM((6, 128, 1024), BF16),
            pltpu.VMEM((4,) + block, BF16),
            pltpu.VMEM((4,) + block, BF16),
            pltpu.VMEM((3,) + block, BF16),
            pltpu.SemaphoreType.DMA((1,)),
        ],
        24,
        24,
        4,
    )(*args)


def last_body(
    first, square, cols, text, o_first, o_square, o_cols, o_norm, o_text,
    f_sib, f_sum, f_in, s_sib, s_sum, s_slots, s_z, s_zin, c_slots, c_sum, c_in, t_in,
    send_sem, recv_sem,
):
    h = Here()
    w = Wire(h, send_sem, recv_sem)
    greet(frame_others(h) + clip_others(h)[:2])
    T_F, T_S, T_C, T_T = 0, 12, 24, 40
    for z in range(4):
        w.send(first.at[2 * z + 1 - h.core], f_sib.at[z], T_F + z, h.c, h.sib)
    for z in range(4):
        w.send(square.at[:, 2 * z + 1 - h.core], s_sib.at[:, z], T_S + z, h.c, h.sib)
    cols_scatter = ClipScatter(
        w,
        lambda c, half: cols.at[c, pl.ds(4 * half, 4)],
        [c_slots.at[i] for i in range(6)],
        T_C,
    )
    cols_scatter.begin()
    for d in range(1, 8):
        f = h.step(d)
        w.send(text.at[pl.ds(pl.multiple_of(f * 16, 16), 16), :], t_in.at[h.f], T_T + d - 1, h.c, f)
    t_in[h.f] = text[pl.ds(pl.multiple_of(h.f * 16, 16), 16), :]
    for z in range(4):
        w.arrived(f_sib.at[z], T_F + z)
        f_sum[z] = (first[2 * z + h.core].astype(F32) + f_sib[z].astype(F32)).astype(BF16)
    other = 2 * (1 - h.pair)
    is_end = jnp.logical_not(h.is_gate)
    w.send(f_sum.at[lax.div(h.partner, 2)], f_in.at[0], T_F + 4, h.c, h.partner)
    to_gate, to_far = [], []
    for j in range(2):
        to_gate.append(w.copy(f_sum.at[other + j], f_in.at[1 + j], T_F + 5 + j, h.c, h.partner))
        pl.when(is_end)(to_gate[j].start)
    for z in range(4):
        w.arrived(s_sib.at[:, z], T_S + z)

    def add_square(i, _):
        c, z = lax.div(i, 4), lax.rem(i, 4)
        s_sum[c, z] = (square[c, 2 * z + h.core].astype(F32) + s_sib[c, z].astype(F32)).astype(BF16)
        return 0

    lax.fori_loop(0, 16, add_square, 0)
    square_scatter = ClipScatter(
        w,
        lambda c, half: s_sum.at[c, :, pl.ds(48 * half, 48), :],
        [s_slots.at[i] for i in range(6)],
        T_S + 4,
    )
    square_scatter.begin()
    for j in range(2):
        @pl.when(h.is_gate)
        def _():
            w.arrived(f_in.at[1 + j], T_F + 5 + j)
            f_sum[other + j] = (f_sum[other + j].astype(F32) + f_in[1 + j].astype(F32)).astype(BF16)

        to_far.append(w.copy(f_sum.at[other + j], f_in.at[3], T_F + 7, h.c, h.far[j]))
        pl.when(h.is_gate)(to_far[j].start)
    cols_scatter.middle()
    square_scatter.middle()
    cols_scatter.end()
    for half in range(2):
        c_sum[4 * half : 4 * half + 4] = cols_scatter.total(half).astype(BF16)
    for d in range(1, 8):
        f = h.step(d)
        w.send(c_sum.at[f], c_in.at[h.f], T_C + 6 + d - 1, h.c, f)
    c_in[h.f] = c_sum[h.f]
    square_scatter.end()
    for half in range(2):
        s_z[:, 48 * half : 48 * half + 48, :] = square_scatter.total(half).astype(BF16)
    for d in range(1, 4):
        w.send(s_z.at[lax.rem(h.z + d, 4)], s_zin.at[d - 1], T_S + 10 + d - 1 if d < 3 else 47, h.c, h.zstep(d))
    w.arrived(f_in.at[0], T_F + 4)
    w.arrived(f_in.at[3], T_F + 7)
    o_first[h.pair] = f_sum[h.z].astype(F32) + f_in[0].astype(F32)
    o_first[1 - h.pair] = f_in[3].astype(F32)
    for d in range(1, 8):
        w.arrived(t_in.at[lax.rem(h.f + 8 - d, 8)], T_T + d - 1)
    for p in range(2):
        o_text[p] = sum(t_in[4 * p + q].astype(F32) for q in range(4)).astype(BF16)
    for d in range(1, 8):
        w.arrived(c_in.at[lax.rem(h.f + 8 - d, 8)], T_C + 6 + d - 1)
    for q in range(4):
        o_cols[:, 256 * q : 256 * q + 256] = c_in[q, 0:160, :].astype(F32) + c_in[4 + q, 0:160, :].astype(F32)
    o_norm[...] = sum(c_in[f, 160:176, 0:128].astype(F32) for f in range(8))
    for d in range(1, 4):
        w.arrived(s_zin.at[d - 1], T_S + 10 + d - 1 if d < 3 else 47)
    o_square[...] = s_z[h.z].astype(F32) + sum(s_zin[d].astype(F32) for d in range(3))
    w.drain()
    for j in range(2):
        pl.when(is_end)(to_gate[j].wait_send)
        pl.when(h.is_gate)(to_far[j].wait_send)


def last_sums(first, square, cols, text):
    def buffer(*dims):
        return pltpu.VMEM(dims, BF16)

    return comm_call(
        last_body,
        (
            shape((2, 128, 1024), F32),
            shape((96, 1024), F32),
            shape((160, 1024), F32),
            shape((16, 128), F32),
            shape((2, 16, 1024)),
        ),
        [VMEM] * 4,
        (VMEM,) * 5,
        [
            buffer(4, 128, 1024),
            buffer(4, 128, 1024),
            buffer(4, 128, 1024),
            buffer(4, 4, 96, 1024),
            buffer(4, 4, 96, 1024),
            buffer(6, 4, 48, 1024),
            buffer(4, 96, 1024),
            buffer(3, 96, 1024),
            buffer(6, 4, 176, 256),
            buffer(8, 176, 256),
            buffer(8, 176, 256),
            buffer(8, 16, 1024),
        ],
        64,
        48,
        5,
    )(first, square, cols, text)


def matmul(left, right):
    return jnp.dot(left, right, preferred_element_type=F32)


def on_device_fast(
    hidden_in,
    text_states,
    out_grad,
    self_qkv,
    self_out,
    cross_qkv,
    cross_out,
    ffn_in,
    ffn_out,
    ln_gain,
    ln_bias,
    clip_len,
    frame_mask,
    text_len,
    text_mask,
):
    frame = lax.axis_index("frame")
    pair = frame // 4
    norms = jnp.concatenate([ln_gain, ln_bias], axis=0)
    placed = lax.dynamic_update_slice(jnp.zeros((16, 256), BF16), norms, (0, 32 * (frame % 4)))
    cols_a = jnp.concatenate(
        [jnp.moveaxis(self_qkv, 1, 0).reshape(96, 1024), jnp.tile(placed, (1, 4))], axis=0
    )
    cols_b = jnp.moveaxis(cross_qkv, 1, 0)[1:].reshape(64, 1024)
    square_here = jnp.concatenate([self_out, cross_qkv[:, 0], cross_out], axis=0)
    columns = jnp.arange(1024, dtype=jnp.int32)
    my_len = lax.dynamic_slice_in_dim(clip_len, pair, 1, 0)
    my_mask = lax.dynamic_slice_in_dim(frame_mask, pair, 1, 0)[0]
    bias = jnp.where((columns < my_len) & (my_mask > 0), 0.0, NEG).astype(F32)
    bias = jnp.broadcast_to(bias[:, None], (1024, 128))
    (
        hid_all, first_low, query, key, value, att_heads, lse, w_a, w_b, params, att, tkv, square, fin_all
    ) = front(my_len, bias, text_states, hidden_in, cols_a, cols_b, square_here, ffn_in)
    square = square.reshape(32, 96, 1024)
    weights = [w_a[:, :, 32 * j : 32 * j + 32].reshape(1024, 256) for j in range(3)]
    weights += [w_b[:, :, 32 * j : 32 * j + 32].reshape(1024, 256) for j in range(2)]
    first_hat, _ = norm_parts(hid_all.reshape(1024, 1024).astype(F32))
    my_text = lax.dynamic_slice_in_dim(text_states, pair, 1, 0)[0]
    slots = jnp.arange(128, dtype=jnp.int32)
    text_ok = (slots[None] < text_len[:, None]) & ((text_mask > 0) | (slots[None] == 0))
    text_bias = jnp.where(text_ok, 0.0, NEG).astype(F32)
    after_self, second, cross_query, crossed, after_cross, third, grad_all, ffn_w_in = middle(
        hidden_in, att, square, tkv, text_bias, params, out_grad.reshape(256, 1024), fin_all
    )
    third_sum, out_terms, ffn_terms = feed(third, grad_all, ffn_w_in, ffn_out)
    ffn_sum = lax.psum_scatter(ffn_terms, "frame", scatter_dimension=0, tiled=True)[0]
    grad_ffn_out = ffn_sum[:128].astype(F32)
    grad_ffn_in = lax.all_to_all(
        ffn_sum[128:].reshape(4, 32, 1024), "clip", split_axis=0, concat_axis=2, tiled=True
    )[0].astype(F32)
    g_after_self, g_square, g_heads, g_tkv, g_norms, output = middle_back(
        third_sum, out_grad, after_cross, after_self, second, cross_query, crossed, att, square, tkv,
        text_bias, params, out_terms,
    )
    output = output.reshape(2, 128, 1024)
    g_query, g_key, g_value = attend_back(
        my_len, bias, query, key, value, att_heads, lse, g_heads.reshape(1024, 256)
    )

    def back(grad, weight):
        return lax.dot_general(grad, weight, (((1,), (1,)), ((), ())), preferred_element_type=F32)

    def weight_term(left, grad):
        return lax.dot_general(left, grad, (((0,), (0,)), ((), ())), preferred_element_type=F32)

    g_first = back(g_query, weights[0]) + back(g_key, weights[1]) + back(g_value, weights[2])
    gain_first = jnp.sum(g_first * first_hat, axis=0)
    shift_first = jnp.sum(g_first, axis=0)
    text_terms = (back(g_tkv[0], weights[3]) + back(g_tkv[1], weights[4])).astype(BF16)
    terms = jnp.stack(
        [weight_term(first_low, g) for g in (g_query, g_key, g_value)]
        + [weight_term(my_text, g_tkv[i]) for i in range(2)]
    )
    terms = terms.astype(BF16).reshape(5, 4, 8, 32, 256).transpose(1, 2, 0, 3, 4).reshape(4, 8, 160, 256)
    norm_terms = jnp.stack([gain_first, g_norms[2], g_norms[0], shift_first, g_norms[3], g_norms[1]])
    norm_terms = norm_terms.astype(BF16).reshape(6, 4, 8, 32).transpose(1, 2, 0, 3)
    norm_terms = jnp.pad(norm_terms, ((0, 0), (0, 0), (0, 10), (0, 224)))
    cols = jnp.concatenate([terms, norm_terms], axis=2)
    first_sum, square_sum, cols_sum, norm_sum, grad_text = last_sums(
        g_first.astype(BF16).reshape(8, 128, 1024), g_square.reshape(4, 8, 96, 1024), cols, text_terms
    )
    own_hat, own_scale = norm_parts(hidden_in.astype(F32))
    grad_hidden = (
        g_after_self.reshape(2, 128, 1024) + norm_back(own_hat, own_scale, first_sum, params[0])
    ).astype(BF16)
    cols_sum = cols_sum.reshape(5, 32, 1024)
    return (
        output,
        grad_hidden,
        grad_text,
        jnp.stack([cols_sum[0], cols_sum[1], cols_sum[2]], axis=1),
        square_sum[0:32],
        jnp.stack([square_sum[32:64], cols_sum[3], cols_sum[4]], axis=1),
        square_sum[64:96],
        grad_ffn_in,
        grad_ffn_out,
        norm_sum[0:3, 0:32],
        norm_sum[3:6, 0:32],
    )

def solution(mesh):
    return jax.shard_map(
        on_device_fast if fits(mesh) else on_device_any,
        mesh=mesh,
        in_specs=(
            P("clip", "frame", None),
            P("clip", None, None),
            P("clip", "frame", None),
            P(("clip", "frame"), None, None),
            P(("clip", "frame"), None),
            P(("clip", "frame"), None, None),
            P(("clip", "frame"), None),
            P(("clip", "frame"), None),
            P(("clip", "frame"), None),
            P(None, ("clip", "frame")),
            P(None, ("clip", "frame")),
            P("clip"),
            P("clip", None),
            P("clip"),
            P("clip", None),
        ),
        out_specs=(
            P("clip", "frame", None),
            P("clip", "frame", None),
            P("clip", "frame", None),
            P(("clip", "frame"), None, None),
            P(("clip", "frame"), None),
            P(("clip", "frame"), None, None),
            P(("clip", "frame"), None),
            P(("clip", "frame"), None),
            P(("clip", "frame"), None),
            P(None, ("clip", "frame")),
            P(None, ("clip", "frame")),
        ),
        check_vma=False,
    )
```

```python
import functools

import jax
import jax.numpy as jnp
from jax import lax
from jax.experimental import pallas as pl
from jax.experimental.pallas import tpu as pltpu
from jax.sharding import PartitionSpec as P

HD = 64


MASKED = -1000000000.0
EPSILON = 1e-05


def layer_norm(value, gain, shift):
    average = jnp.mean(value, axis=-1, keepdims=True)
    centered = value - average
    variance = jnp.mean(centered * centered, axis=-1, keepdims=True)
    return centered * lax.rsqrt(variance + EPSILON) * gain + shift


def activate(value):
    return jax.nn.gelu(value, approximate=False)


def project(left, right):
    return jnp.einsum("cnd,de->cne", left, right, preferred_element_type=jnp.float32)


def project_back(grad_rows, weight):
    return jnp.einsum("cne,de->cnd", grad_rows, weight, preferred_element_type=jnp.float32)


def weight_grad(left, right):
    return jnp.einsum("cnd,cne->de", left, right, preferred_element_type=jnp.float32)


def fetch_attention(self_qkv, self_out, cross_qkv, cross_out, ln_gain, ln_bias):
    return (
        lax.all_gather(self_qkv, ("clip", "frame"), axis=0, tiled=True),
        lax.all_gather(self_out, ("clip", "frame"), axis=0, tiled=True),
        lax.all_gather(cross_qkv, ("clip", "frame"), axis=0, tiled=True),
        lax.all_gather(cross_out, ("clip", "frame"), axis=0, tiled=True),
        lax.all_gather(ln_gain, ("clip", "frame"), axis=1, tiled=True),
        lax.all_gather(ln_bias, ("clip", "frame"), axis=1, tiled=True),
    )


def fetch_ffn(ffn_in, ffn_out):
    return (
        lax.all_gather(ffn_in, ("clip", "frame"), axis=0, tiled=True),
        lax.all_gather(ffn_out, ("clip", "frame"), axis=0, tiled=True),
    )


def self_masks(first_row, block_rows, clip_len, key_valid):
    columns = jnp.arange(key_valid.shape[1], dtype=jnp.int32)
    row_ids = first_row + jnp.arange(block_rows, dtype=jnp.int32)
    diagonal = columns[None, :] == row_ids[:, None]
    allowed = (columns[None, :] <= row_ids[:, None])[None] & (
        key_valid[:, None, :] | diagonal[None]
    )
    live_rows = (row_ids[None, :] < clip_len[:, None]).astype(jnp.float32)
    return (allowed[:, None], live_rows[:, None, :, None])


def self_forward(query_rows, key_rows, value_rows, clip_len, key_valid):
    length = query_rows.shape[1]
    block_rows = min(512, length)
    score_scale = query_rows.shape[3] ** (-0.5)

    def one_block(block_index):
        first_row = block_index * block_rows
        query_block = lax.dynamic_slice_in_dim(query_rows, first_row, block_rows, 1)
        raw_scores = jnp.einsum(
            "cqhd,ckhd->chqk", query_block, key_rows, preferred_element_type=jnp.float32
        )
        allowed, live_rows = self_masks(first_row, block_rows, clip_len, key_valid)
        logits = jnp.where(allowed, raw_scores * score_scale, MASKED)
        row_max = jnp.max(logits, axis=-1, keepdims=True)
        exponent = jnp.exp(logits - row_max)
        row_sum = jnp.sum(exponent, axis=-1, keepdims=True)
        weights = (exponent / row_sum * live_rows).astype(jnp.bfloat16)
        attended = jnp.einsum(
            "chqk,ckhd->cqhd", weights, value_rows, preferred_element_type=jnp.float32
        )
        return (attended.astype(jnp.bfloat16), row_max + jnp.log(row_sum))

    blocks, log_sums = lax.map(one_block, jnp.arange(length // block_rows, dtype=jnp.int32))
    return (jnp.moveaxis(blocks, 0, 1).reshape(query_rows.shape), log_sums)


def self_backward(query_rows, key_rows, value_rows, grad_rows, log_sums, clip_len, key_valid):
    length = query_rows.shape[1]
    block_rows = min(512, length)
    score_scale = query_rows.shape[3] ** (-0.5)

    def one_block(totals, block_index):
        grad_keys, grad_values = totals
        first_row = block_index * block_rows
        query_block = lax.dynamic_slice_in_dim(query_rows, first_row, block_rows, 1)
        grad_block = lax.dynamic_slice_in_dim(grad_rows, first_row, block_rows, 1)
        raw_scores = jnp.einsum(
            "cqhd,ckhd->chqk", query_block, key_rows, preferred_element_type=jnp.float32
        )
        allowed, live_rows = self_masks(first_row, block_rows, clip_len, key_valid)
        logits = jnp.where(allowed, raw_scores * score_scale, MASKED)
        probs = jnp.exp(logits - log_sums[block_index])
        weights = (probs * live_rows).astype(jnp.bfloat16)
        grad_probs = (
            jnp.einsum(
                "cqhd,ckhd->chqk", grad_block, value_rows, preferred_element_type=jnp.float32
            )
            * live_rows
        )
        row_dot = jnp.sum(probs * grad_probs, axis=-1, keepdims=True)
        grad_scores = (probs * (grad_probs - row_dot)).astype(jnp.bfloat16)
        grad_query = (
            jnp.einsum("chqk,ckhd->cqhd", grad_scores, key_rows, preferred_element_type=jnp.float32)
            * score_scale
        )
        grad_keys = (
            grad_keys
            + jnp.einsum(
                "chqk,cqhd->ckhd", grad_scores, query_block, preferred_element_type=jnp.float32
            )
            * score_scale
        )
        grad_values = grad_values + jnp.einsum(
            "chqk,cqhd->ckhd", weights, grad_block, preferred_element_type=jnp.float32
        )
        return ((grad_keys, grad_values), grad_query)

    zeros = jnp.zeros(key_rows.shape, jnp.float32)
    (grad_keys, grad_values), grad_blocks = lax.scan(
        one_block, (zeros, zeros), jnp.arange(length // block_rows, dtype=jnp.int32)
    )
    grad_query = jnp.moveaxis(grad_blocks, 0, 1).reshape(query_rows.shape)
    return (grad_query, grad_keys, grad_values)


def text_allowed(text_len, text_mask):
    slots = jnp.arange(text_mask.shape[1], dtype=jnp.int32)
    allowed = (slots[None, :] < text_len[:, None]) & ((text_mask > 0) | (slots[None, :] == 0))
    return allowed[:, None, None, :]


def cross_forward(query_rows, key_rows, value_rows, allowed):
    score_scale = query_rows.shape[3] ** (-0.5)
    raw_scores = jnp.einsum(
        "cqhd,ckhd->chqk", query_rows, key_rows, preferred_element_type=jnp.float32
    )
    logits = jnp.where(allowed, raw_scores * score_scale, MASKED)
    row_max = jnp.max(logits, axis=-1, keepdims=True)
    exponent = jnp.exp(logits - row_max)
    row_sum = jnp.sum(exponent, axis=-1, keepdims=True)
    weights = (exponent / row_sum).astype(jnp.bfloat16)
    crossed = jnp.einsum("chqk,ckhd->cqhd", weights, value_rows, preferred_element_type=jnp.float32)
    return (crossed.astype(jnp.bfloat16), row_max + jnp.log(row_sum))


def cross_backward(query_rows, key_rows, value_rows, grad_rows, log_sums, allowed):
    score_scale = query_rows.shape[3] ** (-0.5)
    raw_scores = jnp.einsum(
        "cqhd,ckhd->chqk", query_rows, key_rows, preferred_element_type=jnp.float32
    )
    logits = jnp.where(allowed, raw_scores * score_scale, MASKED)
    probs = jnp.exp(logits - log_sums)
    weights = probs.astype(jnp.bfloat16)
    grad_probs = jnp.einsum(
        "cqhd,ckhd->chqk", grad_rows, value_rows, preferred_element_type=jnp.float32
    )
    row_dot = jnp.sum(probs * grad_probs, axis=-1, keepdims=True)
    grad_scores = (probs * (grad_probs - row_dot)).astype(jnp.bfloat16)
    grad_query = (
        jnp.einsum("chqk,ckhd->cqhd", grad_scores, key_rows, preferred_element_type=jnp.float32)
        * score_scale
    )
    grad_keys = (
        jnp.einsum("chqk,cqhd->ckhd", grad_scores, query_rows, preferred_element_type=jnp.float32)
        * score_scale
    )
    grad_values = jnp.einsum(
        "chqk,cqhd->ckhd", weights, grad_rows, preferred_element_type=jnp.float32
    )
    return (grad_query, grad_keys, grad_values)


def sum_ffn(grad_ffn_in, grad_ffn_out):
    return (
        lax.psum_scatter(grad_ffn_in, ("clip", "frame"), scatter_dimension=0, tiled=True),
        lax.psum_scatter(grad_ffn_out, ("clip", "frame"), scatter_dimension=0, tiled=True),
    )


def sum_attention(
    grad_self_qkv, grad_self_out, grad_cross_qkv, grad_cross_out, grad_gains, grad_shifts
):
    return (
        lax.psum_scatter(grad_self_qkv, ("clip", "frame"), scatter_dimension=0, tiled=True),
        lax.psum_scatter(grad_self_out, ("clip", "frame"), scatter_dimension=0, tiled=True),
        lax.psum_scatter(grad_cross_qkv, ("clip", "frame"), scatter_dimension=0, tiled=True),
        lax.psum_scatter(grad_cross_out, ("clip", "frame"), scatter_dimension=0, tiled=True),
        lax.psum_scatter(grad_gains, ("clip", "frame"), scatter_dimension=1, tiled=True),
        lax.psum_scatter(grad_shifts, ("clip", "frame"), scatter_dimension=1, tiled=True),
    )


def on_device_any(
    hidden_in,
    text_states,
    out_grad,
    self_qkv,
    self_out,
    cross_qkv,
    cross_out,
    ffn_in,
    ffn_out,
    ln_gain,
    ln_bias,
    clip_len,
    frame_mask,
    text_len,
    text_mask,
):
    clip_count, frames, model_width = hidden_in.shape
    text_slots = text_states.shape[1]
    group_count = lax.axis_size("frame")
    columns_here = model_width // group_count
    heads_here = columns_here // HD
    length = frames * group_count
    frame_index = lax.axis_index("frame")
    full_qkv, full_out, full_cross, full_cross_out, gains_low, shifts_low = fetch_attention(
        self_qkv, self_out, cross_qkv, cross_out, ln_gain, ln_bias
    )
    gains = gains_low.astype(jnp.float32)
    shifts = shifts_low.astype(jnp.float32)
    hidden = hidden_in.astype(jnp.float32)
    first_norm, first_pull = jax.vjp(layer_norm, hidden, gains[0], shifts[0])
    first_low = first_norm.astype(jnp.bfloat16)
    query_low = project(first_low, full_qkv[:, 0]).astype(jnp.bfloat16)
    key_low = project(first_low, full_qkv[:, 1]).astype(jnp.bfloat16)
    value_low = project(first_low, full_qkv[:, 2]).astype(jnp.bfloat16)
    query_heads, key_heads, value_heads = (
        lax.all_to_all(query_low, "frame", split_axis=2, concat_axis=1, tiled=True),
        lax.all_to_all(key_low, "frame", split_axis=2, concat_axis=1, tiled=True),
        lax.all_to_all(value_low, "frame", split_axis=2, concat_axis=1, tiled=True),
    )
    head_shape = (clip_count, length, heads_here, HD)
    query_heads = query_heads.reshape(head_shape)
    key_heads = key_heads.reshape(head_shape)
    value_heads = value_heads.reshape(head_shape)
    columns = jnp.arange(length, dtype=jnp.int32)
    key_valid = (columns[None, :] < clip_len[:, None]) & (frame_mask > 0)
    attended_heads, self_sums = self_forward(
        query_heads, key_heads, value_heads, clip_len, key_valid
    )
    attended = lax.all_to_all(
        attended_heads.reshape(clip_count, length, columns_here),
        "frame",
        split_axis=1,
        concat_axis=2,
        tiled=True,
    )
    after_self = hidden + project(attended, full_out)
    second_norm, second_pull = jax.vjp(layer_norm, after_self, gains[1], shifts[1])
    second_low = second_norm.astype(jnp.bfloat16)
    cross_query = project(second_low, full_cross[:, 0]).astype(jnp.bfloat16)
    cross_query_heads = lax.all_to_all(
        cross_query, "frame", split_axis=2, concat_axis=1, tiled=True
    ).reshape(head_shape)
    key_columns = lax.dynamic_slice_in_dim(
        full_cross[:, 1], frame_index * columns_here, columns_here, 1
    )
    value_columns = lax.dynamic_slice_in_dim(
        full_cross[:, 2], frame_index * columns_here, columns_here, 1
    )
    text_shape = (clip_count, text_slots, heads_here, HD)
    text_keys = project(text_states, key_columns).astype(jnp.bfloat16).reshape(text_shape)
    text_values = project(text_states, value_columns).astype(jnp.bfloat16).reshape(text_shape)
    allowed_text = text_allowed(text_len, text_mask)
    crossed_heads, cross_sums = cross_forward(
        cross_query_heads, text_keys, text_values, allowed_text
    )
    crossed = lax.all_to_all(
        crossed_heads.reshape(clip_count, length, columns_here),
        "frame",
        split_axis=1,
        concat_axis=2,
        tiled=True,
    )
    after_cross = after_self + project(crossed, full_cross_out)
    ffn_weight_in, ffn_weight_out = fetch_ffn(ffn_in, ffn_out)
    third_norm, third_pull = jax.vjp(layer_norm, after_cross, gains[2], shifts[2])
    third_low = third_norm.astype(jnp.bfloat16)
    pre_act = project(third_low, ffn_weight_in)
    activated, gelu_pull = jax.vjp(activate, pre_act)
    inner_low = activated.astype(jnp.bfloat16)
    output = (after_cross + project(inner_low, ffn_weight_out)).astype(jnp.bfloat16)
    ffn_weight_in, ffn_weight_out = fetch_ffn(ffn_in, ffn_out)
    grad_ffn_out = weight_grad(inner_low, out_grad)
    (grad_pre,) = gelu_pull(project_back(out_grad, ffn_weight_out))
    grad_pre_low = grad_pre.astype(jnp.bfloat16)
    grad_ffn_in = weight_grad(third_low, grad_pre_low)
    ffn_sums = sum_ffn(grad_ffn_in, grad_ffn_out)
    grad_third, gain_third, shift_third = third_pull(project_back(grad_pre_low, ffn_weight_in))
    grad_after_cross = out_grad.astype(jnp.float32) + grad_third
    full_qkv, full_out, full_cross, full_cross_out, gains_low, shifts_low = fetch_attention(
        self_qkv, self_out, cross_qkv, cross_out, ln_gain, ln_bias
    )
    key_columns = lax.dynamic_slice_in_dim(
        full_cross[:, 1], frame_index * columns_here, columns_here, 1
    )
    value_columns = lax.dynamic_slice_in_dim(
        full_cross[:, 2], frame_index * columns_here, columns_here, 1
    )
    cross_branch = grad_after_cross.astype(jnp.bfloat16)
    grad_cross_out = weight_grad(crossed, cross_branch)
    grad_crossed = project_back(cross_branch, full_cross_out).astype(jnp.bfloat16)
    grad_crossed_heads = lax.all_to_all(
        grad_crossed, "frame", split_axis=2, concat_axis=1, tiled=True
    ).reshape(head_shape)
    grad_cq, grad_tk, grad_tv = cross_backward(
        cross_query_heads, text_keys, text_values, grad_crossed_heads, cross_sums, allowed_text
    )
    grad_tk_low = grad_tk.astype(jnp.bfloat16).reshape(clip_count, text_slots, columns_here)
    grad_tv_low = grad_tv.astype(jnp.bfloat16).reshape(clip_count, text_slots, columns_here)
    text_terms = project_back(grad_tk_low, key_columns) + project_back(grad_tv_low, value_columns)
    grad_text = lax.psum_scatter(
        text_terms.astype(jnp.bfloat16), "frame", scatter_dimension=1, tiled=True
    )
    empty_square = jnp.zeros((model_width, model_width), jnp.float32)
    grad_cross_key = lax.dynamic_update_slice_in_dim(
        empty_square, weight_grad(text_states, grad_tk_low), frame_index * columns_here, 1
    )
    grad_cross_value = lax.dynamic_update_slice_in_dim(
        empty_square, weight_grad(text_states, grad_tv_low), frame_index * columns_here, 1
    )
    grad_cq_low = grad_cq.astype(jnp.bfloat16).reshape(clip_count, length, columns_here)
    grad_cross_query = lax.all_to_all(grad_cq_low, "frame", split_axis=1, concat_axis=2, tiled=True)
    grad_cross_qw = weight_grad(second_low, grad_cross_query)
    grad_second, gain_second, shift_second = second_pull(
        project_back(grad_cross_query, full_cross[:, 0])
    )
    grad_after_self = grad_after_cross + grad_second
    self_branch = grad_after_self.astype(jnp.bfloat16)
    grad_self_out = weight_grad(attended, self_branch)
    grad_attended = project_back(self_branch, full_out).astype(jnp.bfloat16)
    grad_attended_heads = lax.all_to_all(
        grad_attended, "frame", split_axis=2, concat_axis=1, tiled=True
    ).reshape(head_shape)
    grad_query, grad_keys, grad_values = self_backward(
        query_heads, key_heads, value_heads, grad_attended_heads, self_sums, clip_len, key_valid
    )
    flat_shape = (clip_count, length, columns_here)
    grad_query, grad_keys, grad_values = (
        lax.all_to_all(
            grad_query.astype(jnp.bfloat16).reshape(flat_shape),
            "frame",
            split_axis=1,
            concat_axis=2,
            tiled=True,
        ),
        lax.all_to_all(
            grad_keys.astype(jnp.bfloat16).reshape(flat_shape),
            "frame",
            split_axis=1,
            concat_axis=2,
            tiled=True,
        ),
        lax.all_to_all(
            grad_values.astype(jnp.bfloat16).reshape(flat_shape),
            "frame",
            split_axis=1,
            concat_axis=2,
            tiled=True,
        ),
    )
    grad_self_qkv = jnp.stack(
        [
            weight_grad(first_low, grad_query),
            weight_grad(first_low, grad_keys),
            weight_grad(first_low, grad_values),
        ],
        axis=1,
    )
    grad_first_norm = (
        project_back(grad_query, full_qkv[:, 0])
        + project_back(grad_keys, full_qkv[:, 1])
        + project_back(grad_values, full_qkv[:, 2])
    )
    grad_first, gain_first, shift_first = first_pull(grad_first_norm)
    grad_hidden = (grad_after_self + grad_first).astype(jnp.bfloat16)
    grad_cross_qkv = jnp.stack([grad_cross_qw, grad_cross_key, grad_cross_value], axis=1)
    grad_gains = jnp.stack([gain_first, gain_second, gain_third])
    grad_shifts = jnp.stack([shift_first, shift_second, shift_third])
    attn_sums = sum_attention(
        grad_self_qkv, grad_self_out, grad_cross_qkv, grad_cross_out, grad_gains, grad_shifts
    )
    return (
        output,
        grad_hidden,
        grad_text,
        attn_sums[0],
        attn_sums[1],
        attn_sums[2],
        attn_sums[3],
        ffn_sums[0],
        ffn_sums[1],
        attn_sums[4],
        attn_sums[5],
    )


MESH = pl.DeviceIdType.MESH
HBM = pl.BlockSpec(memory_space=pl.ANY)
VMEM = pl.BlockSpec(memory_space=pltpu.VMEM)
SMEM = pl.BlockSpec(memory_space=pltpu.SMEM)
NEG = -1e30
F32 = jnp.float32
BF16 = jnp.bfloat16


def fits(mesh):
    return mesh.shape["clip"] == 4 and mesh.shape["frame"] == 8


class Here:
    def __init__(self):
        self.c = lax.axis_index("clip")
        self.f = lax.axis_index("frame")
        self.core = lax.rem(self.f, 2)
        self.z = lax.div(self.f, 2)
        self.pair = lax.div(self.z, 2)
        self.role = lax.rem(self.z, 2)
        self.group = lax.rem(self.f, 4)
        self.cx = self.c + 1 - 2 * lax.rem(self.c, 2)
        self.cy = lax.rem(self.c + 2, 4)
        self.cd = 3 - self.c
        self.sib = self.f + 1 - 2 * self.core
        self.partner = self.f + 2 - 4 * self.role
        self.far_gate = 2 * (2 - self.pair) + self.core
        self.is_gate = self.role + self.pair == 1
        self.far = [2 * (2 * (1 - self.pair) + j) + self.core for j in range(2)]

    def step(self, d):
        return lax.rem(self.f + d, 8)

    def zstep(self, d):
        return lax.rem(self.f + 2 * d, 8)


class Wire:
    def __init__(self, here, send_sem, recv_sem):
        self.here, self.send_sem, self.recv_sem = here, send_sem, recv_sem
        self.used = 0
        self.open = []

    def copy(self, src, dst, tag, c, f):
        self.used += 1
        return pltpu.make_async_remote_copy(
            src_ref=src,
            dst_ref=dst,
            send_sem=self.send_sem.at[self.used - 1],
            recv_sem=self.recv_sem.at[tag],
            device_id=(c, f),
            device_id_type=MESH,
        )

    def send(self, src, dst, tag, c, f):
        copy = self.copy(src, dst, tag, c, f)
        copy.start()
        self.open.append(copy)

    def arrived(self, dst, tag):
        pltpu.make_async_remote_copy(
            src_ref=dst,
            dst_ref=dst,
            send_sem=self.send_sem.at[0],
            recv_sem=self.recv_sem.at[tag],
            device_id=(self.here.c, self.here.sib),
            device_id_type=MESH,
        ).wait_recv()

    def drain(self):
        for copy in self.open:
            copy.wait_send()
        self.open = []


def greet(devices):
    barrier = pltpu.get_barrier_semaphore()
    for device in devices:
        pl.semaphore_signal(barrier, inc=1, device_id=device, device_id_type=MESH)
    pl.semaphore_wait(barrier, len(devices))


def frame_others(here):
    return [(here.c, here.step(d)) for d in range(1, 8)]


def clip_others(here):
    return [(here.cx, here.f), (here.cy, here.f), (here.cd, here.f)]


class ClipGather:
    def __init__(self, wire, block, tag, own=None):
        self.wire, self.block, self.tag = wire, block, tag
        self.own = own or (lambda half: block(wire.here.c, half))

    def begin(self):
        h, w, b, t, own = self.wire.here, self.wire, self.block, self.tag, self.own
        w.send(own(0), b(h.c, 0), t, h.cx, h.f)
        w.send(own(1), b(h.c, 1), t + 2, h.cy, h.f)
        w.send(own(1), b(h.c, 1), t + 1, h.cx, h.f)
        w.send(own(0), b(h.c, 0), t + 3, h.cy, h.f)

    def middle(self):
        h, w, b, t = self.wire.here, self.wire, self.block, self.tag
        w.arrived(b(h.cx, 0), t)
        w.send(b(h.cx, 0), b(h.cx, 0), t + 4, h.cy, h.f)
        w.arrived(b(h.cy, 1), t + 2)
        w.send(b(h.cy, 1), b(h.cy, 1), t + 5, h.cx, h.f)

    def near(self):
        h, w, b, t = self.wire.here, self.wire, self.block, self.tag
        w.arrived(b(h.cx, 1), t + 1)
        w.arrived(b(h.cy, 0), t + 3)

    def end(self):
        h, w, b, t = self.wire.here, self.wire, self.block, self.tag
        w.arrived(b(h.cd, 0), t + 4)
        w.arrived(b(h.cd, 1), t + 5)


class ZGather:
    def __init__(self, wire, slot, tag, own=None):
        self.wire, self.slot, self.tag = wire, slot, tag
        self.own = own if own is not None else slot(wire.here.f)
        self.open = []

    def step(self, s):
        h, w = self.wire.here, self.wire
        left, right = h.f - 2 * (s - 1), h.f + 2 * (s - 1)
        if s > 1:

            @pl.when(left >= 0)
            def _():
                w.arrived(self.slot(left), self.tag + s - 2)

            @pl.when(right <= 7)
            def _():
                w.arrived(self.slot(right), self.tag + 3 + s - 2)

        if s > 3:
            return
        for block, tag, go, to in (
            (left, self.tag, (left >= 0) & (h.z <= 2), h.f + 2),
            (right, self.tag + 3, (right <= 7) & (h.z >= 1), h.f - 2),
        ):
            src = self.own if s == 1 else self.slot(block)
            copy = w.copy(src, self.slot(block), tag + s - 1, h.c, to)
            pl.when(go)(copy.start)
            self.open.append((go, copy))

    def relay(self, d):
        h, w = self.wire.here, self.wire
        f = h.zstep(d)
        w.send(self.own if d == 0 else self.slot(f), self.slot(f), self.tag + 6 + d, h.c, h.sib)

    def end(self):
        h, w = self.wire.here, self.wire
        for d in range(4):
            w.arrived(self.slot(h.zstep(d) + h.sib - h.f), self.tag + 6 + d)
        for go, copy in self.open:
            pl.when(go)(copy.wait_send)


class ClipScatter:
    def __init__(self, wire, parts, slots, tag):
        self.wire, self.parts, self.slots, self.tag = wire, parts, slots, tag

    def begin(self, which=None):
        h, w, p, s, t = self.wire.here, self.wire, self.parts, self.slots, self.tag
        if which != 1:
            w.send(p(h.cd, 0), s[0], t, h.cx, h.f)
            w.send(p(h.cd, 1), s[1], t + 1, h.cy, h.f)
        if which != 0:
            w.send(p(h.cx, 0), s[2], t + 2, h.cx, h.f)
            w.send(p(h.cy, 1), s[3], t + 3, h.cy, h.f)

    def middle(self):
        h, w, p, s, t = self.wire.here, self.wire, self.parts, self.slots, self.tag
        w.arrived(s[0], t)
        add_into(s[0], p(h.cy, 0))
        w.send(s[0], s[4], t + 4, h.cy, h.f)
        w.arrived(s[1], t + 1)
        add_into(s[1], p(h.cx, 1))
        w.send(s[1], s[5], t + 5, h.cx, h.f)

    def end(self):
        w, s, t = self.wire, self.slots, self.tag
        for i in range(2, 6):
            w.arrived(s[i], t + i)

    def total(self, half):
        s = self.slots
        first, second = (s[2], s[4]) if half == 0 else (s[5], s[3])
        own = self.parts(self.wire.here.c, half)
        return own[...].astype(F32) + first[...].astype(F32) + second[...].astype(F32)


class ZScatter:
    def __init__(self, wire, terms, near, far, tag):
        self.wire, self.terms, self.near, self.far, self.tag = wire, terms, near, far, tag
        self.open = []

    def term(self, m):
        pair = self.wire.here.pair
        return self.terms.at[m + pair * (3 - 2 * m)]

    def _start(self, go, src, dst, tag, f):
        copy = self.wire.copy(src, dst, self.tag + tag, self.wire.here.c, f)
        pl.when(go)(copy.start)
        self.open.append((go, copy))

    def begin(self):
        h = self.wire.here
        for i, m in enumerate((3, 2, 1)):
            self._start(jnp.logical_not(h.is_gate), self.term(m), self.near.at[i], i, h.partner)

    def step(self, s):
        h, w = self.wire.here, self.wire
        block, m, tag, to, f = (
            (self.near.at[0], 3, 0, 0, h.far_gate),
            (self.near.at[1], 2, 1, 1, h.far_gate),
            (self.far.at[0], 0, 3, 0, h.partner),
        )[s - 1]

        @pl.when(h.is_gate)
        def _():
            w.arrived(block, self.tag + tag)
            add_into(block, self.term(m))

        self._start(h.is_gate, block, self.far.at[to], 3 + to, f)

    def end(self):
        h, w = self.wire.here, self.wire

        @pl.when(h.is_gate)
        def _():
            w.arrived(self.near.at[2], self.tag + 2)
            w.arrived(self.far.at[1], self.tag + 4)

        @pl.when(jnp.logical_not(h.is_gate))
        def _():
            w.arrived(self.far.at[0], self.tag + 3)

    def total(self, out):
        h = self.wire.here
        self.end()

        @pl.when(h.is_gate)
        def _():
            others = self.near[2].astype(F32) + self.far[1].astype(F32)
            out[...] = self.terms[h.z].astype(F32) + others

        @pl.when(jnp.logical_not(h.is_gate))
        def _():
            out[...] = self.terms[h.z].astype(F32) + self.far[0].astype(F32)

    def drain(self):
        for go, copy in self.open:
            pl.when(go)(copy.wait_send)


class SiblingSum:
    def __init__(self, wire, terms, inbox, sums, tag):
        self.wire, self.terms, self.inbox, self.sums, self.tag = wire, terms, inbox, sums, tag

    def begin(self):
        h, w = self.wire.here, self.wire
        for z in range(4):
            w.send(self.terms(2 * z + 1 - h.core), self.inbox(z), self.tag + z, h.c, h.sib)

    def end(self):
        h, w = self.wire.here, self.wire
        for z in range(4):
            w.arrived(self.inbox(z), self.tag + z)
            own, other = self.terms(2 * z + h.core), self.inbox(z)
            self.sums(z)[...] = (own[...].astype(F32) + other[...].astype(F32)).astype(BF16)


def add_into(into, other):
    into[...] = (into[...].astype(F32) + other[...].astype(F32)).astype(BF16)


class LocalCopy:
    def __init__(self, src, through, dst, sem):
        self.a = pltpu.make_async_copy(src, through, sem)
        self.b = pltpu.make_async_copy(through, dst, sem)
        self.a.start()

    def turn(self):
        self.a.wait()
        self.b.start()

    def wait(self):
        self.b.wait()


def comm_call(body, out_shape, in_specs, out_specs, scratch, copies, tags, collective_id, cost=None):
    return pl.pallas_call(
        body,
        out_shape=out_shape,
        in_specs=in_specs,
        out_specs=out_specs,
        scratch_shapes=list(scratch)
        + [pltpu.SemaphoreType.DMA((copies,)), pltpu.SemaphoreType.DMA((tags,))],
        compiler_params=pltpu.CompilerParams(
            collective_id=collective_id, has_side_effects=True, vmem_limit_bytes=60 * 2**20
        ),
    )


def shape(dims, dtype=BF16):
    return jax.ShapeDtypeStruct(dims, dtype)


ROWS = 256


def dot(left, right, contract):
    return lax.dot_general(left, right, ((contract[:1], contract[1:]), ((), ())), preferred_element_type=F32)


def mask_scores(scores, bias_ref, first, rows):
    low = scores[first:] + bias_ref[first : first + rows, 0:1]
    key = lax.broadcasted_iota(jnp.int32, (rows, rows), 0)
    query = lax.broadcasted_iota(jnp.int32, (rows, rows), 1)
    low = jnp.where(key < query, low, jnp.where(key == query, scores[first:], NEG))
    if first == 0:
        return low
    return jnp.concatenate([scores[:first] + bias_ref[0:first, 0:1], low], axis=0)


def norm_parts(value):
    centered = value - jnp.mean(value, axis=-1, keepdims=True)
    scale = lax.rsqrt(jnp.mean(centered * centered, axis=-1, keepdims=True) + EPSILON)
    return centered * scale, scale


def column_weight(cols, j):
    return cols[:, :, 32 * j : 32 * j + 32, :].reshape(1024, 256)


def attend_rows(i, length, bias, q_ref, k_ref, v_t, o_ref, lse_ref, out_t):
    lane_head = lax.broadcasted_iota(jnp.int32, (ROWS, 256), 1) // HD
    first, n = i * ROWS, (i + 1) * ROWS
    q = q_ref[first:n, :]

    def head(j, _):
        q_head = jnp.where(lane_head == j, q, 0) * jnp.asarray(HD**-0.5, BF16)
        scores = mask_scores(dot(k_ref[0:n, :], q_head, (1, 1)), bias, first, ROWS)
        top = jnp.max(scores, axis=0, keepdims=True)
        weight = jnp.exp(scores - top)
        total = jnp.sum(weight, axis=0, keepdims=True)
        at = pl.ds(pl.multiple_of(j * HD, HD), HD)
        out_t[at, :] = dot(v_t[at, 0:n], weight.astype(BF16), (1, 0)) / total
        lse_ref[pl.ds(j, 1), first:n] = top + jnp.log(total)
        return 0

    lax.fori_loop(0, 4, head, 0)
    live = first + lax.broadcasted_iota(jnp.int32, (ROWS, 256), 0) < length[0]
    o_ref[first:n, :] = jnp.where(live, out_t[...].T, 0).astype(BF16)


def front_body(
    length, bias, text, hid, cols_a, cols_b, square, fin,
    o_hid, o_first, o_q, o_k, o_v, o_heads, o_lse, o_cols_a, o_cols_b, o_params, o_att, o_tkv, o_square, o_fin,
    out_t, v_t, tkv, v_square, v_fin, local, send_sem, recv_sem,
):
    h = Here()
    w = Wire(h, send_sem, recv_sem)
    T_HID, T_A, T_B, T_FIN, T_AXY, T_BXY = 0, 10, 17, 24, 27, 33
    T_Z, T_SXY, T_SIB, T_ATT, T_TKV = 39, 49, 73, 85, 93

    def my_columns(f):
        return pl.ds(pl.multiple_of(lax.rem(f, 4) * 256, 256), 256)

    def fin_part(c):
        return fin.at[:, pl.ds(pl.multiple_of(c * 1024, 1024), 1024)]

    plain = [
        pltpu.make_async_copy(cols_a.at[:, my_columns(h.f)], o_cols_a.at[h.c, h.f], local.at[0]),
        pltpu.make_async_copy(cols_b.at[:, my_columns(h.f)], o_cols_b.at[h.c, h.f], local.at[1]),
        pltpu.make_async_copy(hid.at[h.pair], o_hid.at[h.f], local.at[2]),
    ]
    for copy in plain:
        copy.start()
    turned = [
        LocalCopy(square, v_square, o_square.at[h.c, h.f], local.at[3]),
        LocalCopy(fin_part(h.c), v_fin, o_fin.at[h.c], local.at[4]),
    ]
    greet(frame_others(h) + clip_others(h))

    for d in (2, 6, 4, 3, 5, 1, 7):
        f = h.step(d)
        w.send(cols_a.at[:, my_columns(f)], o_cols_a.at[h.c, h.f], T_A + d - 1, h.c, f)

    def half_of(ref, part):
        return ref.at[pl.ds(64 * part, 64), :]

    for part in range(2):
        w.send(half_of(hid.at[h.pair], part), half_of(o_hid.at[h.f], part), T_HID + 1 + part, h.c, h.partner)
        w.send(
            half_of(hid.at[1 - h.pair], part),
            half_of(o_hid.at[h.f], part),
            T_HID + 3 + 2 * h.role + part,
            h.c,
            h.far_gate,
        )
    w.send(hid.at[h.pair], o_hid.at[h.f], T_HID, h.c, h.sib)

    def square_slot(f):
        return o_square.at[h.c, f]

    z_gather = ZGather(w, square_slot, T_Z, square)

    def square_gather(d):
        f = h.zstep(d)
        return ClipGather(
            w,
            lambda c, half: o_square.at[c, f, pl.ds(48 * half, 48), :],
            T_SXY + 6 * d,
            (lambda half: square.at[pl.ds(48 * half, 48), :]) if d == 0 else None,
        )

    gathers = [square_gather(d) for d in range(4)]
    gathers[0].begin()
    for i, (c, f) in enumerate(clip_others(h)):
        w.send(fin_part(c), o_fin.at[h.c], T_FIN + i, c, f)
    for copy in turned:
        copy.turn()
    plain[0].wait()
    for d in range(1, 8):
        w.arrived(o_cols_a.at[h.c, lax.rem(h.f + 8 - d, 8)], T_A + d - 1)
    a_gather = ClipGather(w, lambda c, half: o_cols_a.at[c, pl.ds(4 * half, 4)], T_AXY)
    a_gather.begin()
    forwards = []
    for part in range(2):
        for j in range(2):
            block = half_of(o_hid.at[h.far[j]], part)
            w.arrived(block, T_HID + 3 + 2 * j + part)
            forward = w.copy(block, block, T_HID + 3 + 2 * j + part, h.c, h.partner)
            pl.when(h.is_gate)(forward.start)
            forwards.append(forward)
    for d in (2, 6, 4, 3, 5, 1, 7):
        f = h.step(d)
        w.send(cols_b.at[:, my_columns(f)], o_cols_b.at[h.c, h.f], T_B + d - 1, h.c, f)
    for part in range(2):
        w.arrived(half_of(o_hid.at[h.partner], part), T_HID + 1 + part)
    w.send(o_hid.at[h.partner], o_hid.at[h.partner], T_HID + 7, h.c, h.sib)
    for j in range(2):
        w.send(o_hid.at[h.far[j]], o_hid.at[h.far[j]], T_HID + 8 + j, h.c, h.sib)
    a_gather.middle()
    z_gather.step(1)
    z_gather.relay(0)
    plain[1].wait()
    for d in range(1, 8):
        w.arrived(o_cols_b.at[h.c, lax.rem(h.f + 8 - d, 8)], T_B + d - 1)
    b_gather = ClipGather(w, lambda c, half: o_cols_b.at[c, pl.ds(4 * half, 4)], T_BXY)
    b_gather.begin()
    gathers[0].middle()
    a_gather.near()
    a_gather.end()
    for g in range(8):
        group = sum(o_cols_a[g // 2, 4 * (g % 2) + i, 96:104, 0:128].astype(F32) for i in range(4))
        o_params[:, 128 * g : 128 * g + 128] = group
    plain[2].wait()
    w.arrived(o_hid.at[h.sib], T_HID)
    w.arrived(o_hid.at[h.partner + h.sib - h.f], T_HID + 7)
    for j in range(2):
        w.arrived(o_hid.at[h.far[j] + h.sib - h.f], T_HID + 8 + j)
    z_gather.step(2)

    def project_rows(i, _):
        at = pl.ds(pl.multiple_of(i * 256, 256), 256)
        rows = o_hid[pl.ds(2 * i, 2)].reshape(256, 1024).astype(F32)
        xhat, _ = norm_parts(rows)
        low = (xhat * o_params[0:1, :] + o_params[3:4, :]).astype(BF16)
        o_first[at, :] = low
        for j, out in enumerate((o_q, o_k, o_v)):
            out[at, :] = dot(low, column_weight(o_cols_a, j), (1, 0)).astype(BF16)
        return 0

    lax.fori_loop(0, 2, project_rows, 0)
    z_gather.step(3)
    gathers[2].begin()
    z_gather.relay(2)
    b_gather.middle()
    lax.fori_loop(2, 4, project_rows, 0)
    v_t[...] = o_v[...].T
    b_gather.near()
    b_gather.end()
    z_gather.step(4)
    for d in (1, 3):
        gathers[d].begin()
        z_gather.relay(d)

    def text_slot(f):
        return o_tkv.at[lax.div(f, 4), :, :, my_columns(f)]

    for j in range(2):
        tkv[j] = dot(text[h.pair], column_weight(o_cols_b, j), (1, 0)).astype(BF16)
    for d in range(1, 4):
        w.send(tkv, text_slot(h.f), T_TKV + d, h.c, h.zstep(d))
    w.send(tkv, text_slot(h.f), T_TKV, h.c, h.sib)
    text_copy = pltpu.make_async_copy(tkv, text_slot(h.f), local.at[5])
    text_copy.start()

    def att_slot(f):
        return o_att.at[lax.div(f, 4), :, my_columns(f)]

    att_sends = []

    def attend_and_send(i):
        attend_rows(i, length, bias, o_q, o_k, v_t, o_heads, o_lse, out_t)
        for f in (2 * i, 2 * i + 1):
            block = o_heads.at[pl.ds(128 * f, 128), :]
            away = h.f != f
            copy = w.copy(block, att_slot(h.f), T_ATT + h.f, h.c, f)
            stay = pltpu.make_async_copy(block, att_slot(h.f), local.at[6])
            pl.when(away)(copy.start)
            pl.when(jnp.logical_not(away))(stay.start)
            att_sends.append((away, copy, stay))

    def square_steps(d):
        f = h.zstep(d)
        if d > 0:
            gathers[d].middle()
        gathers[d].near()
        for i, c in enumerate((h.cx, h.cy)):
            w.send(o_square.at[c, f], o_square.at[c, f], T_SIB + 3 * d + i, h.c, h.sib)

    def square_last(d):
        f = h.zstep(d)
        gathers[d].end()
        w.send(o_square.at[h.cd, f], o_square.at[h.cd, f], T_SIB + 3 * d + 2, h.c, h.sib)

    attend_and_send(3)
    square_steps(0)
    square_steps(2)
    square_last(0)
    attend_and_send(2)
    square_steps(1)
    square_last(2)
    for d in range(1, 4):
        f = lax.rem(h.f + 8 - 2 * d, 8)
        w.arrived(text_slot(f), T_TKV + d)
        w.send(text_slot(f), text_slot(f), T_TKV + 3 + d, h.c, h.sib)
    attend_and_send(1)
    square_steps(3)
    attend_and_send(0)
    square_last(1)
    square_last(3)
    z_gather.end()
    for d in range(4):
        f = h.zstep(d) + h.sib - h.f
        for i, c in enumerate((h.cx, h.cy, h.cd)):
            w.arrived(o_square.at[c, f], T_SIB + 3 * d + i)
    for d in range(1, 8):
        f = lax.rem(h.f + 8 - d, 8)
        w.arrived(att_slot(f), T_ATT + f)
    w.arrived(text_slot(h.sib), T_TKV)
    for d in range(1, 4):
        w.arrived(text_slot(lax.rem(h.sib + 8 - 2 * d, 8)), T_TKV + 3 + d)
    for i, (c, f) in enumerate(clip_others(h)):
        w.arrived(o_fin.at[c], T_FIN + i)
    for copy in turned:
        copy.wait()
    text_copy.wait()
    w.drain()
    for copy in forwards:
        pl.when(h.is_gate)(copy.wait_send)
    for away, copy, stay in att_sends:
        pl.when(away)(copy.wait_send)
        pl.when(jnp.logical_not(away))(stay.wait)


def front(length, bias, text, hid, cols_a, cols_b, square, fin):
    column = (1024, 256)
    return comm_call(
        front_body,
        (
            shape((8, 128, 1024)),
            shape((1024, 1024)),
            shape(column),
            shape(column),
            shape(column),
            shape(column),
            shape((8, 1024), F32),
            shape((4, 8, 112, 256)),
            shape((4, 8, 64, 256)),
            shape((8, 1024), F32),
            shape((2, 128, 1024)),
            shape((2, 2, 128, 1024)),
            shape((4, 8, 96, 1024)),
            shape((4, 32, 1024)),
        ),
        [SMEM, VMEM, VMEM] + [HBM] * 5,
        (VMEM,) * 10 + (HBM,) * 4,
        [
            pltpu.VMEM((256, ROWS), F32),
            pltpu.VMEM((256, 1024), BF16),
            pltpu.VMEM((2, 128, 256), BF16),
            pltpu.VMEM((96, 1024), BF16),
            pltpu.VMEM((32, 1024), BF16),
            pltpu.SemaphoreType.DMA((7,)),
        ],
        128,
        100,
        1,
    )(length, bias, text, hid, cols_a, cols_b, square, fin)


def attend_back_rows(i, length, bias, q_ref, k_ref, v_ref, o_ref, lse_ref, g_ref, dq_ref, dq_t, k_t, dk, dv):
    lane_head = lax.broadcasted_iota(jnp.int32, (ROWS, 256), 1) // HD
    first, n = i * ROWS, (i + 1) * ROWS
    q = q_ref[first:n, :] * jnp.asarray(HD**-0.5, BF16)
    live = first + lax.broadcasted_iota(jnp.int32, (ROWS, 256), 0) < length[0]
    g = jnp.where(live, g_ref[first:n, :], 0)
    both = (g.astype(F32) * o_ref[first:n, :].astype(F32)).T
    row_dots = jnp.concatenate(
        [jnp.sum(both[HD * j : HD * j + HD], axis=0, keepdims=True) for j in range(4)], axis=0
    )
    lse = lse_ref[0:4, first:n]

    def pick(rows, j):
        at = lax.broadcasted_iota(jnp.int32, rows.shape, 0) == j
        return jnp.sum(jnp.where(at, rows, 0), axis=0, keepdims=True)

    def head(j, _):
        q_head = jnp.where(lane_head == j, q, 0)
        g_head = jnp.where(lane_head == j, g, 0)
        scores = mask_scores(dot(k_ref[0:n, :], q_head, (1, 1)), bias, first, ROWS)
        probs = jnp.exp(scores - pick(lse, j))
        grads = dot(v_ref[0:n, :], g_head, (1, 1))
        dlogits = (probs * (grads - pick(row_dots, j))).astype(BF16)
        dv[0:n, :] += dot(probs.astype(BF16), g_head, (1, 0))
        dk[0:n, :] += dot(dlogits, q_head, (1, 0))
        at = pl.ds(pl.multiple_of(j * HD, HD), HD)
        dq_t[at, :] = dot(k_t[at, 0:n], dlogits, (1, 0))
        return 0

    lax.fori_loop(0, 4, head, 0)
    dq_ref[first:n, :] = (dq_t[...].T * (HD**-0.5)).astype(BF16)


def square_of(square, which):
    return square[:, 32 * which : 32 * which + 32, :].reshape(1024, 1024)


def text_probs(query, keys, bias, lane_head):
    heads = [jnp.where(lane_head == j, query, 0) for j in range(4)]
    stacked = jnp.concatenate(heads, axis=0)
    scores = dot(stacked, keys, (1, 1)) + bias
    weight = jnp.exp(scores - jnp.max(scores, axis=1, keepdims=True))
    return weight / jnp.sum(weight, axis=1, keepdims=True), stacked


def pick_heads(stacked, lane_head):
    return sum(jnp.where(lane_head == j, stacked[128 * j : 128 * j + 128], 0) for j in range(4))


def near_devices(here):
    return [(here.c, here.sib)] + [(here.c, here.zstep(d)) for d in range(1, 4)] + clip_others(here)[:2]


def middle_body(
    hid, att, square, tkv, text_bias, params, grad, fin,
    o_self, second_ref, query_ref, crossed_ref, o_cross, third_ref, o_grad, o_win,
    v_grad, v_fin, local, send_sem, recv_sem,
):
    h = Here()
    w = Wire(h, send_sem, recv_sem)

    def win_slot(f):
        return o_win.at[:, f]

    own = [
        LocalCopy(grad, v_grad, o_grad.at[h.c], local.at[0]),
        LocalCopy(fin, v_fin, win_slot(h.f), local.at[1]),
    ]
    greet(near_devices(h))
    z_gather = ZGather(w, win_slot, 0, fin)
    grad_gather = ClipGather(
        w,
        lambda c, half: o_grad.at[c, pl.ds(128 * half, 128), :],
        10,
        lambda half: grad.at[pl.ds(128 * half, 128), :],
    )
    z_gather.step(1)
    grad_gather.begin()
    z_gather.relay(0)
    for copy in own:
        copy.turn()
    att_value = att[...].reshape(256, 1024)
    after_self = hid[...].reshape(256, 1024).astype(F32) + dot(att_value, square_of(square, 0), (1, 0))
    o_self[...] = after_self
    xhat, _ = norm_parts(after_self)
    second_ref[...] = (xhat * params[1:2, :] + params[4:5, :]).astype(BF16)
    z_gather.step(2)
    query_ref[...] = dot(second_ref[...], square_of(square, 1), (1, 0)).astype(BF16)
    grad_gather.middle()
    lane_head = lax.broadcasted_iota(jnp.int32, (128, 256), 1) // HD
    for clip in range(2):
        for group in range(4):
            rows, columns = pl.ds(128 * clip, 128), pl.ds(256 * group, 256)
            query = query_ref[rows, columns] * jnp.asarray(HD**-0.5, BF16)
            probs, _ = text_probs(query, tkv[clip, 0, :, columns], text_bias[clip : clip + 1, :], lane_head)
            part = dot(probs.astype(BF16), tkv[clip, 1, :, columns], (1, 0))
            crossed_ref[rows, columns] = pick_heads(part, lane_head).astype(BF16)
        z_gather.step(3 + clip)
    for d in range(1, 4):
        z_gather.relay(d)
    after_cross = o_self[...] + dot(crossed_ref[...], square_of(square, 2), (1, 0))
    o_cross[...] = after_cross
    xhat, _ = norm_parts(after_cross)
    third_ref[...] = (xhat * params[2:3, :] + params[5:6, :]).astype(BF16)
    grad_gather.near()
    grad_gather.end()
    z_gather.end()
    for copy in own:
        copy.wait()
    w.drain()


def middle(hid, att, square, tkv, text_bias, params, grad, fin):
    rows = (256, 1024)
    return comm_call(
        middle_body,
        (
            shape(rows, F32),
            shape(rows),
            shape(rows),
            shape(rows),
            shape(rows, F32),
            shape(rows),
            shape((4, 256, 1024)),
            shape((4, 8, 32, 1024)),
        ),
        [VMEM] * 6 + [HBM] * 2,
        (VMEM,) * 6 + (HBM,) * 2,
        [
            pltpu.VMEM((256, 1024), BF16),
            pltpu.VMEM((4, 32, 1024), BF16),
            pltpu.SemaphoreType.DMA((2,)),
        ],
        20,
        16,
        2,
    )(hid, att, square, tkv, text_bias, params, grad, fin)


def feed_body(
    third, grad, win, fout, o_third, o_out, o_terms, o_sum,
    tokens, wout, inner, slope, g_pre, terms, slots, out_w, inbox, sums, left, right, local, send_sem, recv_sem,
):
    h = Here()
    w = Wire(h, send_sem, recv_sem)
    own = [
        pltpu.make_async_copy(third, tokens.at[h.c], local.at[0]),
        pltpu.make_async_copy(fout, wout.at[h.f], local.at[1]),
    ]
    for copy in own:
        copy.start()
    greet(near_devices(h))
    gather = ClipGather(
        w,
        lambda c, half: tokens.at[c, pl.ds(128 * half, 128), :],
        0,
        lambda half: third.at[pl.ds(128 * half, 128), :],
    )
    gather.begin()
    z_gather = ZGather(w, lambda f: wout.at[f], 6, fout)
    z_gather.step(1)
    z_gather.relay(0)
    for copy in own:
        copy.wait()

    def hidden(c):
        for part in range(2):
            rows = pl.ds(128 * part, 128)
            pre = dot(tokens[c, rows, :], win[...].reshape(1024, 1024), (1, 0))
            cdf = 0.5 * (1.0 + lax.erf(pre * (0.5**0.5)))
            inner[c, rows, :] = (pre * cdf).astype(BF16)
            slope[c, rows, :] = cdf + pre * jnp.exp(-0.5 * pre * pre) * 0.3989422804014327

    def hidden_back(c):
        g_inner = dot(grad[c], wout[...].reshape(1024, 1024), (1, 1))
        g_pre[c] = (g_inner * slope[c]).astype(BF16)
        terms[c] = dot(g_pre[c], win[...].reshape(1024, 1024), (1, 1)).astype(BF16)

    def out_terms(c):
        o_out[c] = dot(inner[c], wout[...].reshape(1024, 1024), (1, 0)).astype(BF16)

    hidden(h.c)
    z_gather.step(2)
    gather.middle()
    gather.near()
    z_gather.step(3)
    hidden(h.cx)
    z_gather.step(4)
    for d in range(1, 4):
        z_gather.relay(d)
    hidden(h.cy)
    gather.end()
    hidden(h.cd)
    z_gather.end()
    scatter = ClipScatter(
        w,
        lambda c, half: terms.at[c, pl.ds(128 * half, 128), :],
        [slots.at[i] for i in range(6)],
        16,
    )
    sibling = SiblingSum(w, lambda f: out_w.at[f], lambda z: inbox.at[z], lambda z: sums.at[z], 22)
    z_scatter = ZScatter(w, sums, left, right, 26)
    tall = (1024, 1024)

    def out_weight(i, _):
        columns = pl.ds(pl.multiple_of(i * 256, 256), 256)
        out = dot(inner[:, :, columns].reshape(1024, 256), grad[...].reshape(tall), (0, 0))
        out_w[pl.ds(2 * i, 2)] = out.astype(BF16).reshape(2, 128, 1024)
        return 0

    def in_weight(i, _):
        columns = pl.ds(pl.multiple_of(i * 256, 256), 256)
        out = dot(tokens[:, :, columns].reshape(1024, 256), g_pre[...].reshape(tall), (0, 0))
        o_terms[:, pl.ds(pl.multiple_of(32 * i, 32), 32), :] = out.astype(BF16).reshape(8, 32, 1024)
        return 0

    hidden_back(h.cd)
    scatter.begin(0)
    hidden_back(h.cx)
    hidden_back(h.cy)
    scatter.begin(1)
    lax.fori_loop(0, 4, out_weight, 0)
    sibling.begin()
    scatter.middle()
    hidden_back(h.c)
    sibling.end()
    z_scatter.begin()
    lax.fori_loop(0, 2, in_weight, 0)
    z_scatter.step(1)
    lax.fori_loop(2, 4, in_weight, 0)
    out_terms(0)
    z_scatter.step(2)
    z_scatter.step(3)
    out_terms(1)
    out_terms(2)
    out_terms(3)
    scatter.end()
    for half in range(2):
        o_third[128 * half : 128 * half + 128, :] = scatter.total(half)
    z_scatter.total(o_sum)
    w.drain()
    z_scatter.drain()


def feed(third, grad, win, fout):
    full = (4, 256, 1024)
    return comm_call(
        feed_body,
        (shape((256, 1024), F32), shape(full), shape((8, 128, 1024)), shape((128, 1024), F32)),
        [HBM, VMEM, VMEM, HBM],
        (VMEM,) * 4,
        [
            pltpu.VMEM(full, BF16),
            pltpu.VMEM((8, 128, 1024), BF16),
            pltpu.VMEM(full, BF16),
            pltpu.VMEM(full, F32),
            pltpu.VMEM(full, BF16),
            pltpu.VMEM(full, BF16),
            pltpu.VMEM((6, 128, 1024), BF16),
            pltpu.VMEM((8, 128, 1024), BF16),
            pltpu.VMEM((4, 128, 1024), BF16),
            pltpu.VMEM((4, 128, 1024), BF16),
            pltpu.VMEM((3, 128, 1024), BF16),
            pltpu.VMEM((2, 128, 1024), BF16),
            pltpu.SemaphoreType.DMA((2,)),
        ],
        48,
        32,
        3,
    )(third, grad, win, fout)


def norm_back(xhat, scale, grad, gain):
    h = grad * gain
    return scale * (
        h
        - jnp.mean(h, axis=-1, keepdims=True)
        - xhat * jnp.mean(h * xhat, axis=-1, keepdims=True)
    )


def middle_back_body(
    g_third, g_out, after_cross, after_self, second, query_ref, crossed, att, square, tkv, text_bias, params,
    out_terms, in_terms,
    o_after_self, o_square, o_zsquare, o_heads, o_text, o_norm, o_output, o_in,
    g_crossed, g_query, g_att, g_text, slots, sums, from_sib, from_z,
    i_inbox, i_sums, i_left, i_right, i_total, i_out, i_in,
    g_square, s_inbox, s_sums, s_slots, local, send_sem, recv_sem,
):
    h = Here()
    w = Wire(h, send_sem, recv_sem)
    T_HEADS, T_TSIB, T_TZ, T_OUT, T_IN, T_IZ, T_IC, T_SQ = 0, 7, 11, 14, 20, 24, 30, 33
    greet(frame_others(h) + clip_others(h))
    scatter = ClipScatter(
        w,
        lambda c, half: out_terms.at[c, pl.ds(128 * half, 128), :],
        [slots.at[i] for i in range(6)],
        T_OUT,
    )
    scatter.begin()
    in_sibling = SiblingSum(
        w, lambda f: in_terms.at[f], lambda z: i_inbox.at[z], lambda z: i_sums.at[z], T_IN
    )
    in_scatter = ZScatter(w, i_sums, i_left, i_right, T_IZ)
    in_sibling.begin()

    def square_sums(which):
        sibling = SiblingSum(
            w,
            lambda f: g_square.at[which, :, f],
            lambda z: s_inbox.at[which, z],
            lambda z: s_sums.at[which, z],
            T_SQ + 10 * which,
        )
        clip = ClipScatter(
            w,
            lambda c, half: s_sums.at[which, :, c, pl.ds(16 * half, 16), :],
            [s_slots.at[which, i] for i in range(6)],
            T_SQ + 10 * which + 4,
        )
        return sibling, clip

    squares = [square_sums(0), square_sums(1)]

    def put(ref, value):
        ref[...] = value.astype(BF16).reshape(4, 8, 32, 1024)

    def columns_of(f):
        return pl.ds(pl.multiple_of(lax.rem(f, 4) * 256, 256), 256)

    def part_of(f):
        return g_att.at[lax.div(f, 4), :, columns_of(f)]

    def text_part(f):
        return g_text.at[lax.div(f, 4), :, :, columns_of(f)]

    xhat, scale = norm_parts(after_cross[...])
    grad = g_third[...]
    o_norm[0:1, :] = jnp.sum(grad * xhat, axis=0, keepdims=True)
    o_norm[1:2, :] = jnp.sum(grad, axis=0, keepdims=True)
    g_after_cross = g_out[...].reshape(256, 1024).astype(F32) + norm_back(xhat, scale, grad, params[2:3, :])
    o_after_self[...] = g_after_cross
    branch = g_after_cross.astype(BF16)
    g_crossed[...] = dot(branch, square_of(square, 2), (1, 1)).astype(BF16)
    put(g_square.at[1], dot(crossed[...], branch, (0, 0)))
    squares[1][0].begin()
    in_sibling.end()
    in_scatter.begin()
    lane_head = lax.broadcasted_iota(jnp.int32, (128, 256), 1) // HD
    for clip in range(2):
        for group in range(4):
            rows, columns = pl.ds(128 * clip, 128), pl.ds(256 * group, 256)
            keys, values = tkv[clip, 0, :, columns], tkv[clip, 1, :, columns]
            query = query_ref[rows, columns] * jnp.asarray(HD**-0.5, BF16)
            probs, stacked = text_probs(query, keys, text_bias[clip : clip + 1, :], lane_head)
            grads = g_crossed[rows, columns]
            g_stacked = jnp.concatenate([jnp.where(lane_head == j, grads, 0) for j in range(4)], axis=0)
            g_probs = dot(g_stacked, values, (1, 1))
            row_dot = jnp.sum(probs * g_probs, axis=1, keepdims=True)
            g_logits = (probs * (g_probs - row_dot)).astype(BF16)
            part = dot(g_logits, keys, (1, 0))
            g_query[rows, columns] = (pick_heads(part, lane_head) * (HD**-0.5)).astype(BF16)
            g_text[clip, 0, :, columns] = dot(g_logits, stacked, (0, 0)).astype(BF16)
            g_text[clip, 1, :, columns] = dot(probs.astype(BF16), g_stacked, (0, 0)).astype(BF16)
        if clip == 0:
            scatter.middle()
            in_scatter.step(1)
    in_scatter.step(2)
    squares[1][0].end()
    squares[1][1].begin()
    text_sibling = SiblingSum(
        w, text_part, lambda z: from_sib.at[z], lambda z: sums.at[z], T_TSIB
    )
    text_sibling.begin()
    grad = dot(g_query[...], square_of(square, 1), (1, 1))
    xhat, scale = norm_parts(after_self[...])
    o_norm[2:3, :] = jnp.sum(grad * xhat, axis=0, keepdims=True)
    o_norm[3:4, :] = jnp.sum(grad, axis=0, keepdims=True)
    o_norm[4:8, :] = jnp.zeros((4, 1024), F32)
    g_after_self = o_after_self[...] + norm_back(xhat, scale, grad, params[1:2, :])
    o_after_self[...] = g_after_self
    branch = g_after_self.astype(BF16)
    g_att[...] = dot(branch, square_of(square, 0), (1, 1)).astype(BF16).reshape(2, 128, 1024)
    for d in (4, 2, 6, 3, 5, 1, 7):
        f = h.step(d)
        w.send(part_of(f), o_heads.at[h.f], T_HEADS + d - 1, h.c, f)
    copy = pltpu.make_async_copy(part_of(h.f), o_heads.at[h.f], local.at[0])
    copy.start()
    in_scatter.step(3)
    put(g_square.at[0], dot(second[...], g_query[...], (0, 0)))
    squares[0][0].begin()
    text_sibling.end()
    for d in range(1, 4):
        w.send(sums.at[lax.rem(h.z + d, 4)], from_z.at[d - 1], T_TZ + d - 1, h.c, h.zstep(d))
    squares[1][1].middle()
    put(o_square, dot(att[...].reshape(256, 1024), branch, (0, 0)))
    squares[0][0].end()
    squares[0][1].begin()
    in_scatter.total(i_total)
    i_out[...] = i_total[...].astype(BF16).reshape(4, 32, 1024)
    for i, (c, f) in enumerate(clip_others(h)):
        w.send(i_out.at[c], i_in.at[h.c], T_IC + i, c, f)
    i_in[h.c] = i_out[h.c]
    scatter.end()
    for half in range(2):
        rows = pl.ds(128 * half, 128)
        o_output[rows, :] = (after_cross[rows, :] + scatter.total(half)).astype(BF16)
    squares[0][1].middle()
    for which in (1, 0):
        squares[which][1].end()
        for half in range(2):
            total = squares[which][1].total(half)
            o_zsquare[:, 32 * which + 16 * half : 32 * which + 16 * half + 16, :] = total.astype(BF16)
    for d in range(1, 4):
        w.arrived(from_z.at[d - 1], T_TZ + d - 1)
    total = sums[h.z].astype(F32)
    for d in range(3):
        total = total + from_z[d].astype(F32)
    o_text[...] = total.astype(BF16)
    for i, (c, f) in enumerate(clip_others(h)):
        w.arrived(i_in.at[c], T_IC + i)
    for c in range(4):
        o_in[:, 1024 * c : 1024 * c + 1024] = i_in[c].astype(F32)
    for d in range(1, 8):
        w.arrived(o_heads.at[lax.rem(h.f + 8 - d, 8)], T_HEADS + d - 1)
    copy.wait()
    w.drain()
    in_scatter.drain()


def middle_back(*args):
    rows, block, quarter = (256, 1024), (2, 128, 256), (4, 128, 1024)
    return comm_call(
        middle_back_body,
        (
            shape(rows, F32),
            shape((4, 8, 32, 1024)),
            shape((4, 64, 1024)),
            shape((8, 128, 256)),
            shape(block),
            shape((8, 1024), F32),
            shape(rows),
            shape((32, 4096), F32),
        ),
        [VMEM] * 14,
        (VMEM,) * 8,
        [
            pltpu.VMEM(rows, BF16),
            pltpu.VMEM(rows, BF16),
            pltpu.VMEM((2, 128, 1024), BF16),
            pltpu.VMEM((2, 2, 128, 1024), BF16),
            pltpu.VMEM((6, 128, 1024), BF16),
            pltpu.VMEM((4,) + block, BF16),
            pltpu.VMEM((4,) + block, BF16),
            pltpu.VMEM((3,) + block, BF16),
            pltpu.VMEM(quarter, BF16),
            pltpu.VMEM(quarter, BF16),
            pltpu.VMEM((3, 128, 1024), BF16),
            pltpu.VMEM((2, 128, 1024), BF16),
            pltpu.VMEM((128, 1024), F32),
            pltpu.VMEM((4, 32, 1024), BF16),
            pltpu.VMEM((4, 32, 1024), BF16),
            pltpu.VMEM((2, 4, 8, 32, 1024), BF16),
            pltpu.VMEM((2, 4, 4, 32, 1024), BF16),
            pltpu.VMEM((2, 4, 4, 32, 1024), BF16),
            pltpu.VMEM((2, 6, 4, 16, 1024), BF16),
            pltpu.SemaphoreType.DMA((1,)),
        ],
        80,
        53,
        4,
    )(*args)


def last_body(
    length, bias, q_ref, k_ref, v_ref, o_ref, lse, g_heads, hid, first_low, w_a, w_b, text_in, g_tkv,
    square, z_square, norms, own_hid, g_after, params,
    o_hidden, o_square, o_qkv, o_ckv, o_norm, o_text,
    dq_t, k_t, dk, dv, d_cols, f_terms, f_sib, f_sum, f_in, s_inbox, s_sums, s_slots, s_part,
    z_left, z_right, y_left, y_right, a_terms, a_slots, a_sum, a_in, b_terms, b_slots, b_sum, b_in,
    t_terms, t_in, n_row, n_terms, n_slots, n_sum, n_in, send_sem, recv_sem,
):
    h = Here()
    w = Wire(h, send_sem, recv_sem)
    T_S, T_SC, T_Z, T_Y, T_B, T_T, T_A, T_F, T_N = 0, 4, 10, 16, 22, 36, 44, 86, 94
    greet(frame_others(h) + clip_others(h)[:2])
    s_sibling = SiblingSum(
        w, lambda f: square.at[:, f], lambda z: s_inbox.at[z], lambda z: s_sums.at[z], T_S
    )
    s_sibling.begin()
    z_scatter = ZScatter(w, z_square, z_left, z_right, T_Z)
    z_scatter.begin()
    s_scatter = ClipScatter(
        w,
        lambda c, half: s_sums.at[:, c, pl.ds(16 * half, 16), :],
        [s_slots.at[i] for i in range(6)],
        T_SC,
    )
    y_scatter = ZScatter(w, s_part, y_left, y_right, T_Y)

    class Columns:
        def __init__(self, terms, slots, sums, inbox, tag):
            self.sums, self.inbox, self.tag = sums, inbox, tag
            self.clip = ClipScatter(
                w, lambda c, half: terms.at[c, pl.ds(4 * half, 4)], [slots.at[i] for i in range(6)], tag
            )

        def spread(self):
            self.clip.end()
            for half in range(2):
                self.sums[4 * half : 4 * half + 4] = self.clip.total(half).astype(BF16)
            for d in (4, 2, 6, 3, 5, 1, 7):
                f = h.step(d)
                w.send(self.sums.at[f], self.inbox.at[h.f], self.tag + 5 + d, h.c, f)
            self.inbox[h.f] = self.sums[h.f]

        def wait(self):
            for d in range(1, 8):
                w.arrived(self.inbox.at[lax.rem(h.f + 8 - d, 8)], self.tag + 5 + d)

    text = text_in[h.pair]
    for j in range(2):
        b_terms[:, :, 32 * j : 32 * j + 32, :] = (
            dot(text, g_tkv[j], (0, 0)).astype(BF16).reshape(4, 8, 32, 256)
        )
    b_columns = Columns(b_terms, b_slots, b_sum, b_in, T_B)
    b_columns.clip.begin()
    t_terms[...] = (
        dot(g_tkv[0], column_weight(w_b, 0), (1, 1)) + dot(g_tkv[1], column_weight(w_b, 1), (1, 1))
    ).astype(BF16)
    for d in range(1, 8):
        f = h.step(d)
        w.send(
            t_terms.at[pl.ds(pl.multiple_of(f * 16, 16), 16), :], t_in.at[h.f], T_T + d - 1, h.c, f
        )
    t_in[h.f] = t_terms[pl.ds(pl.multiple_of(h.f * 16, 16), 16), :]

    k_t[...] = k_ref[...].T
    dk[...] = jnp.zeros_like(dk)
    dv[...] = jnp.zeros_like(dv)

    def rows_back(i):
        attend_back_rows(
            i, length, bias, q_ref, k_ref, v_ref, o_ref, lse, g_heads, d_cols.at[0], dq_t, k_t, dk, dv
        )

    rows_back(0)
    s_sibling.end()
    s_scatter.begin()
    z_scatter.step(1)
    rows_back(1)
    z_scatter.step(2)
    z_scatter.step(3)
    b_columns.clip.middle()
    rows_back(2)
    s_scatter.middle()
    b_columns.spread()
    rows_back(3)
    d_cols[1] = dk[...].astype(BF16)
    d_cols[2] = dv[...].astype(BF16)
    a_columns = [
        Columns(a_terms.at[j], a_slots.at[j], a_sum.at[j], a_in.at[j], T_A + 13 * j) for j in range(3)
    ]
    for j in range(3):
        a_terms[j] = dot(first_low[...], d_cols[j], (0, 0)).astype(BF16).reshape(4, 8, 32, 256)
        a_columns[j].clip.begin()

    f_sibling = SiblingSum(
        w, lambda f: f_terms.at[f], lambda z: f_sib.at[z], lambda z: f_sum.at[z], T_F
    )
    n_row[...] = jnp.zeros_like(n_row)

    def frame_terms(i, _):
        rows = pl.ds(pl.multiple_of(i * 256, 256), 256)
        grad = sum(dot(d_cols[j, rows, :], column_weight(w_a, j), (1, 1)) for j in range(3))
        f_terms[pl.ds(2 * i, 2)] = grad.astype(BF16).reshape(2, 128, 1024)
        xhat, _ = norm_parts(hid[pl.ds(2 * i, 2)].reshape(256, 1024).astype(F32))
        n_row[0:1, :] += jnp.sum(grad * xhat, axis=0, keepdims=True)
        n_row[3:4, :] += jnp.sum(grad, axis=0, keepdims=True)
        return 0

    lax.fori_loop(0, 4, frame_terms, 0)
    f_sibling.begin()
    s_scatter.end()
    for half in range(2):
        s_part[:, 16 * half : 16 * half + 16, :] = s_scatter.total(half).astype(BF16)
    y_scatter.begin()
    a_columns[0].clip.middle()
    f_sibling.end()
    other = 2 * (1 - h.pair)
    is_end = jnp.logical_not(h.is_gate)
    to_gate, to_far = [], []
    for j in range(2):
        to_gate.append(w.copy(f_sum.at[other + j], f_in.at[1 + j], T_F + 5 + j, h.c, h.partner))
        pl.when(is_end)(to_gate[j].start)
    w.send(f_sum.at[lax.div(h.partner, 2)], f_in.at[0], T_F + 4, h.c, h.partner)
    n_row[1:2, :] = norms[2:3, :]
    n_row[2:3, :] = norms[0:1, :]
    n_row[4:5, :] = norms[3:4, :]
    n_row[5:6, :] = norms[1:2, :]
    for c in range(4):
        for f in range(8):
            group = 2 * c + f // 4
            n_terms[c, f] = n_row[:, 128 * group : 128 * group + 128].astype(BF16)
    n_columns = Columns(n_terms, n_slots, n_sum, n_in, T_N)
    n_columns.clip.begin()
    a_columns[1].clip.middle()
    a_columns[0].spread()
    for j in range(2):

        @pl.when(h.is_gate)
        def _():
            w.arrived(f_in.at[1 + j], T_F + 5 + j)
            add_into(f_sum.at[other + j], f_in.at[1 + j])

        to_far.append(w.copy(f_sum.at[other + j], f_in.at[3], T_F + 7, h.c, h.far[j]))
        pl.when(h.is_gate)(to_far[j].start)
    y_scatter.step(1)
    a_columns[2].clip.middle()
    a_columns[1].spread()
    n_columns.clip.middle()
    y_scatter.step(2)
    y_scatter.step(3)
    a_columns[2].spread()
    n_columns.spread()
    z_scatter.total(o_square.at[pl.ds(32, 64), :])
    b_columns.wait()
    for j in range(2):
        for q in range(4):
            at = pl.ds(32 * j, 32)
            o_ckv[j, :, 256 * q : 256 * q + 256] = b_in[q, at, :].astype(F32) + b_in[4 + q, at, :].astype(F32)
    for d in range(1, 8):
        w.arrived(t_in.at[lax.rem(h.f + 8 - d, 8)], T_T + d - 1)
    for p in range(2):
        o_text[p] = sum(t_in[4 * p + q].astype(F32) for q in range(4)).astype(BF16)
    w.arrived(f_in.at[0], T_F + 4)
    w.arrived(f_in.at[3], T_F + 7)

    def hidden_out(clip, total):
        xhat, scale = norm_parts(own_hid[clip].astype(F32))
        o_hidden[clip] = (g_after[clip] + norm_back(xhat, scale, total, params[0:1, :])).astype(BF16)

    hidden_out(h.pair, f_sum[h.z].astype(F32) + f_in[0].astype(F32))
    hidden_out(1 - h.pair, f_in[3].astype(F32))
    y_scatter.total(o_square.at[pl.ds(0, 32), :])
    for j in range(3):
        a_columns[j].wait()
        for q in range(4):
            o_qkv[j, :, 256 * q : 256 * q + 256] = a_in[j, q].astype(F32) + a_in[j, 4 + q].astype(F32)
    n_columns.wait()
    o_norm[...] = sum(n_in[f].astype(F32) for f in range(8))
    w.drain()
    z_scatter.drain()
    y_scatter.drain()
    for j in range(2):
        pl.when(is_end)(to_gate[j].wait_send)
        pl.when(h.is_gate)(to_far[j].wait_send)


def last(*args):
    def buffer(*dims):
        return pltpu.VMEM(dims, BF16)

    def full(*dims):
        return pltpu.VMEM(dims, F32)

    return comm_call(
        last_body,
        (
            shape((2, 128, 1024)),
            shape((96, 1024), F32),
            shape((3, 32, 1024), F32),
            shape((2, 32, 1024), F32),
            shape((16, 128), F32),
            shape((2, 16, 1024)),
        ),
        [SMEM] + [VMEM] * 19,
        (VMEM,) * 6,
        [
            full(256, ROWS),
            buffer(256, 1024),
            full(1024, 256),
            full(1024, 256),
            buffer(3, 1024, 256),
            buffer(8, 128, 1024),
            buffer(4, 128, 1024),
            buffer(4, 128, 1024),
            buffer(4, 128, 1024),
            buffer(4, 4, 32, 1024),
            buffer(4, 4, 32, 1024),
            buffer(6, 4, 16, 1024),
            buffer(4, 32, 1024),
            buffer(3, 64, 1024),
            buffer(2, 64, 1024),
            buffer(3, 32, 1024),
            buffer(2, 32, 1024),
            buffer(3, 4, 8, 32, 256),
            buffer(3, 6, 4, 32, 256),
            buffer(3, 8, 32, 256),
            buffer(3, 8, 32, 256),
            buffer(4, 8, 64, 256),
            buffer(6, 4, 64, 256),
            buffer(8, 64, 256),
            buffer(8, 64, 256),
            buffer(128, 1024),
            buffer(8, 16, 1024),
            full(16, 1024),
            buffer(4, 8, 16, 128),
            buffer(6, 4, 16, 128),
            buffer(8, 16, 128),
            buffer(8, 16, 128),
        ],
        140,
        107,
        5,
    )(*args)


def on_device_fast(
    hidden_in,
    text_states,
    out_grad,
    self_qkv,
    self_out,
    cross_qkv,
    cross_out,
    ffn_in,
    ffn_out,
    ln_gain,
    ln_bias,
    clip_len,
    frame_mask,
    text_len,
    text_mask,
):
    frame = lax.axis_index("frame")
    pair = frame // 4
    norms = jnp.concatenate([ln_gain, ln_bias], axis=0)
    placed = lax.dynamic_update_slice(jnp.zeros((16, 256), BF16), norms, (0, 32 * (frame % 4)))
    cols_a = jnp.concatenate(
        [jnp.moveaxis(self_qkv, 1, 0).reshape(96, 1024), jnp.tile(placed, (1, 4))], axis=0
    )
    cols_b = jnp.moveaxis(cross_qkv, 1, 0)[1:].reshape(64, 1024)
    square_here = jnp.concatenate([self_out, cross_qkv[:, 0], cross_out], axis=0)
    columns = jnp.arange(1024, dtype=jnp.int32)
    my_len = lax.dynamic_slice_in_dim(clip_len, pair, 1, 0)
    my_mask = lax.dynamic_slice_in_dim(frame_mask, pair, 1, 0)[0]
    bias = jnp.where((columns < my_len) & (my_mask > 0), 0.0, NEG).astype(F32)
    bias = jnp.broadcast_to(bias[:, None], (1024, 128))
    (
        hid_all, first_low, query, key, value, att_heads, lse, w_a, w_b, params, att, tkv, square, fin_all
    ) = front(my_len, bias, text_states, hidden_in, cols_a, cols_b, square_here, ffn_in)
    square = square.reshape(32, 96, 1024)
    slots = jnp.arange(128, dtype=jnp.int32)
    text_ok = (slots[None] < text_len[:, None]) & ((text_mask > 0) | (slots[None] == 0))
    text_bias = jnp.where(text_ok, 0.0, NEG).astype(F32)
    after_self, second, cross_query, crossed, after_cross, third, grad_all, ffn_w_in = middle(
        hidden_in, att, square, tkv, text_bias, params, out_grad.reshape(256, 1024), fin_all
    )
    third_sum, out_terms, in_terms, grad_ffn_out = feed(third, grad_all, ffn_w_in, ffn_out)
    g_after_self, g_square, z_square, g_heads, g_tkv, g_norms, output, grad_ffn_in = middle_back(
        third_sum, out_grad, after_cross, after_self, second, cross_query, crossed, att, square, tkv,
        text_bias, params, out_terms, in_terms,
    )
    grad_hidden, square_sum, qkv_sum, ckv_sum, norm_sum, grad_text = last(
        my_len, bias, query, key, value, att_heads, lse, g_heads.reshape(1024, 256), hid_all, first_low, w_a, w_b,
        text_states, g_tkv, g_square, z_square, g_norms, hidden_in, g_after_self.reshape(2, 128, 1024), params,
    )
    norm_sum = lax.dynamic_slice(norm_sum, (0, 32 * (frame % 4)), (6, 32))
    return (
        output.reshape(2, 128, 1024),
        grad_hidden,
        grad_text,
        jnp.moveaxis(qkv_sum, 0, 1),
        square_sum[0:32],
        jnp.stack([square_sum[32:64], ckv_sum[0], ckv_sum[1]], axis=1),
        square_sum[64:96],
        grad_ffn_in,
        grad_ffn_out,
        norm_sum[0:3],
        norm_sum[3:6],
    )


def solution(mesh):
    return jax.shard_map(
        on_device_fast if fits(mesh) else on_device_any,
        mesh=mesh,
        in_specs=(
            P("clip", "frame", None),
            P("clip", None, None),
            P("clip", "frame", None),
            P(("clip", "frame"), None, None),
            P(("clip", "frame"), None),
            P(("clip", "frame"), None, None),
            P(("clip", "frame"), None),
            P(("clip", "frame"), None),
            P(("clip", "frame"), None),
            P(None, ("clip", "frame")),
            P(None, ("clip", "frame")),
            P("clip"),
            P("clip", None),
            P("clip"),
            P("clip", None),
        ),
        out_specs=(
            P("clip", "frame", None),
            P("clip", "frame", None),
            P("clip", "frame", None),
            P(("clip", "frame"), None, None),
            P(("clip", "frame"), None),
            P(("clip", "frame"), None, None),
            P(("clip", "frame"), None),
            P(("clip", "frame"), None),
            P(("clip", "frame"), None),
            P(None, ("clip", "frame")),
            P(None, ("clip", "frame")),
        ),
        check_vma=False,
    )
```

```python
import functools

import jax
import jax.numpy as jnp
from jax import lax
from jax.experimental import pallas as pl
from jax.experimental.pallas import tpu as pltpu
from jax.sharding import PartitionSpec as P

HD = 64


MASKED = -1000000000.0
EPSILON = 1e-05


def layer_norm(value, gain, shift):
    average = jnp.mean(value, axis=-1, keepdims=True)
    centered = value - average
    variance = jnp.mean(centered * centered, axis=-1, keepdims=True)
    return centered * lax.rsqrt(variance + EPSILON) * gain + shift


def activate(value):
    return jax.nn.gelu(value, approximate=False)


def project(left, right):
    return jnp.einsum("cnd,de->cne", left, right, preferred_element_type=jnp.float32)


def project_back(grad_rows, weight):
    return jnp.einsum("cne,de->cnd", grad_rows, weight, preferred_element_type=jnp.float32)


def weight_grad(left, right):
    return jnp.einsum("cnd,cne->de", left, right, preferred_element_type=jnp.float32)


def fetch_attention(self_qkv, self_out, cross_qkv, cross_out, ln_gain, ln_bias):
    return (
        lax.all_gather(self_qkv, ("clip", "frame"), axis=0, tiled=True),
        lax.all_gather(self_out, ("clip", "frame"), axis=0, tiled=True),
        lax.all_gather(cross_qkv, ("clip", "frame"), axis=0, tiled=True),
        lax.all_gather(cross_out, ("clip", "frame"), axis=0, tiled=True),
        lax.all_gather(ln_gain, ("clip", "frame"), axis=1, tiled=True),
        lax.all_gather(ln_bias, ("clip", "frame"), axis=1, tiled=True),
    )


def fetch_ffn(ffn_in, ffn_out):
    return (
        lax.all_gather(ffn_in, ("clip", "frame"), axis=0, tiled=True),
        lax.all_gather(ffn_out, ("clip", "frame"), axis=0, tiled=True),
    )


def self_masks(first_row, block_rows, clip_len, key_valid):
    columns = jnp.arange(key_valid.shape[1], dtype=jnp.int32)
    row_ids = first_row + jnp.arange(block_rows, dtype=jnp.int32)
    diagonal = columns[None, :] == row_ids[:, None]
    allowed = (columns[None, :] <= row_ids[:, None])[None] & (
        key_valid[:, None, :] | diagonal[None]
    )
    live_rows = (row_ids[None, :] < clip_len[:, None]).astype(jnp.float32)
    return (allowed[:, None], live_rows[:, None, :, None])


def self_forward(query_rows, key_rows, value_rows, clip_len, key_valid):
    length = query_rows.shape[1]
    block_rows = min(512, length)
    score_scale = query_rows.shape[3] ** (-0.5)

    def one_block(block_index):
        first_row = block_index * block_rows
        query_block = lax.dynamic_slice_in_dim(query_rows, first_row, block_rows, 1)
        raw_scores = jnp.einsum(
            "cqhd,ckhd->chqk", query_block, key_rows, preferred_element_type=jnp.float32
        )
        allowed, live_rows = self_masks(first_row, block_rows, clip_len, key_valid)
        logits = jnp.where(allowed, raw_scores * score_scale, MASKED)
        row_max = jnp.max(logits, axis=-1, keepdims=True)
        exponent = jnp.exp(logits - row_max)
        row_sum = jnp.sum(exponent, axis=-1, keepdims=True)
        weights = (exponent / row_sum * live_rows).astype(jnp.bfloat16)
        attended = jnp.einsum(
            "chqk,ckhd->cqhd", weights, value_rows, preferred_element_type=jnp.float32
        )
        return (attended.astype(jnp.bfloat16), row_max + jnp.log(row_sum))

    blocks, log_sums = lax.map(one_block, jnp.arange(length // block_rows, dtype=jnp.int32))
    return (jnp.moveaxis(blocks, 0, 1).reshape(query_rows.shape), log_sums)


def self_backward(query_rows, key_rows, value_rows, grad_rows, log_sums, clip_len, key_valid):
    length = query_rows.shape[1]
    block_rows = min(512, length)
    score_scale = query_rows.shape[3] ** (-0.5)

    def one_block(totals, block_index):
        grad_keys, grad_values = totals
        first_row = block_index * block_rows
        query_block = lax.dynamic_slice_in_dim(query_rows, first_row, block_rows, 1)
        grad_block = lax.dynamic_slice_in_dim(grad_rows, first_row, block_rows, 1)
        raw_scores = jnp.einsum(
            "cqhd,ckhd->chqk", query_block, key_rows, preferred_element_type=jnp.float32
        )
        allowed, live_rows = self_masks(first_row, block_rows, clip_len, key_valid)
        logits = jnp.where(allowed, raw_scores * score_scale, MASKED)
        probs = jnp.exp(logits - log_sums[block_index])
        weights = (probs * live_rows).astype(jnp.bfloat16)
        grad_probs = (
            jnp.einsum(
                "cqhd,ckhd->chqk", grad_block, value_rows, preferred_element_type=jnp.float32
            )
            * live_rows
        )
        row_dot = jnp.sum(probs * grad_probs, axis=-1, keepdims=True)
        grad_scores = (probs * (grad_probs - row_dot)).astype(jnp.bfloat16)
        grad_query = (
            jnp.einsum("chqk,ckhd->cqhd", grad_scores, key_rows, preferred_element_type=jnp.float32)
            * score_scale
        )
        grad_keys = (
            grad_keys
            + jnp.einsum(
                "chqk,cqhd->ckhd", grad_scores, query_block, preferred_element_type=jnp.float32
            )
            * score_scale
        )
        grad_values = grad_values + jnp.einsum(
            "chqk,cqhd->ckhd", weights, grad_block, preferred_element_type=jnp.float32
        )
        return ((grad_keys, grad_values), grad_query)

    zeros = jnp.zeros(key_rows.shape, jnp.float32)
    (grad_keys, grad_values), grad_blocks = lax.scan(
        one_block, (zeros, zeros), jnp.arange(length // block_rows, dtype=jnp.int32)
    )
    grad_query = jnp.moveaxis(grad_blocks, 0, 1).reshape(query_rows.shape)
    return (grad_query, grad_keys, grad_values)


def text_allowed(text_len, text_mask):
    slots = jnp.arange(text_mask.shape[1], dtype=jnp.int32)
    allowed = (slots[None, :] < text_len[:, None]) & ((text_mask > 0) | (slots[None, :] == 0))
    return allowed[:, None, None, :]


def cross_forward(query_rows, key_rows, value_rows, allowed):
    score_scale = query_rows.shape[3] ** (-0.5)
    raw_scores = jnp.einsum(
        "cqhd,ckhd->chqk", query_rows, key_rows, preferred_element_type=jnp.float32
    )
    logits = jnp.where(allowed, raw_scores * score_scale, MASKED)
    row_max = jnp.max(logits, axis=-1, keepdims=True)
    exponent = jnp.exp(logits - row_max)
    row_sum = jnp.sum(exponent, axis=-1, keepdims=True)
    weights = (exponent / row_sum).astype(jnp.bfloat16)
    crossed = jnp.einsum("chqk,ckhd->cqhd", weights, value_rows, preferred_element_type=jnp.float32)
    return (crossed.astype(jnp.bfloat16), row_max + jnp.log(row_sum))


def cross_backward(query_rows, key_rows, value_rows, grad_rows, log_sums, allowed):
    score_scale = query_rows.shape[3] ** (-0.5)
    raw_scores = jnp.einsum(
        "cqhd,ckhd->chqk", query_rows, key_rows, preferred_element_type=jnp.float32
    )
    logits = jnp.where(allowed, raw_scores * score_scale, MASKED)
    probs = jnp.exp(logits - log_sums)
    weights = probs.astype(jnp.bfloat16)
    grad_probs = jnp.einsum(
        "cqhd,ckhd->chqk", grad_rows, value_rows, preferred_element_type=jnp.float32
    )
    row_dot = jnp.sum(probs * grad_probs, axis=-1, keepdims=True)
    grad_scores = (probs * (grad_probs - row_dot)).astype(jnp.bfloat16)
    grad_query = (
        jnp.einsum("chqk,ckhd->cqhd", grad_scores, key_rows, preferred_element_type=jnp.float32)
        * score_scale
    )
    grad_keys = (
        jnp.einsum("chqk,cqhd->ckhd", grad_scores, query_rows, preferred_element_type=jnp.float32)
        * score_scale
    )
    grad_values = jnp.einsum(
        "chqk,cqhd->ckhd", weights, grad_rows, preferred_element_type=jnp.float32
    )
    return (grad_query, grad_keys, grad_values)


def sum_ffn(grad_ffn_in, grad_ffn_out):
    return (
        lax.psum_scatter(grad_ffn_in, ("clip", "frame"), scatter_dimension=0, tiled=True),
        lax.psum_scatter(grad_ffn_out, ("clip", "frame"), scatter_dimension=0, tiled=True),
    )


def sum_attention(
    grad_self_qkv, grad_self_out, grad_cross_qkv, grad_cross_out, grad_gains, grad_shifts
):
    return (
        lax.psum_scatter(grad_self_qkv, ("clip", "frame"), scatter_dimension=0, tiled=True),
        lax.psum_scatter(grad_self_out, ("clip", "frame"), scatter_dimension=0, tiled=True),
        lax.psum_scatter(grad_cross_qkv, ("clip", "frame"), scatter_dimension=0, tiled=True),
        lax.psum_scatter(grad_cross_out, ("clip", "frame"), scatter_dimension=0, tiled=True),
        lax.psum_scatter(grad_gains, ("clip", "frame"), scatter_dimension=1, tiled=True),
        lax.psum_scatter(grad_shifts, ("clip", "frame"), scatter_dimension=1, tiled=True),
    )


def on_device_any(
    hidden_in,
    text_states,
    out_grad,
    self_qkv,
    self_out,
    cross_qkv,
    cross_out,
    ffn_in,
    ffn_out,
    ln_gain,
    ln_bias,
    clip_len,
    frame_mask,
    text_len,
    text_mask,
):
    clip_count, frames, model_width = hidden_in.shape
    text_slots = text_states.shape[1]
    group_count = lax.axis_size("frame")
    columns_here = model_width // group_count
    heads_here = columns_here // HD
    length = frames * group_count
    frame_index = lax.axis_index("frame")
    full_qkv, full_out, full_cross, full_cross_out, gains_low, shifts_low = fetch_attention(
        self_qkv, self_out, cross_qkv, cross_out, ln_gain, ln_bias
    )
    gains = gains_low.astype(jnp.float32)
    shifts = shifts_low.astype(jnp.float32)
    hidden = hidden_in.astype(jnp.float32)
    first_norm, first_pull = jax.vjp(layer_norm, hidden, gains[0], shifts[0])
    first_low = first_norm.astype(jnp.bfloat16)
    query_low = project(first_low, full_qkv[:, 0]).astype(jnp.bfloat16)
    key_low = project(first_low, full_qkv[:, 1]).astype(jnp.bfloat16)
    value_low = project(first_low, full_qkv[:, 2]).astype(jnp.bfloat16)
    query_heads, key_heads, value_heads = (
        lax.all_to_all(query_low, "frame", split_axis=2, concat_axis=1, tiled=True),
        lax.all_to_all(key_low, "frame", split_axis=2, concat_axis=1, tiled=True),
        lax.all_to_all(value_low, "frame", split_axis=2, concat_axis=1, tiled=True),
    )
    head_shape = (clip_count, length, heads_here, HD)
    query_heads = query_heads.reshape(head_shape)
    key_heads = key_heads.reshape(head_shape)
    value_heads = value_heads.reshape(head_shape)
    columns = jnp.arange(length, dtype=jnp.int32)
    key_valid = (columns[None, :] < clip_len[:, None]) & (frame_mask > 0)
    attended_heads, self_sums = self_forward(
        query_heads, key_heads, value_heads, clip_len, key_valid
    )
    attended = lax.all_to_all(
        attended_heads.reshape(clip_count, length, columns_here),
        "frame",
        split_axis=1,
        concat_axis=2,
        tiled=True,
    )
    after_self = hidden + project(attended, full_out)
    second_norm, second_pull = jax.vjp(layer_norm, after_self, gains[1], shifts[1])
    second_low = second_norm.astype(jnp.bfloat16)
    cross_query = project(second_low, full_cross[:, 0]).astype(jnp.bfloat16)
    cross_query_heads = lax.all_to_all(
        cross_query, "frame", split_axis=2, concat_axis=1, tiled=True
    ).reshape(head_shape)
    key_columns = lax.dynamic_slice_in_dim(
        full_cross[:, 1], frame_index * columns_here, columns_here, 1
    )
    value_columns = lax.dynamic_slice_in_dim(
        full_cross[:, 2], frame_index * columns_here, columns_here, 1
    )
    text_shape = (clip_count, text_slots, heads_here, HD)
    text_keys = project(text_states, key_columns).astype(jnp.bfloat16).reshape(text_shape)
    text_values = project(text_states, value_columns).astype(jnp.bfloat16).reshape(text_shape)
    allowed_text = text_allowed(text_len, text_mask)
    crossed_heads, cross_sums = cross_forward(
        cross_query_heads, text_keys, text_values, allowed_text
    )
    crossed = lax.all_to_all(
        crossed_heads.reshape(clip_count, length, columns_here),
        "frame",
        split_axis=1,
        concat_axis=2,
        tiled=True,
    )
    after_cross = after_self + project(crossed, full_cross_out)
    ffn_weight_in, ffn_weight_out = fetch_ffn(ffn_in, ffn_out)
    third_norm, third_pull = jax.vjp(layer_norm, after_cross, gains[2], shifts[2])
    third_low = third_norm.astype(jnp.bfloat16)
    pre_act = project(third_low, ffn_weight_in)
    activated, gelu_pull = jax.vjp(activate, pre_act)
    inner_low = activated.astype(jnp.bfloat16)
    output = (after_cross + project(inner_low, ffn_weight_out)).astype(jnp.bfloat16)
    ffn_weight_in, ffn_weight_out = fetch_ffn(ffn_in, ffn_out)
    grad_ffn_out = weight_grad(inner_low, out_grad)
    (grad_pre,) = gelu_pull(project_back(out_grad, ffn_weight_out))
    grad_pre_low = grad_pre.astype(jnp.bfloat16)
    grad_ffn_in = weight_grad(third_low, grad_pre_low)
    ffn_sums = sum_ffn(grad_ffn_in, grad_ffn_out)
    grad_third, gain_third, shift_third = third_pull(project_back(grad_pre_low, ffn_weight_in))
    grad_after_cross = out_grad.astype(jnp.float32) + grad_third
    full_qkv, full_out, full_cross, full_cross_out, gains_low, shifts_low = fetch_attention(
        self_qkv, self_out, cross_qkv, cross_out, ln_gain, ln_bias
    )
    key_columns = lax.dynamic_slice_in_dim(
        full_cross[:, 1], frame_index * columns_here, columns_here, 1
    )
    value_columns = lax.dynamic_slice_in_dim(
        full_cross[:, 2], frame_index * columns_here, columns_here, 1
    )
    cross_branch = grad_after_cross.astype(jnp.bfloat16)
    grad_cross_out = weight_grad(crossed, cross_branch)
    grad_crossed = project_back(cross_branch, full_cross_out).astype(jnp.bfloat16)
    grad_crossed_heads = lax.all_to_all(
        grad_crossed, "frame", split_axis=2, concat_axis=1, tiled=True
    ).reshape(head_shape)
    grad_cq, grad_tk, grad_tv = cross_backward(
        cross_query_heads, text_keys, text_values, grad_crossed_heads, cross_sums, allowed_text
    )
    grad_tk_low = grad_tk.astype(jnp.bfloat16).reshape(clip_count, text_slots, columns_here)
    grad_tv_low = grad_tv.astype(jnp.bfloat16).reshape(clip_count, text_slots, columns_here)
    text_terms = project_back(grad_tk_low, key_columns) + project_back(grad_tv_low, value_columns)
    grad_text = lax.psum_scatter(
        text_terms.astype(jnp.bfloat16), "frame", scatter_dimension=1, tiled=True
    )
    empty_square = jnp.zeros((model_width, model_width), jnp.float32)
    grad_cross_key = lax.dynamic_update_slice_in_dim(
        empty_square, weight_grad(text_states, grad_tk_low), frame_index * columns_here, 1
    )
    grad_cross_value = lax.dynamic_update_slice_in_dim(
        empty_square, weight_grad(text_states, grad_tv_low), frame_index * columns_here, 1
    )
    grad_cq_low = grad_cq.astype(jnp.bfloat16).reshape(clip_count, length, columns_here)
    grad_cross_query = lax.all_to_all(grad_cq_low, "frame", split_axis=1, concat_axis=2, tiled=True)
    grad_cross_qw = weight_grad(second_low, grad_cross_query)
    grad_second, gain_second, shift_second = second_pull(
        project_back(grad_cross_query, full_cross[:, 0])
    )
    grad_after_self = grad_after_cross + grad_second
    self_branch = grad_after_self.astype(jnp.bfloat16)
    grad_self_out = weight_grad(attended, self_branch)
    grad_attended = project_back(self_branch, full_out).astype(jnp.bfloat16)
    grad_attended_heads = lax.all_to_all(
        grad_attended, "frame", split_axis=2, concat_axis=1, tiled=True
    ).reshape(head_shape)
    grad_query, grad_keys, grad_values = self_backward(
        query_heads, key_heads, value_heads, grad_attended_heads, self_sums, clip_len, key_valid
    )
    flat_shape = (clip_count, length, columns_here)
    grad_query, grad_keys, grad_values = (
        lax.all_to_all(
            grad_query.astype(jnp.bfloat16).reshape(flat_shape),
            "frame",
            split_axis=1,
            concat_axis=2,
            tiled=True,
        ),
        lax.all_to_all(
            grad_keys.astype(jnp.bfloat16).reshape(flat_shape),
            "frame",
            split_axis=1,
            concat_axis=2,
            tiled=True,
        ),
        lax.all_to_all(
            grad_values.astype(jnp.bfloat16).reshape(flat_shape),
            "frame",
            split_axis=1,
            concat_axis=2,
            tiled=True,
        ),
    )
    grad_self_qkv = jnp.stack(
        [
            weight_grad(first_low, grad_query),
            weight_grad(first_low, grad_keys),
            weight_grad(first_low, grad_values),
        ],
        axis=1,
    )
    grad_first_norm = (
        project_back(grad_query, full_qkv[:, 0])
        + project_back(grad_keys, full_qkv[:, 1])
        + project_back(grad_values, full_qkv[:, 2])
    )
    grad_first, gain_first, shift_first = first_pull(grad_first_norm)
    grad_hidden = (grad_after_self + grad_first).astype(jnp.bfloat16)
    grad_cross_qkv = jnp.stack([grad_cross_qw, grad_cross_key, grad_cross_value], axis=1)
    grad_gains = jnp.stack([gain_first, gain_second, gain_third])
    grad_shifts = jnp.stack([shift_first, shift_second, shift_third])
    attn_sums = sum_attention(
        grad_self_qkv, grad_self_out, grad_cross_qkv, grad_cross_out, grad_gains, grad_shifts
    )
    return (
        output,
        grad_hidden,
        grad_text,
        attn_sums[0],
        attn_sums[1],
        attn_sums[2],
        attn_sums[3],
        ffn_sums[0],
        ffn_sums[1],
        attn_sums[4],
        attn_sums[5],
    )


MESH = pl.DeviceIdType.MESH
HBM = pl.BlockSpec(memory_space=pl.ANY)
VMEM = pl.BlockSpec(memory_space=pltpu.VMEM)
SMEM = pl.BlockSpec(memory_space=pltpu.SMEM)
NEG = -1e30
F32 = jnp.float32
BF16 = jnp.bfloat16


def fits(mesh):
    return mesh.shape["clip"] == 4 and mesh.shape["frame"] == 8


class Here:
    def __init__(self):
        self.c = lax.axis_index("clip")
        self.f = lax.axis_index("frame")
        self.core = lax.rem(self.f, 2)
        self.z = lax.div(self.f, 2)
        self.pair = lax.div(self.z, 2)
        self.role = lax.rem(self.z, 2)
        self.group = lax.rem(self.f, 4)
        self.cx = self.c + 1 - 2 * lax.rem(self.c, 2)
        self.cy = lax.rem(self.c + 2, 4)
        self.cd = 3 - self.c
        self.sib = self.f + 1 - 2 * self.core
        self.partner = self.f + 2 - 4 * self.role
        self.far_gate = 2 * (2 - self.pair) + self.core
        self.is_gate = self.role + self.pair == 1
        self.far = [2 * (2 * (1 - self.pair) + j) + self.core for j in range(2)]

    def step(self, d):
        return lax.rem(self.f + d, 8)

    def zstep(self, d):
        return lax.rem(self.f + 2 * d, 8)


class Wire:
    def __init__(self, here, send_sem, recv_sem):
        self.here, self.send_sem, self.recv_sem = here, send_sem, recv_sem
        self.used = 0
        self.open = []

    def copy(self, src, dst, tag, c, f):
        self.used += 1
        return pltpu.make_async_remote_copy(
            src_ref=src,
            dst_ref=dst,
            send_sem=self.send_sem.at[self.used - 1],
            recv_sem=self.recv_sem.at[tag],
            device_id=(c, f),
            device_id_type=MESH,
        )

    def send(self, src, dst, tag, c, f):
        copy = self.copy(src, dst, tag, c, f)
        copy.start()
        self.open.append(copy)

    def arrived(self, dst, tag):
        pltpu.make_async_remote_copy(
            src_ref=dst,
            dst_ref=dst,
            send_sem=self.send_sem.at[0],
            recv_sem=self.recv_sem.at[tag],
            device_id=(self.here.c, self.here.sib),
            device_id_type=MESH,
        ).wait_recv()

    def drain(self):
        for copy in self.open:
            copy.wait_send()
        self.open = []


def greet(devices):
    barrier = pltpu.get_barrier_semaphore()
    for device in devices:
        pl.semaphore_signal(barrier, inc=1, device_id=device, device_id_type=MESH)
    pl.semaphore_wait(barrier, len(devices))


def frame_others(here):
    return [(here.c, here.step(d)) for d in range(1, 8)]


def clip_others(here):
    return [(here.cx, here.f), (here.cy, here.f), (here.cd, here.f)]


class ClipGather:
    def __init__(self, wire, block, tag, own=None):
        self.wire, self.block, self.tag = wire, block, tag
        self.own = own or (lambda half: block(wire.here.c, half))

    def begin(self):
        h, w, b, t, own = self.wire.here, self.wire, self.block, self.tag, self.own
        w.send(own(0), b(h.c, 0), t, h.cx, h.f)
        w.send(own(1), b(h.c, 1), t + 2, h.cy, h.f)
        w.send(own(1), b(h.c, 1), t + 1, h.cx, h.f)
        w.send(own(0), b(h.c, 0), t + 3, h.cy, h.f)

    def middle(self):
        h, w, b, t = self.wire.here, self.wire, self.block, self.tag
        w.arrived(b(h.cx, 0), t)
        w.send(b(h.cx, 0), b(h.cx, 0), t + 4, h.cy, h.f)
        w.arrived(b(h.cy, 1), t + 2)
        w.send(b(h.cy, 1), b(h.cy, 1), t + 5, h.cx, h.f)

    def near(self):
        h, w, b, t = self.wire.here, self.wire, self.block, self.tag
        w.arrived(b(h.cx, 1), t + 1)
        w.arrived(b(h.cy, 0), t + 3)

    def end(self):
        h, w, b, t = self.wire.here, self.wire, self.block, self.tag
        w.arrived(b(h.cd, 0), t + 4)
        w.arrived(b(h.cd, 1), t + 5)


class ZGather:
    def __init__(self, wire, slot, tag, own=None):
        self.wire, self.slot, self.tag = wire, slot, tag
        self.own = own if own is not None else slot(wire.here.f)
        self.open = []

    def step(self, s):
        h, w = self.wire.here, self.wire
        left, right = h.f - 2 * (s - 1), h.f + 2 * (s - 1)
        if s > 1:

            @pl.when(left >= 0)
            def _():
                w.arrived(self.slot(left), self.tag + s - 2)

            @pl.when(right <= 7)
            def _():
                w.arrived(self.slot(right), self.tag + 3 + s - 2)

        if s > 3:
            return
        for block, tag, go, to in (
            (left, self.tag, (left >= 0) & (h.z <= 2), h.f + 2),
            (right, self.tag + 3, (right <= 7) & (h.z >= 1), h.f - 2),
        ):
            src = self.own if s == 1 else self.slot(block)
            copy = w.copy(src, self.slot(block), tag + s - 1, h.c, to)
            pl.when(go)(copy.start)
            self.open.append((go, copy))

    def relay(self, d):
        h, w = self.wire.here, self.wire
        f = h.zstep(d)
        w.send(self.own if d == 0 else self.slot(f), self.slot(f), self.tag + 6 + d, h.c, h.sib)

    def end(self):
        h, w = self.wire.here, self.wire
        for d in range(4):
            w.arrived(self.slot(h.zstep(d) + h.sib - h.f), self.tag + 6 + d)

    def drain(self):
        for go, copy in self.open:
            pl.when(go)(copy.wait_send)


class ClipScatter:
    def __init__(self, wire, parts, slots, tag):
        self.wire, self.parts, self.slots, self.tag = wire, parts, slots, tag

    def begin(self, which=None):
        h, w, p, s, t = self.wire.here, self.wire, self.parts, self.slots, self.tag
        if which != 1:
            w.send(p(h.cd, 0), s[0], t, h.cx, h.f)
            w.send(p(h.cd, 1), s[1], t + 1, h.cy, h.f)
        if which != 0:
            w.send(p(h.cx, 0), s[2], t + 2, h.cx, h.f)
            w.send(p(h.cy, 1), s[3], t + 3, h.cy, h.f)

    def middle(self):
        h, w, p, s, t = self.wire.here, self.wire, self.parts, self.slots, self.tag
        w.arrived(s[0], t)
        add_into(s[0], p(h.cy, 0))
        w.send(s[0], s[4], t + 4, h.cy, h.f)
        w.arrived(s[1], t + 1)
        add_into(s[1], p(h.cx, 1))
        w.send(s[1], s[5], t + 5, h.cx, h.f)

    def end(self):
        w, s, t = self.wire, self.slots, self.tag
        for i in range(2, 6):
            w.arrived(s[i], t + i)

    def total(self, half):
        s = self.slots
        first, second = (s[2], s[4]) if half == 0 else (s[5], s[3])
        own = self.parts(self.wire.here.c, half)
        return own[...].astype(F32) + first[...].astype(F32) + second[...].astype(F32)


class ZScatter:
    def __init__(self, wire, terms, near, far, tag):
        self.wire, self.terms, self.near, self.far, self.tag = wire, terms, near, far, tag
        self.open = []

    def term(self, m):
        pair = self.wire.here.pair
        return self.terms.at[m + pair * (3 - 2 * m)]

    def _start(self, go, src, dst, tag, f):
        copy = self.wire.copy(src, dst, self.tag + tag, self.wire.here.c, f)
        pl.when(go)(copy.start)
        self.open.append((go, copy))

    def begin(self):
        h = self.wire.here
        for i, m in enumerate((3, 2, 1)):
            self._start(jnp.logical_not(h.is_gate), self.term(m), self.near.at[i], i, h.partner)

    def step(self, s):
        h, w = self.wire.here, self.wire
        block, m, tag, to, f = (
            (self.near.at[0], 3, 0, 0, h.far_gate),
            (self.near.at[1], 2, 1, 1, h.far_gate),
            (self.far.at[0], 0, 3, 0, h.partner),
        )[s - 1]

        @pl.when(h.is_gate)
        def _():
            w.arrived(block, self.tag + tag)
            add_into(block, self.term(m))

        self._start(h.is_gate, block, self.far.at[to], 3 + to, f)

    def end(self):
        h, w = self.wire.here, self.wire

        @pl.when(h.is_gate)
        def _():
            w.arrived(self.near.at[2], self.tag + 2)
            w.arrived(self.far.at[1], self.tag + 4)

        @pl.when(jnp.logical_not(h.is_gate))
        def _():
            w.arrived(self.far.at[0], self.tag + 3)

    def total(self, out):
        h = self.wire.here
        self.end()

        @pl.when(h.is_gate)
        def _():
            others = self.near[2].astype(F32) + self.far[1].astype(F32)
            out[...] = self.terms[h.z].astype(F32) + others

        @pl.when(jnp.logical_not(h.is_gate))
        def _():
            out[...] = self.terms[h.z].astype(F32) + self.far[0].astype(F32)

    def drain(self):
        for go, copy in self.open:
            pl.when(go)(copy.wait_send)


class SiblingSum:
    def __init__(self, wire, terms, inbox, sums, tag):
        self.wire, self.terms, self.inbox, self.sums, self.tag = wire, terms, inbox, sums, tag

    def begin(self):
        h, w = self.wire.here, self.wire
        for z in range(4):
            w.send(self.terms(2 * z + 1 - h.core), self.inbox(z), self.tag + z, h.c, h.sib)

    def end(self):
        h, w = self.wire.here, self.wire
        for z in range(4):
            w.arrived(self.inbox(z), self.tag + z)
            own, other = self.terms(2 * z + h.core), self.inbox(z)
            self.sums(z)[...] = (own[...].astype(F32) + other[...].astype(F32)).astype(BF16)


def add_into(into, other):
    into[...] = (into[...].astype(F32) + other[...].astype(F32)).astype(BF16)


class LocalCopy:
    def __init__(self, src, through, dst, sem):
        self.a = pltpu.make_async_copy(src, through, sem)
        self.b = pltpu.make_async_copy(through, dst, sem)
        self.a.start()

    def turn(self):
        self.a.wait()
        self.b.start()

    def wait(self):
        self.b.wait()


def comm_call(body, out_shape, in_specs, out_specs, scratch, copies, tags, collective_id, cost=None):
    return pl.pallas_call(
        body,
        out_shape=out_shape,
        in_specs=in_specs,
        out_specs=out_specs,
        scratch_shapes=list(scratch)
        + [pltpu.SemaphoreType.DMA((copies,)), pltpu.SemaphoreType.DMA((tags,))],
        compiler_params=pltpu.CompilerParams(
            collective_id=collective_id, has_side_effects=True, vmem_limit_bytes=60 * 2**20
        ),
    )


def shape(dims, dtype=BF16):
    return jax.ShapeDtypeStruct(dims, dtype)


ROWS = 256


def dot(left, right, contract):
    return lax.dot_general(left, right, ((contract[:1], contract[1:]), ((), ())), preferred_element_type=F32)


def mask_scores(scores, bias_ref, first, rows):
    low = scores[first:] + bias_ref[first : first + rows, 0:1]
    key = lax.broadcasted_iota(jnp.int32, (rows, rows), 0)
    query = lax.broadcasted_iota(jnp.int32, (rows, rows), 1)
    low = jnp.where(key < query, low, jnp.where(key == query, scores[first:], NEG))
    if first == 0:
        return low
    return jnp.concatenate([scores[:first] + bias_ref[0:first, 0:1], low], axis=0)


def norm_parts(value):
    centered = value - jnp.mean(value, axis=-1, keepdims=True)
    scale = lax.rsqrt(jnp.mean(centered * centered, axis=-1, keepdims=True) + EPSILON)
    return centered * scale, scale


def column_weight(cols, j):
    return cols[:, :, 32 * j : 32 * j + 32, :].reshape(1024, 256)


def attend_rows(i, length, bias, q_ref, k_ref, v_t, o_ref, lse_ref, out_t):
    lane_head = lax.broadcasted_iota(jnp.int32, (ROWS, 256), 1) // HD
    first, n = i * ROWS, (i + 1) * ROWS
    q = q_ref[first:n, :]

    def head(j, _):
        q_head = jnp.where(lane_head == j, q, 0) * jnp.asarray(HD**-0.5, BF16)
        scores = mask_scores(dot(k_ref[0:n, :], q_head, (1, 1)), bias, first, ROWS)
        top = jnp.max(scores, axis=0, keepdims=True)
        weight = jnp.exp(scores - top)
        total = jnp.sum(weight, axis=0, keepdims=True)
        at = pl.ds(pl.multiple_of(j * HD, HD), HD)
        out_t[at, :] = dot(v_t[at, 0:n], weight.astype(BF16), (1, 0)) / total
        lse_ref[pl.ds(j, 1), first:n] = top + jnp.log(total)
        return 0

    lax.fori_loop(0, 4, head, 0)
    live = first + lax.broadcasted_iota(jnp.int32, (ROWS, 256), 0) < length[0]
    o_ref[first:n, :] = jnp.where(live, out_t[...].T, 0).astype(BF16)


def square_of(square, which):
    return square[:, :, 32 * which : 32 * which + 32, :].reshape(1024, 1024)


def text_probs(query, keys, bias, lane_head):
    heads = [jnp.where(lane_head == j, query, 0) for j in range(4)]
    stacked = jnp.concatenate(heads, axis=0)
    scores = dot(stacked, keys, (1, 1)) + bias
    weight = jnp.exp(scores - jnp.max(scores, axis=1, keepdims=True))
    return weight / jnp.sum(weight, axis=1, keepdims=True), stacked


def pick_heads(stacked, lane_head):
    return sum(jnp.where(lane_head == j, stacked[128 * j : 128 * j + 128], 0) for j in range(4))


def forward_body(
    length, bias, text_bias, text, hid, cols_a, cols_b, square, fin, fout, grad,
    o_hid, o_first, o_q, o_k, o_v, o_heads, o_lse, o_w_a, o_w_b, o_params, o_att, o_tkv, o_square,
    o_second, o_query, o_crossed, o_self, o_cross, o_out, o_in, o_third, o_sum,
    hid_all, first, q_ref, k_ref, v_ref, heads, lse, w_a, w_b, params, att, tkv, sq,
    second, query_ref, crossed, after_self, after_cross, out_ref, in_ref,
    out_t, v_t, own_tkv, own_text, own_hid, fin_in, grad_all, win, wout,
    tokens, inner, slope, g_pre, terms, slots, out_w, inbox, sums, near, far,
    local, saved, send_sem, recv_sem,
):
    h = Here()
    w = Wire(h, send_sem, recv_sem)
    T_HID, T_A, T_B, T_FIN, T_AXY, T_BXY = 0, 10, 17, 24, 27, 33
    T_Z, T_SXY, T_SIB, T_ATT, T_TKV = 39, 49, 73, 85, 93
    T_WIN, T_GRAD, T_TOK, T_WOUT, T_TERM, T_OSIB, T_OZ = 96, 106, 112, 118, 128, 134, 138

    def my_columns(f):
        return pl.ds(pl.multiple_of(lax.rem(f, 4) * 256, 256), 256)

    def fin_part(c):
        return fin.at[:, pl.ds(pl.multiple_of(c * 1024, 1024), 1024)]

    own = [
        pltpu.make_async_copy(src, dst, local.at[i])
        for i, (src, dst) in enumerate(
            (
                (cols_a.at[:, my_columns(h.f)], w_a.at[h.c, h.f]),
                (cols_b.at[:, my_columns(h.f)], w_b.at[h.c, h.f]),
                (hid.at[h.pair], hid_all.at[h.f]),
                (square, sq.at[h.c, h.f]),
                (fin_part(h.c), fin_in.at[h.c]),
                (text, own_text),
                (hid, own_hid),
                (grad, grad_all.at[h.c]),
                (fout, wout.at[h.f]),
            )
        )
    ]
    for copy in own:
        copy.start()
    saves = []

    def save(src, dst):
        copy = pltpu.make_async_copy(src, dst, saved.at[len(saves)])
        copy.start()
        saves.append(copy)

    greet(frame_others(h) + clip_others(h))

    for d in (2, 6, 4, 3, 5, 1, 7):
        f = h.step(d)
        w.send(cols_a.at[:, my_columns(f)], w_a.at[h.c, h.f], T_A + d - 1, h.c, f)

    def square_gather(d):
        f = h.zstep(d)
        return ClipGather(
            w,
            lambda c, half: sq.at[c, f, pl.ds(48 * half, 48), :],
            T_SXY + 6 * d,
            (lambda half: square.at[pl.ds(48 * half, 48), :]) if d == 0 else None,
        )

    gathers = [square_gather(d) for d in range(4)]
    gathers[0].begin()

    def half_of(ref, part):
        return ref.at[pl.ds(64 * part, 64), :]

    for part in range(2):
        w.send(
            half_of(hid.at[1 - h.pair], part),
            half_of(hid_all.at[h.f], part),
            T_HID + 3 + 2 * h.role + part,
            h.c,
            h.far_gate,
        )
        w.send(half_of(hid.at[h.pair], part), half_of(hid_all.at[h.f], part), T_HID + 1 + part, h.c, h.partner)
    w.send(hid.at[h.pair], hid_all.at[h.f], T_HID, h.c, h.sib)
    for i, (c, f) in enumerate(clip_others(h)):
        w.send(fin_part(c), fin_in.at[h.c], T_FIN + i, c, f)
    own[0].wait()
    for d in range(1, 8):
        w.arrived(w_a.at[h.c, lax.rem(h.f + 8 - d, 8)], T_A + d - 1)
    a_gather = ClipGather(w, lambda c, half: w_a.at[c, pl.ds(4 * half, 4)], T_AXY)
    a_gather.begin()
    forwards = []
    for part in range(2):
        for j in range(2):
            block = half_of(hid_all.at[h.far[j]], part)
            w.arrived(block, T_HID + 3 + 2 * j + part)
            forward = w.copy(block, block, T_HID + 3 + 2 * j + part, h.c, h.partner)
            pl.when(h.is_gate)(forward.start)
            forwards.append(forward)
    for d in (2, 6, 4, 3, 5, 1, 7):
        f = h.step(d)
        w.send(cols_b.at[:, my_columns(f)], w_b.at[h.c, h.f], T_B + d - 1, h.c, f)
    for part in range(2):
        w.arrived(half_of(hid_all.at[h.partner], part), T_HID + 1 + part)
    w.send(hid_all.at[h.partner], hid_all.at[h.partner], T_HID + 7, h.c, h.sib)
    for j in range(2):
        w.send(hid_all.at[h.far[j]], hid_all.at[h.far[j]], T_HID + 8 + j, h.c, h.sib)
    a_gather.middle()
    own[3].wait()
    z_gather = ZGather(w, lambda f: sq.at[h.c, f], T_Z)
    z_gather.step(1)
    z_gather.relay(0)
    gathers[0].middle()
    own[1].wait()
    for d in range(1, 8):
        w.arrived(w_b.at[h.c, lax.rem(h.f + 8 - d, 8)], T_B + d - 1)
    b_gather = ClipGather(w, lambda c, half: w_b.at[c, pl.ds(4 * half, 4)], T_BXY)
    b_gather.begin()
    a_gather.near()
    a_gather.end()
    for g in range(8):
        group = sum(w_a[g // 2, 4 * (g % 2) + i, 96:104, 0:128].astype(F32) for i in range(4))
        params[:, 128 * g : 128 * g + 128] = group
    own[2].wait()
    w.arrived(hid_all.at[h.sib], T_HID)
    w.arrived(hid_all.at[h.partner + h.sib - h.f], T_HID + 7)
    for j in range(2):
        w.arrived(hid_all.at[h.far[j] + h.sib - h.f], T_HID + 8 + j)
    z_gather.step(2)

    def project_rows(i, _):
        at = pl.ds(pl.multiple_of(i * 256, 256), 256)
        rows = hid_all[pl.ds(2 * i, 2)].reshape(256, 1024).astype(F32)
        xhat, _ = norm_parts(rows)
        low = (xhat * params[0:1, :] + params[3:4, :]).astype(BF16)
        first[at, :] = low
        for j, out in enumerate((q_ref, k_ref, v_ref)):
            out[at, :] = dot(low, column_weight(w_a, j), (1, 0)).astype(BF16)
        return 0

    lax.fori_loop(0, 2, project_rows, 0)
    z_gather.step(3)
    gathers[2].begin()
    z_gather.relay(2)
    b_gather.middle()
    lax.fori_loop(2, 4, project_rows, 0)
    v_t[...] = v_ref[...].T
    z_gather.step(4)
    for d in (1, 3):
        gathers[d].begin()
        z_gather.relay(d)

    def att_slot(f):
        return att.at[lax.div(f, 4), :, my_columns(f)]

    att_sends = []

    def attend_and_send(i):
        attend_rows(i, length, bias, q_ref, k_ref, v_t, heads, lse, out_t)
        for f in (2 * i, 2 * i + 1):
            block = heads.at[pl.ds(128 * f, 128), :]
            away = h.f != f
            copy = w.copy(block, att_slot(h.f), T_ATT + h.f, h.c, f)
            stay = pltpu.make_async_copy(block, att_slot(h.f), local.at[9])
            pl.when(away)(copy.start)
            pl.when(jnp.logical_not(away))(stay.start)
            att_sends.append((away, copy, stay))

    def square_steps(d):
        f = h.zstep(d)
        if d > 0:
            gathers[d].middle()
        gathers[d].near()
        for i, c in enumerate((h.cx, h.cy)):
            w.send(sq.at[c, f], sq.at[c, f], T_SIB + 3 * d + i, h.c, h.sib)

    def square_last(d):
        f = h.zstep(d)
        gathers[d].end()
        w.send(sq.at[h.cd, f], sq.at[h.cd, f], T_SIB + 3 * d + 2, h.c, h.sib)

    attend_and_send(3)
    def text_slot(f):
        return tkv.at[:, :, :, my_columns(f)]

    b_gather.near()
    b_gather.end()
    own[5].wait()
    for clip in range(2):
        for j in range(2):
            own_tkv[clip, j] = dot(own_text[clip], column_weight(w_b, j), (1, 0)).astype(BF16)
    w.send(own_tkv, text_slot(h.f), T_TKV, h.c, h.partner)
    w.send(own_tkv, text_slot(h.f), T_TKV + 1, h.c, h.sib)
    text_copy = pltpu.make_async_copy(own_tkv, text_slot(h.f), local.at[10])
    text_copy.start()
    square_steps(0)
    square_last(0)
    attend_and_send(2)
    square_steps(2)
    w.arrived(text_slot(h.partner), T_TKV)
    w.send(text_slot(h.partner), text_slot(h.partner), T_TKV + 2, h.c, h.sib)
    attend_and_send(1)
    square_last(2)
    square_steps(1)
    attend_and_send(0)
    own[4].wait()
    for i, (c, f) in enumerate(clip_others(h)):
        w.arrived(fin_in.at[c], T_FIN + i)
    win_gather = ZGather(w, lambda f: win.at[:, f], T_WIN, fin_in)
    win_copy = pltpu.make_async_copy(fin_in, win.at[:, h.f], local.at[11])
    win_copy.start()
    win_gather.step(1)
    win_gather.relay(0)
    square_steps(3)
    square_last(1)
    square_last(3)
    own[7].wait()
    grad_gather = ClipGather(w, lambda c, half: grad_all.at[c, pl.ds(128 * half, 128), :], T_GRAD)
    grad_gather.begin()
    for src, dst in (
        (hid_all, o_hid), (first, o_first), (q_ref, o_q), (k_ref, o_k), (v_ref, o_v), (heads, o_heads), (lse, o_lse),
        (w_a, o_w_a), (w_b, o_w_b), (params, o_params),
    ):
        save(src, dst)
    z_gather.end()
    for d in range(4):
        f = h.zstep(d) + h.sib - h.f
        for i, c in enumerate((h.cx, h.cy, h.cd)):
            w.arrived(sq.at[c, f], T_SIB + 3 * d + i)
    for d in range(1, 8):
        f = lax.rem(h.f + 8 - d, 8)
        w.arrived(att_slot(f), T_ATT + f)
    for away, _, stay in att_sends:
        pl.when(jnp.logical_not(away))(stay.wait)
    win_gather.step(2)

    own[6].wait()
    value = own_hid[...].reshape(256, 1024).astype(F32) + dot(
        att[...].reshape(256, 1024), square_of(sq, 0), (1, 0)
    )
    after_self[...] = value
    xhat, _ = norm_parts(value)
    second[...] = (xhat * params[1:2, :] + params[4:5, :]).astype(BF16)
    query_ref[...] = dot(second[...], square_of(sq, 1), (1, 0)).astype(BF16)
    win_gather.step(3)
    grad_gather.middle()
    w.arrived(text_slot(h.sib), T_TKV + 1)
    w.arrived(text_slot(h.partner + h.sib - h.f), T_TKV + 2)
    text_copy.wait()
    lane_head = lax.broadcasted_iota(jnp.int32, (128, 256), 1) // HD
    for clip in range(2):
        for group in range(4):
            rows, columns = pl.ds(128 * clip, 128), pl.ds(256 * group, 256)
            query = query_ref[rows, columns] * jnp.asarray(HD**-0.5, BF16)
            probs, _ = text_probs(query, tkv[clip, 0, :, columns], text_bias[clip : clip + 1, :], lane_head)
            part = dot(probs.astype(BF16), tkv[clip, 1, :, columns], (1, 0))
            crossed[rows, columns] = pick_heads(part, lane_head).astype(BF16)
        if clip == 0:
            win_gather.step(4)
            for d in range(1, 4):
                win_gather.relay(d)
    own[8].wait()
    out_gather = ZGather(w, lambda f: wout.at[f], T_WOUT)
    out_gather.step(1)
    out_gather.relay(0)
    value = after_self[...] + dot(crossed[...], square_of(sq, 2), (1, 0))
    after_cross[...] = value
    xhat, _ = norm_parts(value)
    tokens[h.c] = (xhat * params[2:3, :] + params[5:6, :]).astype(BF16)

    token_gather = ClipGather(w, lambda c, half: tokens.at[c, pl.ds(128 * half, 128), :], T_TOK)
    token_gather.begin()
    for src, dst in (
        (att, o_att), (tkv, o_tkv), (sq, o_square), (second, o_second), (query_ref, o_query), (crossed, o_crossed),
        (after_self, o_self), (after_cross, o_cross),
    ):
        save(src, dst)
    win_copy.wait()
    win_gather.end()

    def hidden(c):
        for part in range(2):
            rows = pl.ds(128 * part, 128)
            pre = dot(tokens[c, rows, :], win[...].reshape(1024, 1024), (1, 0))
            cdf = 0.5 * (1.0 + lax.erf(pre * (0.5**0.5)))
            inner[c, rows, :] = (pre * cdf).astype(BF16)
            slope[c, rows, :] = cdf + pre * jnp.exp(-0.5 * pre * pre) * 0.3989422804014327

    def hidden_back(c):
        g_inner = dot(grad_all[c], wout[...].reshape(1024, 1024), (1, 1))
        g_pre[c] = (g_inner * slope[c]).astype(BF16)
        terms[c] = dot(g_pre[c], win[...].reshape(1024, 1024), (1, 1)).astype(BF16)

    def out_terms(c):
        out_ref[c] = dot(inner[c], wout[...].reshape(1024, 1024), (1, 0)).astype(BF16)

    sibling = SiblingSum(w, lambda f: out_w.at[f], lambda z: inbox.at[z], lambda z: sums.at[z], T_OSIB)
    z_scatter = ZScatter(w, sums, near, far, T_OZ)
    tall = (1024, 1024)

    def out_weight(i, _):
        columns = pl.ds(pl.multiple_of(i * 256, 256), 256)
        out = dot(inner[:, :, columns].reshape(1024, 256), grad_all[...].reshape(tall), (0, 0))
        out_w[pl.ds(2 * i, 2)] = out.astype(BF16).reshape(2, 128, 1024)
        return 0

    def in_weight(i, _):
        columns = pl.ds(pl.multiple_of(i * 256, 256), 256)
        out = dot(tokens[:, :, columns].reshape(1024, 256), g_pre[...].reshape(tall), (0, 0))
        in_ref[:, pl.ds(pl.multiple_of(32 * i, 32), 32), :] = out.astype(BF16).reshape(8, 32, 1024)
        return 0

    hidden(h.c)
    out_gather.step(2)
    grad_gather.near()
    grad_gather.end()
    token_gather.middle()
    token_gather.near()
    out_gather.step(3)
    hidden(h.cx)
    hidden(h.cy)
    out_gather.step(4)
    for d in range(1, 4):
        out_gather.relay(d)
    token_gather.end()
    hidden(h.cd)
    out_gather.end()
    scatter = ClipScatter(
        w, lambda c, half: terms.at[c, pl.ds(128 * half, 128), :], [slots.at[i] for i in range(6)], T_TERM
    )
    hidden_back(h.cd)
    scatter.begin(0)
    hidden_back(h.cx)
    hidden_back(h.cy)
    scatter.begin(1)
    lax.fori_loop(0, 4, out_weight, 0)
    sibling.begin()
    scatter.middle()
    hidden_back(h.c)
    sibling.end()
    z_scatter.begin()
    lax.fori_loop(0, 2, in_weight, 0)
    z_scatter.step(1)
    lax.fori_loop(2, 4, in_weight, 0)
    save(in_ref, o_in)
    out_terms(0)
    z_scatter.step(2)
    z_scatter.step(3)
    out_terms(1)
    out_terms(2)
    out_terms(3)
    save(out_ref, o_out)
    scatter.end()
    for half in range(2):
        o_third[128 * half : 128 * half + 128, :] = scatter.total(half)
    z_scatter.total(o_sum)
    w.drain()
    for copy in forwards:
        pl.when(h.is_gate)(copy.wait_send)
    for away, copy, _ in att_sends:
        pl.when(away)(copy.wait_send)
    for one in (z_gather, win_gather, out_gather, z_scatter):
        one.drain()
    for copy in saves:
        copy.wait()


def forward(*args):
    column, rows, full, quarter = (1024, 256), (256, 1024), (4, 256, 1024), (4, 128, 1024)
    kept = [
        shape((8, 128, 1024)),
        shape((1024, 1024)),
        shape(column),
        shape(column),
        shape(column),
        shape(column),
        shape((8, 1024), F32),
        shape((4, 8, 112, 256)),
        shape((4, 8, 64, 256)),
        shape((8, 1024), F32),
        shape((2, 128, 1024)),
        shape((2, 2, 128, 1024)),
        shape((4, 8, 96, 1024)),
        shape(rows),
        shape(rows),
        shape(rows),
        shape(rows, F32),
        shape(rows, F32),
        shape(full),
        shape((8, 128, 1024)),
    ]
    return comm_call(
        forward_body,
        tuple(kept) + (shape(rows, F32), shape((128, 1024), F32)),
        [SMEM, VMEM, VMEM] + [HBM] * 8,
        (HBM,) * len(kept) + (VMEM,) * 2,
        [pltpu.VMEM(one.shape, one.dtype) for one in kept]
        + [
            pltpu.VMEM((256, ROWS), F32),
            pltpu.VMEM((256, 1024), BF16),
            pltpu.VMEM((2, 2, 128, 256), BF16),
            pltpu.VMEM((2, 128, 1024), BF16),
            pltpu.VMEM((2, 128, 1024), BF16),
            pltpu.VMEM((4, 32, 1024), BF16),
            pltpu.VMEM(full, BF16),
            pltpu.VMEM((4, 8, 32, 1024), BF16),
            pltpu.VMEM((8, 128, 1024), BF16),
            pltpu.VMEM(full, BF16),
            pltpu.VMEM(full, BF16),
            pltpu.VMEM(full, F32),
            pltpu.VMEM(full, BF16),
            pltpu.VMEM(full, BF16),
            pltpu.VMEM((6, 128, 1024), BF16),
            pltpu.VMEM((8, 128, 1024), BF16),
            pltpu.VMEM(quarter, BF16),
            pltpu.VMEM(quarter, BF16),
            pltpu.VMEM((3, 128, 1024), BF16),
            pltpu.VMEM((2, 128, 1024), BF16),
            pltpu.SemaphoreType.DMA((12,)),
            pltpu.SemaphoreType.DMA((24,)),
        ],
        192,
        144,
        1,
    )(*args)


def attend_back_rows(i, length, bias, q_ref, k_ref, v_ref, o_ref, lse_ref, g_ref, dq_ref, dq_t, k_t, dk, dv):
    lane_head = lax.broadcasted_iota(jnp.int32, (ROWS, 256), 1) // HD
    first, n = i * ROWS, (i + 1) * ROWS
    q = q_ref[first:n, :] * jnp.asarray(HD**-0.5, BF16)
    live = first + lax.broadcasted_iota(jnp.int32, (ROWS, 256), 0) < length[0]
    g = jnp.where(live, g_ref[first:n, :], 0)
    both = (g.astype(F32) * o_ref[first:n, :].astype(F32)).T
    row_dots = jnp.concatenate(
        [jnp.sum(both[HD * j : HD * j + HD], axis=0, keepdims=True) for j in range(4)], axis=0
    )
    lse = lse_ref[0:4, first:n]

    def pick(rows, j):
        at = lax.broadcasted_iota(jnp.int32, rows.shape, 0) == j
        return jnp.sum(jnp.where(at, rows, 0), axis=0, keepdims=True)

    def head(j, _):
        q_head = jnp.where(lane_head == j, q, 0)
        g_head = jnp.where(lane_head == j, g, 0)
        scores = mask_scores(dot(k_ref[0:n, :], q_head, (1, 1)), bias, first, ROWS)
        probs = jnp.exp(scores - pick(lse, j))
        grads = dot(v_ref[0:n, :], g_head, (1, 1))
        dlogits = (probs * (grads - pick(row_dots, j))).astype(BF16)
        dv[0:n, :] += dot(probs.astype(BF16), g_head, (1, 0))
        dk[0:n, :] += dot(dlogits, q_head, (1, 0))
        at = pl.ds(pl.multiple_of(j * HD, HD), HD)
        dq_t[at, :] = dot(k_t[at, 0:n], dlogits, (1, 0))
        return 0

    lax.fori_loop(0, 4, head, 0)
    dq_ref[first:n, :] = (dq_t[...].T * (HD**-0.5)).astype(BF16)


def norm_back(xhat, scale, grad, gain):
    h = grad * gain
    return scale * (
        h
        - jnp.mean(h, axis=-1, keepdims=True)
        - xhat * jnp.mean(h * xhat, axis=-1, keepdims=True)
    )


def middle_back_body(
    g_third, g_out, after_cross, after_self, second, query_ref, crossed, att, square, tkv, text_bias, params,
    out_terms, in_terms,
    o_after_self, o_square, o_zsquare, o_heads, o_text, o_norm, o_output, o_in,
    g_crossed, g_query, g_att, g_text, slots, sums, from_sib, from_z,
    i_inbox, i_sums, i_left, i_right, i_total, i_out, i_in,
    g_square, s_inbox, s_sums, s_slots, local, send_sem, recv_sem,
):
    h = Here()
    w = Wire(h, send_sem, recv_sem)
    T_HEADS, T_TSIB, T_TZ, T_OUT, T_IN, T_IZ, T_IC, T_SQ = 0, 7, 11, 14, 20, 24, 30, 33
    greet(frame_others(h) + clip_others(h))
    scatter = ClipScatter(
        w,
        lambda c, half: out_terms.at[c, pl.ds(128 * half, 128), :],
        [slots.at[i] for i in range(6)],
        T_OUT,
    )
    scatter.begin()
    in_sibling = SiblingSum(
        w, lambda f: in_terms.at[f], lambda z: i_inbox.at[z], lambda z: i_sums.at[z], T_IN
    )
    in_scatter = ZScatter(w, i_sums, i_left, i_right, T_IZ)
    in_sibling.begin()

    def square_sums(which):
        sibling = SiblingSum(
            w,
            lambda f: g_square.at[which, :, f],
            lambda z: s_inbox.at[which, z],
            lambda z: s_sums.at[which, z],
            T_SQ + 10 * which,
        )
        clip = ClipScatter(
            w,
            lambda c, half: s_sums.at[which, :, c, pl.ds(16 * half, 16), :],
            [s_slots.at[which, i] for i in range(6)],
            T_SQ + 10 * which + 4,
        )
        return sibling, clip

    squares = [square_sums(0), square_sums(1)]

    def put(ref, value):
        ref[...] = value.astype(BF16).reshape(4, 8, 32, 1024)

    def columns_of(f):
        return pl.ds(pl.multiple_of(lax.rem(f, 4) * 256, 256), 256)

    def part_of(f):
        return g_att.at[lax.div(f, 4), :, columns_of(f)]

    def text_part(f):
        return g_text.at[lax.div(f, 4), :, :, columns_of(f)]

    xhat, scale = norm_parts(after_cross[...])
    grad = g_third[...]
    o_norm[0:1, :] = jnp.sum(grad * xhat, axis=0, keepdims=True)
    o_norm[1:2, :] = jnp.sum(grad, axis=0, keepdims=True)
    g_after_cross = g_out[...].reshape(256, 1024).astype(F32) + norm_back(xhat, scale, grad, params[2:3, :])
    o_after_self[...] = g_after_cross
    branch = g_after_cross.astype(BF16)
    g_crossed[...] = dot(branch, square_of(square, 2), (1, 1)).astype(BF16)
    put(g_square.at[1], dot(crossed[...], branch, (0, 0)))
    squares[1][0].begin()
    in_sibling.end()
    in_scatter.begin()
    lane_head = lax.broadcasted_iota(jnp.int32, (128, 256), 1) // HD
    for clip in range(2):
        for group in range(4):
            rows, columns = pl.ds(128 * clip, 128), pl.ds(256 * group, 256)
            keys, values = tkv[clip, 0, :, columns], tkv[clip, 1, :, columns]
            query = query_ref[rows, columns] * jnp.asarray(HD**-0.5, BF16)
            probs, stacked = text_probs(query, keys, text_bias[clip : clip + 1, :], lane_head)
            grads = g_crossed[rows, columns]
            g_stacked = jnp.concatenate([jnp.where(lane_head == j, grads, 0) for j in range(4)], axis=0)
            g_probs = dot(g_stacked, values, (1, 1))
            row_dot = jnp.sum(probs * g_probs, axis=1, keepdims=True)
            g_logits = (probs * (g_probs - row_dot)).astype(BF16)
            part = dot(g_logits, keys, (1, 0))
            g_query[rows, columns] = (pick_heads(part, lane_head) * (HD**-0.5)).astype(BF16)
            g_text[clip, 0, :, columns] = dot(g_logits, stacked, (0, 0)).astype(BF16)
            g_text[clip, 1, :, columns] = dot(probs.astype(BF16), g_stacked, (0, 0)).astype(BF16)
        if clip == 0:
            scatter.middle()
            in_scatter.step(1)
    in_scatter.step(2)
    squares[1][0].end()
    squares[1][1].begin()
    text_sibling = SiblingSum(
        w, text_part, lambda z: from_sib.at[z], lambda z: sums.at[z], T_TSIB
    )
    text_sibling.begin()
    grad = dot(g_query[...], square_of(square, 1), (1, 1))
    xhat, scale = norm_parts(after_self[...])
    o_norm[2:3, :] = jnp.sum(grad * xhat, axis=0, keepdims=True)
    o_norm[3:4, :] = jnp.sum(grad, axis=0, keepdims=True)
    o_norm[4:8, :] = jnp.zeros((4, 1024), F32)
    g_after_self = o_after_self[...] + norm_back(xhat, scale, grad, params[1:2, :])
    o_after_self[...] = g_after_self
    branch = g_after_self.astype(BF16)
    g_att[...] = dot(branch, square_of(square, 0), (1, 1)).astype(BF16).reshape(2, 128, 1024)
    for d in (4, 2, 6, 3, 5, 1, 7):
        f = h.step(d)
        w.send(part_of(f), o_heads.at[h.f], T_HEADS + d - 1, h.c, f)
    copy = pltpu.make_async_copy(part_of(h.f), o_heads.at[h.f], local.at[0])
    copy.start()
    in_scatter.step(3)
    put(g_square.at[0], dot(second[...], g_query[...], (0, 0)))
    squares[0][0].begin()
    text_sibling.end()
    for d in range(1, 4):
        w.send(sums.at[lax.rem(h.z + d, 4)], from_z.at[d - 1], T_TZ + d - 1, h.c, h.zstep(d))
    squares[1][1].middle()
    put(o_square, dot(att[...].reshape(256, 1024), branch, (0, 0)))
    squares[0][0].end()
    squares[0][1].begin()
    in_scatter.total(i_total)
    i_out[...] = i_total[...].astype(BF16).reshape(4, 32, 1024)
    for i, (c, f) in enumerate(clip_others(h)):
        w.send(i_out.at[c], i_in.at[h.c], T_IC + i, c, f)
    i_in[h.c] = i_out[h.c]
    scatter.end()
    for half in range(2):
        rows = pl.ds(128 * half, 128)
        o_output[rows, :] = (after_cross[rows, :] + scatter.total(half)).astype(BF16)
    squares[0][1].middle()
    for which in (1, 0):
        squares[which][1].end()
        for half in range(2):
            total = squares[which][1].total(half)
            o_zsquare[:, 32 * which + 16 * half : 32 * which + 16 * half + 16, :] = total.astype(BF16)
    for d in range(1, 4):
        w.arrived(from_z.at[d - 1], T_TZ + d - 1)
    total = sums[h.z].astype(F32)
    for d in range(3):
        total = total + from_z[d].astype(F32)
    o_text[...] = total.astype(BF16)
    for i, (c, f) in enumerate(clip_others(h)):
        w.arrived(i_in.at[c], T_IC + i)
    for c in range(4):
        o_in[:, 1024 * c : 1024 * c + 1024] = i_in[c].astype(F32)
    for d in range(1, 8):
        w.arrived(o_heads.at[lax.rem(h.f + 8 - d, 8)], T_HEADS + d - 1)
    copy.wait()
    w.drain()
    in_scatter.drain()


def middle_back(*args):
    rows, block, quarter = (256, 1024), (2, 128, 256), (4, 128, 1024)
    return comm_call(
        middle_back_body,
        (
            shape(rows, F32),
            shape((4, 8, 32, 1024)),
            shape((4, 64, 1024)),
            shape((8, 128, 256)),
            shape(block),
            shape((8, 1024), F32),
            shape(rows),
            shape((32, 4096), F32),
        ),
        [VMEM] * 14,
        (VMEM,) * 8,
        [
            pltpu.VMEM(rows, BF16),
            pltpu.VMEM(rows, BF16),
            pltpu.VMEM((2, 128, 1024), BF16),
            pltpu.VMEM((2, 2, 128, 1024), BF16),
            pltpu.VMEM((6, 128, 1024), BF16),
            pltpu.VMEM((4,) + block, BF16),
            pltpu.VMEM((4,) + block, BF16),
            pltpu.VMEM((3,) + block, BF16),
            pltpu.VMEM(quarter, BF16),
            pltpu.VMEM(quarter, BF16),
            pltpu.VMEM((3, 128, 1024), BF16),
            pltpu.VMEM((2, 128, 1024), BF16),
            pltpu.VMEM((128, 1024), F32),
            pltpu.VMEM((4, 32, 1024), BF16),
            pltpu.VMEM((4, 32, 1024), BF16),
            pltpu.VMEM((2, 4, 8, 32, 1024), BF16),
            pltpu.VMEM((2, 4, 4, 32, 1024), BF16),
            pltpu.VMEM((2, 4, 4, 32, 1024), BF16),
            pltpu.VMEM((2, 6, 4, 16, 1024), BF16),
            pltpu.SemaphoreType.DMA((1,)),
        ],
        80,
        53,
        4,
    )(*args)


def last_body(
    length, bias, q_ref, k_ref, v_ref, o_ref, lse, g_heads, hid, first_low, w_a, w_b, text_in, g_tkv,
    square, z_square, norms, own_hid, g_after, params,
    o_hidden, o_square, o_qkv, o_ckv, o_norm, o_text,
    dq_t, k_t, dk, dv, d_cols, f_terms, f_sib, f_sum, f_in, s_inbox, s_sums, s_slots, s_part,
    z_left, z_right, y_left, y_right, a_terms, a_slots, a_sum, a_in, b_terms, b_slots, b_sum, b_in,
    t_terms, t_in, n_row, n_terms, n_slots, n_sum, n_in, send_sem, recv_sem,
):
    h = Here()
    w = Wire(h, send_sem, recv_sem)
    T_S, T_SC, T_Z, T_Y, T_B, T_T, T_A, T_F, T_N = 0, 4, 10, 16, 22, 36, 44, 86, 94
    greet(frame_others(h) + clip_others(h)[:2])
    s_sibling = SiblingSum(
        w, lambda f: square.at[:, f], lambda z: s_inbox.at[z], lambda z: s_sums.at[z], T_S
    )
    s_sibling.begin()
    z_scatter = ZScatter(w, z_square, z_left, z_right, T_Z)
    z_scatter.begin()
    s_scatter = ClipScatter(
        w,
        lambda c, half: s_sums.at[:, c, pl.ds(16 * half, 16), :],
        [s_slots.at[i] for i in range(6)],
        T_SC,
    )
    y_scatter = ZScatter(w, s_part, y_left, y_right, T_Y)

    class Columns:
        def __init__(self, terms, slots, sums, inbox, tag):
            self.sums, self.inbox, self.tag = sums, inbox, tag
            self.clip = ClipScatter(
                w, lambda c, half: terms.at[c, pl.ds(4 * half, 4)], [slots.at[i] for i in range(6)], tag
            )

        def spread(self):
            self.clip.end()
            for half in range(2):
                self.sums[4 * half : 4 * half + 4] = self.clip.total(half).astype(BF16)
            for d in (4, 2, 6, 3, 5, 1, 7):
                f = h.step(d)
                w.send(self.sums.at[f], self.inbox.at[h.f], self.tag + 5 + d, h.c, f)
            self.inbox[h.f] = self.sums[h.f]

        def wait(self):
            for d in range(1, 8):
                w.arrived(self.inbox.at[lax.rem(h.f + 8 - d, 8)], self.tag + 5 + d)

    text = text_in[h.pair]
    for j in range(2):
        b_terms[:, :, 32 * j : 32 * j + 32, :] = (
            dot(text, g_tkv[j], (0, 0)).astype(BF16).reshape(4, 8, 32, 256)
        )
    b_columns = Columns(b_terms, b_slots, b_sum, b_in, T_B)
    b_columns.clip.begin()
    t_terms[...] = (
        dot(g_tkv[0], column_weight(w_b, 0), (1, 1)) + dot(g_tkv[1], column_weight(w_b, 1), (1, 1))
    ).astype(BF16)
    for d in range(1, 8):
        f = h.step(d)
        w.send(
            t_terms.at[pl.ds(pl.multiple_of(f * 16, 16), 16), :], t_in.at[h.f], T_T + d - 1, h.c, f
        )
    t_in[h.f] = t_terms[pl.ds(pl.multiple_of(h.f * 16, 16), 16), :]

    k_t[...] = k_ref[...].T
    dk[...] = jnp.zeros_like(dk)
    dv[...] = jnp.zeros_like(dv)

    def rows_back(i):
        attend_back_rows(
            i, length, bias, q_ref, k_ref, v_ref, o_ref, lse, g_heads, d_cols.at[0], dq_t, k_t, dk, dv
        )

    rows_back(0)
    s_sibling.end()
    s_scatter.begin()
    z_scatter.step(1)
    rows_back(1)
    z_scatter.step(2)
    z_scatter.step(3)
    b_columns.clip.middle()
    rows_back(2)
    s_scatter.middle()
    b_columns.spread()
    rows_back(3)
    d_cols[1] = dk[...].astype(BF16)
    d_cols[2] = dv[...].astype(BF16)
    a_columns = [
        Columns(a_terms.at[j], a_slots.at[j], a_sum.at[j], a_in.at[j], T_A + 13 * j) for j in range(3)
    ]
    for j in range(3):
        a_terms[j] = dot(first_low[...], d_cols[j], (0, 0)).astype(BF16).reshape(4, 8, 32, 256)
        a_columns[j].clip.begin()

    f_sibling = SiblingSum(
        w, lambda f: f_terms.at[f], lambda z: f_sib.at[z], lambda z: f_sum.at[z], T_F
    )
    n_row[...] = jnp.zeros_like(n_row)

    def frame_terms(i, _):
        rows = pl.ds(pl.multiple_of(i * 256, 256), 256)
        grad = sum(dot(d_cols[j, rows, :], column_weight(w_a, j), (1, 1)) for j in range(3))
        f_terms[pl.ds(2 * i, 2)] = grad.astype(BF16).reshape(2, 128, 1024)
        xhat, _ = norm_parts(hid[pl.ds(2 * i, 2)].reshape(256, 1024).astype(F32))
        n_row[0:1, :] += jnp.sum(grad * xhat, axis=0, keepdims=True)
        n_row[3:4, :] += jnp.sum(grad, axis=0, keepdims=True)
        return 0

    lax.fori_loop(0, 4, frame_terms, 0)
    f_sibling.begin()
    s_scatter.end()
    for half in range(2):
        s_part[:, 16 * half : 16 * half + 16, :] = s_scatter.total(half).astype(BF16)
    y_scatter.begin()
    a_columns[0].clip.middle()
    f_sibling.end()
    other = 2 * (1 - h.pair)
    is_end = jnp.logical_not(h.is_gate)
    to_gate, to_far = [], []
    for j in range(2):
        to_gate.append(w.copy(f_sum.at[other + j], f_in.at[1 + j], T_F + 5 + j, h.c, h.partner))
        pl.when(is_end)(to_gate[j].start)
    w.send(f_sum.at[lax.div(h.partner, 2)], f_in.at[0], T_F + 4, h.c, h.partner)
    n_row[1:2, :] = norms[2:3, :]
    n_row[2:3, :] = norms[0:1, :]
    n_row[4:5, :] = norms[3:4, :]
    n_row[5:6, :] = norms[1:2, :]
    for c in range(4):
        for f in range(8):
            group = 2 * c + f // 4
            n_terms[c, f] = n_row[:, 128 * group : 128 * group + 128].astype(BF16)
    n_columns = Columns(n_terms, n_slots, n_sum, n_in, T_N)
    n_columns.clip.begin()
    a_columns[1].clip.middle()
    a_columns[0].spread()
    for j in range(2):

        @pl.when(h.is_gate)
        def _():
            w.arrived(f_in.at[1 + j], T_F + 5 + j)
            add_into(f_sum.at[other + j], f_in.at[1 + j])

        to_far.append(w.copy(f_sum.at[other + j], f_in.at[3], T_F + 7, h.c, h.far[j]))
        pl.when(h.is_gate)(to_far[j].start)
    y_scatter.step(1)
    a_columns[2].clip.middle()
    a_columns[1].spread()
    n_columns.clip.middle()
    y_scatter.step(2)
    y_scatter.step(3)
    a_columns[2].spread()
    n_columns.spread()
    z_scatter.total(o_square.at[pl.ds(32, 64), :])
    b_columns.wait()
    for j in range(2):
        for q in range(4):
            at = pl.ds(32 * j, 32)
            o_ckv[j, :, 256 * q : 256 * q + 256] = b_in[q, at, :].astype(F32) + b_in[4 + q, at, :].astype(F32)
    for d in range(1, 8):
        w.arrived(t_in.at[lax.rem(h.f + 8 - d, 8)], T_T + d - 1)
    for p in range(2):
        o_text[p] = sum(t_in[4 * p + q].astype(F32) for q in range(4)).astype(BF16)
    w.arrived(f_in.at[0], T_F + 4)
    w.arrived(f_in.at[3], T_F + 7)

    def hidden_out(clip, total):
        xhat, scale = norm_parts(own_hid[clip].astype(F32))
        o_hidden[clip] = (g_after[clip] + norm_back(xhat, scale, total, params[0:1, :])).astype(BF16)

    hidden_out(h.pair, f_sum[h.z].astype(F32) + f_in[0].astype(F32))
    hidden_out(1 - h.pair, f_in[3].astype(F32))
    y_scatter.total(o_square.at[pl.ds(0, 32), :])
    for j in range(3):
        a_columns[j].wait()
        for q in range(4):
            o_qkv[j, :, 256 * q : 256 * q + 256] = a_in[j, q].astype(F32) + a_in[j, 4 + q].astype(F32)
    n_columns.wait()
    o_norm[...] = sum(n_in[f].astype(F32) for f in range(8))
    w.drain()
    z_scatter.drain()
    y_scatter.drain()
    for j in range(2):
        pl.when(is_end)(to_gate[j].wait_send)
        pl.when(h.is_gate)(to_far[j].wait_send)


def last(*args):
    def buffer(*dims):
        return pltpu.VMEM(dims, BF16)

    def full(*dims):
        return pltpu.VMEM(dims, F32)

    return comm_call(
        last_body,
        (
            shape((2, 128, 1024)),
            shape((96, 1024), F32),
            shape((3, 32, 1024), F32),
            shape((2, 32, 1024), F32),
            shape((16, 128), F32),
            shape((2, 16, 1024)),
        ),
        [SMEM] + [VMEM] * 19,
        (VMEM,) * 6,
        [
            full(256, ROWS),
            buffer(256, 1024),
            full(1024, 256),
            full(1024, 256),
            buffer(3, 1024, 256),
            buffer(8, 128, 1024),
            buffer(4, 128, 1024),
            buffer(4, 128, 1024),
            buffer(4, 128, 1024),
            buffer(4, 4, 32, 1024),
            buffer(4, 4, 32, 1024),
            buffer(6, 4, 16, 1024),
            buffer(4, 32, 1024),
            buffer(3, 64, 1024),
            buffer(2, 64, 1024),
            buffer(3, 32, 1024),
            buffer(2, 32, 1024),
            buffer(3, 4, 8, 32, 256),
            buffer(3, 6, 4, 32, 256),
            buffer(3, 8, 32, 256),
            buffer(3, 8, 32, 256),
            buffer(4, 8, 64, 256),
            buffer(6, 4, 64, 256),
            buffer(8, 64, 256),
            buffer(8, 64, 256),
            buffer(128, 1024),
            buffer(8, 16, 1024),
            full(16, 1024),
            buffer(4, 8, 16, 128),
            buffer(6, 4, 16, 128),
            buffer(8, 16, 128),
            buffer(8, 16, 128),
        ],
        140,
        107,
        5,
    )(*args)


def on_device_fast(
    hidden_in,
    text_states,
    out_grad,
    self_qkv,
    self_out,
    cross_qkv,
    cross_out,
    ffn_in,
    ffn_out,
    ln_gain,
    ln_bias,
    clip_len,
    frame_mask,
    text_len,
    text_mask,
):
    frame = lax.axis_index("frame")
    pair = frame // 4
    norms = jnp.concatenate([ln_gain, ln_bias], axis=0)
    placed = lax.dynamic_update_slice(jnp.zeros((16, 256), BF16), norms, (0, 32 * (frame % 4)))
    cols_a = jnp.concatenate(
        [jnp.moveaxis(self_qkv, 1, 0).reshape(96, 1024), jnp.tile(placed, (1, 4))], axis=0
    )
    cols_b = jnp.moveaxis(cross_qkv, 1, 0)[1:].reshape(64, 1024)
    square_here = jnp.concatenate([self_out, cross_qkv[:, 0], cross_out], axis=0)
    columns = jnp.arange(1024, dtype=jnp.int32)
    my_len = lax.dynamic_slice_in_dim(clip_len, pair, 1, 0)
    my_mask = lax.dynamic_slice_in_dim(frame_mask, pair, 1, 0)[0]
    bias = jnp.where((columns < my_len) & (my_mask > 0), 0.0, NEG).astype(F32)
    bias = jnp.broadcast_to(bias[:, None], (1024, 128))
    slots = jnp.arange(128, dtype=jnp.int32)
    text_ok = (slots[None] < text_len[:, None]) & ((text_mask > 0) | (slots[None] == 0))
    text_bias = jnp.where(text_ok, 0.0, NEG).astype(F32)
    (
        hid_all, first_low, query, key, value, att_heads, lse, w_a, w_b, params, att, tkv, square,
        second, cross_query, crossed, after_self, after_cross, out_terms, in_terms, third_sum, grad_ffn_out,
    ) = forward(
        my_len, bias, text_bias, text_states, hidden_in, cols_a, cols_b, square_here, ffn_in, ffn_out,
        out_grad.reshape(256, 1024),
    )
    g_after_self, g_square, z_square, g_heads, g_tkv, g_norms, output, grad_ffn_in = middle_back(
        third_sum, out_grad, after_cross, after_self, second, cross_query, crossed, att, square, tkv,
        text_bias, params, out_terms, in_terms,
    )
    grad_hidden, square_sum, qkv_sum, ckv_sum, norm_sum, grad_text = last(
        my_len, bias, query, key, value, att_heads, lse, g_heads.reshape(1024, 256), hid_all, first_low, w_a, w_b,
        text_states, g_tkv, g_square, z_square, g_norms, hidden_in, g_after_self.reshape(2, 128, 1024), params,
    )
    norm_sum = lax.dynamic_slice(norm_sum, (0, 32 * (frame % 4)), (6, 32))
    return (
        output.reshape(2, 128, 1024),
        grad_hidden,
        grad_text,
        jnp.moveaxis(qkv_sum, 0, 1),
        square_sum[0:32],
        jnp.stack([square_sum[32:64], ckv_sum[0], ckv_sum[1]], axis=1),
        square_sum[64:96],
        grad_ffn_in,
        grad_ffn_out,
        norm_sum[0:3],
        norm_sum[3:6],
    )


def solution(mesh):
    return jax.shard_map(
        on_device_fast if fits(mesh) else on_device_any,
        mesh=mesh,
        in_specs=(
            P("clip", "frame", None),
            P("clip", None, None),
            P("clip", "frame", None),
            P(("clip", "frame"), None, None),
            P(("clip", "frame"), None),
            P(("clip", "frame"), None, None),
            P(("clip", "frame"), None),
            P(("clip", "frame"), None),
            P(("clip", "frame"), None),
            P(None, ("clip", "frame")),
            P(None, ("clip", "frame")),
            P("clip"),
            P("clip", None),
            P("clip"),
            P("clip", None),
        ),
        out_specs=(
            P("clip", "frame", None),
            P("clip", "frame", None),
            P("clip", "frame", None),
            P(("clip", "frame"), None, None),
            P(("clip", "frame"), None),
            P(("clip", "frame"), None, None),
            P(("clip", "frame"), None),
            P(("clip", "frame"), None),
            P(("clip", "frame"), None),
            P(None, ("clip", "frame")),
            P(None, ("clip", "frame")),
        ),
        check_vma=False,
    )
```

```python
import functools

import jax
import jax.numpy as jnp
from jax import lax
from jax.experimental import pallas as pl
from jax.experimental.pallas import tpu as pltpu
from jax.sharding import PartitionSpec as P

HD = 64


MASKED = -1000000000.0
EPSILON = 1e-05


def layer_norm(value, gain, shift):
    average = jnp.mean(value, axis=-1, keepdims=True)
    centered = value - average
    variance = jnp.mean(centered * centered, axis=-1, keepdims=True)
    return centered * lax.rsqrt(variance + EPSILON) * gain + shift


def activate(value):
    return jax.nn.gelu(value, approximate=False)


def project(left, right):
    return jnp.einsum("cnd,de->cne", left, right, preferred_element_type=jnp.float32)


def project_back(grad_rows, weight):
    return jnp.einsum("cne,de->cnd", grad_rows, weight, preferred_element_type=jnp.float32)


def weight_grad(left, right):
    return jnp.einsum("cnd,cne->de", left, right, preferred_element_type=jnp.float32)


def fetch_attention(self_qkv, self_out, cross_qkv, cross_out, ln_gain, ln_bias):
    return (
        lax.all_gather(self_qkv, ("clip", "frame"), axis=0, tiled=True),
        lax.all_gather(self_out, ("clip", "frame"), axis=0, tiled=True),
        lax.all_gather(cross_qkv, ("clip", "frame"), axis=0, tiled=True),
        lax.all_gather(cross_out, ("clip", "frame"), axis=0, tiled=True),
        lax.all_gather(ln_gain, ("clip", "frame"), axis=1, tiled=True),
        lax.all_gather(ln_bias, ("clip", "frame"), axis=1, tiled=True),
    )


def fetch_ffn(ffn_in, ffn_out):
    return (
        lax.all_gather(ffn_in, ("clip", "frame"), axis=0, tiled=True),
        lax.all_gather(ffn_out, ("clip", "frame"), axis=0, tiled=True),
    )


def self_masks(first_row, block_rows, clip_len, key_valid):
    columns = jnp.arange(key_valid.shape[1], dtype=jnp.int32)
    row_ids = first_row + jnp.arange(block_rows, dtype=jnp.int32)
    diagonal = columns[None, :] == row_ids[:, None]
    allowed = (columns[None, :] <= row_ids[:, None])[None] & (
        key_valid[:, None, :] | diagonal[None]
    )
    live_rows = (row_ids[None, :] < clip_len[:, None]).astype(jnp.float32)
    return (allowed[:, None], live_rows[:, None, :, None])


def self_forward(query_rows, key_rows, value_rows, clip_len, key_valid):
    length = query_rows.shape[1]
    block_rows = min(512, length)
    score_scale = query_rows.shape[3] ** (-0.5)

    def one_block(block_index):
        first_row = block_index * block_rows
        query_block = lax.dynamic_slice_in_dim(query_rows, first_row, block_rows, 1)
        raw_scores = jnp.einsum(
            "cqhd,ckhd->chqk", query_block, key_rows, preferred_element_type=jnp.float32
        )
        allowed, live_rows = self_masks(first_row, block_rows, clip_len, key_valid)
        logits = jnp.where(allowed, raw_scores * score_scale, MASKED)
        row_max = jnp.max(logits, axis=-1, keepdims=True)
        exponent = jnp.exp(logits - row_max)
        row_sum = jnp.sum(exponent, axis=-1, keepdims=True)
        weights = (exponent / row_sum * live_rows).astype(jnp.bfloat16)
        attended = jnp.einsum(
            "chqk,ckhd->cqhd", weights, value_rows, preferred_element_type=jnp.float32
        )
        return (attended.astype(jnp.bfloat16), row_max + jnp.log(row_sum))

    blocks, log_sums = lax.map(one_block, jnp.arange(length // block_rows, dtype=jnp.int32))
    return (jnp.moveaxis(blocks, 0, 1).reshape(query_rows.shape), log_sums)


def self_backward(query_rows, key_rows, value_rows, grad_rows, log_sums, clip_len, key_valid):
    length = query_rows.shape[1]
    block_rows = min(512, length)
    score_scale = query_rows.shape[3] ** (-0.5)

    def one_block(totals, block_index):
        grad_keys, grad_values = totals
        first_row = block_index * block_rows
        query_block = lax.dynamic_slice_in_dim(query_rows, first_row, block_rows, 1)
        grad_block = lax.dynamic_slice_in_dim(grad_rows, first_row, block_rows, 1)
        raw_scores = jnp.einsum(
            "cqhd,ckhd->chqk", query_block, key_rows, preferred_element_type=jnp.float32
        )
        allowed, live_rows = self_masks(first_row, block_rows, clip_len, key_valid)
        logits = jnp.where(allowed, raw_scores * score_scale, MASKED)
        probs = jnp.exp(logits - log_sums[block_index])
        weights = (probs * live_rows).astype(jnp.bfloat16)
        grad_probs = (
            jnp.einsum(
                "cqhd,ckhd->chqk", grad_block, value_rows, preferred_element_type=jnp.float32
            )
            * live_rows
        )
        row_dot = jnp.sum(probs * grad_probs, axis=-1, keepdims=True)
        grad_scores = (probs * (grad_probs - row_dot)).astype(jnp.bfloat16)
        grad_query = (
            jnp.einsum("chqk,ckhd->cqhd", grad_scores, key_rows, preferred_element_type=jnp.float32)
            * score_scale
        )
        grad_keys = (
            grad_keys
            + jnp.einsum(
                "chqk,cqhd->ckhd", grad_scores, query_block, preferred_element_type=jnp.float32
            )
            * score_scale
        )
        grad_values = grad_values + jnp.einsum(
            "chqk,cqhd->ckhd", weights, grad_block, preferred_element_type=jnp.float32
        )
        return ((grad_keys, grad_values), grad_query)

    zeros = jnp.zeros(key_rows.shape, jnp.float32)
    (grad_keys, grad_values), grad_blocks = lax.scan(
        one_block, (zeros, zeros), jnp.arange(length // block_rows, dtype=jnp.int32)
    )
    grad_query = jnp.moveaxis(grad_blocks, 0, 1).reshape(query_rows.shape)
    return (grad_query, grad_keys, grad_values)


def text_allowed(text_len, text_mask):
    slots = jnp.arange(text_mask.shape[1], dtype=jnp.int32)
    allowed = (slots[None, :] < text_len[:, None]) & ((text_mask > 0) | (slots[None, :] == 0))
    return allowed[:, None, None, :]


def cross_forward(query_rows, key_rows, value_rows, allowed):
    score_scale = query_rows.shape[3] ** (-0.5)
    raw_scores = jnp.einsum(
        "cqhd,ckhd->chqk", query_rows, key_rows, preferred_element_type=jnp.float32
    )
    logits = jnp.where(allowed, raw_scores * score_scale, MASKED)
    row_max = jnp.max(logits, axis=-1, keepdims=True)
    exponent = jnp.exp(logits - row_max)
    row_sum = jnp.sum(exponent, axis=-1, keepdims=True)
    weights = (exponent / row_sum).astype(jnp.bfloat16)
    crossed = jnp.einsum("chqk,ckhd->cqhd", weights, value_rows, preferred_element_type=jnp.float32)
    return (crossed.astype(jnp.bfloat16), row_max + jnp.log(row_sum))


def cross_backward(query_rows, key_rows, value_rows, grad_rows, log_sums, allowed):
    score_scale = query_rows.shape[3] ** (-0.5)
    raw_scores = jnp.einsum(
        "cqhd,ckhd->chqk", query_rows, key_rows, preferred_element_type=jnp.float32
    )
    logits = jnp.where(allowed, raw_scores * score_scale, MASKED)
    probs = jnp.exp(logits - log_sums)
    weights = probs.astype(jnp.bfloat16)
    grad_probs = jnp.einsum(
        "cqhd,ckhd->chqk", grad_rows, value_rows, preferred_element_type=jnp.float32
    )
    row_dot = jnp.sum(probs * grad_probs, axis=-1, keepdims=True)
    grad_scores = (probs * (grad_probs - row_dot)).astype(jnp.bfloat16)
    grad_query = (
        jnp.einsum("chqk,ckhd->cqhd", grad_scores, key_rows, preferred_element_type=jnp.float32)
        * score_scale
    )
    grad_keys = (
        jnp.einsum("chqk,cqhd->ckhd", grad_scores, query_rows, preferred_element_type=jnp.float32)
        * score_scale
    )
    grad_values = jnp.einsum(
        "chqk,cqhd->ckhd", weights, grad_rows, preferred_element_type=jnp.float32
    )
    return (grad_query, grad_keys, grad_values)


def sum_ffn(grad_ffn_in, grad_ffn_out):
    return (
        lax.psum_scatter(grad_ffn_in, ("clip", "frame"), scatter_dimension=0, tiled=True),
        lax.psum_scatter(grad_ffn_out, ("clip", "frame"), scatter_dimension=0, tiled=True),
    )


def sum_attention(
    grad_self_qkv, grad_self_out, grad_cross_qkv, grad_cross_out, grad_gains, grad_shifts
):
    return (
        lax.psum_scatter(grad_self_qkv, ("clip", "frame"), scatter_dimension=0, tiled=True),
        lax.psum_scatter(grad_self_out, ("clip", "frame"), scatter_dimension=0, tiled=True),
        lax.psum_scatter(grad_cross_qkv, ("clip", "frame"), scatter_dimension=0, tiled=True),
        lax.psum_scatter(grad_cross_out, ("clip", "frame"), scatter_dimension=0, tiled=True),
        lax.psum_scatter(grad_gains, ("clip", "frame"), scatter_dimension=1, tiled=True),
        lax.psum_scatter(grad_shifts, ("clip", "frame"), scatter_dimension=1, tiled=True),
    )


def on_device_any(
    hidden_in,
    text_states,
    out_grad,
    self_qkv,
    self_out,
    cross_qkv,
    cross_out,
    ffn_in,
    ffn_out,
    ln_gain,
    ln_bias,
    clip_len,
    frame_mask,
    text_len,
    text_mask,
):
    clip_count, frames, model_width = hidden_in.shape
    text_slots = text_states.shape[1]
    group_count = lax.axis_size("frame")
    columns_here = model_width // group_count
    heads_here = columns_here // HD
    length = frames * group_count
    frame_index = lax.axis_index("frame")
    full_qkv, full_out, full_cross, full_cross_out, gains_low, shifts_low = fetch_attention(
        self_qkv, self_out, cross_qkv, cross_out, ln_gain, ln_bias
    )
    gains = gains_low.astype(jnp.float32)
    shifts = shifts_low.astype(jnp.float32)
    hidden = hidden_in.astype(jnp.float32)
    first_norm, first_pull = jax.vjp(layer_norm, hidden, gains[0], shifts[0])
    first_low = first_norm.astype(jnp.bfloat16)
    query_low = project(first_low, full_qkv[:, 0]).astype(jnp.bfloat16)
    key_low = project(first_low, full_qkv[:, 1]).astype(jnp.bfloat16)
    value_low = project(first_low, full_qkv[:, 2]).astype(jnp.bfloat16)
    query_heads, key_heads, value_heads = (
        lax.all_to_all(query_low, "frame", split_axis=2, concat_axis=1, tiled=True),
        lax.all_to_all(key_low, "frame", split_axis=2, concat_axis=1, tiled=True),
        lax.all_to_all(value_low, "frame", split_axis=2, concat_axis=1, tiled=True),
    )
    head_shape = (clip_count, length, heads_here, HD)
    query_heads = query_heads.reshape(head_shape)
    key_heads = key_heads.reshape(head_shape)
    value_heads = value_heads.reshape(head_shape)
    columns = jnp.arange(length, dtype=jnp.int32)
    key_valid = (columns[None, :] < clip_len[:, None]) & (frame_mask > 0)
    attended_heads, self_sums = self_forward(
        query_heads, key_heads, value_heads, clip_len, key_valid
    )
    attended = lax.all_to_all(
        attended_heads.reshape(clip_count, length, columns_here),
        "frame",
        split_axis=1,
        concat_axis=2,
        tiled=True,
    )
    after_self = hidden + project(attended, full_out)
    second_norm, second_pull = jax.vjp(layer_norm, after_self, gains[1], shifts[1])
    second_low = second_norm.astype(jnp.bfloat16)
    cross_query = project(second_low, full_cross[:, 0]).astype(jnp.bfloat16)
    cross_query_heads = lax.all_to_all(
        cross_query, "frame", split_axis=2, concat_axis=1, tiled=True
    ).reshape(head_shape)
    key_columns = lax.dynamic_slice_in_dim(
        full_cross[:, 1], frame_index * columns_here, columns_here, 1
    )
    value_columns = lax.dynamic_slice_in_dim(
        full_cross[:, 2], frame_index * columns_here, columns_here, 1
    )
    text_shape = (clip_count, text_slots, heads_here, HD)
    text_keys = project(text_states, key_columns).astype(jnp.bfloat16).reshape(text_shape)
    text_values = project(text_states, value_columns).astype(jnp.bfloat16).reshape(text_shape)
    allowed_text = text_allowed(text_len, text_mask)
    crossed_heads, cross_sums = cross_forward(
        cross_query_heads, text_keys, text_values, allowed_text
    )
    crossed = lax.all_to_all(
        crossed_heads.reshape(clip_count, length, columns_here),
        "frame",
        split_axis=1,
        concat_axis=2,
        tiled=True,
    )
    after_cross = after_self + project(crossed, full_cross_out)
    ffn_weight_in, ffn_weight_out = fetch_ffn(ffn_in, ffn_out)
    third_norm, third_pull = jax.vjp(layer_norm, after_cross, gains[2], shifts[2])
    third_low = third_norm.astype(jnp.bfloat16)
    pre_act = project(third_low, ffn_weight_in)
    activated, gelu_pull = jax.vjp(activate, pre_act)
    inner_low = activated.astype(jnp.bfloat16)
    output = (after_cross + project(inner_low, ffn_weight_out)).astype(jnp.bfloat16)
    ffn_weight_in, ffn_weight_out = fetch_ffn(ffn_in, ffn_out)
    grad_ffn_out = weight_grad(inner_low, out_grad)
    (grad_pre,) = gelu_pull(project_back(out_grad, ffn_weight_out))
    grad_pre_low = grad_pre.astype(jnp.bfloat16)
    grad_ffn_in = weight_grad(third_low, grad_pre_low)
    ffn_sums = sum_ffn(grad_ffn_in, grad_ffn_out)
    grad_third, gain_third, shift_third = third_pull(project_back(grad_pre_low, ffn_weight_in))
    grad_after_cross = out_grad.astype(jnp.float32) + grad_third
    full_qkv, full_out, full_cross, full_cross_out, gains_low, shifts_low = fetch_attention(
        self_qkv, self_out, cross_qkv, cross_out, ln_gain, ln_bias
    )
    key_columns = lax.dynamic_slice_in_dim(
        full_cross[:, 1], frame_index * columns_here, columns_here, 1
    )
    value_columns = lax.dynamic_slice_in_dim(
        full_cross[:, 2], frame_index * columns_here, columns_here, 1
    )
    cross_branch = grad_after_cross.astype(jnp.bfloat16)
    grad_cross_out = weight_grad(crossed, cross_branch)
    grad_crossed = project_back(cross_branch, full_cross_out).astype(jnp.bfloat16)
    grad_crossed_heads = lax.all_to_all(
        grad_crossed, "frame", split_axis=2, concat_axis=1, tiled=True
    ).reshape(head_shape)
    grad_cq, grad_tk, grad_tv = cross_backward(
        cross_query_heads, text_keys, text_values, grad_crossed_heads, cross_sums, allowed_text
    )
    grad_tk_low = grad_tk.astype(jnp.bfloat16).reshape(clip_count, text_slots, columns_here)
    grad_tv_low = grad_tv.astype(jnp.bfloat16).reshape(clip_count, text_slots, columns_here)
    text_terms = project_back(grad_tk_low, key_columns) + project_back(grad_tv_low, value_columns)
    grad_text = lax.psum_scatter(
        text_terms.astype(jnp.bfloat16), "frame", scatter_dimension=1, tiled=True
    )
    empty_square = jnp.zeros((model_width, model_width), jnp.float32)
    grad_cross_key = lax.dynamic_update_slice_in_dim(
        empty_square, weight_grad(text_states, grad_tk_low), frame_index * columns_here, 1
    )
    grad_cross_value = lax.dynamic_update_slice_in_dim(
        empty_square, weight_grad(text_states, grad_tv_low), frame_index * columns_here, 1
    )
    grad_cq_low = grad_cq.astype(jnp.bfloat16).reshape(clip_count, length, columns_here)
    grad_cross_query = lax.all_to_all(grad_cq_low, "frame", split_axis=1, concat_axis=2, tiled=True)
    grad_cross_qw = weight_grad(second_low, grad_cross_query)
    grad_second, gain_second, shift_second = second_pull(
        project_back(grad_cross_query, full_cross[:, 0])
    )
    grad_after_self = grad_after_cross + grad_second
    self_branch = grad_after_self.astype(jnp.bfloat16)
    grad_self_out = weight_grad(attended, self_branch)
    grad_attended = project_back(self_branch, full_out).astype(jnp.bfloat16)
    grad_attended_heads = lax.all_to_all(
        grad_attended, "frame", split_axis=2, concat_axis=1, tiled=True
    ).reshape(head_shape)
    grad_query, grad_keys, grad_values = self_backward(
        query_heads, key_heads, value_heads, grad_attended_heads, self_sums, clip_len, key_valid
    )
    flat_shape = (clip_count, length, columns_here)
    grad_query, grad_keys, grad_values = (
        lax.all_to_all(
            grad_query.astype(jnp.bfloat16).reshape(flat_shape),
            "frame",
            split_axis=1,
            concat_axis=2,
            tiled=True,
        ),
        lax.all_to_all(
            grad_keys.astype(jnp.bfloat16).reshape(flat_shape),
            "frame",
            split_axis=1,
            concat_axis=2,
            tiled=True,
        ),
        lax.all_to_all(
            grad_values.astype(jnp.bfloat16).reshape(flat_shape),
            "frame",
            split_axis=1,
            concat_axis=2,
            tiled=True,
        ),
    )
    grad_self_qkv = jnp.stack(
        [
            weight_grad(first_low, grad_query),
            weight_grad(first_low, grad_keys),
            weight_grad(first_low, grad_values),
        ],
        axis=1,
    )
    grad_first_norm = (
        project_back(grad_query, full_qkv[:, 0])
        + project_back(grad_keys, full_qkv[:, 1])
        + project_back(grad_values, full_qkv[:, 2])
    )
    grad_first, gain_first, shift_first = first_pull(grad_first_norm)
    grad_hidden = (grad_after_self + grad_first).astype(jnp.bfloat16)
    grad_cross_qkv = jnp.stack([grad_cross_qw, grad_cross_key, grad_cross_value], axis=1)
    grad_gains = jnp.stack([gain_first, gain_second, gain_third])
    grad_shifts = jnp.stack([shift_first, shift_second, shift_third])
    attn_sums = sum_attention(
        grad_self_qkv, grad_self_out, grad_cross_qkv, grad_cross_out, grad_gains, grad_shifts
    )
    return (
        output,
        grad_hidden,
        grad_text,
        attn_sums[0],
        attn_sums[1],
        attn_sums[2],
        attn_sums[3],
        ffn_sums[0],
        ffn_sums[1],
        attn_sums[4],
        attn_sums[5],
    )


MESH = pl.DeviceIdType.MESH
HBM = pl.BlockSpec(memory_space=pl.ANY)
VMEM = pl.BlockSpec(memory_space=pltpu.VMEM)
SMEM = pl.BlockSpec(memory_space=pltpu.SMEM)
NEG = -1e30
F32 = jnp.float32
BF16 = jnp.bfloat16


def fits(mesh):
    return mesh.shape["clip"] == 4 and mesh.shape["frame"] == 8


class Here:
    def __init__(self):
        self.c = lax.axis_index("clip")
        self.f = lax.axis_index("frame")
        self.core = lax.rem(self.f, 2)
        self.z = lax.div(self.f, 2)
        self.pair = lax.div(self.z, 2)
        self.role = lax.rem(self.z, 2)
        self.group = lax.rem(self.f, 4)
        self.cx = self.c + 1 - 2 * lax.rem(self.c, 2)
        self.cy = lax.rem(self.c + 2, 4)
        self.cd = 3 - self.c
        self.sib = self.f + 1 - 2 * self.core
        self.partner = self.f + 2 - 4 * self.role
        self.far_gate = 2 * (2 - self.pair) + self.core
        self.is_gate = self.role + self.pair == 1
        self.far = [2 * (2 * (1 - self.pair) + j) + self.core for j in range(2)]

    def step(self, d):
        return lax.rem(self.f + d, 8)

    def zstep(self, d):
        return lax.rem(self.f + 2 * d, 8)


class Wire:
    def __init__(self, here, send_sem, recv_sem):
        self.here, self.send_sem, self.recv_sem = here, send_sem, recv_sem
        self.used = 0
        self.open = []

    def copy(self, src, dst, tag, c, f):
        self.used += 1
        return pltpu.make_async_remote_copy(
            src_ref=src,
            dst_ref=dst,
            send_sem=self.send_sem.at[self.used - 1],
            recv_sem=self.recv_sem.at[tag],
            device_id=(c, f),
            device_id_type=MESH,
        )

    def send(self, src, dst, tag, c, f):
        copy = self.copy(src, dst, tag, c, f)
        copy.start()
        self.open.append(copy)

    def arrived(self, dst, tag):
        pltpu.make_async_remote_copy(
            src_ref=dst,
            dst_ref=dst,
            send_sem=self.send_sem.at[0],
            recv_sem=self.recv_sem.at[tag],
            device_id=(self.here.c, self.here.sib),
            device_id_type=MESH,
        ).wait_recv()

    def drain(self):
        for copy in self.open:
            copy.wait_send()
        self.open = []


def greet(devices):
    barrier = pltpu.get_barrier_semaphore()
    for device in devices:
        pl.semaphore_signal(barrier, inc=1, device_id=device, device_id_type=MESH)
    pl.semaphore_wait(barrier, len(devices))


def frame_others(here):
    return [(here.c, here.step(d)) for d in range(1, 8)]


def clip_others(here):
    return [(here.cx, here.f), (here.cy, here.f), (here.cd, here.f)]


class ClipGather:
    def __init__(self, wire, block, tag, own=None):
        self.wire, self.block, self.tag = wire, block, tag
        self.own = own or (lambda half: block(wire.here.c, half))

    def begin(self):
        h, w, b, t, own = self.wire.here, self.wire, self.block, self.tag, self.own
        w.send(own(0), b(h.c, 0), t, h.cx, h.f)
        w.send(own(1), b(h.c, 1), t + 2, h.cy, h.f)
        w.send(own(1), b(h.c, 1), t + 1, h.cx, h.f)
        w.send(own(0), b(h.c, 0), t + 3, h.cy, h.f)

    def middle(self):
        h, w, b, t = self.wire.here, self.wire, self.block, self.tag
        w.arrived(b(h.cx, 0), t)
        w.send(b(h.cx, 0), b(h.cx, 0), t + 4, h.cy, h.f)
        w.arrived(b(h.cy, 1), t + 2)
        w.send(b(h.cy, 1), b(h.cy, 1), t + 5, h.cx, h.f)

    def near(self):
        h, w, b, t = self.wire.here, self.wire, self.block, self.tag
        w.arrived(b(h.cx, 1), t + 1)
        w.arrived(b(h.cy, 0), t + 3)

    def end(self):
        h, w, b, t = self.wire.here, self.wire, self.block, self.tag
        w.arrived(b(h.cd, 0), t + 4)
        w.arrived(b(h.cd, 1), t + 5)


class ZGather:
    def __init__(self, wire, slot, tag, own=None):
        self.wire, self.slot, self.tag = wire, slot, tag
        self.own = own if own is not None else slot(wire.here.f)
        self.open = []

    def step(self, s):
        h, w = self.wire.here, self.wire
        left, right = h.f - 2 * (s - 1), h.f + 2 * (s - 1)
        if s > 1:

            @pl.when(left >= 0)
            def _():
                w.arrived(self.slot(left), self.tag + s - 2)

            @pl.when(right <= 7)
            def _():
                w.arrived(self.slot(right), self.tag + 3 + s - 2)

        if s > 3:
            return
        for block, tag, go, to in (
            (left, self.tag, (left >= 0) & (h.z <= 2), h.f + 2),
            (right, self.tag + 3, (right <= 7) & (h.z >= 1), h.f - 2),
        ):
            src = self.own if s == 1 else self.slot(block)
            copy = w.copy(src, self.slot(block), tag + s - 1, h.c, to)
            pl.when(go)(copy.start)
            self.open.append((go, copy))

    def relay(self, d):
        h, w = self.wire.here, self.wire
        f = h.zstep(d)
        w.send(self.own if d == 0 else self.slot(f), self.slot(f), self.tag + 6 + d, h.c, h.sib)

    def end(self):
        h, w = self.wire.here, self.wire
        for d in range(4):
            w.arrived(self.slot(h.zstep(d) + h.sib - h.f), self.tag + 6 + d)

    def drain(self):
        for go, copy in self.open:
            pl.when(go)(copy.wait_send)


class ClipScatter:
    def __init__(self, wire, parts, slots, tag):
        self.wire, self.parts, self.slots, self.tag = wire, parts, slots, tag

    def begin(self, which=None):
        h, w, p, s, t = self.wire.here, self.wire, self.parts, self.slots, self.tag
        if which != 1:
            w.send(p(h.cd, 0), s[0], t, h.cx, h.f)
            w.send(p(h.cd, 1), s[1], t + 1, h.cy, h.f)
        if which != 0:
            w.send(p(h.cx, 0), s[2], t + 2, h.cx, h.f)
            w.send(p(h.cy, 1), s[3], t + 3, h.cy, h.f)

    def middle(self):
        h, w, p, s, t = self.wire.here, self.wire, self.parts, self.slots, self.tag
        w.arrived(s[0], t)
        add_into(s[0], p(h.cy, 0))
        w.send(s[0], s[4], t + 4, h.cy, h.f)
        w.arrived(s[1], t + 1)
        add_into(s[1], p(h.cx, 1))
        w.send(s[1], s[5], t + 5, h.cx, h.f)

    def end(self):
        w, s, t = self.wire, self.slots, self.tag
        for i in range(2, 6):
            w.arrived(s[i], t + i)

    def total(self, half):
        s = self.slots
        first, second = (s[2], s[4]) if half == 0 else (s[5], s[3])
        own = self.parts(self.wire.here.c, half)
        return own[...].astype(F32) + first[...].astype(F32) + second[...].astype(F32)


class ZScatter:
    def __init__(self, wire, terms, near, far, tag):
        self.wire, self.terms, self.near, self.far, self.tag = wire, terms, near, far, tag
        self.open = []

    def term(self, m):
        pair = self.wire.here.pair
        return self.terms.at[m + pair * (3 - 2 * m)]

    def _start(self, go, src, dst, tag, f):
        copy = self.wire.copy(src, dst, self.tag + tag, self.wire.here.c, f)
        pl.when(go)(copy.start)
        self.open.append((go, copy))

    def begin(self):
        h = self.wire.here
        for i, m in enumerate((3, 2, 1)):
            self._start(jnp.logical_not(h.is_gate), self.term(m), self.near.at[i], i, h.partner)

    def step(self, s):
        h, w = self.wire.here, self.wire
        block, m, tag, to, f = (
            (self.near.at[0], 3, 0, 0, h.far_gate),
            (self.near.at[1], 2, 1, 1, h.far_gate),
            (self.far.at[0], 0, 3, 0, h.partner),
        )[s - 1]

        @pl.when(h.is_gate)
        def _():
            w.arrived(block, self.tag + tag)
            add_into(block, self.term(m))

        self._start(h.is_gate, block, self.far.at[to], 3 + to, f)

    def end(self):
        h, w = self.wire.here, self.wire

        @pl.when(h.is_gate)
        def _():
            w.arrived(self.near.at[2], self.tag + 2)
            w.arrived(self.far.at[1], self.tag + 4)

        @pl.when(jnp.logical_not(h.is_gate))
        def _():
            w.arrived(self.far.at[0], self.tag + 3)

    def total(self, out):
        h = self.wire.here
        self.end()

        @pl.when(h.is_gate)
        def _():
            others = self.near[2].astype(F32) + self.far[1].astype(F32)
            out[...] = (self.terms[h.z].astype(F32) + others).astype(out.dtype)

        @pl.when(jnp.logical_not(h.is_gate))
        def _():
            out[...] = (self.terms[h.z].astype(F32) + self.far[0].astype(F32)).astype(out.dtype)

    def drain(self):
        for go, copy in self.open:
            pl.when(go)(copy.wait_send)


class SiblingSum:
    def __init__(self, wire, terms, inbox, sums, tag):
        self.wire, self.terms, self.inbox, self.sums, self.tag = wire, terms, inbox, sums, tag

    def begin(self):
        h, w = self.wire.here, self.wire
        for z in range(4):
            w.send(self.terms(2 * z + 1 - h.core), self.inbox(z), self.tag + z, h.c, h.sib)

    def end(self):
        h, w = self.wire.here, self.wire
        for z in range(4):
            w.arrived(self.inbox(z), self.tag + z)
            own, other = self.terms(2 * z + h.core), self.inbox(z)
            self.sums(z)[...] = (own[...].astype(F32) + other[...].astype(F32)).astype(BF16)


def add_into(into, other):
    into[...] = (into[...].astype(F32) + other[...].astype(F32)).astype(BF16)


class LocalCopy:
    def __init__(self, src, through, dst, sem):
        self.a = pltpu.make_async_copy(src, through, sem)
        self.b = pltpu.make_async_copy(through, dst, sem)
        self.a.start()

    def turn(self):
        self.a.wait()
        self.b.start()

    def wait(self):
        self.b.wait()


def comm_call(body, out_shape, in_specs, out_specs, scratch, copies, tags, collective_id, cost=None):
    return pl.pallas_call(
        body,
        out_shape=out_shape,
        in_specs=in_specs,
        out_specs=out_specs,
        scratch_shapes=list(scratch)
        + [pltpu.SemaphoreType.DMA((copies,)), pltpu.SemaphoreType.DMA((tags,))],
        compiler_params=pltpu.CompilerParams(
            collective_id=collective_id, has_side_effects=True, vmem_limit_bytes=60 * 2**20
        ),
    )


def shape(dims, dtype=BF16):
    return jax.ShapeDtypeStruct(dims, dtype)


ROWS = 256


def dot(left, right, contract):
    return lax.dot_general(left, right, ((contract[:1], contract[1:]), ((), ())), preferred_element_type=F32)


def mask_scores(scores, bias_ref, first, rows):
    low = scores[first:] + bias_ref[first : first + rows, 0:1]
    key = lax.broadcasted_iota(jnp.int32, (rows, rows), 0)
    query = lax.broadcasted_iota(jnp.int32, (rows, rows), 1)
    low = jnp.where(key < query, low, jnp.where(key == query, scores[first:], NEG))
    if first == 0:
        return low
    return jnp.concatenate([scores[:first] + bias_ref[0:first, 0:1], low], axis=0)


def norm_parts(value):
    centered = value - jnp.mean(value, axis=-1, keepdims=True)
    scale = lax.rsqrt(jnp.mean(centered * centered, axis=-1, keepdims=True) + EPSILON)
    return centered * scale, scale


def column_weight(cols, j):
    return cols[:, :, 32 * j : 32 * j + 32, :].reshape(1024, 256)


def attend_rows(i, length, bias, q_ref, k_ref, v_t, o_ref, lse_ref, out_t):
    lane_head = lax.broadcasted_iota(jnp.int32, (ROWS, 256), 1) // HD
    first, n = i * ROWS, (i + 1) * ROWS
    q = q_ref[first:n, :]

    def head(j, _):
        q_head = jnp.where(lane_head == j, q, 0) * jnp.asarray(HD**-0.5, BF16)
        scores = mask_scores(dot(k_ref[0:n, :], q_head, (1, 1)), bias, first, ROWS)
        top = jnp.max(scores, axis=0, keepdims=True)
        weight = jnp.exp(scores - top)
        total = jnp.sum(weight, axis=0, keepdims=True)
        at = pl.ds(pl.multiple_of(j * HD, HD), HD)
        out_t[at, :] = dot(v_t[at, 0:n], weight.astype(BF16), (1, 0)) / total
        lse_ref[pl.ds(j, 1), first:n] = top + jnp.log(total)
        return 0

    lax.fori_loop(0, 4, head, 0)
    live = first + lax.broadcasted_iota(jnp.int32, (ROWS, 256), 0) < length[0]
    o_ref[first:n, :] = jnp.where(live, out_t[...].T, 0).astype(BF16)


def square_of(square, which):
    return square[:, :, 32 * which : 32 * which + 32, :].reshape(1024, 1024)


def text_probs(query, keys, bias, lane_head):
    heads = [jnp.where(lane_head == j, query, 0) for j in range(4)]
    stacked = jnp.concatenate(heads, axis=0)
    scores = dot(stacked, keys, (1, 1)) + bias
    weight = jnp.exp(scores - jnp.max(scores, axis=1, keepdims=True))
    return weight / jnp.sum(weight, axis=1, keepdims=True), stacked


def pick_heads(stacked, lane_head):
    return sum(jnp.where(lane_head == j, stacked[128 * j : 128 * j + 128], 0) for j in range(4))


def forward_body(
    length, bias, text_bias, text, hid, cols_a, cols_b, square, fin, fout, grad,
    o_hid, o_first, o_q, o_k, o_v, o_heads, o_lse, o_w_a, o_w_b, o_params, o_att, o_tkv, o_square,
    o_second, o_query, o_crossed, o_self, o_cross, o_out, o_in, o_third, o_sum,
    hid_all, first, q_ref, k_ref, v_ref, heads, lse, w_a, w_b, params, att, tkv, sq,
    second, query_ref, crossed, after_self, after_cross, out_ref, in_ref,
    out_t, v_t, own_tkv, own_text, own_hid, fin_in, grad_all, win, wout,
    tokens, inner, slope, g_pre, terms, slots, out_w, inbox, sums, near, far,
    local, saved, send_sem, recv_sem,
):
    h = Here()
    w = Wire(h, send_sem, recv_sem)
    T_HID, T_A, T_B, T_FIN, T_AXY, T_BXY = 0, 10, 17, 24, 27, 33
    T_Z, T_SXY, T_SIB, T_ATT, T_TKV = 39, 49, 73, 85, 93
    T_WIN, T_GRAD, T_TOK, T_WOUT, T_TERM, T_OSIB, T_OZ = 96, 106, 112, 118, 128, 134, 138

    def my_columns(f):
        return pl.ds(pl.multiple_of(lax.rem(f, 4) * 256, 256), 256)

    def fin_part(c):
        return fin.at[:, pl.ds(pl.multiple_of(c * 1024, 1024), 1024)]

    own = [
        pltpu.make_async_copy(src, dst, local.at[i])
        for i, (src, dst) in enumerate(
            (
                (cols_a.at[:, my_columns(h.f)], w_a.at[h.c, h.f]),
                (cols_b.at[:, my_columns(h.f)], w_b.at[h.c, h.f]),
                (hid.at[h.pair], hid_all.at[h.f]),
                (square, sq.at[h.c, h.f]),
                (fin_part(h.c), fin_in.at[h.c]),
                (text, own_text),
                (hid, own_hid),
                (grad, grad_all.at[h.c]),
                (fout, wout.at[h.f]),
            )
        )
    ]
    for copy in own:
        copy.start()
    saves = []

    def save(src, dst):
        copy = pltpu.make_async_copy(src, dst, saved.at[len(saves)])
        copy.start()
        saves.append(copy)

    greet(frame_others(h) + clip_others(h))

    for d in (2, 6, 4, 3, 5, 1, 7):
        f = h.step(d)
        w.send(cols_a.at[:, my_columns(f)], w_a.at[h.c, h.f], T_A + d - 1, h.c, f)

    def square_gather(d):
        f = h.zstep(d)
        return ClipGather(
            w,
            lambda c, half: sq.at[c, f, pl.ds(48 * half, 48), :],
            T_SXY + 6 * d,
            (lambda half: square.at[pl.ds(48 * half, 48), :]) if d == 0 else None,
        )

    gathers = [square_gather(d) for d in range(4)]
    gathers[0].begin()

    def half_of(ref, part):
        return ref.at[pl.ds(64 * part, 64), :]

    for part in range(2):
        w.send(
            half_of(hid.at[1 - h.pair], part),
            half_of(hid_all.at[h.f], part),
            T_HID + 3 + 2 * h.role + part,
            h.c,
            h.far_gate,
        )
        w.send(half_of(hid.at[h.pair], part), half_of(hid_all.at[h.f], part), T_HID + 1 + part, h.c, h.partner)
    w.send(hid.at[h.pair], hid_all.at[h.f], T_HID, h.c, h.sib)
    for i, (c, f) in enumerate(clip_others(h)):
        w.send(fin_part(c), fin_in.at[h.c], T_FIN + i, c, f)
    own[0].wait()
    for d in range(1, 8):
        w.arrived(w_a.at[h.c, lax.rem(h.f + 8 - d, 8)], T_A + d - 1)
    a_gather = ClipGather(w, lambda c, half: w_a.at[c, pl.ds(4 * half, 4)], T_AXY)
    a_gather.begin()
    forwards = []
    for part in range(2):
        for j in range(2):
            block = half_of(hid_all.at[h.far[j]], part)
            w.arrived(block, T_HID + 3 + 2 * j + part)
            forward = w.copy(block, block, T_HID + 3 + 2 * j + part, h.c, h.partner)
            pl.when(h.is_gate)(forward.start)
            forwards.append(forward)
    for d in (2, 6, 4, 3, 5, 1, 7):
        f = h.step(d)
        w.send(cols_b.at[:, my_columns(f)], w_b.at[h.c, h.f], T_B + d - 1, h.c, f)
    for part in range(2):
        w.arrived(half_of(hid_all.at[h.partner], part), T_HID + 1 + part)
    w.send(hid_all.at[h.partner], hid_all.at[h.partner], T_HID + 7, h.c, h.sib)
    for j in range(2):
        w.send(hid_all.at[h.far[j]], hid_all.at[h.far[j]], T_HID + 8 + j, h.c, h.sib)
    a_gather.middle()
    own[3].wait()
    z_gather = ZGather(w, lambda f: sq.at[h.c, f], T_Z)
    z_gather.step(1)
    z_gather.relay(0)
    gathers[0].middle()
    own[1].wait()
    for d in range(1, 8):
        w.arrived(w_b.at[h.c, lax.rem(h.f + 8 - d, 8)], T_B + d - 1)
    b_gather = ClipGather(w, lambda c, half: w_b.at[c, pl.ds(4 * half, 4)], T_BXY)
    b_gather.begin()
    a_gather.near()
    a_gather.end()
    for g in range(8):
        group = sum(w_a[g // 2, 4 * (g % 2) + i, 96:104, 0:128].astype(F32) for i in range(4))
        params[:, 128 * g : 128 * g + 128] = group
    own[2].wait()
    w.arrived(hid_all.at[h.sib], T_HID)
    w.arrived(hid_all.at[h.partner + h.sib - h.f], T_HID + 7)
    for j in range(2):
        w.arrived(hid_all.at[h.far[j] + h.sib - h.f], T_HID + 8 + j)
    z_gather.step(2)

    def project_rows(i, _):
        at = pl.ds(pl.multiple_of(i * 256, 256), 256)
        rows = hid_all[pl.ds(2 * i, 2)].reshape(256, 1024).astype(F32)
        xhat, _ = norm_parts(rows)
        low = (xhat * params[0:1, :] + params[3:4, :]).astype(BF16)
        first[at, :] = low
        for j, out in enumerate((q_ref, k_ref, v_ref)):
            out[at, :] = dot(low, column_weight(w_a, j), (1, 0)).astype(BF16)
        return 0

    lax.fori_loop(0, 2, project_rows, 0)
    z_gather.step(3)
    gathers[2].begin()
    z_gather.relay(2)
    b_gather.middle()
    lax.fori_loop(2, 4, project_rows, 0)
    v_t[...] = v_ref[...].T
    z_gather.step(4)
    for d in (1, 3):
        gathers[d].begin()
        z_gather.relay(d)

    def att_slot(f):
        return att.at[lax.div(f, 4), :, my_columns(f)]

    att_sends = []

    def attend_and_send(i):
        attend_rows(i, length, bias, q_ref, k_ref, v_t, heads, lse, out_t)
        for f in (2 * i, 2 * i + 1):
            block = heads.at[pl.ds(128 * f, 128), :]
            away = h.f != f
            copy = w.copy(block, att_slot(h.f), T_ATT + h.f, h.c, f)
            stay = pltpu.make_async_copy(block, att_slot(h.f), local.at[9])
            pl.when(away)(copy.start)
            pl.when(jnp.logical_not(away))(stay.start)
            att_sends.append((away, copy, stay))

    def square_steps(d):
        f = h.zstep(d)
        if d > 0:
            gathers[d].middle()
        gathers[d].near()
        for i, c in enumerate((h.cx, h.cy)):
            w.send(sq.at[c, f], sq.at[c, f], T_SIB + 3 * d + i, h.c, h.sib)

    def square_last(d):
        f = h.zstep(d)
        gathers[d].end()
        w.send(sq.at[h.cd, f], sq.at[h.cd, f], T_SIB + 3 * d + 2, h.c, h.sib)

    attend_and_send(3)
    def text_slot(f):
        return tkv.at[:, :, :, my_columns(f)]

    b_gather.near()
    b_gather.end()
    own[5].wait()
    for clip in range(2):
        for j in range(2):
            own_tkv[clip, j] = dot(own_text[clip], column_weight(w_b, j), (1, 0)).astype(BF16)
    w.send(own_tkv, text_slot(h.f), T_TKV, h.c, h.partner)
    w.send(own_tkv, text_slot(h.f), T_TKV + 1, h.c, h.sib)
    text_copy = pltpu.make_async_copy(own_tkv, text_slot(h.f), local.at[10])
    text_copy.start()
    square_steps(0)
    square_last(0)
    attend_and_send(2)
    square_steps(2)
    w.arrived(text_slot(h.partner), T_TKV)
    w.send(text_slot(h.partner), text_slot(h.partner), T_TKV + 2, h.c, h.sib)
    attend_and_send(1)
    square_last(2)
    square_steps(1)
    attend_and_send(0)
    own[4].wait()
    for i, (c, f) in enumerate(clip_others(h)):
        w.arrived(fin_in.at[c], T_FIN + i)
    win_gather = ZGather(w, lambda f: win.at[:, f], T_WIN, fin_in)
    win_copy = pltpu.make_async_copy(fin_in, win.at[:, h.f], local.at[11])
    win_copy.start()
    win_gather.step(1)
    win_gather.relay(0)
    square_steps(3)
    square_last(1)
    square_last(3)
    own[7].wait()
    grad_gather = ClipGather(w, lambda c, half: grad_all.at[c, pl.ds(128 * half, 128), :], T_GRAD)
    grad_gather.begin()
    for src, dst in (
        (hid_all, o_hid), (first, o_first), (q_ref, o_q), (k_ref, o_k), (v_ref, o_v), (heads, o_heads), (lse, o_lse),
        (w_a, o_w_a), (w_b, o_w_b), (params, o_params),
    ):
        save(src, dst)
    z_gather.end()
    for d in range(4):
        f = h.zstep(d) + h.sib - h.f
        for i, c in enumerate((h.cx, h.cy, h.cd)):
            w.arrived(sq.at[c, f], T_SIB + 3 * d + i)
    for d in range(1, 8):
        f = lax.rem(h.f + 8 - d, 8)
        w.arrived(att_slot(f), T_ATT + f)
    for away, _, stay in att_sends:
        pl.when(jnp.logical_not(away))(stay.wait)
    win_gather.step(2)

    own[6].wait()
    value = own_hid[...].reshape(256, 1024).astype(F32) + dot(
        att[...].reshape(256, 1024), square_of(sq, 0), (1, 0)
    )
    after_self[...] = value
    xhat, _ = norm_parts(value)
    second[...] = (xhat * params[1:2, :] + params[4:5, :]).astype(BF16)
    query_ref[...] = dot(second[...], square_of(sq, 1), (1, 0)).astype(BF16)
    win_gather.step(3)
    grad_gather.middle()
    w.arrived(text_slot(h.sib), T_TKV + 1)
    w.arrived(text_slot(h.partner + h.sib - h.f), T_TKV + 2)
    text_copy.wait()
    lane_head = lax.broadcasted_iota(jnp.int32, (128, 256), 1) // HD
    for clip in range(2):
        for group in range(4):
            rows, columns = pl.ds(128 * clip, 128), pl.ds(256 * group, 256)
            query = query_ref[rows, columns] * jnp.asarray(HD**-0.5, BF16)
            probs, _ = text_probs(query, tkv[clip, 0, :, columns], text_bias[clip : clip + 1, :], lane_head)
            part = dot(probs.astype(BF16), tkv[clip, 1, :, columns], (1, 0))
            crossed[rows, columns] = pick_heads(part, lane_head).astype(BF16)
        if clip == 0:
            win_gather.step(4)
            for d in range(1, 4):
                win_gather.relay(d)
    own[8].wait()
    out_gather = ZGather(w, lambda f: wout.at[f], T_WOUT)
    out_gather.step(1)
    out_gather.relay(0)
    value = after_self[...] + dot(crossed[...], square_of(sq, 2), (1, 0))
    after_cross[...] = value
    xhat, _ = norm_parts(value)
    tokens[h.c] = (xhat * params[2:3, :] + params[5:6, :]).astype(BF16)

    token_gather = ClipGather(w, lambda c, half: tokens.at[c, pl.ds(128 * half, 128), :], T_TOK)
    token_gather.begin()
    for src, dst in (
        (att, o_att), (tkv, o_tkv), (second, o_second), (query_ref, o_query), (crossed, o_crossed),
        (after_self, o_self), (after_cross, o_cross),
    ):
        save(src, dst)
    for which in range(3):
        save(sq.at[:, :, pl.ds(32 * which, 32), :], o_square.at[which])
    win_copy.wait()
    win_gather.end()

    def hidden(c):
        for part in range(2):
            rows = pl.ds(128 * part, 128)
            pre = dot(tokens[c, rows, :], win[...].reshape(1024, 1024), (1, 0))
            cdf = 0.5 * (1.0 + lax.erf(pre * (0.5**0.5)))
            inner[c, rows, :] = (pre * cdf).astype(BF16)
            slope[c, rows, :] = cdf + pre * jnp.exp(-0.5 * pre * pre) * 0.3989422804014327

    def hidden_back(c):
        g_inner = dot(grad_all[c], wout[...].reshape(1024, 1024), (1, 1))
        g_pre[c] = (g_inner * slope[c]).astype(BF16)
        terms[c] = dot(g_pre[c], win[...].reshape(1024, 1024), (1, 1)).astype(BF16)

    def out_terms(c):
        out_ref[c] = dot(inner[c], wout[...].reshape(1024, 1024), (1, 0)).astype(BF16)

    sibling = SiblingSum(w, lambda f: out_w.at[f], lambda z: inbox.at[z], lambda z: sums.at[z], T_OSIB)
    z_scatter = ZScatter(w, sums, near, far, T_OZ)
    tall = (1024, 1024)

    def out_weight(i, _):
        columns = pl.ds(pl.multiple_of(i * 256, 256), 256)
        out = dot(inner[:, :, columns].reshape(1024, 256), grad_all[...].reshape(tall), (0, 0))
        out_w[pl.ds(2 * i, 2)] = out.astype(BF16).reshape(2, 128, 1024)
        return 0

    def in_weight(i, _):
        columns = pl.ds(pl.multiple_of(i * 256, 256), 256)
        out = dot(tokens[:, :, columns].reshape(1024, 256), g_pre[...].reshape(tall), (0, 0))
        in_ref[:, pl.ds(pl.multiple_of(32 * i, 32), 32), :] = out.astype(BF16).reshape(8, 32, 1024)
        return 0

    hidden(h.c)
    out_gather.step(2)
    grad_gather.near()
    grad_gather.end()
    token_gather.middle()
    token_gather.near()
    out_gather.step(3)
    hidden(h.cx)
    hidden(h.cy)
    out_gather.step(4)
    for d in range(1, 4):
        out_gather.relay(d)
    token_gather.end()
    hidden(h.cd)
    out_gather.end()
    scatter = ClipScatter(
        w, lambda c, half: terms.at[c, pl.ds(128 * half, 128), :], [slots.at[i] for i in range(6)], T_TERM
    )
    hidden_back(h.cd)
    scatter.begin(0)
    hidden_back(h.cx)
    hidden_back(h.cy)
    scatter.begin(1)
    lax.fori_loop(0, 4, out_weight, 0)
    sibling.begin()
    scatter.middle()
    hidden_back(h.c)
    sibling.end()
    z_scatter.begin()
    lax.fori_loop(0, 2, in_weight, 0)
    z_scatter.step(1)
    lax.fori_loop(2, 4, in_weight, 0)
    save(in_ref, o_in)
    out_terms(0)
    z_scatter.step(2)
    z_scatter.step(3)
    out_terms(1)
    out_terms(2)
    out_terms(3)
    save(out_ref, o_out)
    scatter.end()
    for half in range(2):
        o_third[128 * half : 128 * half + 128, :] = scatter.total(half)
    z_scatter.total(o_sum)
    w.drain()
    for copy in forwards:
        pl.when(h.is_gate)(copy.wait_send)
    for away, copy, _ in att_sends:
        pl.when(away)(copy.wait_send)
    for one in (z_gather, win_gather, out_gather, z_scatter):
        one.drain()
    for copy in saves:
        copy.wait()


def forward(*args):
    column, rows, full, quarter = (1024, 256), (256, 1024), (4, 256, 1024), (4, 128, 1024)
    kept = [
        shape((8, 128, 1024)),
        shape((1024, 1024)),
        shape(column),
        shape(column),
        shape(column),
        shape(column),
        shape((8, 1024), F32),
        shape((4, 8, 112, 256)),
        shape((4, 8, 64, 256)),
        shape((8, 1024), F32),
        shape((2, 128, 1024)),
        shape((2, 2, 128, 1024)),
        shape((4, 8, 96, 1024)),
        shape(rows),
        shape(rows),
        shape(rows),
        shape(rows, F32),
        shape(rows, F32),
        shape(full),
        shape((8, 128, 1024)),
    ]
    scratch = [pltpu.VMEM(one.shape, one.dtype) for one in kept]
    kept[12] = shape((3, 4, 8, 32, 1024))
    return comm_call(
        forward_body,
        tuple(kept) + (shape(rows, F32), shape((128, 1024), F32)),
        [SMEM, VMEM, VMEM] + [HBM] * 8,
        (HBM,) * len(kept) + (VMEM,) * 2,
        scratch
        + [
            pltpu.VMEM((256, ROWS), F32),
            pltpu.VMEM((256, 1024), BF16),
            pltpu.VMEM((2, 2, 128, 256), BF16),
            pltpu.VMEM((2, 128, 1024), BF16),
            pltpu.VMEM((2, 128, 1024), BF16),
            pltpu.VMEM((4, 32, 1024), BF16),
            pltpu.VMEM(full, BF16),
            pltpu.VMEM((4, 8, 32, 1024), BF16),
            pltpu.VMEM((8, 128, 1024), BF16),
            pltpu.VMEM(full, BF16),
            pltpu.VMEM(full, BF16),
            pltpu.VMEM(full, F32),
            pltpu.VMEM(full, BF16),
            pltpu.VMEM(full, BF16),
            pltpu.VMEM((6, 128, 1024), BF16),
            pltpu.VMEM((8, 128, 1024), BF16),
            pltpu.VMEM(quarter, BF16),
            pltpu.VMEM(quarter, BF16),
            pltpu.VMEM((3, 128, 1024), BF16),
            pltpu.VMEM((2, 128, 1024), BF16),
            pltpu.SemaphoreType.DMA((12,)),
            pltpu.SemaphoreType.DMA((24,)),
        ],
        192,
        144,
        1,
    )(*args)


def attend_back_rows(i, length, bias, q_ref, k_ref, v_ref, o_ref, lse_ref, g_ref, dq_ref, dq_t, k_t, dk, dv):
    lane_head = lax.broadcasted_iota(jnp.int32, (ROWS, 256), 1) // HD
    first, n = i * ROWS, (i + 1) * ROWS
    q = q_ref[first:n, :] * jnp.asarray(HD**-0.5, BF16)
    live = first + lax.broadcasted_iota(jnp.int32, (ROWS, 256), 0) < length[0]
    g = jnp.where(live, g_ref[first:n, :], 0)
    both = (g.astype(F32) * o_ref[first:n, :].astype(F32)).T
    row_dots = jnp.concatenate(
        [jnp.sum(both[HD * j : HD * j + HD], axis=0, keepdims=True) for j in range(4)], axis=0
    )
    lse = lse_ref[0:4, first:n]

    def pick(rows, j):
        at = lax.broadcasted_iota(jnp.int32, rows.shape, 0) == j
        return jnp.sum(jnp.where(at, rows, 0), axis=0, keepdims=True)

    def head(j, _):
        q_head = jnp.where(lane_head == j, q, 0)
        g_head = jnp.where(lane_head == j, g, 0)
        scores = mask_scores(dot(k_ref[0:n, :], q_head, (1, 1)), bias, first, ROWS)
        probs = jnp.exp(scores - pick(lse, j))
        grads = dot(v_ref[0:n, :], g_head, (1, 1))
        dlogits = (probs * (grads - pick(row_dots, j))).astype(BF16)
        dv[0:n, :] += dot(probs.astype(BF16), g_head, (1, 0))
        dk[0:n, :] += dot(dlogits, q_head, (1, 0))
        at = pl.ds(pl.multiple_of(j * HD, HD), HD)
        dq_t[at, :] = dot(k_t[at, 0:n], dlogits, (1, 0))
        return 0

    lax.fori_loop(0, 4, head, 0)
    dq_ref[first:n, :] = (dq_t[...].T * (HD**-0.5)).astype(BF16)


def norm_back(xhat, scale, grad, gain):
    h = grad * gain
    return scale * (
        h
        - jnp.mean(h, axis=-1, keepdims=True)
        - xhat * jnp.mean(h * xhat, axis=-1, keepdims=True)
    )


def backward_body(
    length, bias, text_bias, norms_in,
    h_third, h_out, h_cross, h_self, h_second, h_query, h_crossed, h_att, h_square, h_tkv, h_out_terms, h_in_terms,
    h_q, h_k, h_v, h_o, h_lse, h_hid, h_first, h_wa, h_wb, h_text, h_own,
    o_output, o_in, o_hidden, o_square, o_qkv, o_ckv, o_norm, o_text,
    v_third, v_out, after_cross, query_ref, crossed, att, mats, tkv, out_terms,
    q_ref, k_ref, v_ref, o_ref, lse, w_a, w_b, text_in,
    g_crossed, g_att, g_after, slots, t_inbox, t_near, t_far, t_total,
    i_inbox, i_near, i_far, i_out, i_in,
    g_square, s_inbox, s_slots, s_part, y_part, z_near, z_far, y_near, y_far,
    g_heads, dq_t, k_t, dk, dv, d_cols, f_inbox, f_in,
    a_terms, a_slots, a_sum, a_in, b_terms, b_slots, b_sum, b_in,
    t_terms, tt_in, n_row, n_terms, n_slots, n_sum, n_in,
    loaded, local, send_sem, recv_sem,
):
    h = Here()
    w = Wire(h, send_sem, recv_sem)
    tag = [0]

    def tags(n):
        tag[0] += n
        return tag[0] - n

    loads = []

    def load(src, dst):
        copy = pltpu.make_async_copy(src, dst, loaded.at[len(loads)])
        copy.start()
        loads.append(copy)
        return copy

    l_terms = load(h_out_terms, out_terms)
    own_terms = [mats.at[0, z, pl.ds(0, 4)] for z in range(4)]
    l_own = [load(h_in_terms.at[2 * z + h.core], own_terms[z]) for z in range(4)]
    l_third, l_cross = load(h_third, v_third), load(h_cross, after_cross)
    l_out, l_m2 = load(h_out, v_out), load(h_square.at[2], mats.at[2])
    l_middle = [load(*pair) for pair in ((h_crossed, crossed), (h_query, query_ref), (h_tkv, tkv))]
    l_m1 = load(h_square.at[1], mats.at[1])
    l_att = load(h_att, att)
    l_heads = [
        load(*pair)
        for pair in (
            (h_q, q_ref), (h_k, k_ref), (h_v, v_ref), (h_o, o_ref), (h_lse, lse), (h_wb, w_b), (h_text, text_in),
            (h_wa, w_a),
        )
    ]
    greet(frame_others(h) + clip_others(h))

    def matrix(which):
        return mats[which].reshape(1024, 1024)

    out_scatter = ClipScatter(
        w,
        lambda c, half: out_terms.at[c, pl.ds(128 * half, 128), :],
        [slots.at[i] for i in range(6)],
        tags(6),
    )
    in_tag = tags(4)
    for z in range(4):
        w.send(h_in_terms.at[2 * z + 1 - h.core], i_inbox.at[z], in_tag + z, h.c, h.sib)
    in_scatter = ZScatter(w, i_inbox, i_near, i_far, tags(5))
    l_terms.wait()
    out_scatter.begin()

    def square_sums(which):
        sibling = SiblingSum(
            w,
            lambda f: g_square.at[which, :, f],
            lambda z: s_inbox.at[which, z],
            lambda z: s_inbox.at[which, z],
            tags(4),
        )
        clip = ClipScatter(
            w,
            lambda c, half: s_inbox.at[which, :, c, pl.ds(16 * half, 16), :],
            [s_slots.at[which, i] for i in range(6)],
            tags(6),
        )
        return sibling, clip

    squares = [square_sums(which) for which in range(3)]

    def put(which, value):
        g_square[which] = value.astype(BF16).reshape(4, 8, 32, 1024)

    def columns_of(f):
        return pl.ds(pl.multiple_of(lax.rem(f, 4) * 256, 256), 256)

    def part_of(f):
        return g_att.at[lax.div(f, 4), :, columns_of(f)]

    def text_part(f):
        return g_text.at[lax.div(f, 4), :, :, columns_of(f)]

    for copy in (l_third, l_cross, l_out):
        copy.wait()
    xhat, scale = norm_parts(after_cross[...])
    grad = v_third[...]
    gain_third = jnp.sum(grad * xhat, axis=0, keepdims=True)
    shift_third = jnp.sum(grad, axis=0, keepdims=True)
    n_row[...] = jnp.zeros_like(n_row)
    n_row[2:3, :] = gain_third
    n_row[5:6, :] = shift_third
    g_after_cross = v_out[...].reshape(256, 1024).astype(F32) + norm_back(xhat, scale, grad, norms_in[2:3, :])
    g_after[...] = g_after_cross
    after_self, own_hid = v_third, v_out
    l_self, l_own_hid = load(h_self, after_self), load(h_own, own_hid)
    branch = g_after_cross.astype(BF16)
    l_m2.wait()
    g_crossed[...] = dot(branch, matrix(2), (1, 1)).astype(BF16)
    l_first = load(h_first, mats.at[2])
    for copy in l_middle + l_own:
        copy.wait()
    put(2, dot(crossed[...], branch, (0, 0)))
    squares[2][0].begin()
    second = crossed
    l_second = load(h_second, second)
    for z in range(4):
        w.arrived(i_inbox.at[z], in_tag + z)
        add_into(i_inbox.at[z], own_terms[z])
    in_scatter.begin()
    l_m0 = load(h_square.at[0], mats.at[0])
    g_query, g_text = query_ref, tkv
    lane_head = lax.broadcasted_iota(jnp.int32, (128, 256), 1) // HD
    for clip in range(2):
        for group in range(4):
            rows, columns = pl.ds(128 * clip, 128), pl.ds(256 * group, 256)
            keys, values = tkv[clip, 0, :, columns], tkv[clip, 1, :, columns]
            query = query_ref[rows, columns] * jnp.asarray(HD**-0.5, BF16)
            probs, stacked = text_probs(query, keys, text_bias[clip : clip + 1, :], lane_head)
            grads = g_crossed[rows, columns]
            g_stacked = jnp.concatenate([jnp.where(lane_head == j, grads, 0) for j in range(4)], axis=0)
            g_probs = dot(g_stacked, values, (1, 1))
            row_dot = jnp.sum(probs * g_probs, axis=1, keepdims=True)
            g_logits = (probs * (g_probs - row_dot)).astype(BF16)
            part = dot(g_logits, keys, (1, 0))
            g_query[rows, columns] = (pick_heads(part, lane_head) * (HD**-0.5)).astype(BF16)
            g_text[clip, 0, :, columns] = dot(g_logits, stacked, (0, 0)).astype(BF16)
            g_text[clip, 1, :, columns] = dot(probs.astype(BF16), g_stacked, (0, 0)).astype(BF16)
        if clip == 0:
            out_scatter.middle()
            in_scatter.step(1)
            squares[2][0].end()
            squares[2][1].begin()
    text_sibling = SiblingSum(w, text_part, lambda z: t_inbox.at[z], lambda z: t_inbox.at[z], tags(4))
    text_sibling.begin()
    l_m1.wait()
    grad = dot(g_query[...], matrix(1), (1, 1))
    l_hid = load(h_hid, mats.at[1])
    l_self.wait()
    xhat, scale = norm_parts(after_self[...])
    n_row[1:2, :] = jnp.sum(grad * xhat, axis=0, keepdims=True)
    n_row[4:5, :] = jnp.sum(grad, axis=0, keepdims=True)
    g_after_self = g_after[...] + norm_back(xhat, scale, grad, norms_in[1:2, :])
    g_after[...] = g_after_self
    branch = g_after_self.astype(BF16)
    l_m0.wait()
    g_att[...] = dot(branch, matrix(0), (1, 1)).astype(BF16).reshape(2, 128, 1024)
    heads_tag = tags(7)
    for d in (4, 2, 6, 3, 5, 1, 7):
        f = h.step(d)
        w.send(part_of(f), g_heads.at[h.f], heads_tag + d - 1, h.c, f)
    own_part = pltpu.make_async_copy(part_of(h.f), g_heads.at[h.f], local.at[0])
    own_part.start()
    in_scatter.step(2)
    in_scatter.step(3)
    l_second.wait()
    l_att.wait()
    put(1, dot(second[...], g_query[...], (0, 0)))
    squares[1][0].begin()
    put(0, dot(att[...].reshape(256, 1024), branch, (0, 0)))
    squares[0][0].begin()
    text_sibling.end()
    text_scatter = ZScatter(w, t_inbox, t_near, t_far, tags(5))
    text_scatter.begin()
    squares[2][1].middle()
    squares[1][0].end()
    squares[1][1].begin()
    out_scatter.end()
    for half in range(2):
        rows = pl.ds(128 * half, 128)
        o_output[rows, :] = (after_cross[rows, :] + out_scatter.total(half)).astype(BF16)
    squares[0][0].end()
    squares[0][1].begin()
    in_scatter.total(i_out)
    i_tag = tags(3)
    for i, (c, f) in enumerate(clip_others(h)):
        w.send(i_out.at[c], i_in.at[h.c], i_tag + i, c, f)
    i_in[h.c] = i_out[h.c]
    squares[1][1].middle()

    def square_part(which, out, row):
        squares[which][1].end()
        for half in range(2):
            total = squares[which][1].total(half)
            out[:, row + 16 * half : row + 16 * half + 16, :] = total.astype(BF16)

    text_scatter.step(1)
    for copy in l_heads:
        copy.wait()
    k_t[...] = k_ref[...].T
    dk[...] = jnp.zeros_like(dk)
    dv[...] = jnp.zeros_like(dv)
    for d in range(1, 8):
        w.arrived(g_heads.at[lax.rem(h.f + 8 - d, 8)], heads_tag + d - 1)
    own_part.wait()
    g_rows = g_heads[...].reshape(1024, 256)

    def rows_back(i):
        attend_back_rows(
            i, length, bias, q_ref, k_ref, v_ref, o_ref, lse, g_rows, d_cols.at[0], dq_t, k_t, dk, dv
        )

    text_scatter.step(2)
    text_scatter.step(3)
    squares[0][1].middle()
    rows_back(0)
    square_part(2, s_part, 32)
    square_part(1, s_part, 0)
    z_scatter = ZScatter(w, s_part, z_near, z_far, tags(5))
    z_scatter.begin()
    rows_back(1)

    class Columns:
        def __init__(self, terms, slots, sums, inbox):
            self.sums, self.inbox, self.tag = sums, inbox, tags(13)
            self.clip = ClipScatter(
                w,
                lambda c, half: terms.at[c, pl.ds(4 * half, 4)],
                [slots.at[i] for i in range(6)],
                self.tag,
            )

        def spread(self):
            self.clip.end()
            for half in range(2):
                self.sums[4 * half : 4 * half + 4] = self.clip.total(half).astype(BF16)
            for d in (4, 2, 6, 3, 5, 1, 7):
                f = h.step(d)
                w.send(self.sums.at[f], self.inbox.at[h.f], self.tag + 5 + d, h.c, f)
            self.inbox[h.f] = self.sums[h.f]

        def wait(self):
            for d in range(1, 8):
                w.arrived(self.inbox.at[lax.rem(h.f + 8 - d, 8)], self.tag + 5 + d)

    text_scatter.total(t_total)
    g_tkv = [t_total[j].astype(BF16) for j in range(2)]
    text = text_in[h.pair]
    for j in range(2):
        b_terms[:, :, 32 * j : 32 * j + 32, :] = (
            dot(text, g_tkv[j], (0, 0)).astype(BF16).reshape(4, 8, 32, 256)
        )
    b_columns = Columns(b_terms, b_slots, b_sum, b_in)
    b_columns.clip.begin()
    t_terms[...] = (
        dot(g_tkv[0], column_weight(w_b, 0), (1, 1)) + dot(g_tkv[1], column_weight(w_b, 1), (1, 1))
    ).astype(BF16)
    tt_tag = tags(7)
    for d in range(1, 8):
        f = h.step(d)
        w.send(
            t_terms.at[pl.ds(pl.multiple_of(f * 16, 16), 16), :], tt_in.at[h.f], tt_tag + d - 1, h.c, f
        )
    tt_in[h.f] = t_terms[pl.ds(pl.multiple_of(h.f * 16, 16), 16), :]
    z_scatter.step(1)
    rows_back(2)
    square_part(0, y_part, 0)
    y_scatter = ZScatter(w, y_part, y_near, y_far, tags(5))
    y_scatter.begin()
    z_scatter.step(2)
    z_scatter.step(3)
    b_columns.clip.middle()
    rows_back(3)
    d_cols[1] = dk[...].astype(BF16)
    d_cols[2] = dv[...].astype(BF16)
    l_first.wait()
    a_columns = [Columns(a_terms.at[j], a_slots.at[j], a_sum.at[j], a_in.at[j]) for j in range(3)]
    for j in range(3):
        a_terms[j] = dot(mats[2].reshape(1024, 1024), d_cols[j], (0, 0)).astype(BF16).reshape(4, 8, 32, 256)
        a_columns[j].clip.begin()
    y_scatter.step(1)

    f_terms = mats.at[0]
    f_sibling = SiblingSum(
        w,
        lambda f: f_terms.at[lax.div(f, 2), pl.ds(pl.multiple_of(lax.rem(f, 2) * 4, 4), 4)],
        lambda z: f_inbox.at[z],
        lambda z: f_inbox.at[z],
        tags(4),
    )
    l_hid.wait()

    def frame_terms(i, _):
        rows = pl.ds(pl.multiple_of(i * 256, 256), 256)
        grad = sum(dot(d_cols[j, rows, :], column_weight(w_a, j), (1, 1)) for j in range(3))
        f_terms[i] = grad.astype(BF16).reshape(8, 32, 1024)
        xhat, _ = norm_parts(mats[1, i].reshape(256, 1024).astype(F32))
        n_row[0:1, :] += jnp.sum(grad * xhat, axis=0, keepdims=True)
        n_row[3:4, :] += jnp.sum(grad, axis=0, keepdims=True)
        return 0

    lax.fori_loop(0, 4, frame_terms, 0)
    f_sibling.begin()
    y_scatter.step(2)
    a_columns[0].clip.middle()
    f_sibling.end()
    f_tag = tags(4)
    other = 2 * (1 - h.pair)
    is_end = jnp.logical_not(h.is_gate)
    to_gate, to_far = [], []
    for j in range(2):
        to_gate.append(w.copy(f_inbox.at[other + j], f_in.at[1 + j], f_tag + 1 + j, h.c, h.partner))
        pl.when(is_end)(to_gate[j].start)
    w.send(f_inbox.at[lax.div(h.partner, 2)], f_in.at[0], f_tag, h.c, h.partner)
    for c in range(4):
        for f in range(8):
            group = 2 * c + f // 4
            n_terms[c, f] = n_row[:, 128 * group : 128 * group + 128].astype(BF16)
    n_columns = Columns(n_terms, n_slots, n_sum, n_in)
    n_columns.clip.begin()
    a_columns[1].clip.middle()
    a_columns[0].spread()
    for j in range(2):

        @pl.when(h.is_gate)
        def _():
            w.arrived(f_in.at[1 + j], f_tag + 1 + j)
            add_into(f_inbox.at[other + j], f_in.at[1 + j])

        to_far.append(w.copy(f_inbox.at[other + j], f_in.at[3], f_tag + 3, h.c, h.far[j]))
        pl.when(h.is_gate)(to_far[j].start)
    a_columns[2].clip.middle()
    a_columns[1].spread()
    n_columns.clip.middle()
    y_scatter.step(3)
    a_columns[2].spread()
    n_columns.spread()
    b_columns.spread()
    z_scatter.total(o_square.at[pl.ds(32, 64), :])
    for i, (c, f) in enumerate(clip_others(h)):
        w.arrived(i_in.at[c], i_tag + i)
    for c in range(4):
        o_in[:, 1024 * c : 1024 * c + 1024] = i_in[c].astype(F32)
    for d in range(1, 8):
        w.arrived(tt_in.at[lax.rem(h.f + 8 - d, 8)], tt_tag + d - 1)
    for p in range(2):
        o_text[p] = sum(tt_in[4 * p + q].astype(F32) for q in range(4)).astype(BF16)
    y_scatter.total(o_square.at[pl.ds(0, 32), :])
    w.arrived(f_in.at[0], f_tag)
    w.arrived(f_in.at[3], f_tag + 3)

    def hidden_out(clip, total):
        xhat, scale = norm_parts(own_hid[clip].astype(F32))
        rows = pl.ds(pl.multiple_of(clip * 128, 128), 128)
        o_hidden[clip] = (g_after[rows, :] + norm_back(xhat, scale, total, norms_in[0:1, :])).astype(BF16)

    l_own_hid.wait()
    hidden_out(h.pair, (f_inbox[h.z].astype(F32) + f_in[0].astype(F32)).reshape(128, 1024))
    hidden_out(1 - h.pair, f_in[3].astype(F32).reshape(128, 1024))
    for j in range(3):
        a_columns[j].wait()
        for q in range(4):
            o_qkv[j, :, 256 * q : 256 * q + 256] = a_in[j, q].astype(F32) + a_in[j, 4 + q].astype(F32)
    b_columns.wait()
    for j in range(2):
        for q in range(4):
            at = pl.ds(32 * j, 32)
            o_ckv[j, :, 256 * q : 256 * q + 256] = b_in[q, at, :].astype(F32) + b_in[4 + q, at, :].astype(F32)
    n_columns.wait()
    o_norm[...] = sum(n_in[f].astype(F32) for f in range(8))
    w.drain()
    for one in (in_scatter, text_scatter, z_scatter, y_scatter):
        one.drain()
    for j in range(2):
        pl.when(is_end)(to_gate[j].wait_send)
        pl.when(h.is_gate)(to_far[j].wait_send)


def backward(*args):
    def buffer(*dims):
        return pltpu.VMEM(dims, BF16)

    def full(*dims):
        return pltpu.VMEM(dims, F32)

    return comm_call(
        backward_body,
        (
            shape((256, 1024)),
            shape((32, 4096), F32),
            shape((2, 128, 1024)),
            shape((96, 1024), F32),
            shape((3, 32, 1024), F32),
            shape((2, 32, 1024), F32),
            shape((16, 128), F32),
            shape((2, 16, 1024)),
        ),
        [SMEM] + [VMEM] * 3 + [HBM] * 23,
        (VMEM,) * 8,
        [
            full(256, 1024), buffer(2, 128, 1024), full(256, 1024), buffer(256, 1024), buffer(256, 1024),
            buffer(2, 128, 1024), buffer(3, 4, 8, 32, 1024), buffer(2, 2, 128, 1024), buffer(4, 256, 1024),
            buffer(1024, 256), buffer(1024, 256), buffer(1024, 256), buffer(1024, 256), full(8, 1024),
            buffer(4, 8, 112, 256), buffer(4, 8, 64, 256), buffer(2, 128, 1024),
            buffer(256, 1024), buffer(2, 128, 1024), full(256, 1024),
            buffer(6, 128, 1024), buffer(4, 2, 128, 256), buffer(3, 2, 128, 256), buffer(2, 2, 128, 256),
            full(2, 128, 256),
            buffer(4, 4, 32, 1024), buffer(3, 4, 32, 1024), buffer(2, 4, 32, 1024),
            buffer(4, 32, 1024), buffer(4, 32, 1024),
            buffer(3, 4, 8, 32, 1024), buffer(3, 4, 4, 32, 1024), buffer(3, 6, 4, 16, 1024),
            buffer(4, 64, 1024), buffer(4, 32, 1024), buffer(3, 64, 1024), buffer(2, 64, 1024),
            buffer(3, 32, 1024), buffer(2, 32, 1024),
            buffer(8, 128, 256), full(256, ROWS), buffer(256, 1024), full(1024, 256), full(1024, 256),
            buffer(3, 1024, 256), buffer(4, 4, 32, 1024), buffer(4, 4, 32, 1024),
            buffer(3, 4, 8, 32, 256), buffer(3, 6, 4, 32, 256), buffer(3, 8, 32, 256), buffer(3, 8, 32, 256),
            buffer(4, 8, 64, 256), buffer(6, 4, 64, 256), buffer(8, 64, 256), buffer(8, 64, 256),
            buffer(128, 1024), buffer(8, 16, 1024), full(16, 1024), buffer(4, 8, 16, 128), buffer(6, 4, 16, 128),
            buffer(8, 16, 128), buffer(8, 16, 128),
            pltpu.SemaphoreType.DMA((32,)),
            pltpu.SemaphoreType.DMA((1,)),
        ],
        208,
        160,
        2,
    )(*args)


def on_device_fast(
    hidden_in,
    text_states,
    out_grad,
    self_qkv,
    self_out,
    cross_qkv,
    cross_out,
    ffn_in,
    ffn_out,
    ln_gain,
    ln_bias,
    clip_len,
    frame_mask,
    text_len,
    text_mask,
):
    frame = lax.axis_index("frame")
    pair = frame // 4
    norms = jnp.concatenate([ln_gain, ln_bias], axis=0)
    placed = lax.dynamic_update_slice(jnp.zeros((16, 256), BF16), norms, (0, 32 * (frame % 4)))
    cols_a = jnp.concatenate(
        [jnp.moveaxis(self_qkv, 1, 0).reshape(96, 1024), jnp.tile(placed, (1, 4))], axis=0
    )
    cols_b = jnp.moveaxis(cross_qkv, 1, 0)[1:].reshape(64, 1024)
    square_here = jnp.concatenate([self_out, cross_qkv[:, 0], cross_out], axis=0)
    columns = jnp.arange(1024, dtype=jnp.int32)
    my_len = lax.dynamic_slice_in_dim(clip_len, pair, 1, 0)
    my_mask = lax.dynamic_slice_in_dim(frame_mask, pair, 1, 0)[0]
    bias = jnp.where((columns < my_len) & (my_mask > 0), 0.0, NEG).astype(F32)
    bias = jnp.broadcast_to(bias[:, None], (1024, 128))
    slots = jnp.arange(128, dtype=jnp.int32)
    text_ok = (slots[None] < text_len[:, None]) & ((text_mask > 0) | (slots[None] == 0))
    text_bias = jnp.where(text_ok, 0.0, NEG).astype(F32)
    (
        hid_all, first_low, query, key, value, att_heads, lse, w_a, w_b, params, att, tkv, square,
        second, cross_query, crossed, after_self, after_cross, out_terms, in_terms, third_sum, grad_ffn_out,
    ) = forward(
        my_len, bias, text_bias, text_states, hidden_in, cols_a, cols_b, square_here, ffn_in, ffn_out,
        out_grad.reshape(256, 1024),
    )
    output, grad_ffn_in, grad_hidden, square_sum, qkv_sum, ckv_sum, norm_sum, grad_text = backward(
        my_len, bias, text_bias, params,
        third_sum, out_grad, after_cross, after_self, second, cross_query, crossed, att, square, tkv,
        out_terms, in_terms.reshape(8, 4, 32, 1024), query, key, value, att_heads, lse, hid_all.reshape(4, 8, 32, 1024),
        first_low.reshape(4, 8, 32, 1024), w_a, w_b, text_states, hidden_in,
    )
    norm_sum = lax.dynamic_slice(norm_sum, (0, 32 * (frame % 4)), (6, 32))
    return (
        output.reshape(2, 128, 1024),
        grad_hidden,
        grad_text,
        jnp.moveaxis(qkv_sum, 0, 1),
        square_sum[0:32],
        jnp.stack([square_sum[32:64], ckv_sum[0], ckv_sum[1]], axis=1),
        square_sum[64:96],
        grad_ffn_in,
        grad_ffn_out,
        norm_sum[0:3],
        norm_sum[3:6],
    )


def solution(mesh):
    return jax.shard_map(
        on_device_fast if fits(mesh) else on_device_any,
        mesh=mesh,
        in_specs=(
            P("clip", "frame", None),
            P("clip", None, None),
            P("clip", "frame", None),
            P(("clip", "frame"), None, None),
            P(("clip", "frame"), None),
            P(("clip", "frame"), None, None),
            P(("clip", "frame"), None),
            P(("clip", "frame"), None),
            P(("clip", "frame"), None),
            P(None, ("clip", "frame")),
            P(None, ("clip", "frame")),
            P("clip"),
            P("clip", None),
            P("clip"),
            P("clip", None),
        ),
        out_specs=(
            P("clip", "frame", None),
            P("clip", "frame", None),
            P("clip", "frame", None),
            P(("clip", "frame"), None, None),
            P(("clip", "frame"), None),
            P(("clip", "frame"), None, None),
            P(("clip", "frame"), None),
            P(("clip", "frame"), None),
            P(("clip", "frame"), None),
            P(None, ("clip", "frame")),
            P(None, ("clip", "frame")),
        ),
        check_vma=False,
    )
```

```python
import functools

import jax
import jax.numpy as jnp
from jax import lax
from jax.experimental import pallas as pl
from jax.experimental.pallas import tpu as pltpu
from jax.sharding import PartitionSpec as P

HD = 64


MASKED = -1000000000.0
EPSILON = 1e-05


def layer_norm(value, gain, shift):
    average = jnp.mean(value, axis=-1, keepdims=True)
    centered = value - average
    variance = jnp.mean(centered * centered, axis=-1, keepdims=True)
    return centered * lax.rsqrt(variance + EPSILON) * gain + shift


def activate(value):
    return jax.nn.gelu(value, approximate=False)


def project(left, right):
    return jnp.einsum("cnd,de->cne", left, right, preferred_element_type=jnp.float32)


def project_back(grad_rows, weight):
    return jnp.einsum("cne,de->cnd", grad_rows, weight, preferred_element_type=jnp.float32)


def weight_grad(left, right):
    return jnp.einsum("cnd,cne->de", left, right, preferred_element_type=jnp.float32)


def fetch_attention(self_qkv, self_out, cross_qkv, cross_out, ln_gain, ln_bias):
    return (
        lax.all_gather(self_qkv, ("clip", "frame"), axis=0, tiled=True),
        lax.all_gather(self_out, ("clip", "frame"), axis=0, tiled=True),
        lax.all_gather(cross_qkv, ("clip", "frame"), axis=0, tiled=True),
        lax.all_gather(cross_out, ("clip", "frame"), axis=0, tiled=True),
        lax.all_gather(ln_gain, ("clip", "frame"), axis=1, tiled=True),
        lax.all_gather(ln_bias, ("clip", "frame"), axis=1, tiled=True),
    )


def fetch_ffn(ffn_in, ffn_out):
    return (
        lax.all_gather(ffn_in, ("clip", "frame"), axis=0, tiled=True),
        lax.all_gather(ffn_out, ("clip", "frame"), axis=0, tiled=True),
    )


def self_masks(first_row, block_rows, clip_len, key_valid):
    columns = jnp.arange(key_valid.shape[1], dtype=jnp.int32)
    row_ids = first_row + jnp.arange(block_rows, dtype=jnp.int32)
    diagonal = columns[None, :] == row_ids[:, None]
    allowed = (columns[None, :] <= row_ids[:, None])[None] & (
        key_valid[:, None, :] | diagonal[None]
    )
    live_rows = (row_ids[None, :] < clip_len[:, None]).astype(jnp.float32)
    return (allowed[:, None], live_rows[:, None, :, None])


def self_forward(query_rows, key_rows, value_rows, clip_len, key_valid):
    length = query_rows.shape[1]
    block_rows = min(512, length)
    score_scale = query_rows.shape[3] ** (-0.5)

    def one_block(block_index):
        first_row = block_index * block_rows
        query_block = lax.dynamic_slice_in_dim(query_rows, first_row, block_rows, 1)
        raw_scores = jnp.einsum(
            "cqhd,ckhd->chqk", query_block, key_rows, preferred_element_type=jnp.float32
        )
        allowed, live_rows = self_masks(first_row, block_rows, clip_len, key_valid)
        logits = jnp.where(allowed, raw_scores * score_scale, MASKED)
        row_max = jnp.max(logits, axis=-1, keepdims=True)
        exponent = jnp.exp(logits - row_max)
        row_sum = jnp.sum(exponent, axis=-1, keepdims=True)
        weights = (exponent / row_sum * live_rows).astype(jnp.bfloat16)
        attended = jnp.einsum(
            "chqk,ckhd->cqhd", weights, value_rows, preferred_element_type=jnp.float32
        )
        return (attended.astype(jnp.bfloat16), row_max + jnp.log(row_sum))

    blocks, log_sums = lax.map(one_block, jnp.arange(length // block_rows, dtype=jnp.int32))
    return (jnp.moveaxis(blocks, 0, 1).reshape(query_rows.shape), log_sums)


def self_backward(query_rows, key_rows, value_rows, grad_rows, log_sums, clip_len, key_valid):
    length = query_rows.shape[1]
    block_rows = min(512, length)
    score_scale = query_rows.shape[3] ** (-0.5)

    def one_block(totals, block_index):
        grad_keys, grad_values = totals
        first_row = block_index * block_rows
        query_block = lax.dynamic_slice_in_dim(query_rows, first_row, block_rows, 1)
        grad_block = lax.dynamic_slice_in_dim(grad_rows, first_row, block_rows, 1)
        raw_scores = jnp.einsum(
            "cqhd,ckhd->chqk", query_block, key_rows, preferred_element_type=jnp.float32
        )
        allowed, live_rows = self_masks(first_row, block_rows, clip_len, key_valid)
        logits = jnp.where(allowed, raw_scores * score_scale, MASKED)
        probs = jnp.exp(logits - log_sums[block_index])
        weights = (probs * live_rows).astype(jnp.bfloat16)
        grad_probs = (
            jnp.einsum(
                "cqhd,ckhd->chqk", grad_block, value_rows, preferred_element_type=jnp.float32
            )
            * live_rows
        )
        row_dot = jnp.sum(probs * grad_probs, axis=-1, keepdims=True)
        grad_scores = (probs * (grad_probs - row_dot)).astype(jnp.bfloat16)
        grad_query = (
            jnp.einsum("chqk,ckhd->cqhd", grad_scores, key_rows, preferred_element_type=jnp.float32)
            * score_scale
        )
        grad_keys = (
            grad_keys
            + jnp.einsum(
                "chqk,cqhd->ckhd", grad_scores, query_block, preferred_element_type=jnp.float32
            )
            * score_scale
        )
        grad_values = grad_values + jnp.einsum(
            "chqk,cqhd->ckhd", weights, grad_block, preferred_element_type=jnp.float32
        )
        return ((grad_keys, grad_values), grad_query)

    zeros = jnp.zeros(key_rows.shape, jnp.float32)
    (grad_keys, grad_values), grad_blocks = lax.scan(
        one_block, (zeros, zeros), jnp.arange(length // block_rows, dtype=jnp.int32)
    )
    grad_query = jnp.moveaxis(grad_blocks, 0, 1).reshape(query_rows.shape)
    return (grad_query, grad_keys, grad_values)


def text_allowed(text_len, text_mask):
    slots = jnp.arange(text_mask.shape[1], dtype=jnp.int32)
    allowed = (slots[None, :] < text_len[:, None]) & ((text_mask > 0) | (slots[None, :] == 0))
    return allowed[:, None, None, :]


def cross_forward(query_rows, key_rows, value_rows, allowed):
    score_scale = query_rows.shape[3] ** (-0.5)
    raw_scores = jnp.einsum(
        "cqhd,ckhd->chqk", query_rows, key_rows, preferred_element_type=jnp.float32
    )
    logits = jnp.where(allowed, raw_scores * score_scale, MASKED)
    row_max = jnp.max(logits, axis=-1, keepdims=True)
    exponent = jnp.exp(logits - row_max)
    row_sum = jnp.sum(exponent, axis=-1, keepdims=True)
    weights = (exponent / row_sum).astype(jnp.bfloat16)
    crossed = jnp.einsum("chqk,ckhd->cqhd", weights, value_rows, preferred_element_type=jnp.float32)
    return (crossed.astype(jnp.bfloat16), row_max + jnp.log(row_sum))


def cross_backward(query_rows, key_rows, value_rows, grad_rows, log_sums, allowed):
    score_scale = query_rows.shape[3] ** (-0.5)
    raw_scores = jnp.einsum(
        "cqhd,ckhd->chqk", query_rows, key_rows, preferred_element_type=jnp.float32
    )
    logits = jnp.where(allowed, raw_scores * score_scale, MASKED)
    probs = jnp.exp(logits - log_sums)
    weights = probs.astype(jnp.bfloat16)
    grad_probs = jnp.einsum(
        "cqhd,ckhd->chqk", grad_rows, value_rows, preferred_element_type=jnp.float32
    )
    row_dot = jnp.sum(probs * grad_probs, axis=-1, keepdims=True)
    grad_scores = (probs * (grad_probs - row_dot)).astype(jnp.bfloat16)
    grad_query = (
        jnp.einsum("chqk,ckhd->cqhd", grad_scores, key_rows, preferred_element_type=jnp.float32)
        * score_scale
    )
    grad_keys = (
        jnp.einsum("chqk,cqhd->ckhd", grad_scores, query_rows, preferred_element_type=jnp.float32)
        * score_scale
    )
    grad_values = jnp.einsum(
        "chqk,cqhd->ckhd", weights, grad_rows, preferred_element_type=jnp.float32
    )
    return (grad_query, grad_keys, grad_values)


def sum_ffn(grad_ffn_in, grad_ffn_out):
    return (
        lax.psum_scatter(grad_ffn_in, ("clip", "frame"), scatter_dimension=0, tiled=True),
        lax.psum_scatter(grad_ffn_out, ("clip", "frame"), scatter_dimension=0, tiled=True),
    )


def sum_attention(
    grad_self_qkv, grad_self_out, grad_cross_qkv, grad_cross_out, grad_gains, grad_shifts
):
    return (
        lax.psum_scatter(grad_self_qkv, ("clip", "frame"), scatter_dimension=0, tiled=True),
        lax.psum_scatter(grad_self_out, ("clip", "frame"), scatter_dimension=0, tiled=True),
        lax.psum_scatter(grad_cross_qkv, ("clip", "frame"), scatter_dimension=0, tiled=True),
        lax.psum_scatter(grad_cross_out, ("clip", "frame"), scatter_dimension=0, tiled=True),
        lax.psum_scatter(grad_gains, ("clip", "frame"), scatter_dimension=1, tiled=True),
        lax.psum_scatter(grad_shifts, ("clip", "frame"), scatter_dimension=1, tiled=True),
    )


def on_device_any(
    hidden_in,
    text_states,
    out_grad,
    self_qkv,
    self_out,
    cross_qkv,
    cross_out,
    ffn_in,
    ffn_out,
    ln_gain,
    ln_bias,
    clip_len,
    frame_mask,
    text_len,
    text_mask,
):
    clip_count, frames, model_width = hidden_in.shape
    text_slots = text_states.shape[1]
    group_count = lax.axis_size("frame")
    columns_here = model_width // group_count
    heads_here = columns_here // HD
    length = frames * group_count
    frame_index = lax.axis_index("frame")
    full_qkv, full_out, full_cross, full_cross_out, gains_low, shifts_low = fetch_attention(
        self_qkv, self_out, cross_qkv, cross_out, ln_gain, ln_bias
    )
    gains = gains_low.astype(jnp.float32)
    shifts = shifts_low.astype(jnp.float32)
    hidden = hidden_in.astype(jnp.float32)
    first_norm, first_pull = jax.vjp(layer_norm, hidden, gains[0], shifts[0])
    first_low = first_norm.astype(jnp.bfloat16)
    query_low = project(first_low, full_qkv[:, 0]).astype(jnp.bfloat16)
    key_low = project(first_low, full_qkv[:, 1]).astype(jnp.bfloat16)
    value_low = project(first_low, full_qkv[:, 2]).astype(jnp.bfloat16)
    query_heads, key_heads, value_heads = (
        lax.all_to_all(query_low, "frame", split_axis=2, concat_axis=1, tiled=True),
        lax.all_to_all(key_low, "frame", split_axis=2, concat_axis=1, tiled=True),
        lax.all_to_all(value_low, "frame", split_axis=2, concat_axis=1, tiled=True),
    )
    head_shape = (clip_count, length, heads_here, HD)
    query_heads = query_heads.reshape(head_shape)
    key_heads = key_heads.reshape(head_shape)
    value_heads = value_heads.reshape(head_shape)
    columns = jnp.arange(length, dtype=jnp.int32)
    key_valid = (columns[None, :] < clip_len[:, None]) & (frame_mask > 0)
    attended_heads, self_sums = self_forward(
        query_heads, key_heads, value_heads, clip_len, key_valid
    )
    attended = lax.all_to_all(
        attended_heads.reshape(clip_count, length, columns_here),
        "frame",
        split_axis=1,
        concat_axis=2,
        tiled=True,
    )
    after_self = hidden + project(attended, full_out)
    second_norm, second_pull = jax.vjp(layer_norm, after_self, gains[1], shifts[1])
    second_low = second_norm.astype(jnp.bfloat16)
    cross_query = project(second_low, full_cross[:, 0]).astype(jnp.bfloat16)
    cross_query_heads = lax.all_to_all(
        cross_query, "frame", split_axis=2, concat_axis=1, tiled=True
    ).reshape(head_shape)
    key_columns = lax.dynamic_slice_in_dim(
        full_cross[:, 1], frame_index * columns_here, columns_here, 1
    )
    value_columns = lax.dynamic_slice_in_dim(
        full_cross[:, 2], frame_index * columns_here, columns_here, 1
    )
    text_shape = (clip_count, text_slots, heads_here, HD)
    text_keys = project(text_states, key_columns).astype(jnp.bfloat16).reshape(text_shape)
    text_values = project(text_states, value_columns).astype(jnp.bfloat16).reshape(text_shape)
    allowed_text = text_allowed(text_len, text_mask)
    crossed_heads, cross_sums = cross_forward(
        cross_query_heads, text_keys, text_values, allowed_text
    )
    crossed = lax.all_to_all(
        crossed_heads.reshape(clip_count, length, columns_here),
        "frame",
        split_axis=1,
        concat_axis=2,
        tiled=True,
    )
    after_cross = after_self + project(crossed, full_cross_out)
    ffn_weight_in, ffn_weight_out = fetch_ffn(ffn_in, ffn_out)
    third_norm, third_pull = jax.vjp(layer_norm, after_cross, gains[2], shifts[2])
    third_low = third_norm.astype(jnp.bfloat16)
    pre_act = project(third_low, ffn_weight_in)
    activated, gelu_pull = jax.vjp(activate, pre_act)
    inner_low = activated.astype(jnp.bfloat16)
    output = (after_cross + project(inner_low, ffn_weight_out)).astype(jnp.bfloat16)
    ffn_weight_in, ffn_weight_out = fetch_ffn(ffn_in, ffn_out)
    grad_ffn_out = weight_grad(inner_low, out_grad)
    (grad_pre,) = gelu_pull(project_back(out_grad, ffn_weight_out))
    grad_pre_low = grad_pre.astype(jnp.bfloat16)
    grad_ffn_in = weight_grad(third_low, grad_pre_low)
    ffn_sums = sum_ffn(grad_ffn_in, grad_ffn_out)
    grad_third, gain_third, shift_third = third_pull(project_back(grad_pre_low, ffn_weight_in))
    grad_after_cross = out_grad.astype(jnp.float32) + grad_third
    full_qkv, full_out, full_cross, full_cross_out, gains_low, shifts_low = fetch_attention(
        self_qkv, self_out, cross_qkv, cross_out, ln_gain, ln_bias
    )
    key_columns = lax.dynamic_slice_in_dim(
        full_cross[:, 1], frame_index * columns_here, columns_here, 1
    )
    value_columns = lax.dynamic_slice_in_dim(
        full_cross[:, 2], frame_index * columns_here, columns_here, 1
    )
    cross_branch = grad_after_cross.astype(jnp.bfloat16)
    grad_cross_out = weight_grad(crossed, cross_branch)
    grad_crossed = project_back(cross_branch, full_cross_out).astype(jnp.bfloat16)
    grad_crossed_heads = lax.all_to_all(
        grad_crossed, "frame", split_axis=2, concat_axis=1, tiled=True
    ).reshape(head_shape)
    grad_cq, grad_tk, grad_tv = cross_backward(
        cross_query_heads, text_keys, text_values, grad_crossed_heads, cross_sums, allowed_text
    )
    grad_tk_low = grad_tk.astype(jnp.bfloat16).reshape(clip_count, text_slots, columns_here)
    grad_tv_low = grad_tv.astype(jnp.bfloat16).reshape(clip_count, text_slots, columns_here)
    text_terms = project_back(grad_tk_low, key_columns) + project_back(grad_tv_low, value_columns)
    grad_text = lax.psum_scatter(
        text_terms.astype(jnp.bfloat16), "frame", scatter_dimension=1, tiled=True
    )
    empty_square = jnp.zeros((model_width, model_width), jnp.float32)
    grad_cross_key = lax.dynamic_update_slice_in_dim(
        empty_square, weight_grad(text_states, grad_tk_low), frame_index * columns_here, 1
    )
    grad_cross_value = lax.dynamic_update_slice_in_dim(
        empty_square, weight_grad(text_states, grad_tv_low), frame_index * columns_here, 1
    )
    grad_cq_low = grad_cq.astype(jnp.bfloat16).reshape(clip_count, length, columns_here)
    grad_cross_query = lax.all_to_all(grad_cq_low, "frame", split_axis=1, concat_axis=2, tiled=True)
    grad_cross_qw = weight_grad(second_low, grad_cross_query)
    grad_second, gain_second, shift_second = second_pull(
        project_back(grad_cross_query, full_cross[:, 0])
    )
    grad_after_self = grad_after_cross + grad_second
    self_branch = grad_after_self.astype(jnp.bfloat16)
    grad_self_out = weight_grad(attended, self_branch)
    grad_attended = project_back(self_branch, full_out).astype(jnp.bfloat16)
    grad_attended_heads = lax.all_to_all(
        grad_attended, "frame", split_axis=2, concat_axis=1, tiled=True
    ).reshape(head_shape)
    grad_query, grad_keys, grad_values = self_backward(
        query_heads, key_heads, value_heads, grad_attended_heads, self_sums, clip_len, key_valid
    )
    flat_shape = (clip_count, length, columns_here)
    grad_query, grad_keys, grad_values = (
        lax.all_to_all(
            grad_query.astype(jnp.bfloat16).reshape(flat_shape),
            "frame",
            split_axis=1,
            concat_axis=2,
            tiled=True,
        ),
        lax.all_to_all(
            grad_keys.astype(jnp.bfloat16).reshape(flat_shape),
            "frame",
            split_axis=1,
            concat_axis=2,
            tiled=True,
        ),
        lax.all_to_all(
            grad_values.astype(jnp.bfloat16).reshape(flat_shape),
            "frame",
            split_axis=1,
            concat_axis=2,
            tiled=True,
        ),
    )
    grad_self_qkv = jnp.stack(
        [
            weight_grad(first_low, grad_query),
            weight_grad(first_low, grad_keys),
            weight_grad(first_low, grad_values),
        ],
        axis=1,
    )
    grad_first_norm = (
        project_back(grad_query, full_qkv[:, 0])
        + project_back(grad_keys, full_qkv[:, 1])
        + project_back(grad_values, full_qkv[:, 2])
    )
    grad_first, gain_first, shift_first = first_pull(grad_first_norm)
    grad_hidden = (grad_after_self + grad_first).astype(jnp.bfloat16)
    grad_cross_qkv = jnp.stack([grad_cross_qw, grad_cross_key, grad_cross_value], axis=1)
    grad_gains = jnp.stack([gain_first, gain_second, gain_third])
    grad_shifts = jnp.stack([shift_first, shift_second, shift_third])
    attn_sums = sum_attention(
        grad_self_qkv, grad_self_out, grad_cross_qkv, grad_cross_out, grad_gains, grad_shifts
    )
    return (
        output,
        grad_hidden,
        grad_text,
        attn_sums[0],
        attn_sums[1],
        attn_sums[2],
        attn_sums[3],
        ffn_sums[0],
        ffn_sums[1],
        attn_sums[4],
        attn_sums[5],
    )


MESH = pl.DeviceIdType.MESH
HBM = pl.BlockSpec(memory_space=pl.ANY)
VMEM = pl.BlockSpec(memory_space=pltpu.VMEM)
SMEM = pl.BlockSpec(memory_space=pltpu.SMEM)
NEG = -1e30
F32 = jnp.float32
BF16 = jnp.bfloat16


def fits(mesh):
    return mesh.shape["clip"] == 4 and mesh.shape["frame"] == 8


class Here:
    def __init__(self):
        self.c = lax.axis_index("clip")
        self.f = lax.axis_index("frame")
        self.core = lax.rem(self.f, 2)
        self.z = lax.div(self.f, 2)
        self.pair = lax.div(self.z, 2)
        self.role = lax.rem(self.z, 2)
        self.group = lax.rem(self.f, 4)
        self.cx = self.c + 1 - 2 * lax.rem(self.c, 2)
        self.cy = lax.rem(self.c + 2, 4)
        self.cd = 3 - self.c
        self.sib = self.f + 1 - 2 * self.core
        self.partner = self.f + 2 - 4 * self.role
        self.far_gate = 2 * (2 - self.pair) + self.core
        self.is_gate = self.role + self.pair == 1
        self.far = [2 * (2 * (1 - self.pair) + j) + self.core for j in range(2)]

    def step(self, d):
        return lax.rem(self.f + d, 8)

    def zstep(self, d):
        return lax.rem(self.f + 2 * d, 8)


class Wire:
    def __init__(self, here, send_sem, recv_sem):
        self.here, self.send_sem, self.recv_sem = here, send_sem, recv_sem
        self.used = 0
        self.open = []

    def copy(self, src, dst, tag, c, f):
        self.used += 1
        return pltpu.make_async_remote_copy(
            src_ref=src,
            dst_ref=dst,
            send_sem=self.send_sem.at[self.used - 1],
            recv_sem=self.recv_sem.at[tag],
            device_id=(c, f),
            device_id_type=MESH,
        )

    def send(self, src, dst, tag, c, f):
        copy = self.copy(src, dst, tag, c, f)
        copy.start()
        self.open.append(copy)

    def arrived(self, dst, tag):
        pltpu.make_async_remote_copy(
            src_ref=dst,
            dst_ref=dst,
            send_sem=self.send_sem.at[0],
            recv_sem=self.recv_sem.at[tag],
            device_id=(self.here.c, self.here.sib),
            device_id_type=MESH,
        ).wait_recv()

    def drain(self):
        for copy in self.open:
            copy.wait_send()
        self.open = []


def greet(devices):
    barrier = pltpu.get_barrier_semaphore()
    for device in devices:
        pl.semaphore_signal(barrier, inc=1, device_id=device, device_id_type=MESH)
    pl.semaphore_wait(barrier, len(devices))


def frame_others(here):
    return [(here.c, here.step(d)) for d in range(1, 8)]


def clip_others(here):
    return [(here.cx, here.f), (here.cy, here.f), (here.cd, here.f)]


class ClipGather:
    def __init__(self, wire, block, tag, own=None):
        self.wire, self.block, self.tag = wire, block, tag
        self.own = own or (lambda half: block(wire.here.c, half))

    def begin(self):
        h, w, b, t, own = self.wire.here, self.wire, self.block, self.tag, self.own
        w.send(own(0), b(h.c, 0), t, h.cx, h.f)
        w.send(own(1), b(h.c, 1), t + 2, h.cy, h.f)
        w.send(own(1), b(h.c, 1), t + 1, h.cx, h.f)
        w.send(own(0), b(h.c, 0), t + 3, h.cy, h.f)

    def middle(self):
        h, w, b, t = self.wire.here, self.wire, self.block, self.tag
        w.arrived(b(h.cx, 0), t)
        w.send(b(h.cx, 0), b(h.cx, 0), t + 4, h.cy, h.f)
        w.arrived(b(h.cy, 1), t + 2)
        w.send(b(h.cy, 1), b(h.cy, 1), t + 5, h.cx, h.f)

    def near(self):
        h, w, b, t = self.wire.here, self.wire, self.block, self.tag
        w.arrived(b(h.cx, 1), t + 1)
        w.arrived(b(h.cy, 0), t + 3)

    def end(self):
        h, w, b, t = self.wire.here, self.wire, self.block, self.tag
        w.arrived(b(h.cd, 0), t + 4)
        w.arrived(b(h.cd, 1), t + 5)


class ZGather:
    def __init__(self, wire, slot, tag, own=None):
        self.wire, self.slot, self.tag = wire, slot, tag
        self.own = own if own is not None else slot(wire.here.f)
        self.open = []

    def step(self, s):
        h, w = self.wire.here, self.wire
        left, right = h.f - 2 * (s - 1), h.f + 2 * (s - 1)
        if s > 1:

            @pl.when(left >= 0)
            def _():
                w.arrived(self.slot(left), self.tag + s - 2)

            @pl.when(right <= 7)
            def _():
                w.arrived(self.slot(right), self.tag + 3 + s - 2)

        if s > 3:
            return
        for block, tag, go, to in (
            (left, self.tag, (left >= 0) & (h.z <= 2), h.f + 2),
            (right, self.tag + 3, (right <= 7) & (h.z >= 1), h.f - 2),
        ):
            src = self.own if s == 1 else self.slot(block)
            copy = w.copy(src, self.slot(block), tag + s - 1, h.c, to)
            pl.when(go)(copy.start)
            self.open.append((go, copy))

    def relay(self, d):
        h, w = self.wire.here, self.wire
        f = h.zstep(d)
        w.send(self.own if d == 0 else self.slot(f), self.slot(f), self.tag + 6 + d, h.c, h.sib)

    def end(self):
        h, w = self.wire.here, self.wire
        for d in range(4):
            w.arrived(self.slot(h.zstep(d) + h.sib - h.f), self.tag + 6 + d)

    def drain(self):
        for go, copy in self.open:
            pl.when(go)(copy.wait_send)


class MatrixGather:
    def __init__(self, wire, block, rows, tag):
        h = wire.here
        self.wire, self.block, self.tag = wire, block, tag
        self.z = ZGather(wire, lambda f: block(h.c, f), tag)
        toward = 2 - 4 * h.pair
        at_end = jnp.logical_not(h.is_gate)
        self.order = [
            h.f,
            h.f + toward,
            jnp.where(at_end, h.f + 2 * toward, h.f - toward),
            jnp.where(at_end, h.f + 3 * toward, h.f + 2 * toward),
        ]
        self.clip = [
            ClipGather(
                wire,
                lambda c, half, f=f: block(c, f).at[pl.ds(rows // 2 * half, rows // 2), :],
                tag + 10 + 6 * d,
            )
            for d, f in enumerate(self.order)
        ]

    def step(self, s):
        self.z.step(s)
        self.clip[s - 1].begin()
        self.z.relay(s - 1) if s == 1 else None
        if s == 4:
            for d in range(1, 4):
                self.z.relay(d)

    def _relay(self, d, i, c):
        h, w = self.wire.here, self.wire
        block = self.block(c, self.order[d])
        w.send(block, block, self.tag + 34 + 3 * d + i, h.c, h.sib)

    def middle(self, d):
        self.clip[d].middle()

    def near(self, d):
        h = self.wire.here
        self.clip[d].near()
        self._relay(d, 0, h.cx)
        self._relay(d, 1, h.cy)

    def last(self, d):
        self.clip[d].end()
        self._relay(d, 2, self.wire.here.cd)

    def end(self):
        h, w = self.wire.here, self.wire
        self.z.end()
        for d in range(4):
            f = self.order[d] + h.sib - h.f
            for i, c in enumerate((h.cx, h.cy, h.cd)):
                w.arrived(self.block(c, f), self.tag + 34 + 3 * d + i)


class ClipScatter:
    def __init__(self, wire, parts, slots, tag):
        self.wire, self.parts, self.slots, self.tag = wire, parts, slots, tag

    def begin(self, which=None):
        h, w, p, s, t = self.wire.here, self.wire, self.parts, self.slots, self.tag
        if which != 1:
            w.send(p(h.cd, 0), s[0], t, h.cx, h.f)
            w.send(p(h.cd, 1), s[1], t + 1, h.cy, h.f)
        if which != 0:
            w.send(p(h.cx, 0), s[2], t + 2, h.cx, h.f)
            w.send(p(h.cy, 1), s[3], t + 3, h.cy, h.f)

    def middle(self):
        h, w, p, s, t = self.wire.here, self.wire, self.parts, self.slots, self.tag
        w.arrived(s[0], t)
        add_into(s[0], p(h.cy, 0))
        w.send(s[0], s[4], t + 4, h.cy, h.f)
        w.arrived(s[1], t + 1)
        add_into(s[1], p(h.cx, 1))
        w.send(s[1], s[5], t + 5, h.cx, h.f)

    def end(self):
        w, s, t = self.wire, self.slots, self.tag
        for i in range(2, 6):
            w.arrived(s[i], t + i)

    def total(self, half):
        s = self.slots
        first, second = (s[2], s[4]) if half == 0 else (s[5], s[3])
        own = self.parts(self.wire.here.c, half)
        return own[...].astype(F32) + first[...].astype(F32) + second[...].astype(F32)


class ZScatter:
    def __init__(self, wire, terms, near, far, tag):
        self.wire, self.terms, self.near, self.far, self.tag = wire, terms, near, far, tag
        self.open = []

    def term(self, m):
        pair = self.wire.here.pair
        return self.terms.at[m + pair * (3 - 2 * m)]

    def _start(self, go, src, dst, tag, f):
        copy = self.wire.copy(src, dst, self.tag + tag, self.wire.here.c, f)
        pl.when(go)(copy.start)
        self.open.append((go, copy))

    def begin(self):
        h = self.wire.here
        for i, m in enumerate((3, 2, 1)):
            self._start(jnp.logical_not(h.is_gate), self.term(m), self.near.at[i], i, h.partner)

    def step(self, s):
        h, w = self.wire.here, self.wire
        block, m, tag, to, f = (
            (self.near.at[0], 3, 0, 0, h.far_gate),
            (self.near.at[1], 2, 1, 1, h.far_gate),
            (self.far.at[0], 0, 3, 0, h.partner),
        )[s - 1]

        @pl.when(h.is_gate)
        def _():
            w.arrived(block, self.tag + tag)
            add_into(block, self.term(m))

        self._start(h.is_gate, block, self.far.at[to], 3 + to, f)

    def end(self):
        h, w = self.wire.here, self.wire

        @pl.when(h.is_gate)
        def _():
            w.arrived(self.near.at[2], self.tag + 2)
            w.arrived(self.far.at[1], self.tag + 4)

        @pl.when(jnp.logical_not(h.is_gate))
        def _():
            w.arrived(self.far.at[0], self.tag + 3)

    def total(self, out):
        h = self.wire.here
        self.end()

        @pl.when(h.is_gate)
        def _():
            others = self.near[2].astype(F32) + self.far[1].astype(F32)
            out[...] = (self.terms[h.z].astype(F32) + others).astype(out.dtype)

        @pl.when(jnp.logical_not(h.is_gate))
        def _():
            out[...] = (self.terms[h.z].astype(F32) + self.far[0].astype(F32)).astype(out.dtype)

    def drain(self):
        for go, copy in self.open:
            pl.when(go)(copy.wait_send)


class SiblingSum:
    def __init__(self, wire, terms, inbox, sums, tag):
        self.wire, self.terms, self.inbox, self.sums, self.tag = wire, terms, inbox, sums, tag

    def begin(self):
        h, w = self.wire.here, self.wire
        for z in range(4):
            w.send(self.terms(2 * z + 1 - h.core), self.inbox(z), self.tag + z, h.c, h.sib)

    def end(self):
        h, w = self.wire.here, self.wire
        for z in range(4):
            w.arrived(self.inbox(z), self.tag + z)
            own, other = self.terms(2 * z + h.core), self.inbox(z)
            self.sums(z)[...] = (own[...].astype(F32) + other[...].astype(F32)).astype(BF16)


def add_into(into, other):
    into[...] = (into[...].astype(F32) + other[...].astype(F32)).astype(BF16)


class LocalCopy:
    def __init__(self, src, through, dst, sem):
        self.a = pltpu.make_async_copy(src, through, sem)
        self.b = pltpu.make_async_copy(through, dst, sem)
        self.a.start()

    def turn(self):
        self.a.wait()
        self.b.start()

    def wait(self):
        self.b.wait()


def comm_call(body, out_shape, in_specs, out_specs, scratch, copies, tags, collective_id, cost=None):
    return pl.pallas_call(
        body,
        out_shape=out_shape,
        in_specs=in_specs,
        out_specs=out_specs,
        scratch_shapes=list(scratch)
        + [pltpu.SemaphoreType.DMA((copies,)), pltpu.SemaphoreType.DMA((tags,))],
        compiler_params=pltpu.CompilerParams(
            collective_id=collective_id, has_side_effects=True, vmem_limit_bytes=60 * 2**20
        ),
    )


def shape(dims, dtype=BF16):
    return jax.ShapeDtypeStruct(dims, dtype)


ROWS = 256


def dot(left, right, contract):
    return lax.dot_general(left, right, ((contract[:1], contract[1:]), ((), ())), preferred_element_type=F32)


def fill_key_bias(bias, clip_len, frame_mask, clip):
    column = lax.broadcasted_iota(jnp.int32, (1, 1024), 1)
    valid = (column < clip_len[clip]) & (frame_mask[pl.ds(clip, 1), :] > 0)
    row = jnp.where(valid, 0.0, NEG).astype(F32)
    bias[...] = jnp.broadcast_to(row, (128, 1024)).T


def text_bias_rows(text_len, text_mask):
    slot = lax.broadcasted_iota(jnp.int32, (1, 128), 1)
    rows = []
    for clip in range(2):
        valid = (slot < text_len[clip]) & ((text_mask[clip : clip + 1, :] > 0) | (slot == 0))
        rows.append(jnp.where(valid, 0.0, NEG).astype(F32))
    return rows


def mask_scores(scores, bias_ref, first, rows):
    low = scores[first:] + bias_ref[first : first + rows, 0:1]
    key = lax.broadcasted_iota(jnp.int32, (rows, rows), 0)
    query = lax.broadcasted_iota(jnp.int32, (rows, rows), 1)
    low = jnp.where(key < query, low, jnp.where(key == query, scores[first:], NEG))
    if first == 0:
        return low
    return jnp.concatenate([scores[:first] + bias_ref[0:first, 0:1], low], axis=0)


def norm_parts(value):
    centered = value - jnp.mean(value, axis=-1, keepdims=True)
    scale = lax.rsqrt(jnp.mean(centered * centered, axis=-1, keepdims=True) + EPSILON)
    return centered * scale, scale


def column_weight(cols, j):
    return cols[:, :, 32 * j : 32 * j + 32, :].reshape(1024, 256)


def attend_rows(i, length, bias, q_ref, k_ref, v_t, o_ref, lse_ref, out_t):
    lane_head = lax.broadcasted_iota(jnp.int32, (ROWS, 256), 1) // HD
    first, n = i * ROWS, (i + 1) * ROWS
    q = q_ref[first:n, :]

    def head(j, _):
        q_head = jnp.where(lane_head == j, q, 0) * jnp.asarray(HD**-0.5, BF16)
        scores = mask_scores(dot(k_ref[0:n, :], q_head, (1, 1)), bias, first, ROWS)
        top = jnp.max(scores, axis=0, keepdims=True)
        weight = jnp.exp(scores - top)
        total = jnp.sum(weight, axis=0, keepdims=True)
        at = pl.ds(pl.multiple_of(j * HD, HD), HD)
        out_t[at, :] = dot(v_t[at, 0:n], weight.astype(BF16), (1, 0)) / total
        lse_ref[pl.ds(j, 1), first:n] = top + jnp.log(total)
        return 0

    lax.fori_loop(0, 4, head, 0)
    live = first + lax.broadcasted_iota(jnp.int32, (ROWS, 256), 0) < length
    o_ref[first:n, :] = jnp.where(live, out_t[...].T, 0).astype(BF16)


def square_of(square, which):
    return square[:, :, 32 * which : 32 * which + 32, :].reshape(1024, 1024)


def text_probs(query, keys, bias, lane_head):
    heads = [jnp.where(lane_head == j, query, 0) for j in range(4)]
    stacked = jnp.concatenate(heads, axis=0)
    scores = dot(stacked, keys, (1, 1)) + bias
    weight = jnp.exp(scores - jnp.max(scores, axis=1, keepdims=True))
    return weight / jnp.sum(weight, axis=1, keepdims=True), stacked


def pick_heads(stacked, lane_head):
    return sum(jnp.where(lane_head == j, stacked[128 * j : 128 * j + 128], 0) for j in range(4))


def forward_body(
    clip_len, text_len, frame_mask, text_mask, gain, shift, self_qkv, cross_qkv, self_out, cross_out,
    text, hid, fin, fout, grad,
    o_hid, o_first, o_q, o_k, o_v, o_heads, o_lse, o_w_a, o_w_b, o_params, o_att, o_tkv, o_square,
    o_second, o_query, o_crossed, o_self, o_cross, o_out, o_in, o_third, o_sum,
    hid_all, first, q_ref, k_ref, v_ref, heads, lse, w_a, w_b, params, att, tkv, sq_self, sq_cross,
    second, query_ref, crossed, after_self, after_cross, out_ref, in_ref,
    out_t, v_t, own_tkv, own_text, own_hid, fin_in, grad_all, win, wout,
    tokens, inner, slope, g_pre, terms, slots, out_w, inbox, sums, near, far,
    bias, cols_a, cols_b, square, placed, local, saved, send_sem, recv_sem,
):
    h = Here()
    w = Wire(h, send_sem, recv_sem)
    length = clip_len[h.pair]
    tag = [0]

    def tags(n):
        tag[0] += n
        return tag[0] - n

    T_HID, T_A, T_B, T_FIN, T_AXY, T_BXY = tags(10), tags(7), tags(7), tags(3), tags(6), tags(6)
    T_SELF, T_CROSS, T_ATT, T_TKV, T_WIN, T_GRAD = tags(46), tags(46), tags(8), tags(3), tags(10), tags(6)
    T_TOK, T_WOUT, T_TERM, T_OSIB, T_OZ = tags(6), tags(10), tags(6), tags(4), tags(5)

    def my_columns(f):
        return pl.ds(pl.multiple_of(lax.rem(f, 4) * 256, 256), 256)

    def fin_part(c):
        return fin.at[:, pl.ds(pl.multiple_of(c * 1024, 1024), 1024)]

    spread = lax.broadcasted_iota(jnp.int32, (32, 128), 0) + 32 * lax.rem(h.f, 4)
    spread = jnp.where(spread == lax.broadcasted_iota(jnp.int32, (32, 128), 1), 1.0, 0.0).astype(BF16)
    placed[...] = jnp.zeros_like(placed)
    placed[0:3, :] = dot(gain[...], spread, (1, 0))
    placed[3:6, :] = dot(shift[...], spread, (1, 0))
    for q in range(8):
        group = placed[...] if q % 2 == 0 else jnp.zeros((16, 128), F32)
        cols_a[96:112, 128 * q : 128 * q + 128] = group.astype(BF16)
    for j in range(3):
        cols_a[32 * j : 32 * j + 32, :] = self_qkv[j]
    for j in range(2):
        cols_b[32 * j : 32 * j + 32, :] = cross_qkv[1 + j]
    square[0:32, :] = self_out[...]
    square[32:64, :] = cross_qkv[0]
    square[64:96, :] = cross_out[...]
    own = [
        pltpu.make_async_copy(src, dst, local.at[i])
        for i, (src, dst) in enumerate(
            (
                (cols_a.at[:, my_columns(h.f)], w_a.at[h.c, h.f]),
                (cols_b.at[:, my_columns(h.f)], w_b.at[h.c, h.f]),
                (hid.at[h.pair], hid_all.at[h.f]),
                (square.at[pl.ds(0, 32)], sq_self.at[h.c, h.f]),
                (fin_part(h.c), fin_in.at[h.c]),
                (text, own_text),
                (hid, own_hid),
                (grad, grad_all.at[h.c]),
                (fout, wout.at[h.f]),
                (square.at[pl.ds(32, 64)], sq_cross.at[h.c, h.f]),
            )
        )
    ]
    for copy in own:
        copy.start()
    saves = []

    def save(src, dst):
        copy = pltpu.make_async_copy(src, dst, saved.at[len(saves)])
        copy.start()
        saves.append(copy)

    greet(frame_others(h) + clip_others(h))

    own[0].wait()
    for d in (2, 6, 4, 3, 5, 1, 7):
        f = h.step(d)
        w.send(cols_a.at[:, my_columns(f)], w_a.at[h.c, h.f], T_A + d - 1, h.c, f)
    own[7].wait()
    grad_gather = ClipGather(w, lambda c, half: grad_all.at[c, pl.ds(128 * half, 128), :], T_GRAD)
    grad_gather.begin()
    for i, (c, f) in enumerate(clip_others(h)):
        w.send(fin_part(c), fin_in.at[h.c], T_FIN + i, c, f)
    w.send(hid.at[h.pair], hid_all.at[h.f], T_HID, h.c, h.sib)

    def half_of(ref, part):
        return ref.at[pl.ds(64 * part, 64), :]

    for d in range(1, 8):
        w.arrived(w_a.at[h.c, lax.rem(h.f + 8 - d, 8)], T_A + d - 1)
    a_gather = ClipGather(w, lambda c, half: w_a.at[c, pl.ds(4 * half, 4)], T_AXY)
    a_gather.begin()
    for part in range(2):
        w.send(
            half_of(hid.at[1 - h.pair], part),
            half_of(hid_all.at[h.f], part),
            T_HID + 3 + 2 * h.role + part,
            h.c,
            h.far_gate,
        )
        w.send(half_of(hid.at[h.pair], part), half_of(hid_all.at[h.f], part), T_HID + 1 + part, h.c, h.partner)
    own[3].wait()
    self_gather = MatrixGather(w, lambda c, f: sq_self.at[c, f], 32, T_SELF)
    self_gather.step(1)
    forwards = []
    for part in range(2):
        for j in range(2):
            block = half_of(hid_all.at[h.far[j]], part)
            w.arrived(block, T_HID + 3 + 2 * j + part)
            forward = w.copy(block, block, T_HID + 3 + 2 * j + part, h.c, h.partner)
            pl.when(h.is_gate)(forward.start)
            forwards.append(forward)
    self_gather.step(2)
    a_gather.middle()
    for part in range(2):
        w.arrived(half_of(hid_all.at[h.partner], part), T_HID + 1 + part)
    w.send(hid_all.at[h.partner], hid_all.at[h.partner], T_HID + 7, h.c, h.sib)
    for j in range(2):
        w.send(hid_all.at[h.far[j]], hid_all.at[h.far[j]], T_HID + 8 + j, h.c, h.sib)
    self_gather.step(3)
    own[1].wait()
    for d in (2, 6, 4, 3, 5, 1, 7):
        f = h.step(d)
        w.send(cols_b.at[:, my_columns(f)], w_b.at[h.c, h.f], T_B + d - 1, h.c, f)
    fill_key_bias(bias, clip_len, frame_mask, h.pair)
    text_bias = text_bias_rows(text_len, text_mask)
    self_gather.middle(0)
    self_gather.step(4)
    self_gather.middle(1)
    own[9].wait()
    cross_gather = MatrixGather(w, lambda c, f: sq_cross.at[c, f], 64, T_CROSS)
    a_gather.near()
    a_gather.end()
    grad_gather.middle()
    cross_gather.step(1)
    own[4].wait()
    for i, (c, f) in enumerate(clip_others(h)):
        w.arrived(fin_in.at[c], T_FIN + i)
    win_gather = ZGather(w, lambda f: win.at[:, f], T_WIN, fin_in)
    win_copy = pltpu.make_async_copy(fin_in, win.at[:, h.f], local.at[11])
    win_copy.start()
    win_gather.step(1)
    win_gather.relay(0)
    for g in range(8):
        group = sum(w_a[g // 2, 4 * (g % 2) + i, 96:104, 0:128].astype(F32) for i in range(4))
        params[:, 128 * g : 128 * g + 128] = group
    own[2].wait()
    w.arrived(hid_all.at[h.sib], T_HID)
    w.arrived(hid_all.at[h.partner + h.sib - h.f], T_HID + 7)
    for j in range(2):
        w.arrived(hid_all.at[h.far[j] + h.sib - h.f], T_HID + 8 + j)

    def project_rows(i, _):
        at = pl.ds(pl.multiple_of(i * 256, 256), 256)
        rows = hid_all[pl.ds(2 * i, 2)].reshape(256, 1024).astype(F32)
        xhat, _ = norm_parts(rows)
        low = (xhat * params[0:1, :] + params[3:4, :]).astype(BF16)
        first[at, :] = low
        for j, out in enumerate((q_ref, k_ref, v_ref)):
            out[at, :] = dot(low, column_weight(w_a, j), (1, 0)).astype(BF16)
        return 0

    lax.fori_loop(0, 2, project_rows, 0)
    self_gather.middle(2)
    for d in range(1, 8):
        w.arrived(w_b.at[h.c, lax.rem(h.f + 8 - d, 8)], T_B + d - 1)
    b_gather = ClipGather(w, lambda c, half: w_b.at[c, pl.ds(4 * half, 4)], T_BXY)
    b_gather.begin()
    cross_gather.step(2)
    lax.fori_loop(2, 4, project_rows, 0)
    v_t[...] = v_ref[...].T
    win_gather.step(2)
    self_gather.middle(3)
    cross_gather.step(3)
    b_gather.middle()

    def att_slot(f):
        return att.at[lax.div(f, 4), :, my_columns(f)]

    att_sends = []

    def attend_and_send(i):
        attend_rows(i, length, bias, q_ref, k_ref, v_t, heads, lse, out_t)
        for f in (2 * i, 2 * i + 1):
            block = heads.at[pl.ds(128 * f, 128), :]
            away = h.f != f
            copy = w.copy(block, att_slot(h.f), T_ATT + h.f, h.c, f)
            stay = pltpu.make_async_copy(block, att_slot(h.f), local.at[12])
            pl.when(away)(copy.start)
            pl.when(jnp.logical_not(away))(stay.start)
            att_sends.append((away, copy, stay))

    attend_and_send(3)
    def text_slot(f):
        return tkv.at[:, :, :, my_columns(f)]

    b_gather.near()
    b_gather.end()
    own[5].wait()
    for clip in range(2):
        for j in range(2):
            own_tkv[clip, j] = dot(own_text[clip], column_weight(w_b, j), (1, 0)).astype(BF16)
    w.send(own_tkv, text_slot(h.f), T_TKV, h.c, h.partner)
    w.send(own_tkv, text_slot(h.f), T_TKV + 1, h.c, h.sib)
    text_copy = pltpu.make_async_copy(own_tkv, text_slot(h.f), local.at[10])
    text_copy.start()
    cross_gather.step(4)
    win_gather.step(3)
    cross_gather.middle(0)
    attend_and_send(2)
    for d in range(4):
        self_gather.near(d)
        self_gather.last(d)
    cross_gather.middle(1)
    w.arrived(text_slot(h.partner), T_TKV)
    w.send(text_slot(h.partner), text_slot(h.partner), T_TKV + 2, h.c, h.sib)
    attend_and_send(1)
    win_gather.step(4)
    for d in range(1, 4):
        win_gather.relay(d)
    cross_gather.middle(2)
    attend_and_send(0)
    cross_gather.middle(3)
    for src, dst in (
        (hid_all, o_hid), (first, o_first), (q_ref, o_q), (k_ref, o_k), (v_ref, o_v), (heads, o_heads), (lse, o_lse),
        (w_a, o_w_a), (w_b, o_w_b), (params, o_params),
    ):
        save(src, dst)
    self_gather.end()
    for d in range(1, 8):
        f = lax.rem(h.f + 8 - d, 8)
        w.arrived(att_slot(f), T_ATT + f)
    for away, _, stay in att_sends:
        pl.when(jnp.logical_not(away))(stay.wait)

    own[6].wait()
    value = own_hid[...].reshape(256, 1024).astype(F32) + dot(
        att[...].reshape(256, 1024), square_of(sq_self, 0), (1, 0)
    )
    after_self[...] = value
    xhat, _ = norm_parts(value)
    second[...] = (xhat * params[1:2, :] + params[4:5, :]).astype(BF16)
    for d in range(4):
        cross_gather.near(d)
        cross_gather.last(d)
    cross_gather.end()
    query_ref[...] = dot(second[...], square_of(sq_cross, 0), (1, 0)).astype(BF16)
    w.arrived(text_slot(h.sib), T_TKV + 1)
    w.arrived(text_slot(h.partner + h.sib - h.f), T_TKV + 2)
    text_copy.wait()
    lane_head = lax.broadcasted_iota(jnp.int32, (128, 256), 1) // HD
    for clip in range(2):
        for group in range(4):
            rows, columns = pl.ds(128 * clip, 128), pl.ds(256 * group, 256)
            query = query_ref[rows, columns] * jnp.asarray(HD**-0.5, BF16)
            probs, _ = text_probs(query, tkv[clip, 0, :, columns], text_bias[clip], lane_head)
            part = dot(probs.astype(BF16), tkv[clip, 1, :, columns], (1, 0))
            crossed[rows, columns] = pick_heads(part, lane_head).astype(BF16)
    own[8].wait()
    out_gather = ZGather(w, lambda f: wout.at[f], T_WOUT)
    out_gather.step(1)
    out_gather.relay(0)
    value = after_self[...] + dot(crossed[...], square_of(sq_cross, 1), (1, 0))
    after_cross[...] = value
    xhat, _ = norm_parts(value)
    tokens[h.c] = (xhat * params[2:3, :] + params[5:6, :]).astype(BF16)

    token_gather = ClipGather(w, lambda c, half: tokens.at[c, pl.ds(128 * half, 128), :], T_TOK)
    token_gather.begin()
    for src, dst in (
        (att, o_att), (tkv, o_tkv), (second, o_second), (query_ref, o_query), (crossed, o_crossed),
        (after_self, o_self), (after_cross, o_cross),
    ):
        save(src, dst)
    save(sq_self, o_square.at[0])
    for which in range(2):
        save(sq_cross.at[:, :, pl.ds(32 * which, 32), :], o_square.at[1 + which])
    win_copy.wait()
    win_gather.end()

    def hidden(c):
        for part in range(2):
            rows = pl.ds(128 * part, 128)
            pre = dot(tokens[c, rows, :], win[...].reshape(1024, 1024), (1, 0))
            cdf = 0.5 * (1.0 + lax.erf(pre * (0.5**0.5)))
            inner[c, rows, :] = (pre * cdf).astype(BF16)
            slope[c, rows, :] = cdf + pre * jnp.exp(-0.5 * pre * pre) * 0.3989422804014327

    def hidden_back(c):
        g_inner = dot(grad_all[c], wout[...].reshape(1024, 1024), (1, 1))
        g_pre[c] = (g_inner * slope[c]).astype(BF16)
        terms[c] = dot(g_pre[c], win[...].reshape(1024, 1024), (1, 1)).astype(BF16)

    def out_terms(c):
        out_ref[c] = dot(inner[c], wout[...].reshape(1024, 1024), (1, 0)).astype(BF16)

    sibling = SiblingSum(w, lambda f: out_w.at[f], lambda z: inbox.at[z], lambda z: sums.at[z], T_OSIB)
    z_scatter = ZScatter(w, sums, near, far, T_OZ)
    tall = (1024, 1024)

    def out_weight(i, _):
        columns = pl.ds(pl.multiple_of(i * 256, 256), 256)
        out = dot(inner[:, :, columns].reshape(1024, 256), grad_all[...].reshape(tall), (0, 0))
        out_w[pl.ds(2 * i, 2)] = out.astype(BF16).reshape(2, 128, 1024)
        return 0

    def in_weight(i, _):
        columns = pl.ds(pl.multiple_of(i * 256, 256), 256)
        out = dot(tokens[:, :, columns].reshape(1024, 256), g_pre[...].reshape(tall), (0, 0))
        in_ref[:, pl.ds(pl.multiple_of(32 * i, 32), 32), :] = out.astype(BF16).reshape(8, 32, 1024)
        return 0

    hidden(h.c)
    out_gather.step(2)
    grad_gather.near()
    grad_gather.end()
    token_gather.middle()
    token_gather.near()
    out_gather.step(3)
    hidden(h.cx)
    hidden(h.cy)
    out_gather.step(4)
    for d in range(1, 4):
        out_gather.relay(d)
    token_gather.end()
    hidden(h.cd)
    lax.fori_loop(0, 4, out_weight, 0)
    sibling.begin()
    out_gather.end()
    scatter = ClipScatter(
        w, lambda c, half: terms.at[c, pl.ds(128 * half, 128), :], [slots.at[i] for i in range(6)], T_TERM
    )
    hidden_back(h.cd)
    scatter.begin(0)
    sibling.end()
    z_scatter.begin()
    hidden_back(h.cx)
    hidden_back(h.cy)
    scatter.begin(1)
    hidden_back(h.c)
    scatter.middle()
    z_scatter.step(1)
    lax.fori_loop(0, 2, in_weight, 0)
    lax.fori_loop(2, 4, in_weight, 0)
    save(in_ref, o_in)
    out_terms(0)
    z_scatter.step(2)
    z_scatter.step(3)
    out_terms(1)
    out_terms(2)
    out_terms(3)
    save(out_ref, o_out)
    scatter.end()
    for half in range(2):
        o_third[128 * half : 128 * half + 128, :] = scatter.total(half)
    z_scatter.total(o_sum)
    w.drain()
    for copy in forwards:
        pl.when(h.is_gate)(copy.wait_send)
    for away, copy, _ in att_sends:
        pl.when(away)(copy.wait_send)
    for one in (self_gather.z, cross_gather.z, win_gather, out_gather, z_scatter):
        one.drain()
    for copy in saves:
        copy.wait()


def forward(*args):
    column, rows, full, quarter = (1024, 256), (256, 1024), (4, 256, 1024), (4, 128, 1024)
    kept = [
        shape((8, 128, 1024)),
        shape((1024, 1024)),
        shape(column),
        shape(column),
        shape(column),
        shape(column),
        shape((8, 1024), F32),
        shape((4, 8, 112, 256)),
        shape((4, 8, 64, 256)),
        shape((8, 1024), F32),
        shape((2, 128, 1024)),
        shape((2, 2, 128, 1024)),
        shape((4, 8, 96, 1024)),
        shape(rows),
        shape(rows),
        shape(rows),
        shape(rows, F32),
        shape(rows, F32),
        shape(full),
        shape((8, 128, 1024)),
    ]
    scratch = [pltpu.VMEM(one.shape, one.dtype) for one in kept]
    scratch[12:13] = [pltpu.VMEM((4, 8, rows, 1024), BF16) for rows in (32, 64)]
    kept[12] = shape((3, 4, 8, 32, 1024))
    return comm_call(
        forward_body,
        tuple(kept) + (shape(rows, F32), shape((128, 1024), F32)),
        [SMEM] * 2 + [VMEM] * 8 + [HBM] * 5,
        (HBM,) * len(kept) + (VMEM,) * 2,
        scratch
        + [
            pltpu.VMEM((256, ROWS), F32),
            pltpu.VMEM((256, 1024), BF16),
            pltpu.VMEM((2, 2, 128, 256), BF16),
            pltpu.VMEM((2, 128, 1024), BF16),
            pltpu.VMEM((2, 128, 1024), BF16),
            pltpu.VMEM((4, 32, 1024), BF16),
            pltpu.VMEM(full, BF16),
            pltpu.VMEM((4, 8, 32, 1024), BF16),
            pltpu.VMEM((8, 128, 1024), BF16),
            pltpu.VMEM(full, BF16),
            pltpu.VMEM(full, BF16),
            pltpu.VMEM(full, F32),
            pltpu.VMEM(full, BF16),
            pltpu.VMEM(full, BF16),
            pltpu.VMEM((6, 128, 1024), BF16),
            pltpu.VMEM((8, 128, 1024), BF16),
            pltpu.VMEM(quarter, BF16),
            pltpu.VMEM(quarter, BF16),
            pltpu.VMEM((3, 128, 1024), BF16),
            pltpu.VMEM((2, 128, 1024), BF16),
            pltpu.VMEM((1024, 128), F32),
            pltpu.VMEM((112, 1024), BF16),
            pltpu.VMEM((64, 1024), BF16),
            pltpu.VMEM((96, 1024), BF16),
            pltpu.VMEM((16, 128), F32),
            pltpu.SemaphoreType.DMA((13,)),
            pltpu.SemaphoreType.DMA((24,)),
        ],
        216,
        192,
        1,
    )(*args)


def attend_back_rows(i, length, bias, q_ref, k_ref, v_ref, o_ref, lse_ref, g_ref, dq_ref, dq_t, k_t, dk, dv):
    lane_head = lax.broadcasted_iota(jnp.int32, (ROWS, 256), 1) // HD
    first, n = i * ROWS, (i + 1) * ROWS
    q = q_ref[first:n, :] * jnp.asarray(HD**-0.5, BF16)
    live = first + lax.broadcasted_iota(jnp.int32, (ROWS, 256), 0) < length
    g = jnp.where(live, g_ref[first:n, :], 0)
    both = (g.astype(F32) * o_ref[first:n, :].astype(F32)).T
    row_dots = jnp.concatenate(
        [jnp.sum(both[HD * j : HD * j + HD], axis=0, keepdims=True) for j in range(4)], axis=0
    )
    lse = lse_ref[0:4, first:n]

    def pick(rows, j):
        at = lax.broadcasted_iota(jnp.int32, rows.shape, 0) == j
        return jnp.sum(jnp.where(at, rows, 0), axis=0, keepdims=True)

    def head(j, _):
        q_head = jnp.where(lane_head == j, q, 0)
        g_head = jnp.where(lane_head == j, g, 0)
        scores = mask_scores(dot(k_ref[0:n, :], q_head, (1, 1)), bias, first, ROWS)
        probs = jnp.exp(scores - pick(lse, j))
        grads = dot(v_ref[0:n, :], g_head, (1, 1))
        dlogits = (probs * (grads - pick(row_dots, j))).astype(BF16)
        dv[0:n, :] += dot(probs.astype(BF16), g_head, (1, 0))
        dk[0:n, :] += dot(dlogits, q_head, (1, 0))
        at = pl.ds(pl.multiple_of(j * HD, HD), HD)
        dq_t[at, :] = dot(k_t[at, 0:n], dlogits, (1, 0))
        return 0

    lax.fori_loop(0, 4, head, 0)
    dq_ref[first:n, :] = (dq_t[...].T * (HD**-0.5)).astype(BF16)


def norm_back(xhat, scale, grad, gain):
    h = grad * gain
    return scale * (
        h
        - jnp.mean(h, axis=-1, keepdims=True)
        - xhat * jnp.mean(h * xhat, axis=-1, keepdims=True)
    )


def backward_body(
    clip_len, text_len, frame_mask, text_mask, norms_in,
    h_third, h_out, h_cross, h_self, h_second, h_query, h_crossed, h_att, h_square, h_tkv, h_out_terms, h_in_terms,
    h_q, h_k, h_v, h_o, h_lse, h_hid, h_first, h_wa, h_wb, h_text, h_own,
    o_output, o_in, o_hidden, o_square, o_qkv, o_ckv, o_norm, o_text,
    v_third, v_out, after_cross, query_ref, crossed, att, mats, tkv, out_terms,
    q_ref, k_ref, v_ref, o_ref, lse, w_a, w_b, text_in,
    g_crossed, g_att, g_after, slots, t_inbox, t_near, t_far, t_total,
    i_inbox, i_near, i_far, i_out, i_in,
    g_square, s_inbox, s_slots, s_part, y_part, z_near, z_far, y_near, y_far,
    g_heads, dq_t, k_t, dk, dv, d_cols, f_inbox, f_in,
    a_terms, a_slots, a_sum, a_in, b_terms, b_slots, b_sum, b_in,
    t_terms, tt_in, n_row, n_terms, n_slots, n_sum, n_in,
    bias, loaded, local, send_sem, recv_sem,
):
    h = Here()
    w = Wire(h, send_sem, recv_sem)
    length = clip_len[h.pair]
    tag = [0]

    def tags(n):
        tag[0] += n
        return tag[0] - n

    loads = []

    def load(src, dst):
        copy = pltpu.make_async_copy(src, dst, loaded.at[len(loads)])
        copy.start()
        loads.append(copy)
        return copy

    l_terms = load(h_out_terms, out_terms)
    own_terms = [mats.at[0, z, pl.ds(0, 4)] for z in range(4)]
    l_own = [load(h_in_terms.at[2 * z + h.core], own_terms[z]) for z in range(4)]
    l_third, l_cross = load(h_third, v_third), load(h_cross, after_cross)
    l_out, l_m2 = load(h_out, v_out), load(h_square.at[2], mats.at[2])
    l_middle = [load(*pair) for pair in ((h_crossed, crossed), (h_query, query_ref), (h_tkv, tkv))]
    l_m1 = load(h_square.at[1], mats.at[1])
    l_att = load(h_att, att)
    l_heads = [
        load(*pair)
        for pair in (
            (h_q, q_ref), (h_k, k_ref), (h_v, v_ref), (h_o, o_ref), (h_lse, lse), (h_wb, w_b), (h_text, text_in),
            (h_wa, w_a),
        )
    ]
    greet(frame_others(h) + clip_others(h))

    def matrix(which):
        return mats[which].reshape(1024, 1024)

    out_scatter = ClipScatter(
        w,
        lambda c, half: out_terms.at[c, pl.ds(128 * half, 128), :],
        [slots.at[i] for i in range(6)],
        tags(6),
    )
    in_tag = tags(4)
    for z in range(4):
        w.send(h_in_terms.at[2 * z + 1 - h.core], i_inbox.at[z], in_tag + z, h.c, h.sib)
    in_scatter = ZScatter(w, i_inbox, i_near, i_far, tags(5))
    l_terms.wait()
    out_scatter.begin()

    def square_sums(which):
        sibling = SiblingSum(
            w,
            lambda f: g_square.at[which, :, f],
            lambda z: s_inbox.at[which, z],
            lambda z: s_inbox.at[which, z],
            tags(4),
        )
        clip = ClipScatter(
            w,
            lambda c, half: s_inbox.at[which, :, c, pl.ds(16 * half, 16), :],
            [s_slots.at[which, i] for i in range(6)],
            tags(6),
        )
        return sibling, clip

    squares = [square_sums(which) for which in range(3)]

    def put(which, value):
        g_square[which] = value.astype(BF16).reshape(4, 8, 32, 1024)

    def columns_of(f):
        return pl.ds(pl.multiple_of(lax.rem(f, 4) * 256, 256), 256)

    def part_of(f):
        return g_att.at[lax.div(f, 4), :, columns_of(f)]

    def text_part(f):
        return g_text.at[lax.div(f, 4), :, :, columns_of(f)]

    fill_key_bias(bias, clip_len, frame_mask, h.pair)
    text_bias = text_bias_rows(text_len, text_mask)
    for copy in (l_third, l_cross, l_out):
        copy.wait()
    xhat, scale = norm_parts(after_cross[...])
    grad = v_third[...]
    gain_third = jnp.sum(grad * xhat, axis=0, keepdims=True)
    shift_third = jnp.sum(grad, axis=0, keepdims=True)
    n_row[...] = jnp.zeros_like(n_row)
    n_row[2:3, :] = gain_third
    n_row[5:6, :] = shift_third
    g_after_cross = v_out[...].reshape(256, 1024).astype(F32) + norm_back(xhat, scale, grad, norms_in[2:3, :])
    g_after[...] = g_after_cross
    after_self, own_hid = v_third, v_out
    l_self, l_own_hid = load(h_self, after_self), load(h_own, own_hid)
    branch = g_after_cross.astype(BF16)
    l_m2.wait()
    g_crossed[...] = dot(branch, matrix(2), (1, 1)).astype(BF16)
    l_first = load(h_first, mats.at[2])
    for copy in l_middle + l_own:
        copy.wait()
    put(2, dot(crossed[...], branch, (0, 0)))
    squares[2][0].begin()
    second = crossed
    l_second = load(h_second, second)
    for z in range(4):
        w.arrived(i_inbox.at[z], in_tag + z)
        add_into(i_inbox.at[z], own_terms[z])
    in_scatter.begin()
    l_m0 = load(h_square.at[0], mats.at[0])
    g_query, g_text = query_ref, tkv
    lane_head = lax.broadcasted_iota(jnp.int32, (128, 256), 1) // HD
    for clip in range(2):
        for group in range(4):
            rows, columns = pl.ds(128 * clip, 128), pl.ds(256 * group, 256)
            keys, values = tkv[clip, 0, :, columns], tkv[clip, 1, :, columns]
            query = query_ref[rows, columns] * jnp.asarray(HD**-0.5, BF16)
            probs, stacked = text_probs(query, keys, text_bias[clip], lane_head)
            grads = g_crossed[rows, columns]
            g_stacked = jnp.concatenate([jnp.where(lane_head == j, grads, 0) for j in range(4)], axis=0)
            g_probs = dot(g_stacked, values, (1, 1))
            row_dot = jnp.sum(probs * g_probs, axis=1, keepdims=True)
            g_logits = (probs * (g_probs - row_dot)).astype(BF16)
            part = dot(g_logits, keys, (1, 0))
            g_query[rows, columns] = (pick_heads(part, lane_head) * (HD**-0.5)).astype(BF16)
            g_text[clip, 0, :, columns] = dot(g_logits, stacked, (0, 0)).astype(BF16)
            g_text[clip, 1, :, columns] = dot(probs.astype(BF16), g_stacked, (0, 0)).astype(BF16)
        if clip == 0:
            out_scatter.middle()
            in_scatter.step(1)
            squares[2][0].end()
            squares[2][1].begin()
    text_sibling = SiblingSum(w, text_part, lambda z: t_inbox.at[z], lambda z: t_inbox.at[z], tags(4))
    text_sibling.begin()
    l_m1.wait()
    grad = dot(g_query[...], matrix(1), (1, 1))
    l_hid = load(h_hid, mats.at[1])
    l_self.wait()
    xhat, scale = norm_parts(after_self[...])
    n_row[1:2, :] = jnp.sum(grad * xhat, axis=0, keepdims=True)
    n_row[4:5, :] = jnp.sum(grad, axis=0, keepdims=True)
    g_after_self = g_after[...] + norm_back(xhat, scale, grad, norms_in[1:2, :])
    g_after[...] = g_after_self
    branch = g_after_self.astype(BF16)
    l_m0.wait()
    g_att[...] = dot(branch, matrix(0), (1, 1)).astype(BF16).reshape(2, 128, 1024)
    heads_tag = tags(7)
    for d in (4, 2, 6, 3, 5, 1, 7):
        f = h.step(d)
        w.send(part_of(f), g_heads.at[h.f], heads_tag + d - 1, h.c, f)
    own_part = pltpu.make_async_copy(part_of(h.f), g_heads.at[h.f], local.at[0])
    own_part.start()
    in_scatter.step(2)
    in_scatter.step(3)
    l_second.wait()
    l_att.wait()
    put(1, dot(second[...], g_query[...], (0, 0)))
    squares[1][0].begin()
    put(0, dot(att[...].reshape(256, 1024), branch, (0, 0)))
    squares[0][0].begin()
    text_sibling.end()
    text_scatter = ZScatter(w, t_inbox, t_near, t_far, tags(5))
    text_scatter.begin()
    squares[2][1].middle()
    squares[1][0].end()
    squares[1][1].begin()
    out_scatter.end()
    for half in range(2):
        rows = pl.ds(128 * half, 128)
        o_output[rows, :] = (after_cross[rows, :] + out_scatter.total(half)).astype(BF16)
    squares[0][0].end()
    squares[0][1].begin()
    in_scatter.total(i_out)
    i_tag = tags(3)
    for i, (c, f) in enumerate(clip_others(h)):
        w.send(i_out.at[c], i_in.at[h.c], i_tag + i, c, f)
    i_in[h.c] = i_out[h.c]
    squares[1][1].middle()

    def square_part(which, out, row):
        squares[which][1].end()
        for half in range(2):
            total = squares[which][1].total(half)
            out[:, row + 16 * half : row + 16 * half + 16, :] = total.astype(BF16)

    text_scatter.step(1)
    for copy in l_heads:
        copy.wait()
    k_t[...] = k_ref[...].T
    dk[...] = jnp.zeros_like(dk)
    dv[...] = jnp.zeros_like(dv)
    for d in range(1, 8):
        w.arrived(g_heads.at[lax.rem(h.f + 8 - d, 8)], heads_tag + d - 1)
    own_part.wait()
    g_rows = g_heads[...].reshape(1024, 256)

    def rows_back(i):
        attend_back_rows(
            i, length, bias, q_ref, k_ref, v_ref, o_ref, lse, g_rows, d_cols.at[0], dq_t, k_t, dk, dv
        )

    text_scatter.step(2)
    text_scatter.step(3)
    squares[0][1].middle()
    rows_back(0)
    square_part(2, s_part, 32)
    square_part(1, s_part, 0)
    z_scatter = ZScatter(w, s_part, z_near, z_far, tags(5))
    z_scatter.begin()
    rows_back(1)

    class Columns:
        def __init__(self, terms, slots, sums, inbox):
            self.sums, self.inbox, self.tag = sums, inbox, tags(13)
            self.clip = ClipScatter(
                w,
                lambda c, half: terms.at[c, pl.ds(4 * half, 4)],
                [slots.at[i] for i in range(6)],
                self.tag,
            )

        def spread(self):
            self.clip.end()
            for half in range(2):
                self.sums[4 * half : 4 * half + 4] = self.clip.total(half).astype(BF16)
            for d in (4, 2, 6, 3, 5, 1, 7):
                f = h.step(d)
                w.send(self.sums.at[f], self.inbox.at[h.f], self.tag + 5 + d, h.c, f)
            self.inbox[h.f] = self.sums[h.f]

        def wait(self):
            for d in range(1, 8):
                w.arrived(self.inbox.at[lax.rem(h.f + 8 - d, 8)], self.tag + 5 + d)

    text_scatter.total(t_total)
    g_tkv = [t_total[j].astype(BF16) for j in range(2)]
    text = text_in[h.pair]
    for j in range(2):
        b_terms[:, :, 32 * j : 32 * j + 32, :] = (
            dot(text, g_tkv[j], (0, 0)).astype(BF16).reshape(4, 8, 32, 256)
        )
    b_columns = Columns(b_terms, b_slots, b_sum, b_in)
    b_columns.clip.begin()
    t_terms[...] = (
        dot(g_tkv[0], column_weight(w_b, 0), (1, 1)) + dot(g_tkv[1], column_weight(w_b, 1), (1, 1))
    ).astype(BF16)
    tt_tag = tags(7)
    for d in range(1, 8):
        f = h.step(d)
        w.send(
            t_terms.at[pl.ds(pl.multiple_of(f * 16, 16), 16), :], tt_in.at[h.f], tt_tag + d - 1, h.c, f
        )
    tt_in[h.f] = t_terms[pl.ds(pl.multiple_of(h.f * 16, 16), 16), :]
    z_scatter.step(1)
    rows_back(2)
    square_part(0, y_part, 0)
    y_scatter = ZScatter(w, y_part, y_near, y_far, tags(5))
    y_scatter.begin()
    z_scatter.step(2)
    z_scatter.step(3)
    b_columns.clip.middle()
    rows_back(3)
    d_cols[1] = dk[...].astype(BF16)
    d_cols[2] = dv[...].astype(BF16)
    l_first.wait()
    a_columns = [Columns(a_terms.at[j], a_slots.at[j], a_sum.at[j], a_in.at[j]) for j in range(3)]
    for j in range(3):
        a_terms[j] = dot(mats[2].reshape(1024, 1024), d_cols[j], (0, 0)).astype(BF16).reshape(4, 8, 32, 256)
        a_columns[j].clip.begin()
    y_scatter.step(1)

    f_terms = mats.at[0]
    f_sibling = SiblingSum(
        w,
        lambda f: f_terms.at[lax.div(f, 2), pl.ds(pl.multiple_of(lax.rem(f, 2) * 4, 4), 4)],
        lambda z: f_inbox.at[z],
        lambda z: f_inbox.at[z],
        tags(4),
    )
    l_hid.wait()

    def frame_terms(i, _):
        rows = pl.ds(pl.multiple_of(i * 256, 256), 256)
        grad = sum(dot(d_cols[j, rows, :], column_weight(w_a, j), (1, 1)) for j in range(3))
        f_terms[i] = grad.astype(BF16).reshape(8, 32, 1024)
        xhat, _ = norm_parts(mats[1, i].reshape(256, 1024).astype(F32))
        n_row[0:1, :] += jnp.sum(grad * xhat, axis=0, keepdims=True)
        n_row[3:4, :] += jnp.sum(grad, axis=0, keepdims=True)
        return 0

    lax.fori_loop(0, 4, frame_terms, 0)
    f_sibling.begin()
    y_scatter.step(2)
    a_columns[0].clip.middle()
    f_sibling.end()
    f_tag = tags(4)
    other = 2 * (1 - h.pair)
    is_end = jnp.logical_not(h.is_gate)
    to_gate, to_far = [], []
    for j in range(2):
        to_gate.append(w.copy(f_inbox.at[other + j], f_in.at[1 + j], f_tag + 1 + j, h.c, h.partner))
        pl.when(is_end)(to_gate[j].start)
    w.send(f_inbox.at[lax.div(h.partner, 2)], f_in.at[0], f_tag, h.c, h.partner)
    for c in range(4):
        for f in range(8):
            group = 2 * c + f // 4
            n_terms[c, f] = n_row[:, 128 * group : 128 * group + 128].astype(BF16)
    n_columns = Columns(n_terms, n_slots, n_sum, n_in)
    n_columns.clip.begin()
    a_columns[1].clip.middle()
    a_columns[0].spread()
    for j in range(2):

        @pl.when(h.is_gate)
        def _():
            w.arrived(f_in.at[1 + j], f_tag + 1 + j)
            add_into(f_inbox.at[other + j], f_in.at[1 + j])

        to_far.append(w.copy(f_inbox.at[other + j], f_in.at[3], f_tag + 3, h.c, h.far[j]))
        pl.when(h.is_gate)(to_far[j].start)
    a_columns[2].clip.middle()
    a_columns[1].spread()
    n_columns.clip.middle()
    y_scatter.step(3)
    a_columns[2].spread()
    n_columns.spread()
    b_columns.spread()
    z_scatter.total(o_square.at[pl.ds(32, 64), :])
    for i, (c, f) in enumerate(clip_others(h)):
        w.arrived(i_in.at[c], i_tag + i)
    for c in range(4):
        o_in[:, 1024 * c : 1024 * c + 1024] = i_in[c].astype(F32)
    for d in range(1, 8):
        w.arrived(tt_in.at[lax.rem(h.f + 8 - d, 8)], tt_tag + d - 1)
    for p in range(2):
        o_text[p] = sum(tt_in[4 * p + q].astype(F32) for q in range(4)).astype(BF16)
    y_scatter.total(o_square.at[pl.ds(0, 32), :])
    w.arrived(f_in.at[0], f_tag)
    w.arrived(f_in.at[3], f_tag + 3)

    def hidden_out(clip, total):
        xhat, scale = norm_parts(own_hid[clip].astype(F32))
        rows = pl.ds(pl.multiple_of(clip * 128, 128), 128)
        o_hidden[clip] = (g_after[rows, :] + norm_back(xhat, scale, total, norms_in[0:1, :])).astype(BF16)

    l_own_hid.wait()
    hidden_out(h.pair, (f_inbox[h.z].astype(F32) + f_in[0].astype(F32)).reshape(128, 1024))
    hidden_out(1 - h.pair, f_in[3].astype(F32).reshape(128, 1024))
    for j in range(3):
        a_columns[j].wait()
        for q in range(4):
            o_qkv[j, :, 256 * q : 256 * q + 256] = a_in[j, q].astype(F32) + a_in[j, 4 + q].astype(F32)
    b_columns.wait()
    for j in range(2):
        for q in range(4):
            at = pl.ds(32 * j, 32)
            o_ckv[j, :, 256 * q : 256 * q + 256] = b_in[q, at, :].astype(F32) + b_in[4 + q, at, :].astype(F32)
    n_columns.wait()
    o_norm[...] = sum(n_in[f].astype(F32) for f in range(8))
    w.drain()
    for one in (in_scatter, text_scatter, z_scatter, y_scatter):
        one.drain()
    for j in range(2):
        pl.when(is_end)(to_gate[j].wait_send)
        pl.when(h.is_gate)(to_far[j].wait_send)


def backward(*args):
    def buffer(*dims):
        return pltpu.VMEM(dims, BF16)

    def full(*dims):
        return pltpu.VMEM(dims, F32)

    return comm_call(
        backward_body,
        (
            shape((256, 1024)),
            shape((32, 4096), F32),
            shape((2, 128, 1024)),
            shape((96, 1024), F32),
            shape((3, 32, 1024), F32),
            shape((2, 32, 1024), F32),
            shape((16, 128), F32),
            shape((2, 16, 1024)),
        ),
        [SMEM] * 2 + [VMEM] * 3 + [HBM] * 23,
        (VMEM,) * 8,
        [
            full(256, 1024), buffer(2, 128, 1024), full(256, 1024), buffer(256, 1024), buffer(256, 1024),
            buffer(2, 128, 1024), buffer(3, 4, 8, 32, 1024), buffer(2, 2, 128, 1024), buffer(4, 256, 1024),
            buffer(1024, 256), buffer(1024, 256), buffer(1024, 256), buffer(1024, 256), full(8, 1024),
            buffer(4, 8, 112, 256), buffer(4, 8, 64, 256), buffer(2, 128, 1024),
            buffer(256, 1024), buffer(2, 128, 1024), full(256, 1024),
            buffer(6, 128, 1024), buffer(4, 2, 128, 256), buffer(3, 2, 128, 256), buffer(2, 2, 128, 256),
            full(2, 128, 256),
            buffer(4, 4, 32, 1024), buffer(3, 4, 32, 1024), buffer(2, 4, 32, 1024),
            buffer(4, 32, 1024), buffer(4, 32, 1024),
            buffer(3, 4, 8, 32, 1024), buffer(3, 4, 4, 32, 1024), buffer(3, 6, 4, 16, 1024),
            buffer(4, 64, 1024), buffer(4, 32, 1024), buffer(3, 64, 1024), buffer(2, 64, 1024),
            buffer(3, 32, 1024), buffer(2, 32, 1024),
            buffer(8, 128, 256), full(256, ROWS), buffer(256, 1024), full(1024, 256), full(1024, 256),
            buffer(3, 1024, 256), buffer(4, 4, 32, 1024), buffer(4, 4, 32, 1024),
            buffer(3, 4, 8, 32, 256), buffer(3, 6, 4, 32, 256), buffer(3, 8, 32, 256), buffer(3, 8, 32, 256),
            buffer(4, 8, 64, 256), buffer(6, 4, 64, 256), buffer(8, 64, 256), buffer(8, 64, 256),
            buffer(128, 1024), buffer(8, 16, 1024), full(16, 1024), buffer(4, 8, 16, 128), buffer(6, 4, 16, 128),
            buffer(8, 16, 128), buffer(8, 16, 128), full(1024, 128),
            pltpu.SemaphoreType.DMA((32,)),
            pltpu.SemaphoreType.DMA((1,)),
        ],
        208,
        160,
        2,
    )(*args)


def finish_body(*refs):
    ins, outs = refs[:8], refs[8:]
    output, hidden, text, qkv, square, ckv, fin, norm = ins
    o_output, o_hidden, o_text, o_qkv, o_self_out, o_cross, o_cross_out, o_fin, o_gain, o_shift = outs
    o_output[...] = output[...].reshape(2, 128, 1024)
    o_hidden[...] = hidden[...]
    o_text[...] = text[...]
    o_fin[...] = fin[...]
    o_qkv[...] = qkv[...]
    o_self_out[...] = square[0:32, :]
    o_cross[0] = square[32:64, :]
    o_cross[1:3] = ckv[...]
    o_cross_out[...] = square[64:96, :]
    place = lax.rem(lax.axis_index("frame"), 4)
    for row, out in ((0, o_gain), (3, o_shift)):
        out[...] = sum(
            jnp.where(place == i, norm[row : row + 3, 32 * i : 32 * i + 32], 0) for i in range(4)
        )


def finish(*args):
    return pl.pallas_call(
        finish_body,
        out_shape=(
            shape((2, 128, 1024)),
            shape((2, 128, 1024)),
            shape((2, 16, 1024)),
            shape((3, 32, 1024), F32),
            shape((32, 1024), F32),
            shape((3, 32, 1024), F32),
            shape((32, 1024), F32),
            shape((32, 4096), F32),
            shape((3, 32), F32),
            shape((3, 32), F32),
        ),
        in_specs=[VMEM] * 8,
        out_specs=(VMEM,) * 10,
        compiler_params=pltpu.CompilerParams(vmem_limit_bytes=60 * 2**20),
    )(*args)


def on_device_fast(
    hidden_in,
    text_states,
    out_grad,
    self_qkv,
    self_out,
    cross_qkv,
    cross_out,
    ffn_in,
    ffn_out,
    ln_gain,
    ln_bias,
    clip_len,
    frame_mask,
    text_len,
    text_mask,
):
    (
        hid_all, first_low, query, key, value, att_heads, lse, w_a, w_b, params, att, tkv, square,
        second, cross_query, crossed, after_self, after_cross, out_terms, in_terms, third_sum, grad_ffn_out,
    ) = forward(
        clip_len, text_len, frame_mask, text_mask, ln_gain, ln_bias, jnp.moveaxis(self_qkv, 1, 0),
        jnp.moveaxis(cross_qkv, 1, 0), self_out, cross_out, text_states, hidden_in, ffn_in, ffn_out, out_grad.reshape(256, 1024),
    )
    output, grad_ffn_in, grad_hidden, square_sum, qkv_sum, ckv_sum, norm_sum, grad_text = backward(
        clip_len, text_len, frame_mask, text_mask, params,
        third_sum, out_grad, after_cross, after_self, second, cross_query, crossed, att, square, tkv,
        out_terms, in_terms.reshape(8, 4, 32, 1024), query, key, value, att_heads, lse,
        hid_all.reshape(4, 8, 32, 1024), first_low.reshape(4, 8, 32, 1024), w_a, w_b, text_states, hidden_in,
    )
    results = finish(output, grad_hidden, grad_text, qkv_sum, square_sum, ckv_sum, grad_ffn_in, norm_sum)
    output, grad_hidden, grad_text, qkv, g_self_out, cross, g_cross_out, grad_ffn_in, gains, shifts = results
    return (
        output,
        grad_hidden,
        grad_text,
        jnp.moveaxis(qkv, 0, 1),
        g_self_out,
        jnp.moveaxis(cross, 0, 1),
        g_cross_out,
        grad_ffn_in,
        grad_ffn_out,
        gains,
        shifts,
    )


def solution(mesh):
    return jax.shard_map(
        on_device_fast if fits(mesh) else on_device_any,
        mesh=mesh,
        in_specs=(
            P("clip", "frame", None),
            P("clip", None, None),
            P("clip", "frame", None),
            P(("clip", "frame"), None, None),
            P(("clip", "frame"), None),
            P(("clip", "frame"), None, None),
            P(("clip", "frame"), None),
            P(("clip", "frame"), None),
            P(("clip", "frame"), None),
            P(None, ("clip", "frame")),
            P(None, ("clip", "frame")),
            P("clip"),
            P("clip", None),
            P("clip"),
            P("clip", None),
        ),
        out_specs=(
            P("clip", "frame", None),
            P("clip", "frame", None),
            P("clip", "frame", None),
            P(("clip", "frame"), None, None),
            P(("clip", "frame"), None),
            P(("clip", "frame"), None, None),
            P(("clip", "frame"), None),
            P(("clip", "frame"), None),
            P(("clip", "frame"), None),
            P(None, ("clip", "frame")),
            P(None, ("clip", "frame")),
        ),
        check_vma=False,
    )
```

```python
import functools

import jax
import jax.numpy as jnp
from jax import lax
from jax.experimental import pallas as pl
from jax.experimental.pallas import tpu as pltpu
from jax.sharding import PartitionSpec as P

HD = 64


MASKED = -1000000000.0
EPSILON = 1e-05


def layer_norm(value, gain, shift):
    average = jnp.mean(value, axis=-1, keepdims=True)
    centered = value - average
    variance = jnp.mean(centered * centered, axis=-1, keepdims=True)
    return centered * lax.rsqrt(variance + EPSILON) * gain + shift


def activate(value):
    return jax.nn.gelu(value, approximate=False)


def project(left, right):
    return jnp.einsum("cnd,de->cne", left, right, preferred_element_type=jnp.float32)


def project_back(grad_rows, weight):
    return jnp.einsum("cne,de->cnd", grad_rows, weight, preferred_element_type=jnp.float32)


def weight_grad(left, right):
    return jnp.einsum("cnd,cne->de", left, right, preferred_element_type=jnp.float32)


def fetch_attention(self_qkv, self_out, cross_qkv, cross_out, ln_gain, ln_bias):
    return (
        lax.all_gather(self_qkv, ("clip", "frame"), axis=0, tiled=True),
        lax.all_gather(self_out, ("clip", "frame"), axis=0, tiled=True),
        lax.all_gather(cross_qkv, ("clip", "frame"), axis=0, tiled=True),
        lax.all_gather(cross_out, ("clip", "frame"), axis=0, tiled=True),
        lax.all_gather(ln_gain, ("clip", "frame"), axis=1, tiled=True),
        lax.all_gather(ln_bias, ("clip", "frame"), axis=1, tiled=True),
    )


def fetch_ffn(ffn_in, ffn_out):
    return (
        lax.all_gather(ffn_in, ("clip", "frame"), axis=0, tiled=True),
        lax.all_gather(ffn_out, ("clip", "frame"), axis=0, tiled=True),
    )


def self_masks(first_row, block_rows, clip_len, key_valid):
    columns = jnp.arange(key_valid.shape[1], dtype=jnp.int32)
    row_ids = first_row + jnp.arange(block_rows, dtype=jnp.int32)
    diagonal = columns[None, :] == row_ids[:, None]
    allowed = (columns[None, :] <= row_ids[:, None])[None] & (
        key_valid[:, None, :] | diagonal[None]
    )
    live_rows = (row_ids[None, :] < clip_len[:, None]).astype(jnp.float32)
    return (allowed[:, None], live_rows[:, None, :, None])


def self_forward(query_rows, key_rows, value_rows, clip_len, key_valid):
    length = query_rows.shape[1]
    block_rows = min(512, length)
    score_scale = query_rows.shape[3] ** (-0.5)

    def one_block(block_index):
        first_row = block_index * block_rows
        query_block = lax.dynamic_slice_in_dim(query_rows, first_row, block_rows, 1)
        raw_scores = jnp.einsum(
            "cqhd,ckhd->chqk", query_block, key_rows, preferred_element_type=jnp.float32
        )
        allowed, live_rows = self_masks(first_row, block_rows, clip_len, key_valid)
        logits = jnp.where(allowed, raw_scores * score_scale, MASKED)
        row_max = jnp.max(logits, axis=-1, keepdims=True)
        exponent = jnp.exp(logits - row_max)
        row_sum = jnp.sum(exponent, axis=-1, keepdims=True)
        weights = (exponent / row_sum * live_rows).astype(jnp.bfloat16)
        attended = jnp.einsum(
            "chqk,ckhd->cqhd", weights, value_rows, preferred_element_type=jnp.float32
        )
        return (attended.astype(jnp.bfloat16), row_max + jnp.log(row_sum))

    blocks, log_sums = lax.map(one_block, jnp.arange(length // block_rows, dtype=jnp.int32))
    return (jnp.moveaxis(blocks, 0, 1).reshape(query_rows.shape), log_sums)


def self_backward(query_rows, key_rows, value_rows, grad_rows, log_sums, clip_len, key_valid):
    length = query_rows.shape[1]
    block_rows = min(512, length)
    score_scale = query_rows.shape[3] ** (-0.5)

    def one_block(totals, block_index):
        grad_keys, grad_values = totals
        first_row = block_index * block_rows
        query_block = lax.dynamic_slice_in_dim(query_rows, first_row, block_rows, 1)
        grad_block = lax.dynamic_slice_in_dim(grad_rows, first_row, block_rows, 1)
        raw_scores = jnp.einsum(
            "cqhd,ckhd->chqk", query_block, key_rows, preferred_element_type=jnp.float32
        )
        allowed, live_rows = self_masks(first_row, block_rows, clip_len, key_valid)
        logits = jnp.where(allowed, raw_scores * score_scale, MASKED)
        probs = jnp.exp(logits - log_sums[block_index])
        weights = (probs * live_rows).astype(jnp.bfloat16)
        grad_probs = (
            jnp.einsum(
                "cqhd,ckhd->chqk", grad_block, value_rows, preferred_element_type=jnp.float32
            )
            * live_rows
        )
        row_dot = jnp.sum(probs * grad_probs, axis=-1, keepdims=True)
        grad_scores = (probs * (grad_probs - row_dot)).astype(jnp.bfloat16)
        grad_query = (
            jnp.einsum("chqk,ckhd->cqhd", grad_scores, key_rows, preferred_element_type=jnp.float32)
            * score_scale
        )
        grad_keys = (
            grad_keys
            + jnp.einsum(
                "chqk,cqhd->ckhd", grad_scores, query_block, preferred_element_type=jnp.float32
            )
            * score_scale
        )
        grad_values = grad_values + jnp.einsum(
            "chqk,cqhd->ckhd", weights, grad_block, preferred_element_type=jnp.float32
        )
        return ((grad_keys, grad_values), grad_query)

    zeros = jnp.zeros(key_rows.shape, jnp.float32)
    (grad_keys, grad_values), grad_blocks = lax.scan(
        one_block, (zeros, zeros), jnp.arange(length // block_rows, dtype=jnp.int32)
    )
    grad_query = jnp.moveaxis(grad_blocks, 0, 1).reshape(query_rows.shape)
    return (grad_query, grad_keys, grad_values)


def text_allowed(text_len, text_mask):
    slots = jnp.arange(text_mask.shape[1], dtype=jnp.int32)
    allowed = (slots[None, :] < text_len[:, None]) & ((text_mask > 0) | (slots[None, :] == 0))
    return allowed[:, None, None, :]


def cross_forward(query_rows, key_rows, value_rows, allowed):
    score_scale = query_rows.shape[3] ** (-0.5)
    raw_scores = jnp.einsum(
        "cqhd,ckhd->chqk", query_rows, key_rows, preferred_element_type=jnp.float32
    )
    logits = jnp.where(allowed, raw_scores * score_scale, MASKED)
    row_max = jnp.max(logits, axis=-1, keepdims=True)
    exponent = jnp.exp(logits - row_max)
    row_sum = jnp.sum(exponent, axis=-1, keepdims=True)
    weights = (exponent / row_sum).astype(jnp.bfloat16)
    crossed = jnp.einsum("chqk,ckhd->cqhd", weights, value_rows, preferred_element_type=jnp.float32)
    return (crossed.astype(jnp.bfloat16), row_max + jnp.log(row_sum))


def cross_backward(query_rows, key_rows, value_rows, grad_rows, log_sums, allowed):
    score_scale = query_rows.shape[3] ** (-0.5)
    raw_scores = jnp.einsum(
        "cqhd,ckhd->chqk", query_rows, key_rows, preferred_element_type=jnp.float32
    )
    logits = jnp.where(allowed, raw_scores * score_scale, MASKED)
    probs = jnp.exp(logits - log_sums)
    weights = probs.astype(jnp.bfloat16)
    grad_probs = jnp.einsum(
        "cqhd,ckhd->chqk", grad_rows, value_rows, preferred_element_type=jnp.float32
    )
    row_dot = jnp.sum(probs * grad_probs, axis=-1, keepdims=True)
    grad_scores = (probs * (grad_probs - row_dot)).astype(jnp.bfloat16)
    grad_query = (
        jnp.einsum("chqk,ckhd->cqhd", grad_scores, key_rows, preferred_element_type=jnp.float32)
        * score_scale
    )
    grad_keys = (
        jnp.einsum("chqk,cqhd->ckhd", grad_scores, query_rows, preferred_element_type=jnp.float32)
        * score_scale
    )
    grad_values = jnp.einsum(
        "chqk,cqhd->ckhd", weights, grad_rows, preferred_element_type=jnp.float32
    )
    return (grad_query, grad_keys, grad_values)


def sum_ffn(grad_ffn_in, grad_ffn_out):
    return (
        lax.psum_scatter(grad_ffn_in, ("clip", "frame"), scatter_dimension=0, tiled=True),
        lax.psum_scatter(grad_ffn_out, ("clip", "frame"), scatter_dimension=0, tiled=True),
    )


def sum_attention(
    grad_self_qkv, grad_self_out, grad_cross_qkv, grad_cross_out, grad_gains, grad_shifts
):
    return (
        lax.psum_scatter(grad_self_qkv, ("clip", "frame"), scatter_dimension=0, tiled=True),
        lax.psum_scatter(grad_self_out, ("clip", "frame"), scatter_dimension=0, tiled=True),
        lax.psum_scatter(grad_cross_qkv, ("clip", "frame"), scatter_dimension=0, tiled=True),
        lax.psum_scatter(grad_cross_out, ("clip", "frame"), scatter_dimension=0, tiled=True),
        lax.psum_scatter(grad_gains, ("clip", "frame"), scatter_dimension=1, tiled=True),
        lax.psum_scatter(grad_shifts, ("clip", "frame"), scatter_dimension=1, tiled=True),
    )


def on_device_any(
    hidden_in,
    text_states,
    out_grad,
    self_qkv,
    self_out,
    cross_qkv,
    cross_out,
    ffn_in,
    ffn_out,
    ln_gain,
    ln_bias,
    clip_len,
    frame_mask,
    text_len,
    text_mask,
):
    clip_count, frames, model_width = hidden_in.shape
    text_slots = text_states.shape[1]
    group_count = lax.axis_size("frame")
    columns_here = model_width // group_count
    heads_here = columns_here // HD
    length = frames * group_count
    frame_index = lax.axis_index("frame")
    full_qkv, full_out, full_cross, full_cross_out, gains_low, shifts_low = fetch_attention(
        self_qkv, self_out, cross_qkv, cross_out, ln_gain, ln_bias
    )
    gains = gains_low.astype(jnp.float32)
    shifts = shifts_low.astype(jnp.float32)
    hidden = hidden_in.astype(jnp.float32)
    first_norm, first_pull = jax.vjp(layer_norm, hidden, gains[0], shifts[0])
    first_low = first_norm.astype(jnp.bfloat16)
    query_low = project(first_low, full_qkv[:, 0]).astype(jnp.bfloat16)
    key_low = project(first_low, full_qkv[:, 1]).astype(jnp.bfloat16)
    value_low = project(first_low, full_qkv[:, 2]).astype(jnp.bfloat16)
    query_heads, key_heads, value_heads = (
        lax.all_to_all(query_low, "frame", split_axis=2, concat_axis=1, tiled=True),
        lax.all_to_all(key_low, "frame", split_axis=2, concat_axis=1, tiled=True),
        lax.all_to_all(value_low, "frame", split_axis=2, concat_axis=1, tiled=True),
    )
    head_shape = (clip_count, length, heads_here, HD)
    query_heads = query_heads.reshape(head_shape)
    key_heads = key_heads.reshape(head_shape)
    value_heads = value_heads.reshape(head_shape)
    columns = jnp.arange(length, dtype=jnp.int32)
    key_valid = (columns[None, :] < clip_len[:, None]) & (frame_mask > 0)
    attended_heads, self_sums = self_forward(
        query_heads, key_heads, value_heads, clip_len, key_valid
    )
    attended = lax.all_to_all(
        attended_heads.reshape(clip_count, length, columns_here),
        "frame",
        split_axis=1,
        concat_axis=2,
        tiled=True,
    )
    after_self = hidden + project(attended, full_out)
    second_norm, second_pull = jax.vjp(layer_norm, after_self, gains[1], shifts[1])
    second_low = second_norm.astype(jnp.bfloat16)
    cross_query = project(second_low, full_cross[:, 0]).astype(jnp.bfloat16)
    cross_query_heads = lax.all_to_all(
        cross_query, "frame", split_axis=2, concat_axis=1, tiled=True
    ).reshape(head_shape)
    key_columns = lax.dynamic_slice_in_dim(
        full_cross[:, 1], frame_index * columns_here, columns_here, 1
    )
    value_columns = lax.dynamic_slice_in_dim(
        full_cross[:, 2], frame_index * columns_here, columns_here, 1
    )
    text_shape = (clip_count, text_slots, heads_here, HD)
    text_keys = project(text_states, key_columns).astype(jnp.bfloat16).reshape(text_shape)
    text_values = project(text_states, value_columns).astype(jnp.bfloat16).reshape(text_shape)
    allowed_text = text_allowed(text_len, text_mask)
    crossed_heads, cross_sums = cross_forward(
        cross_query_heads, text_keys, text_values, allowed_text
    )
    crossed = lax.all_to_all(
        crossed_heads.reshape(clip_count, length, columns_here),
        "frame",
        split_axis=1,
        concat_axis=2,
        tiled=True,
    )
    after_cross = after_self + project(crossed, full_cross_out)
    ffn_weight_in, ffn_weight_out = fetch_ffn(ffn_in, ffn_out)
    third_norm, third_pull = jax.vjp(layer_norm, after_cross, gains[2], shifts[2])
    third_low = third_norm.astype(jnp.bfloat16)
    pre_act = project(third_low, ffn_weight_in)
    activated, gelu_pull = jax.vjp(activate, pre_act)
    inner_low = activated.astype(jnp.bfloat16)
    output = (after_cross + project(inner_low, ffn_weight_out)).astype(jnp.bfloat16)
    ffn_weight_in, ffn_weight_out = fetch_ffn(ffn_in, ffn_out)
    grad_ffn_out = weight_grad(inner_low, out_grad)
    (grad_pre,) = gelu_pull(project_back(out_grad, ffn_weight_out))
    grad_pre_low = grad_pre.astype(jnp.bfloat16)
    grad_ffn_in = weight_grad(third_low, grad_pre_low)
    ffn_sums = sum_ffn(grad_ffn_in, grad_ffn_out)
    grad_third, gain_third, shift_third = third_pull(project_back(grad_pre_low, ffn_weight_in))
    grad_after_cross = out_grad.astype(jnp.float32) + grad_third
    full_qkv, full_out, full_cross, full_cross_out, gains_low, shifts_low = fetch_attention(
        self_qkv, self_out, cross_qkv, cross_out, ln_gain, ln_bias
    )
    key_columns = lax.dynamic_slice_in_dim(
        full_cross[:, 1], frame_index * columns_here, columns_here, 1
    )
    value_columns = lax.dynamic_slice_in_dim(
        full_cross[:, 2], frame_index * columns_here, columns_here, 1
    )
    cross_branch = grad_after_cross.astype(jnp.bfloat16)
    grad_cross_out = weight_grad(crossed, cross_branch)
    grad_crossed = project_back(cross_branch, full_cross_out).astype(jnp.bfloat16)
    grad_crossed_heads = lax.all_to_all(
        grad_crossed, "frame", split_axis=2, concat_axis=1, tiled=True
    ).reshape(head_shape)
    grad_cq, grad_tk, grad_tv = cross_backward(
        cross_query_heads, text_keys, text_values, grad_crossed_heads, cross_sums, allowed_text
    )
    grad_tk_low = grad_tk.astype(jnp.bfloat16).reshape(clip_count, text_slots, columns_here)
    grad_tv_low = grad_tv.astype(jnp.bfloat16).reshape(clip_count, text_slots, columns_here)
    text_terms = project_back(grad_tk_low, key_columns) + project_back(grad_tv_low, value_columns)
    grad_text = lax.psum_scatter(
        text_terms.astype(jnp.bfloat16), "frame", scatter_dimension=1, tiled=True
    )
    empty_square = jnp.zeros((model_width, model_width), jnp.float32)
    grad_cross_key = lax.dynamic_update_slice_in_dim(
        empty_square, weight_grad(text_states, grad_tk_low), frame_index * columns_here, 1
    )
    grad_cross_value = lax.dynamic_update_slice_in_dim(
        empty_square, weight_grad(text_states, grad_tv_low), frame_index * columns_here, 1
    )
    grad_cq_low = grad_cq.astype(jnp.bfloat16).reshape(clip_count, length, columns_here)
    grad_cross_query = lax.all_to_all(grad_cq_low, "frame", split_axis=1, concat_axis=2, tiled=True)
    grad_cross_qw = weight_grad(second_low, grad_cross_query)
    grad_second, gain_second, shift_second = second_pull(
        project_back(grad_cross_query, full_cross[:, 0])
    )
    grad_after_self = grad_after_cross + grad_second
    self_branch = grad_after_self.astype(jnp.bfloat16)
    grad_self_out = weight_grad(attended, self_branch)
    grad_attended = project_back(self_branch, full_out).astype(jnp.bfloat16)
    grad_attended_heads = lax.all_to_all(
        grad_attended, "frame", split_axis=2, concat_axis=1, tiled=True
    ).reshape(head_shape)
    grad_query, grad_keys, grad_values = self_backward(
        query_heads, key_heads, value_heads, grad_attended_heads, self_sums, clip_len, key_valid
    )
    flat_shape = (clip_count, length, columns_here)
    grad_query, grad_keys, grad_values = (
        lax.all_to_all(
            grad_query.astype(jnp.bfloat16).reshape(flat_shape),
            "frame",
            split_axis=1,
            concat_axis=2,
            tiled=True,
        ),
        lax.all_to_all(
            grad_keys.astype(jnp.bfloat16).reshape(flat_shape),
            "frame",
            split_axis=1,
            concat_axis=2,
            tiled=True,
        ),
        lax.all_to_all(
            grad_values.astype(jnp.bfloat16).reshape(flat_shape),
            "frame",
            split_axis=1,
            concat_axis=2,
            tiled=True,
        ),
    )
    grad_self_qkv = jnp.stack(
        [
            weight_grad(first_low, grad_query),
            weight_grad(first_low, grad_keys),
            weight_grad(first_low, grad_values),
        ],
        axis=1,
    )
    grad_first_norm = (
        project_back(grad_query, full_qkv[:, 0])
        + project_back(grad_keys, full_qkv[:, 1])
        + project_back(grad_values, full_qkv[:, 2])
    )
    grad_first, gain_first, shift_first = first_pull(grad_first_norm)
    grad_hidden = (grad_after_self + grad_first).astype(jnp.bfloat16)
    grad_cross_qkv = jnp.stack([grad_cross_qw, grad_cross_key, grad_cross_value], axis=1)
    grad_gains = jnp.stack([gain_first, gain_second, gain_third])
    grad_shifts = jnp.stack([shift_first, shift_second, shift_third])
    attn_sums = sum_attention(
        grad_self_qkv, grad_self_out, grad_cross_qkv, grad_cross_out, grad_gains, grad_shifts
    )
    return (
        output,
        grad_hidden,
        grad_text,
        attn_sums[0],
        attn_sums[1],
        attn_sums[2],
        attn_sums[3],
        ffn_sums[0],
        ffn_sums[1],
        attn_sums[4],
        attn_sums[5],
    )


MESH = pl.DeviceIdType.MESH
HBM = pl.BlockSpec(memory_space=pl.ANY)
VMEM = pl.BlockSpec(memory_space=pltpu.VMEM)
SMEM = pl.BlockSpec(memory_space=pltpu.SMEM)
NEG = -1e30
F32 = jnp.float32
BF16 = jnp.bfloat16


def fits(mesh):
    return mesh.shape["clip"] == 4 and mesh.shape["frame"] == 8


class Here:
    def __init__(self):
        self.c = lax.axis_index("clip")
        self.f = lax.axis_index("frame")
        self.core = lax.rem(self.f, 2)
        self.z = lax.div(self.f, 2)
        self.pair = lax.div(self.z, 2)
        self.role = lax.rem(self.z, 2)
        self.group = lax.rem(self.f, 4)
        self.cx = self.c + 1 - 2 * lax.rem(self.c, 2)
        self.cy = lax.rem(self.c + 2, 4)
        self.cd = 3 - self.c
        self.sib = self.f + 1 - 2 * self.core
        self.partner = self.f + 2 - 4 * self.role
        self.far_gate = 2 * (2 - self.pair) + self.core
        self.is_gate = self.role + self.pair == 1
        self.far = [2 * (2 * (1 - self.pair) + j) + self.core for j in range(2)]

    def step(self, d):
        return lax.rem(self.f + d, 8)

    def zstep(self, d):
        return lax.rem(self.f + 2 * d, 8)


class Wire:
    def __init__(self, here, send_sem, recv_sem):
        self.here, self.send_sem, self.recv_sem = here, send_sem, recv_sem
        self.used = 0
        self.open = []

    def copy(self, src, dst, tag, c, f):
        self.used += 1
        return pltpu.make_async_remote_copy(
            src_ref=src,
            dst_ref=dst,
            send_sem=self.send_sem.at[self.used - 1],
            recv_sem=self.recv_sem.at[tag],
            device_id=(c, f),
            device_id_type=MESH,
        )

    def send(self, src, dst, tag, c, f):
        copy = self.copy(src, dst, tag, c, f)
        copy.start()
        self.open.append(copy)

    def arrived(self, dst, tag):
        pltpu.make_async_remote_copy(
            src_ref=dst,
            dst_ref=dst,
            send_sem=self.send_sem.at[0],
            recv_sem=self.recv_sem.at[tag],
            device_id=(self.here.c, self.here.sib),
            device_id_type=MESH,
        ).wait_recv()

    def drain(self):
        for copy in self.open:
            copy.wait_send()
        self.open = []


def call_out(devices):
    barrier = pltpu.get_barrier_semaphore()
    for device in devices:
        pl.semaphore_signal(barrier, inc=1, device_id=device, device_id_type=MESH)


def hear_all(devices):
    pl.semaphore_wait(pltpu.get_barrier_semaphore(), len(devices))


def frame_others(here):
    return [(here.c, here.step(d)) for d in range(1, 8)]


def clip_others(here):
    return [(here.cx, here.f), (here.cy, here.f), (here.cd, here.f)]


class ClipGather:
    def __init__(self, wire, block, tag, own=None):
        self.wire, self.block, self.tag = wire, block, tag
        self.own = own or (lambda half: block(wire.here.c, half))

    def begin(self):
        h, w, b, t, own = self.wire.here, self.wire, self.block, self.tag, self.own
        w.send(own(0), b(h.c, 0), t, h.cx, h.f)
        w.send(own(1), b(h.c, 1), t + 2, h.cy, h.f)
        w.send(own(1), b(h.c, 1), t + 1, h.cx, h.f)
        w.send(own(0), b(h.c, 0), t + 3, h.cy, h.f)

    def middle(self):
        h, w, b, t = self.wire.here, self.wire, self.block, self.tag
        w.arrived(b(h.cx, 0), t)
        w.send(b(h.cx, 0), b(h.cx, 0), t + 4, h.cy, h.f)
        w.arrived(b(h.cy, 1), t + 2)
        w.send(b(h.cy, 1), b(h.cy, 1), t + 5, h.cx, h.f)

    def near(self):
        h, w, b, t = self.wire.here, self.wire, self.block, self.tag
        w.arrived(b(h.cx, 1), t + 1)
        w.arrived(b(h.cy, 0), t + 3)

    def end(self):
        h, w, b, t = self.wire.here, self.wire, self.block, self.tag
        w.arrived(b(h.cd, 0), t + 4)
        w.arrived(b(h.cd, 1), t + 5)


class ZGather:
    def __init__(self, wire, slot, tag, own=None):
        self.wire, self.slot, self.tag = wire, slot, tag
        self.own = own if own is not None else slot(wire.here.f)
        self.open = []

    def step(self, s):
        h, w = self.wire.here, self.wire
        left, right = h.f - 2 * (s - 1), h.f + 2 * (s - 1)
        if s > 1:

            @pl.when(left >= 0)
            def _():
                w.arrived(self.slot(left), self.tag + s - 2)

            @pl.when(right <= 7)
            def _():
                w.arrived(self.slot(right), self.tag + 3 + s - 2)

        if s > 3:
            return
        for block, tag, go, to in (
            (left, self.tag, (left >= 0) & (h.z <= 2), h.f + 2),
            (right, self.tag + 3, (right <= 7) & (h.z >= 1), h.f - 2),
        ):
            src = self.own if s == 1 else self.slot(block)
            copy = w.copy(src, self.slot(block), tag + s - 1, h.c, to)
            pl.when(go)(copy.start)
            self.open.append((go, copy))

    def relay(self, d):
        h, w = self.wire.here, self.wire
        f = h.zstep(d)
        w.send(self.own if d == 0 else self.slot(f), self.slot(f), self.tag + 6 + d, h.c, h.sib)

    def end(self):
        h, w = self.wire.here, self.wire
        for d in range(4):
            w.arrived(self.slot(h.zstep(d) + h.sib - h.f), self.tag + 6 + d)

    def drain(self):
        for go, copy in self.open:
            pl.when(go)(copy.wait_send)


class MatrixGather:
    def __init__(self, wire, block, rows, tag):
        h = wire.here
        self.wire, self.block, self.tag = wire, block, tag
        self.z = ZGather(wire, lambda f: block(h.c, f), tag)
        toward = 2 - 4 * h.pair
        at_end = jnp.logical_not(h.is_gate)
        self.order = [
            h.f,
            h.f + toward,
            jnp.where(at_end, h.f + 2 * toward, h.f - toward),
            jnp.where(at_end, h.f + 3 * toward, h.f + 2 * toward),
        ]
        self.clip = [
            ClipGather(
                wire,
                lambda c, half, f=f: block(c, f).at[pl.ds(rows // 2 * half, rows // 2), :],
                tag + 10 + 6 * d,
            )
            for d, f in enumerate(self.order)
        ]

    def step(self, s):
        self.z.step(s)
        self.clip[s - 1].begin()
        self.z.relay(s - 1) if s == 1 else None
        if s == 4:
            for d in range(1, 4):
                self.z.relay(d)

    def _relay(self, d, i, c):
        h, w = self.wire.here, self.wire
        block = self.block(c, self.order[d])
        w.send(block, block, self.tag + 34 + 3 * d + i, h.c, h.sib)

    def middle(self, d):
        self.clip[d].middle()

    def near(self, d):
        h = self.wire.here
        self.clip[d].near()
        self._relay(d, 0, h.cx)
        self._relay(d, 1, h.cy)

    def last(self, d):
        self.clip[d].end()
        self._relay(d, 2, self.wire.here.cd)

    def end(self):
        h, w = self.wire.here, self.wire
        self.z.end()
        for d in range(4):
            f = self.order[d] + h.sib - h.f
            for i, c in enumerate((h.cx, h.cy, h.cd)):
                w.arrived(self.block(c, f), self.tag + 34 + 3 * d + i)


class ClipScatter:
    def __init__(self, wire, parts, slots, tag):
        self.wire, self.parts, self.slots, self.tag = wire, parts, slots, tag

    def begin(self, which=None):
        h, w, p, s, t = self.wire.here, self.wire, self.parts, self.slots, self.tag
        if which != 1:
            w.send(p(h.cd, 0), s[0], t, h.cx, h.f)
            w.send(p(h.cd, 1), s[1], t + 1, h.cy, h.f)
        if which != 0:
            w.send(p(h.cx, 0), s[2], t + 2, h.cx, h.f)
            w.send(p(h.cy, 1), s[3], t + 3, h.cy, h.f)

    def middle(self):
        h, w, p, s, t = self.wire.here, self.wire, self.parts, self.slots, self.tag
        w.arrived(s[0], t)
        add_into(s[0], p(h.cy, 0))
        w.send(s[0], s[4], t + 4, h.cy, h.f)
        w.arrived(s[1], t + 1)
        add_into(s[1], p(h.cx, 1))
        w.send(s[1], s[5], t + 5, h.cx, h.f)

    def end(self):
        w, s, t = self.wire, self.slots, self.tag
        for i in range(2, 6):
            w.arrived(s[i], t + i)

    def total(self, half):
        s = self.slots
        first, second = (s[2], s[4]) if half == 0 else (s[5], s[3])
        own = self.parts(self.wire.here.c, half)
        return own[...].astype(F32) + first[...].astype(F32) + second[...].astype(F32)


class ZScatter:
    def __init__(self, wire, terms, near, far, tag):
        self.wire, self.terms, self.near, self.far, self.tag = wire, terms, near, far, tag
        self.open = []

    def term(self, m):
        pair = self.wire.here.pair
        return self.terms.at[m + pair * (3 - 2 * m)]

    def _start(self, go, src, dst, tag, f):
        copy = self.wire.copy(src, dst, self.tag + tag, self.wire.here.c, f)
        pl.when(go)(copy.start)
        self.open.append((go, copy))

    def begin(self):
        h = self.wire.here
        for i, m in enumerate((3, 2, 1)):
            self._start(jnp.logical_not(h.is_gate), self.term(m), self.near.at[i], i, h.partner)

    def step(self, s):
        h, w = self.wire.here, self.wire
        block, m, tag, to, f = (
            (self.near.at[0], 3, 0, 0, h.far_gate),
            (self.near.at[1], 2, 1, 1, h.far_gate),
            (self.far.at[0], 0, 3, 0, h.partner),
        )[s - 1]

        @pl.when(h.is_gate)
        def _():
            w.arrived(block, self.tag + tag)
            add_into(block, self.term(m))

        self._start(h.is_gate, block, self.far.at[to], 3 + to, f)

    def end(self):
        h, w = self.wire.here, self.wire

        @pl.when(h.is_gate)
        def _():
            w.arrived(self.near.at[2], self.tag + 2)
            w.arrived(self.far.at[1], self.tag + 4)

        @pl.when(jnp.logical_not(h.is_gate))
        def _():
            w.arrived(self.far.at[0], self.tag + 3)

    def total(self, out):
        h = self.wire.here
        self.end()

        @pl.when(h.is_gate)
        def _():
            others = self.near[2].astype(F32) + self.far[1].astype(F32)
            out[...] = (self.terms[h.z].astype(F32) + others).astype(out.dtype)

        @pl.when(jnp.logical_not(h.is_gate))
        def _():
            out[...] = (self.terms[h.z].astype(F32) + self.far[0].astype(F32)).astype(out.dtype)

    def drain(self):
        for go, copy in self.open:
            pl.when(go)(copy.wait_send)


class SiblingSum:
    def __init__(self, wire, terms, inbox, sums, tag):
        self.wire, self.terms, self.inbox, self.sums, self.tag = wire, terms, inbox, sums, tag

    def begin(self):
        h, w = self.wire.here, self.wire
        for z in range(4):
            w.send(self.terms(2 * z + 1 - h.core), self.inbox(z), self.tag + z, h.c, h.sib)

    def end(self):
        h, w = self.wire.here, self.wire
        for z in range(4):
            w.arrived(self.inbox(z), self.tag + z)
            own, other = self.terms(2 * z + h.core), self.inbox(z)
            self.sums(z)[...] = (own[...].astype(F32) + other[...].astype(F32)).astype(BF16)


def add_into(into, other):
    into[...] = (into[...].astype(F32) + other[...].astype(F32)).astype(BF16)


class LocalCopy:
    def __init__(self, src, through, dst, sem):
        self.a = pltpu.make_async_copy(src, through, sem)
        self.b = pltpu.make_async_copy(through, dst, sem)
        self.a.start()

    def turn(self):
        self.a.wait()
        self.b.start()

    def wait(self):
        self.b.wait()


def comm_call(body, out_shape, in_specs, out_specs, scratch, copies, tags, collective_id, cost=None):
    return pl.pallas_call(
        body,
        out_shape=out_shape,
        in_specs=in_specs,
        out_specs=out_specs,
        scratch_shapes=list(scratch)
        + [pltpu.SemaphoreType.DMA((copies,)), pltpu.SemaphoreType.DMA((tags,))],
        compiler_params=pltpu.CompilerParams(
            collective_id=collective_id, has_side_effects=True, vmem_limit_bytes=60 * 2**20
        ),
    )


def shape(dims, dtype=BF16):
    return jax.ShapeDtypeStruct(dims, dtype)


ROWS = 256


def dot(left, right, contract):
    return lax.dot_general(left, right, ((contract[:1], contract[1:]), ((), ())), preferred_element_type=F32)


def fill_key_bias(bias, clip_len, frame_mask, clip):
    column = lax.broadcasted_iota(jnp.int32, (1, 1024), 1)
    valid = (column < clip_len[clip]) & (frame_mask[pl.ds(clip, 1), :] > 0)
    row = jnp.where(valid, 0.0, NEG).astype(F32)
    bias[...] = jnp.broadcast_to(row, (128, 1024)).T


def text_bias_rows(text_len, text_mask):
    slot = lax.broadcasted_iota(jnp.int32, (1, 128), 1)
    rows = []
    for clip in range(2):
        valid = (slot < text_len[clip]) & ((text_mask[clip : clip + 1, :] > 0) | (slot == 0))
        rows.append(jnp.where(valid, 0.0, NEG).astype(F32))
    return rows


def mask_scores(scores, bias_ref, first, rows):
    low = scores[first:] + bias_ref[first : first + rows, 0:1]
    key = lax.broadcasted_iota(jnp.int32, (rows, rows), 0)
    query = lax.broadcasted_iota(jnp.int32, (rows, rows), 1)
    low = jnp.where(key < query, low, jnp.where(key == query, scores[first:], NEG))
    if first == 0:
        return low
    return jnp.concatenate([scores[:first] + bias_ref[0:first, 0:1], low], axis=0)


def norm_parts(value):
    centered = value - jnp.mean(value, axis=-1, keepdims=True)
    scale = lax.rsqrt(jnp.mean(centered * centered, axis=-1, keepdims=True) + EPSILON)
    return centered * scale, scale


def column_weight(cols, j):
    return cols[:, :, 32 * j : 32 * j + 32, :].reshape(1024, 256)


def attend_rows(i, length, bias, q_ref, k_ref, v_t, o_ref, lse_ref, out_t):
    lane_head = lax.broadcasted_iota(jnp.int32, (ROWS, 256), 1) // HD
    first, n = i * ROWS, (i + 1) * ROWS
    q = q_ref[first:n, :]

    def head(j, _):
        q_head = jnp.where(lane_head == j, q, 0) * jnp.asarray(HD**-0.5, BF16)
        scores = mask_scores(dot(k_ref[0:n, :], q_head, (1, 1)), bias, first, ROWS)
        top = jnp.max(scores, axis=0, keepdims=True)
        weight = jnp.exp(scores - top)
        total = jnp.sum(weight, axis=0, keepdims=True)
        at = pl.ds(pl.multiple_of(j * HD, HD), HD)
        out_t[at, :] = dot(v_t[at, 0:n], weight.astype(BF16), (1, 0)) / total
        lse_ref[pl.ds(j, 1), first:n] = top + jnp.log(total)
        return 0

    lax.fori_loop(0, 4, head, 0, unroll=True)
    live = first + lax.broadcasted_iota(jnp.int32, (ROWS, 256), 0) < length
    o_ref[first:n, :] = jnp.where(live, out_t[...].T, 0).astype(BF16)


def square_of(square, which):
    return square[:, :, 32 * which : 32 * which + 32, :].reshape(1024, 1024)


def text_probs(query, keys, bias, lane_head):
    heads = [jnp.where(lane_head == j, query, 0) for j in range(4)]
    stacked = jnp.concatenate(heads, axis=0)
    scores = dot(stacked, keys, (1, 1)) + bias
    weight = jnp.exp(scores - jnp.max(scores, axis=1, keepdims=True))
    return weight / jnp.sum(weight, axis=1, keepdims=True), stacked


def pick_heads(stacked, lane_head):
    return sum(jnp.where(lane_head == j, stacked[128 * j : 128 * j + 128], 0) for j in range(4))


def forward_body(
    clip_len, text_len, frame_mask, text_mask, gain, shift, self_qkv, cross_qkv, self_out, cross_out,
    text, hid, fin, fout, grad,
    o_hid, o_first, o_q, o_k, o_v, o_heads, o_lse, o_w_a, o_w_b, o_params, o_att, o_tkv, o_square,
    o_second, o_query, o_crossed, o_self, o_cross, o_out, o_in, o_third, o_sum,
    hid_all, first, q_ref, k_ref, v_ref, heads, lse, w_a, w_b, params, att, tkv, sq_self, sq_cross,
    second, query_ref, crossed, after_self, after_cross, out_ref, in_ref,
    out_t, v_t, own_tkv, own_text, own_hid, fin_in, grad_all, win, wout,
    tokens, inner, slope, g_pre, terms, slots, out_w, inbox, sums, near, far,
    bias, cols_a, cols_b, square, placed, local, saved, send_sem, recv_sem,
):
    h = Here()
    w = Wire(h, send_sem, recv_sem)
    partners = frame_others(h) + clip_others(h)
    call_out(partners)
    length = clip_len[h.pair]
    tag = [0]

    def tags(n):
        tag[0] += n
        return tag[0] - n

    T_HID, T_A, T_B, T_FIN, T_AXY, T_BXY = tags(10), tags(7), tags(7), tags(3), tags(6), tags(6)
    T_SELF, T_CROSS, T_ATT, T_TKV, T_WIN, T_GRAD = tags(46), tags(46), tags(8), tags(3), tags(10), tags(6)
    T_TOK, T_WOUT, T_TERM, T_OSIB, T_OZ = tags(6), tags(10), tags(6), tags(4), tags(5)

    def my_columns(f):
        return pl.ds(pl.multiple_of(lax.rem(f, 4) * 256, 256), 256)

    def fin_part(c):
        return fin.at[:, pl.ds(pl.multiple_of(c * 1024, 1024), 1024)]

    spread = lax.broadcasted_iota(jnp.int32, (32, 128), 0) + 32 * lax.rem(h.f, 4)
    spread = jnp.where(spread == lax.broadcasted_iota(jnp.int32, (32, 128), 1), 1.0, 0.0).astype(BF16)
    placed[...] = jnp.zeros_like(placed)
    placed[0:3, :] = dot(gain[...], spread, (1, 0))
    placed[3:6, :] = dot(shift[...], spread, (1, 0))
    for q in range(8):
        group = placed[...] if q % 2 == 0 else jnp.zeros((16, 128), F32)
        cols_a[96:112, 128 * q : 128 * q + 128] = group.astype(BF16)
    for j in range(3):
        cols_a[32 * j : 32 * j + 32, :] = self_qkv[j]
    for j in range(2):
        cols_b[32 * j : 32 * j + 32, :] = cross_qkv[1 + j]
    square[0:32, :] = self_out[...]
    square[32:64, :] = cross_qkv[0]
    square[64:96, :] = cross_out[...]
    own = [
        pltpu.make_async_copy(src, dst, local.at[i])
        for i, (src, dst) in enumerate(
            (
                (cols_a.at[:, my_columns(h.f)], w_a.at[h.c, h.f]),
                (cols_b.at[:, my_columns(h.f)], w_b.at[h.c, h.f]),
                (hid.at[h.pair], hid_all.at[h.f]),
                (square.at[pl.ds(0, 32)], sq_self.at[h.c, h.f]),
                (fin_part(h.c), fin_in.at[h.c]),
                (text, own_text),
                (hid, own_hid),
                (grad, grad_all.at[h.c]),
                (fout, wout.at[h.f]),
                (square.at[pl.ds(32, 64)], sq_cross.at[h.c, h.f]),
            )
        )
    ]
    for copy in own:
        copy.start()
    saves = []

    def save(src, dst):
        copy = pltpu.make_async_copy(src, dst, saved.at[len(saves)])
        copy.start()
        saves.append(copy)

    hear_all(partners)

    own[0].wait()
    for d in (2, 6, 4, 3, 5, 1, 7):
        f = h.step(d)
        w.send(cols_a.at[:, my_columns(f)], w_a.at[h.c, h.f], T_A + d - 1, h.c, f)
    own[7].wait()
    grad_gather = ClipGather(w, lambda c, half: grad_all.at[c, pl.ds(128 * half, 128), :], T_GRAD)
    grad_gather.begin()
    for i, (c, f) in enumerate(clip_others(h)):
        w.send(fin_part(c), fin_in.at[h.c], T_FIN + i, c, f)
    w.send(hid.at[h.pair], hid_all.at[h.f], T_HID, h.c, h.sib)

    def half_of(ref, part):
        return ref.at[pl.ds(64 * part, 64), :]

    for d in range(1, 8):
        w.arrived(w_a.at[h.c, lax.rem(h.f + 8 - d, 8)], T_A + d - 1)
    a_gather = ClipGather(w, lambda c, half: w_a.at[c, pl.ds(4 * half, 4)], T_AXY)
    a_gather.begin()
    for part in range(2):
        w.send(
            half_of(hid.at[1 - h.pair], part),
            half_of(hid_all.at[h.f], part),
            T_HID + 3 + 2 * h.role + part,
            h.c,
            h.far_gate,
        )
        w.send(half_of(hid.at[h.pair], part), half_of(hid_all.at[h.f], part), T_HID + 1 + part, h.c, h.partner)
    own[3].wait()
    self_gather = MatrixGather(w, lambda c, f: sq_self.at[c, f], 32, T_SELF)
    self_gather.step(1)
    forwards = []
    for part in range(2):
        for j in range(2):
            block = half_of(hid_all.at[h.far[j]], part)
            w.arrived(block, T_HID + 3 + 2 * j + part)
            forward = w.copy(block, block, T_HID + 3 + 2 * j + part, h.c, h.partner)
            pl.when(h.is_gate)(forward.start)
            forwards.append(forward)
    self_gather.step(2)
    a_gather.middle()
    for part in range(2):
        w.arrived(half_of(hid_all.at[h.partner], part), T_HID + 1 + part)
    w.send(hid_all.at[h.partner], hid_all.at[h.partner], T_HID + 7, h.c, h.sib)
    for j in range(2):
        w.send(hid_all.at[h.far[j]], hid_all.at[h.far[j]], T_HID + 8 + j, h.c, h.sib)
    self_gather.step(3)
    own[1].wait()
    for d in (2, 6, 4, 3, 5, 1, 7):
        f = h.step(d)
        w.send(cols_b.at[:, my_columns(f)], w_b.at[h.c, h.f], T_B + d - 1, h.c, f)
    fill_key_bias(bias, clip_len, frame_mask, h.pair)
    text_bias = text_bias_rows(text_len, text_mask)
    self_gather.middle(0)
    self_gather.step(4)
    self_gather.middle(1)
    own[9].wait()
    cross_gather = MatrixGather(w, lambda c, f: sq_cross.at[c, f], 64, T_CROSS)
    a_gather.near()
    a_gather.end()
    grad_gather.middle()
    cross_gather.step(1)
    own[4].wait()
    for i, (c, f) in enumerate(clip_others(h)):
        w.arrived(fin_in.at[c], T_FIN + i)
    win_gather = ZGather(w, lambda f: win.at[:, f], T_WIN, fin_in)
    win_copy = pltpu.make_async_copy(fin_in, win.at[:, h.f], local.at[11])
    win_copy.start()
    win_gather.step(1)
    win_gather.relay(0)
    for g in range(8):
        group = sum(w_a[g // 2, 4 * (g % 2) + i, 96:104, 0:128].astype(F32) for i in range(4))
        params[:, 128 * g : 128 * g + 128] = group
    own[2].wait()
    w.arrived(hid_all.at[h.sib], T_HID)
    w.arrived(hid_all.at[h.partner + h.sib - h.f], T_HID + 7)
    for j in range(2):
        w.arrived(hid_all.at[h.far[j] + h.sib - h.f], T_HID + 8 + j)

    def project_rows(i, _):
        at = pl.ds(pl.multiple_of(i * 256, 256), 256)
        rows = hid_all[pl.ds(2 * i, 2)].reshape(256, 1024).astype(F32)
        xhat, _ = norm_parts(rows)
        low = (xhat * params[0:1, :] + params[3:4, :]).astype(BF16)
        first[at, :] = low
        for j, out in enumerate((q_ref, k_ref, v_ref)):
            out[at, :] = dot(low, column_weight(w_a, j), (1, 0)).astype(BF16)
        return 0

    lax.fori_loop(0, 2, project_rows, 0)
    self_gather.middle(2)
    for d in range(1, 8):
        w.arrived(w_b.at[h.c, lax.rem(h.f + 8 - d, 8)], T_B + d - 1)
    b_gather = ClipGather(w, lambda c, half: w_b.at[c, pl.ds(4 * half, 4)], T_BXY)
    b_gather.begin()
    cross_gather.step(2)
    lax.fori_loop(2, 4, project_rows, 0)
    v_t[...] = v_ref[...].T
    win_gather.step(2)
    self_gather.middle(3)
    cross_gather.step(3)
    b_gather.middle()

    def att_slot(f):
        return att.at[lax.div(f, 4), :, my_columns(f)]

    att_sends = []

    def attend_and_send(i):
        attend_rows(i, length, bias, q_ref, k_ref, v_t, heads, lse, out_t)
        for f in (2 * i, 2 * i + 1):
            block = heads.at[pl.ds(128 * f, 128), :]
            away = h.f != f
            copy = w.copy(block, att_slot(h.f), T_ATT + h.f, h.c, f)
            stay = pltpu.make_async_copy(block, att_slot(h.f), local.at[12])
            pl.when(away)(copy.start)
            pl.when(jnp.logical_not(away))(stay.start)
            att_sends.append((away, copy, stay))

    attend_and_send(3)
    def text_slot(f):
        return tkv.at[:, :, :, my_columns(f)]

    b_gather.near()
    b_gather.end()
    own[5].wait()
    for clip in range(2):
        for j in range(2):
            own_tkv[clip, j] = dot(own_text[clip], column_weight(w_b, j), (1, 0)).astype(BF16)
    w.send(own_tkv, text_slot(h.f), T_TKV, h.c, h.partner)
    w.send(own_tkv, text_slot(h.f), T_TKV + 1, h.c, h.sib)
    text_copy = pltpu.make_async_copy(own_tkv, text_slot(h.f), local.at[10])
    text_copy.start()
    cross_gather.step(4)
    win_gather.step(3)
    cross_gather.middle(0)
    attend_and_send(2)
    for d in range(4):
        self_gather.near(d)
        self_gather.last(d)
    cross_gather.middle(1)
    w.arrived(text_slot(h.partner), T_TKV)
    w.send(text_slot(h.partner), text_slot(h.partner), T_TKV + 2, h.c, h.sib)
    attend_and_send(1)
    win_gather.step(4)
    for d in range(1, 4):
        win_gather.relay(d)
    cross_gather.middle(2)
    attend_and_send(0)
    cross_gather.middle(3)
    for src, dst in (
        (hid_all, o_hid), (first, o_first), (q_ref, o_q), (k_ref, o_k), (v_ref, o_v), (heads, o_heads), (lse, o_lse),
        (w_a, o_w_a), (w_b, o_w_b), (params, o_params),
    ):
        save(src, dst)
    self_gather.end()
    for d in range(1, 8):
        f = lax.rem(h.f + 8 - d, 8)
        w.arrived(att_slot(f), T_ATT + f)
    for away, _, stay in att_sends:
        pl.when(jnp.logical_not(away))(stay.wait)

    own[6].wait()
    value = own_hid[...].reshape(256, 1024).astype(F32) + dot(
        att[...].reshape(256, 1024), square_of(sq_self, 0), (1, 0)
    )
    after_self[...] = value
    xhat, _ = norm_parts(value)
    second[...] = (xhat * params[1:2, :] + params[4:5, :]).astype(BF16)
    for d in range(4):
        cross_gather.near(d)
        cross_gather.last(d)
    cross_gather.end()
    query_ref[...] = dot(second[...], square_of(sq_cross, 0), (1, 0)).astype(BF16)
    w.arrived(text_slot(h.sib), T_TKV + 1)
    w.arrived(text_slot(h.partner + h.sib - h.f), T_TKV + 2)
    text_copy.wait()
    lane_head = lax.broadcasted_iota(jnp.int32, (128, 256), 1) // HD
    for clip in range(2):
        for group in range(4):
            rows, columns = pl.ds(128 * clip, 128), pl.ds(256 * group, 256)
            query = query_ref[rows, columns] * jnp.asarray(HD**-0.5, BF16)
            probs, _ = text_probs(query, tkv[clip, 0, :, columns], text_bias[clip], lane_head)
            part = dot(probs.astype(BF16), tkv[clip, 1, :, columns], (1, 0))
            crossed[rows, columns] = pick_heads(part, lane_head).astype(BF16)
    own[8].wait()
    out_gather = ZGather(w, lambda f: wout.at[f], T_WOUT)
    out_gather.step(1)
    out_gather.relay(0)
    value = after_self[...] + dot(crossed[...], square_of(sq_cross, 1), (1, 0))
    after_cross[...] = value
    xhat, _ = norm_parts(value)
    tokens[h.c] = (xhat * params[2:3, :] + params[5:6, :]).astype(BF16)

    token_gather = ClipGather(w, lambda c, half: tokens.at[c, pl.ds(128 * half, 128), :], T_TOK)
    token_gather.begin()
    for src, dst in (
        (att, o_att), (tkv, o_tkv), (second, o_second), (query_ref, o_query), (crossed, o_crossed),
        (after_self, o_self), (after_cross, o_cross),
    ):
        save(src, dst)
    save(sq_self, o_square.at[0])
    for which in range(2):
        save(sq_cross.at[:, :, pl.ds(32 * which, 32), :], o_square.at[1 + which])
    win_copy.wait()
    win_gather.end()

    def hidden(c):
        for part in range(2):
            rows = pl.ds(128 * part, 128)
            pre = dot(tokens[c, rows, :], win[...].reshape(1024, 1024), (1, 0))
            cdf = 0.5 * (1.0 + lax.erf(pre * (0.5**0.5)))
            inner[c, rows, :] = (pre * cdf).astype(BF16)
            slope[c, rows, :] = cdf + pre * jnp.exp(-0.5 * pre * pre) * 0.3989422804014327

    def hidden_back(c):
        g_inner = dot(grad_all[c], wout[...].reshape(1024, 1024), (1, 1))
        g_pre[c] = (g_inner * slope[c]).astype(BF16)
        terms[c] = dot(g_pre[c], win[...].reshape(1024, 1024), (1, 1)).astype(BF16)

    def out_terms(c):
        out_ref[c] = dot(inner[c], wout[...].reshape(1024, 1024), (1, 0)).astype(BF16)

    sibling = SiblingSum(w, lambda f: out_w.at[f], lambda z: inbox.at[z], lambda z: sums.at[z], T_OSIB)
    z_scatter = ZScatter(w, sums, near, far, T_OZ)
    tall = (1024, 1024)

    def out_weight(i, _):
        columns = pl.ds(pl.multiple_of(i * 256, 256), 256)
        out = dot(inner[:, :, columns].reshape(1024, 256), grad_all[...].reshape(tall), (0, 0))
        out_w[pl.ds(2 * i, 2)] = out.astype(BF16).reshape(2, 128, 1024)
        return 0

    def in_weight(i, _):
        columns = pl.ds(pl.multiple_of(i * 256, 256), 256)
        out = dot(tokens[:, :, columns].reshape(1024, 256), g_pre[...].reshape(tall), (0, 0))
        in_ref[:, pl.ds(pl.multiple_of(32 * i, 32), 32), :] = out.astype(BF16).reshape(8, 32, 1024)
        return 0

    hidden(h.c)
    out_gather.step(2)
    grad_gather.near()
    grad_gather.end()
    token_gather.middle()
    token_gather.near()
    out_gather.step(3)
    hidden(h.cx)
    hidden(h.cy)
    out_gather.step(4)
    for d in range(1, 4):
        out_gather.relay(d)
    token_gather.end()
    hidden(h.cd)
    lax.fori_loop(0, 4, out_weight, 0)
    sibling.begin()
    out_gather.end()
    scatter = ClipScatter(
        w, lambda c, half: terms.at[c, pl.ds(128 * half, 128), :], [slots.at[i] for i in range(6)], T_TERM
    )
    hidden_back(h.cd)
    scatter.begin(0)
    sibling.end()
    z_scatter.begin()
    hidden_back(h.cx)
    hidden_back(h.cy)
    scatter.begin(1)
    hidden_back(h.c)
    scatter.middle()
    z_scatter.step(1)
    lax.fori_loop(0, 2, in_weight, 0)
    lax.fori_loop(2, 4, in_weight, 0)
    save(in_ref, o_in)
    out_terms(0)
    z_scatter.step(2)
    z_scatter.step(3)
    out_terms(1)
    out_terms(2)
    out_terms(3)
    save(out_ref, o_out)
    scatter.end()
    for half in range(2):
        o_third[128 * half : 128 * half + 128, :] = scatter.total(half)
    z_scatter.total(o_sum)
    w.drain()
    for copy in forwards:
        pl.when(h.is_gate)(copy.wait_send)
    for away, copy, _ in att_sends:
        pl.when(away)(copy.wait_send)
    for one in (self_gather.z, cross_gather.z, win_gather, out_gather, z_scatter):
        one.drain()
    for copy in saves:
        copy.wait()


def forward(*args):
    column, rows, full, quarter = (1024, 256), (256, 1024), (4, 256, 1024), (4, 128, 1024)
    kept = [
        shape((8, 128, 1024)),
        shape((1024, 1024)),
        shape(column),
        shape(column),
        shape(column),
        shape(column),
        shape((8, 1024), F32),
        shape((4, 8, 112, 256)),
        shape((4, 8, 64, 256)),
        shape((8, 1024), F32),
        shape((2, 128, 1024)),
        shape((2, 2, 128, 1024)),
        shape((4, 8, 96, 1024)),
        shape(rows),
        shape(rows),
        shape(rows),
        shape(rows, F32),
        shape(rows, F32),
        shape(full),
        shape((8, 128, 1024)),
    ]
    scratch = [pltpu.VMEM(one.shape, one.dtype) for one in kept]
    scratch[12:13] = [pltpu.VMEM((4, 8, rows, 1024), BF16) for rows in (32, 64)]
    kept[12] = shape((3, 4, 8, 32, 1024))
    return comm_call(
        forward_body,
        tuple(kept) + (shape(rows, F32), shape((128, 1024), F32)),
        [SMEM] * 2 + [VMEM] * 8 + [HBM] * 5,
        (HBM,) * len(kept) + (VMEM,) * 2,
        scratch
        + [
            pltpu.VMEM((256, ROWS), F32),
            pltpu.VMEM((256, 1024), BF16),
            pltpu.VMEM((2, 2, 128, 256), BF16),
            pltpu.VMEM((2, 128, 1024), BF16),
            pltpu.VMEM((2, 128, 1024), BF16),
            pltpu.VMEM((4, 32, 1024), BF16),
            pltpu.VMEM(full, BF16),
            pltpu.VMEM((4, 8, 32, 1024), BF16),
            pltpu.VMEM((8, 128, 1024), BF16),
            pltpu.VMEM(full, BF16),
            pltpu.VMEM(full, BF16),
            pltpu.VMEM(full, F32),
            pltpu.VMEM(full, BF16),
            pltpu.VMEM(full, BF16),
            pltpu.VMEM((6, 128, 1024), BF16),
            pltpu.VMEM((8, 128, 1024), BF16),
            pltpu.VMEM(quarter, BF16),
            pltpu.VMEM(quarter, BF16),
            pltpu.VMEM((3, 128, 1024), BF16),
            pltpu.VMEM((2, 128, 1024), BF16),
            pltpu.VMEM((1024, 128), F32),
            pltpu.VMEM((112, 1024), BF16),
            pltpu.VMEM((64, 1024), BF16),
            pltpu.VMEM((96, 1024), BF16),
            pltpu.VMEM((16, 128), F32),
            pltpu.SemaphoreType.DMA((13,)),
            pltpu.SemaphoreType.DMA((24,)),
        ],
        216,
        192,
        1,
    )(*args)


def attend_back_rows(i, length, bias, q_ref, k_ref, v_ref, o_ref, lse_ref, g_ref, dq_ref, dq_t, k_t, dk, dv):
    lane_head = lax.broadcasted_iota(jnp.int32, (ROWS, 256), 1) // HD
    first, n = i * ROWS, (i + 1) * ROWS
    q = q_ref[first:n, :] * jnp.asarray(HD**-0.5, BF16)
    live = first + lax.broadcasted_iota(jnp.int32, (ROWS, 256), 0) < length
    g = jnp.where(live, g_ref[first:n, :], 0)
    both = (g.astype(F32) * o_ref[first:n, :].astype(F32)).T
    row_dots = jnp.concatenate(
        [jnp.sum(both[HD * j : HD * j + HD], axis=0, keepdims=True) for j in range(4)], axis=0
    )
    lse = lse_ref[0:4, first:n]

    def pick(rows, j):
        at = lax.broadcasted_iota(jnp.int32, rows.shape, 0) == j
        return jnp.sum(jnp.where(at, rows, 0), axis=0, keepdims=True)

    def head(j, _):
        q_head = jnp.where(lane_head == j, q, 0)
        g_head = jnp.where(lane_head == j, g, 0)
        scores = mask_scores(dot(k_ref[0:n, :], q_head, (1, 1)), bias, first, ROWS)
        probs = jnp.exp(scores - pick(lse, j))
        grads = dot(v_ref[0:n, :], g_head, (1, 1))
        dlogits = (probs * (grads - pick(row_dots, j))).astype(BF16)
        dv[0:n, :] += dot(probs.astype(BF16), g_head, (1, 0))
        dk[0:n, :] += dot(dlogits, q_head, (1, 0))
        at = pl.ds(pl.multiple_of(j * HD, HD), HD)
        dq_t[at, :] = dot(k_t[at, 0:n], dlogits, (1, 0))
        return 0

    lax.fori_loop(0, 4, head, 0, unroll=True)
    dq_ref[first:n, :] = (dq_t[...].T * (HD**-0.5)).astype(BF16)


def norm_back(xhat, scale, grad, gain):
    h = grad * gain
    return scale * (
        h
        - jnp.mean(h, axis=-1, keepdims=True)
        - xhat * jnp.mean(h * xhat, axis=-1, keepdims=True)
    )


def backward_body(
    clip_len, text_len, frame_mask, text_mask, norms_in,
    h_third, h_out, h_cross, h_self, h_second, h_query, h_crossed, h_att, h_square, h_tkv, h_out_terms, h_in_terms,
    h_q, h_k, h_v, h_o, h_lse, h_hid, h_first, h_wa, h_wb, h_text, h_own,
    o_output, o_in, o_hidden, o_square, o_qkv, o_ckv, o_norm, o_text,
    v_third, v_out, after_cross, query_ref, crossed, att, mats, tkv, out_terms,
    q_ref, k_ref, v_ref, o_ref, lse, w_a, w_b, text_in,
    g_crossed, g_att, g_after, slots, t_inbox, t_near, t_far, t_total,
    i_inbox, i_near, i_far, i_out, i_in,
    g_square, s_inbox, s_slots, s_part, y_part, z_near, z_far, y_near, y_far,
    g_heads, dq_t, k_t, dk, dv, d_cols, f_inbox, f_in,
    a_terms, a_slots, a_sum, a_in, b_terms, b_slots, b_sum, b_in,
    t_terms, tt_in, n_row, n_terms, n_slots, n_sum, n_in,
    bias, loaded, local, send_sem, recv_sem,
):
    h = Here()
    w = Wire(h, send_sem, recv_sem)
    partners = frame_others(h) + clip_others(h)
    call_out(partners)
    length = clip_len[h.pair]
    tag = [0]

    def tags(n):
        tag[0] += n
        return tag[0] - n

    loads = []

    def load(src, dst):
        copy = pltpu.make_async_copy(src, dst, loaded.at[len(loads)])
        copy.start()
        loads.append(copy)
        return copy

    l_terms = load(h_out_terms, out_terms)
    own_terms = [mats.at[0, z, pl.ds(0, 4)] for z in range(4)]
    l_own = [load(h_in_terms.at[2 * z + h.core], own_terms[z]) for z in range(4)]
    l_third, l_cross = load(h_third, v_third), load(h_cross, after_cross)
    l_out, l_m2 = load(h_out, v_out), load(h_square.at[2], mats.at[2])
    l_middle = [load(*pair) for pair in ((h_crossed, crossed), (h_query, query_ref), (h_tkv, tkv))]
    l_m1 = load(h_square.at[1], mats.at[1])
    l_att = load(h_att, att)
    l_heads = [
        load(*pair)
        for pair in (
            (h_q, q_ref), (h_k, k_ref), (h_v, v_ref), (h_o, o_ref), (h_lse, lse), (h_wb, w_b), (h_text, text_in),
            (h_wa, w_a),
        )
    ]
    fill_key_bias(bias, clip_len, frame_mask, h.pair)
    text_bias = text_bias_rows(text_len, text_mask)
    hear_all(partners)

    def matrix(which):
        return mats[which].reshape(1024, 1024)

    out_scatter = ClipScatter(
        w,
        lambda c, half: out_terms.at[c, pl.ds(128 * half, 128), :],
        [slots.at[i] for i in range(6)],
        tags(6),
    )
    in_tag = tags(4)
    for z in range(4):
        w.send(h_in_terms.at[2 * z + 1 - h.core], i_inbox.at[z], in_tag + z, h.c, h.sib)
    in_scatter = ZScatter(w, i_inbox, i_near, i_far, tags(5))
    l_terms.wait()
    out_scatter.begin()

    def square_sums(which):
        sibling = SiblingSum(
            w,
            lambda f: g_square.at[which, :, f],
            lambda z: s_inbox.at[which, z],
            lambda z: s_inbox.at[which, z],
            tags(4),
        )
        clip = ClipScatter(
            w,
            lambda c, half: s_inbox.at[which, :, c, pl.ds(16 * half, 16), :],
            [s_slots.at[which, i] for i in range(6)],
            tags(6),
        )
        return sibling, clip

    squares = [square_sums(which) for which in range(3)]

    def put(which, value):
        g_square[which] = value.astype(BF16).reshape(4, 8, 32, 1024)

    def columns_of(f):
        return pl.ds(pl.multiple_of(lax.rem(f, 4) * 256, 256), 256)

    def part_of(f):
        return g_att.at[lax.div(f, 4), :, columns_of(f)]

    def text_part(f):
        return g_text.at[lax.div(f, 4), :, :, columns_of(f)]

    for copy in (l_third, l_cross, l_out):
        copy.wait()
    xhat, scale = norm_parts(after_cross[...])
    grad = v_third[...]
    gain_third = jnp.sum(grad * xhat, axis=0, keepdims=True)
    shift_third = jnp.sum(grad, axis=0, keepdims=True)
    n_row[...] = jnp.zeros_like(n_row)
    n_row[2:3, :] = gain_third
    n_row[5:6, :] = shift_third
    g_after_cross = v_out[...].reshape(256, 1024).astype(F32) + norm_back(xhat, scale, grad, norms_in[2:3, :])
    g_after[...] = g_after_cross
    after_self, own_hid = v_third, v_out
    l_self, l_own_hid = load(h_self, after_self), load(h_own, own_hid)
    branch = g_after_cross.astype(BF16)
    l_m2.wait()
    g_crossed[...] = dot(branch, matrix(2), (1, 1)).astype(BF16)
    l_first = load(h_first, mats.at[2])
    for copy in l_middle + l_own:
        copy.wait()
    put(2, dot(crossed[...], branch, (0, 0)))
    squares[2][0].begin()
    second = crossed
    l_second = load(h_second, second)
    for z in range(4):
        w.arrived(i_inbox.at[z], in_tag + z)
        add_into(i_inbox.at[z], own_terms[z])
    in_scatter.begin()
    l_m0 = load(h_square.at[0], mats.at[0])
    g_query, g_text = query_ref, tkv
    lane_head = lax.broadcasted_iota(jnp.int32, (128, 256), 1) // HD
    for clip in range(2):
        for group in range(4):
            rows, columns = pl.ds(128 * clip, 128), pl.ds(256 * group, 256)
            keys, values = tkv[clip, 0, :, columns], tkv[clip, 1, :, columns]
            query = query_ref[rows, columns] * jnp.asarray(HD**-0.5, BF16)
            probs, stacked = text_probs(query, keys, text_bias[clip], lane_head)
            grads = g_crossed[rows, columns]
            g_stacked = jnp.concatenate([jnp.where(lane_head == j, grads, 0) for j in range(4)], axis=0)
            g_probs = dot(g_stacked, values, (1, 1))
            row_dot = jnp.sum(probs * g_probs, axis=1, keepdims=True)
            g_logits = (probs * (g_probs - row_dot)).astype(BF16)
            part = dot(g_logits, keys, (1, 0))
            g_query[rows, columns] = (pick_heads(part, lane_head) * (HD**-0.5)).astype(BF16)
            g_text[clip, 0, :, columns] = dot(g_logits, stacked, (0, 0)).astype(BF16)
            g_text[clip, 1, :, columns] = dot(probs.astype(BF16), g_stacked, (0, 0)).astype(BF16)
        if clip == 0:
            out_scatter.middle()
            in_scatter.step(1)
            squares[2][0].end()
            squares[2][1].begin()
    text_sibling = SiblingSum(w, text_part, lambda z: t_inbox.at[z], lambda z: t_inbox.at[z], tags(4))
    text_sibling.begin()
    l_m1.wait()
    grad = dot(g_query[...], matrix(1), (1, 1))
    l_hid = load(h_hid, mats.at[1])
    l_self.wait()
    xhat, scale = norm_parts(after_self[...])
    n_row[1:2, :] = jnp.sum(grad * xhat, axis=0, keepdims=True)
    n_row[4:5, :] = jnp.sum(grad, axis=0, keepdims=True)
    g_after_self = g_after[...] + norm_back(xhat, scale, grad, norms_in[1:2, :])
    g_after[...] = g_after_self
    branch = g_after_self.astype(BF16)
    l_m0.wait()
    g_att[...] = dot(branch, matrix(0), (1, 1)).astype(BF16).reshape(2, 128, 1024)
    heads_tag = tags(7)
    for d in (4, 2, 6, 3, 5, 1, 7):
        f = h.step(d)
        w.send(part_of(f), g_heads.at[h.f], heads_tag + d - 1, h.c, f)
    own_part = pltpu.make_async_copy(part_of(h.f), g_heads.at[h.f], local.at[0])
    own_part.start()
    in_scatter.step(2)
    in_scatter.step(3)
    l_second.wait()
    l_att.wait()
    put(1, dot(second[...], g_query[...], (0, 0)))
    squares[1][0].begin()
    put(0, dot(att[...].reshape(256, 1024), branch, (0, 0)))
    squares[0][0].begin()
    text_sibling.end()
    text_scatter = ZScatter(w, t_inbox, t_near, t_far, tags(5))
    text_scatter.begin()
    squares[2][1].middle()
    squares[1][0].end()
    squares[1][1].begin()
    out_scatter.end()
    for half in range(2):
        rows = pl.ds(128 * half, 128)
        o_output[rows, :] = (after_cross[rows, :] + out_scatter.total(half)).astype(BF16)
    squares[0][0].end()
    squares[0][1].begin()
    in_scatter.total(i_out)
    i_tag = tags(3)
    for i, (c, f) in enumerate(clip_others(h)):
        w.send(i_out.at[c], i_in.at[h.c], i_tag + i, c, f)
    i_in[h.c] = i_out[h.c]
    squares[1][1].middle()

    def square_part(which, out, row):
        squares[which][1].end()
        for half in range(2):
            total = squares[which][1].total(half)
            out[:, row + 16 * half : row + 16 * half + 16, :] = total.astype(BF16)

    text_scatter.step(1)
    for copy in l_heads:
        copy.wait()
    k_t[...] = k_ref[...].T
    dk[...] = jnp.zeros_like(dk)
    dv[...] = jnp.zeros_like(dv)
    for d in range(1, 8):
        w.arrived(g_heads.at[lax.rem(h.f + 8 - d, 8)], heads_tag + d - 1)
    own_part.wait()
    g_rows = g_heads[...].reshape(1024, 256)

    def rows_back(i):
        attend_back_rows(
            i, length, bias, q_ref, k_ref, v_ref, o_ref, lse, g_rows, d_cols.at[0], dq_t, k_t, dk, dv
        )

    text_scatter.step(2)
    text_scatter.step(3)
    squares[0][1].middle()
    rows_back(0)
    square_part(2, s_part, 32)
    square_part(1, s_part, 0)
    z_scatter = ZScatter(w, s_part, z_near, z_far, tags(5))
    z_scatter.begin()
    rows_back(1)

    class Columns:
        def __init__(self, terms, slots, sums, inbox):
            self.sums, self.inbox, self.tag = sums, inbox, tags(13)
            self.clip = ClipScatter(
                w,
                lambda c, half: terms.at[c, pl.ds(4 * half, 4)],
                [slots.at[i] for i in range(6)],
                self.tag,
            )

        def spread(self):
            self.clip.end()
            for half in range(2):
                self.sums[4 * half : 4 * half + 4] = self.clip.total(half).astype(BF16)
            for d in (4, 2, 6, 3, 5, 1, 7):
                f = h.step(d)
                w.send(self.sums.at[f], self.inbox.at[h.f], self.tag + 5 + d, h.c, f)
            self.inbox[h.f] = self.sums[h.f]

        def wait(self):
            for d in range(1, 8):
                w.arrived(self.inbox.at[lax.rem(h.f + 8 - d, 8)], self.tag + 5 + d)

    text_scatter.total(t_total)
    g_tkv = [t_total[j].astype(BF16) for j in range(2)]
    text = text_in[h.pair]
    for j in range(2):
        b_terms[:, :, 32 * j : 32 * j + 32, :] = (
            dot(text, g_tkv[j], (0, 0)).astype(BF16).reshape(4, 8, 32, 256)
        )
    b_columns = Columns(b_terms, b_slots, b_sum, b_in)
    b_columns.clip.begin()
    t_terms[...] = (
        dot(g_tkv[0], column_weight(w_b, 0), (1, 1)) + dot(g_tkv[1], column_weight(w_b, 1), (1, 1))
    ).astype(BF16)
    tt_tag = tags(7)
    for d in range(1, 8):
        f = h.step(d)
        w.send(
            t_terms.at[pl.ds(pl.multiple_of(f * 16, 16), 16), :], tt_in.at[h.f], tt_tag + d - 1, h.c, f
        )
    tt_in[h.f] = t_terms[pl.ds(pl.multiple_of(h.f * 16, 16), 16), :]
    z_scatter.step(1)
    rows_back(2)
    square_part(0, y_part, 0)
    y_scatter = ZScatter(w, y_part, y_near, y_far, tags(5))
    y_scatter.begin()
    z_scatter.step(2)
    z_scatter.step(3)
    b_columns.clip.middle()
    rows_back(3)
    d_cols[1] = dk[...].astype(BF16)
    d_cols[2] = dv[...].astype(BF16)
    l_first.wait()
    a_columns = [Columns(a_terms.at[j], a_slots.at[j], a_sum.at[j], a_in.at[j]) for j in range(3)]
    for j in range(3):
        a_terms[j] = dot(mats[2].reshape(1024, 1024), d_cols[j], (0, 0)).astype(BF16).reshape(4, 8, 32, 256)
        a_columns[j].clip.begin()
    y_scatter.step(1)

    f_terms = mats.at[0]
    f_sibling = SiblingSum(
        w,
        lambda f: f_terms.at[lax.div(f, 2), pl.ds(pl.multiple_of(lax.rem(f, 2) * 4, 4), 4)],
        lambda z: f_inbox.at[z],
        lambda z: f_inbox.at[z],
        tags(4),
    )
    l_hid.wait()

    def frame_terms(i, _):
        rows = pl.ds(pl.multiple_of(i * 256, 256), 256)
        grad = sum(dot(d_cols[j, rows, :], column_weight(w_a, j), (1, 1)) for j in range(3))
        f_terms[i] = grad.astype(BF16).reshape(8, 32, 1024)
        xhat, _ = norm_parts(mats[1, i].reshape(256, 1024).astype(F32))
        n_row[0:1, :] += jnp.sum(grad * xhat, axis=0, keepdims=True)
        n_row[3:4, :] += jnp.sum(grad, axis=0, keepdims=True)
        return 0

    lax.fori_loop(0, 4, frame_terms, 0)
    f_sibling.begin()
    y_scatter.step(2)
    a_columns[0].clip.middle()
    f_sibling.end()
    f_tag = tags(4)
    other = 2 * (1 - h.pair)
    is_end = jnp.logical_not(h.is_gate)
    to_gate, to_far = [], []
    for j in range(2):
        to_gate.append(w.copy(f_inbox.at[other + j], f_in.at[1 + j], f_tag + 1 + j, h.c, h.partner))
        pl.when(is_end)(to_gate[j].start)
    w.send(f_inbox.at[lax.div(h.partner, 2)], f_in.at[0], f_tag, h.c, h.partner)
    for c in range(4):
        for f in range(8):
            group = 2 * c + f // 4
            n_terms[c, f] = n_row[:, 128 * group : 128 * group + 128].astype(BF16)
    n_columns = Columns(n_terms, n_slots, n_sum, n_in)
    n_columns.clip.begin()
    a_columns[1].clip.middle()
    a_columns[0].spread()
    for j in range(2):

        @pl.when(h.is_gate)
        def _():
            w.arrived(f_in.at[1 + j], f_tag + 1 + j)
            add_into(f_inbox.at[other + j], f_in.at[1 + j])

        to_far.append(w.copy(f_inbox.at[other + j], f_in.at[3], f_tag + 3, h.c, h.far[j]))
        pl.when(h.is_gate)(to_far[j].start)
    a_columns[2].clip.middle()
    a_columns[1].spread()
    n_columns.clip.middle()
    y_scatter.step(3)
    a_columns[2].spread()
    n_columns.spread()
    b_columns.spread()
    z_scatter.total(o_square.at[pl.ds(32, 64), :])
    for i, (c, f) in enumerate(clip_others(h)):
        w.arrived(i_in.at[c], i_tag + i)
    for c in range(4):
        o_in[:, 1024 * c : 1024 * c + 1024] = i_in[c].astype(F32)
    for d in range(1, 8):
        w.arrived(tt_in.at[lax.rem(h.f + 8 - d, 8)], tt_tag + d - 1)
    for p in range(2):
        o_text[p] = sum(tt_in[4 * p + q].astype(F32) for q in range(4)).astype(BF16)
    y_scatter.total(o_square.at[pl.ds(0, 32), :])
    w.arrived(f_in.at[0], f_tag)
    w.arrived(f_in.at[3], f_tag + 3)

    def hidden_out(clip, total):
        xhat, scale = norm_parts(own_hid[clip].astype(F32))
        rows = pl.ds(pl.multiple_of(clip * 128, 128), 128)
        o_hidden[clip] = (g_after[rows, :] + norm_back(xhat, scale, total, norms_in[0:1, :])).astype(BF16)

    l_own_hid.wait()
    hidden_out(h.pair, (f_inbox[h.z].astype(F32) + f_in[0].astype(F32)).reshape(128, 1024))
    hidden_out(1 - h.pair, f_in[3].astype(F32).reshape(128, 1024))
    for j in range(3):
        a_columns[j].wait()
        for q in range(4):
            o_qkv[j, :, 256 * q : 256 * q + 256] = a_in[j, q].astype(F32) + a_in[j, 4 + q].astype(F32)
    b_columns.wait()
    for j in range(2):
        for q in range(4):
            at = pl.ds(32 * j, 32)
            o_ckv[j, :, 256 * q : 256 * q + 256] = b_in[q, at, :].astype(F32) + b_in[4 + q, at, :].astype(F32)
    n_columns.wait()
    o_norm[...] = sum(n_in[f].astype(F32) for f in range(8))
    w.drain()
    for one in (in_scatter, text_scatter, z_scatter, y_scatter):
        one.drain()
    for j in range(2):
        pl.when(is_end)(to_gate[j].wait_send)
        pl.when(h.is_gate)(to_far[j].wait_send)


def backward(*args):
    def buffer(*dims):
        return pltpu.VMEM(dims, BF16)

    def full(*dims):
        return pltpu.VMEM(dims, F32)

    return comm_call(
        backward_body,
        (
            shape((256, 1024)),
            shape((32, 4096), F32),
            shape((2, 128, 1024)),
            shape((96, 1024), F32),
            shape((3, 32, 1024), F32),
            shape((2, 32, 1024), F32),
            shape((16, 128), F32),
            shape((2, 16, 1024)),
        ),
        [SMEM] * 2 + [VMEM] * 3 + [HBM] * 23,
        (VMEM,) * 8,
        [
            full(256, 1024), buffer(2, 128, 1024), full(256, 1024), buffer(256, 1024), buffer(256, 1024),
            buffer(2, 128, 1024), buffer(3, 4, 8, 32, 1024), buffer(2, 2, 128, 1024), buffer(4, 256, 1024),
            buffer(1024, 256), buffer(1024, 256), buffer(1024, 256), buffer(1024, 256), full(8, 1024),
            buffer(4, 8, 112, 256), buffer(4, 8, 64, 256), buffer(2, 128, 1024),
            buffer(256, 1024), buffer(2, 128, 1024), full(256, 1024),
            buffer(6, 128, 1024), buffer(4, 2, 128, 256), buffer(3, 2, 128, 256), buffer(2, 2, 128, 256),
            full(2, 128, 256),
            buffer(4, 4, 32, 1024), buffer(3, 4, 32, 1024), buffer(2, 4, 32, 1024),
            buffer(4, 32, 1024), buffer(4, 32, 1024),
            buffer(3, 4, 8, 32, 1024), buffer(3, 4, 4, 32, 1024), buffer(3, 6, 4, 16, 1024),
            buffer(4, 64, 1024), buffer(4, 32, 1024), buffer(3, 64, 1024), buffer(2, 64, 1024),
            buffer(3, 32, 1024), buffer(2, 32, 1024),
            buffer(8, 128, 256), full(256, ROWS), buffer(256, 1024), full(1024, 256), full(1024, 256),
            buffer(3, 1024, 256), buffer(4, 4, 32, 1024), buffer(4, 4, 32, 1024),
            buffer(3, 4, 8, 32, 256), buffer(3, 6, 4, 32, 256), buffer(3, 8, 32, 256), buffer(3, 8, 32, 256),
            buffer(4, 8, 64, 256), buffer(6, 4, 64, 256), buffer(8, 64, 256), buffer(8, 64, 256),
            buffer(128, 1024), buffer(8, 16, 1024), full(16, 1024), buffer(4, 8, 16, 128), buffer(6, 4, 16, 128),
            buffer(8, 16, 128), buffer(8, 16, 128), full(1024, 128),
            pltpu.SemaphoreType.DMA((32,)),
            pltpu.SemaphoreType.DMA((1,)),
        ],
        208,
        160,
        2,
    )(*args)


def finish_body(*refs):
    ins, outs = refs[:9], refs[9:]
    output, hidden, text, qkv, square, ckv, fin, fout, norm = ins
    o_output, o_hidden, o_text, o_qkv, o_self_out, o_cross, o_cross_out, o_fin, o_fout, o_gain, o_shift = outs
    o_fout[...] = fout[...]
    o_output[...] = output[...].reshape(2, 128, 1024)
    o_hidden[...] = hidden[...]
    o_text[...] = text[...]
    o_fin[...] = fin[...]
    o_qkv[...] = qkv[...]
    o_self_out[...] = square[0:32, :]
    o_cross[0] = square[32:64, :]
    o_cross[1:3] = ckv[...]
    o_cross_out[...] = square[64:96, :]
    place = lax.rem(lax.axis_index("frame"), 4)
    for row, out in ((0, o_gain), (3, o_shift)):
        out[...] = sum(
            jnp.where(place == i, norm[row : row + 3, 32 * i : 32 * i + 32], 0) for i in range(4)
        )


def finish(*args):
    return pl.pallas_call(
        finish_body,
        out_shape=(
            shape((2, 128, 1024)),
            shape((2, 128, 1024)),
            shape((2, 16, 1024)),
            shape((3, 32, 1024), F32),
            shape((32, 1024), F32),
            shape((3, 32, 1024), F32),
            shape((32, 1024), F32),
            shape((32, 4096), F32),
            shape((128, 1024), F32),
            shape((3, 32), F32),
            shape((3, 32), F32),
        ),
        in_specs=[VMEM] * 9,
        out_specs=(VMEM,) * 11,
        compiler_params=pltpu.CompilerParams(vmem_limit_bytes=60 * 2**20),
    )(*args)


def on_device_fast(
    hidden_in,
    text_states,
    out_grad,
    self_qkv,
    self_out,
    cross_qkv,
    cross_out,
    ffn_in,
    ffn_out,
    ln_gain,
    ln_bias,
    clip_len,
    frame_mask,
    text_len,
    text_mask,
):
    (
        hid_all, first_low, query, key, value, att_heads, lse, w_a, w_b, params, att, tkv, square,
        second, cross_query, crossed, after_self, after_cross, out_terms, in_terms, third_sum, grad_ffn_out,
    ) = forward(
        clip_len, text_len, frame_mask, text_mask, ln_gain, ln_bias, jnp.moveaxis(self_qkv, 1, 0),
        jnp.moveaxis(cross_qkv, 1, 0), self_out, cross_out, text_states, hidden_in, ffn_in, ffn_out, out_grad.reshape(256, 1024),
    )
    output, grad_ffn_in, grad_hidden, square_sum, qkv_sum, ckv_sum, norm_sum, grad_text = backward(
        clip_len, text_len, frame_mask, text_mask, params,
        third_sum, out_grad, after_cross, after_self, second, cross_query, crossed, att, square, tkv,
        out_terms, in_terms.reshape(8, 4, 32, 1024), query, key, value, att_heads, lse,
        hid_all.reshape(4, 8, 32, 1024), first_low.reshape(4, 8, 32, 1024), w_a, w_b, text_states, hidden_in,
    )
    results = finish(output, grad_hidden, grad_text, qkv_sum, square_sum, ckv_sum, grad_ffn_in, grad_ffn_out, norm_sum)
    output, grad_hidden, grad_text, qkv, g_self_out, cross, g_cross_out, grad_ffn_in, grad_ffn_out, gains, shifts = results
    return (
        output,
        grad_hidden,
        grad_text,
        jnp.moveaxis(qkv, 0, 1),
        g_self_out,
        jnp.moveaxis(cross, 0, 1),
        g_cross_out,
        grad_ffn_in,
        grad_ffn_out,
        gains,
        shifts,
    )


def solution(mesh):
    return jax.shard_map(
        on_device_fast if fits(mesh) else on_device_any,
        mesh=mesh,
        in_specs=(
            P("clip", "frame", None),
            P("clip", None, None),
            P("clip", "frame", None),
            P(("clip", "frame"), None, None),
            P(("clip", "frame"), None),
            P(("clip", "frame"), None, None),
            P(("clip", "frame"), None),
            P(("clip", "frame"), None),
            P(("clip", "frame"), None),
            P(None, ("clip", "frame")),
            P(None, ("clip", "frame")),
            P("clip"),
            P("clip", None),
            P("clip"),
            P("clip", None),
        ),
        out_specs=(
            P("clip", "frame", None),
            P("clip", "frame", None),
            P("clip", "frame", None),
            P(("clip", "frame"), None, None),
            P(("clip", "frame"), None),
            P(("clip", "frame"), None, None),
            P(("clip", "frame"), None),
            P(("clip", "frame"), None),
            P(("clip", "frame"), None),
            P(None, ("clip", "frame")),
            P(None, ("clip", "frame")),
        ),
        check_vma=False,
    )
```

```python
import functools

import jax
import jax.numpy as jnp
from jax import lax
from jax.experimental import pallas as pl
from jax.experimental.pallas import tpu as pltpu
from jax.sharding import PartitionSpec as P

HD = 64


MASKED = -1000000000.0
EPSILON = 1e-05


def layer_norm(value, gain, shift):
    average = jnp.mean(value, axis=-1, keepdims=True)
    centered = value - average
    variance = jnp.mean(centered * centered, axis=-1, keepdims=True)
    return centered * lax.rsqrt(variance + EPSILON) * gain + shift


def activate(value):
    return jax.nn.gelu(value, approximate=False)


def project(left, right):
    return jnp.einsum("cnd,de->cne", left, right, preferred_element_type=jnp.float32)


def project_back(grad_rows, weight):
    return jnp.einsum("cne,de->cnd", grad_rows, weight, preferred_element_type=jnp.float32)


def weight_grad(left, right):
    return jnp.einsum("cnd,cne->de", left, right, preferred_element_type=jnp.float32)


def fetch_attention(self_qkv, self_out, cross_qkv, cross_out, ln_gain, ln_bias):
    return (
        lax.all_gather(self_qkv, ("clip", "frame"), axis=0, tiled=True),
        lax.all_gather(self_out, ("clip", "frame"), axis=0, tiled=True),
        lax.all_gather(cross_qkv, ("clip", "frame"), axis=0, tiled=True),
        lax.all_gather(cross_out, ("clip", "frame"), axis=0, tiled=True),
        lax.all_gather(ln_gain, ("clip", "frame"), axis=1, tiled=True),
        lax.all_gather(ln_bias, ("clip", "frame"), axis=1, tiled=True),
    )


def fetch_ffn(ffn_in, ffn_out):
    return (
        lax.all_gather(ffn_in, ("clip", "frame"), axis=0, tiled=True),
        lax.all_gather(ffn_out, ("clip", "frame"), axis=0, tiled=True),
    )


def self_masks(first_row, block_rows, clip_len, key_valid):
    columns = jnp.arange(key_valid.shape[1], dtype=jnp.int32)
    row_ids = first_row + jnp.arange(block_rows, dtype=jnp.int32)
    diagonal = columns[None, :] == row_ids[:, None]
    allowed = (columns[None, :] <= row_ids[:, None])[None] & (
        key_valid[:, None, :] | diagonal[None]
    )
    live_rows = (row_ids[None, :] < clip_len[:, None]).astype(jnp.float32)
    return (allowed[:, None], live_rows[:, None, :, None])


def self_forward(query_rows, key_rows, value_rows, clip_len, key_valid):
    length = query_rows.shape[1]
    block_rows = min(512, length)
    score_scale = query_rows.shape[3] ** (-0.5)

    def one_block(block_index):
        first_row = block_index * block_rows
        query_block = lax.dynamic_slice_in_dim(query_rows, first_row, block_rows, 1)
        raw_scores = jnp.einsum(
            "cqhd,ckhd->chqk", query_block, key_rows, preferred_element_type=jnp.float32
        )
        allowed, live_rows = self_masks(first_row, block_rows, clip_len, key_valid)
        logits = jnp.where(allowed, raw_scores * score_scale, MASKED)
        row_max = jnp.max(logits, axis=-1, keepdims=True)
        exponent = jnp.exp(logits - row_max)
        row_sum = jnp.sum(exponent, axis=-1, keepdims=True)
        weights = (exponent / row_sum * live_rows).astype(jnp.bfloat16)
        attended = jnp.einsum(
            "chqk,ckhd->cqhd", weights, value_rows, preferred_element_type=jnp.float32
        )
        return (attended.astype(jnp.bfloat16), row_max + jnp.log(row_sum))

    blocks, log_sums = lax.map(one_block, jnp.arange(length // block_rows, dtype=jnp.int32))
    return (jnp.moveaxis(blocks, 0, 1).reshape(query_rows.shape), log_sums)


def self_backward(query_rows, key_rows, value_rows, grad_rows, log_sums, clip_len, key_valid):
    length = query_rows.shape[1]
    block_rows = min(512, length)
    score_scale = query_rows.shape[3] ** (-0.5)

    def one_block(totals, block_index):
        grad_keys, grad_values = totals
        first_row = block_index * block_rows
        query_block = lax.dynamic_slice_in_dim(query_rows, first_row, block_rows, 1)
        grad_block = lax.dynamic_slice_in_dim(grad_rows, first_row, block_rows, 1)
        raw_scores = jnp.einsum(
            "cqhd,ckhd->chqk", query_block, key_rows, preferred_element_type=jnp.float32
        )
        allowed, live_rows = self_masks(first_row, block_rows, clip_len, key_valid)
        logits = jnp.where(allowed, raw_scores * score_scale, MASKED)
        probs = jnp.exp(logits - log_sums[block_index])
        weights = (probs * live_rows).astype(jnp.bfloat16)
        grad_probs = (
            jnp.einsum(
                "cqhd,ckhd->chqk", grad_block, value_rows, preferred_element_type=jnp.float32
            )
            * live_rows
        )
        row_dot = jnp.sum(probs * grad_probs, axis=-1, keepdims=True)
        grad_scores = (probs * (grad_probs - row_dot)).astype(jnp.bfloat16)
        grad_query = (
            jnp.einsum("chqk,ckhd->cqhd", grad_scores, key_rows, preferred_element_type=jnp.float32)
            * score_scale
        )
        grad_keys = (
            grad_keys
            + jnp.einsum(
                "chqk,cqhd->ckhd", grad_scores, query_block, preferred_element_type=jnp.float32
            )
            * score_scale
        )
        grad_values = grad_values + jnp.einsum(
            "chqk,cqhd->ckhd", weights, grad_block, preferred_element_type=jnp.float32
        )
        return ((grad_keys, grad_values), grad_query)

    zeros = jnp.zeros(key_rows.shape, jnp.float32)
    (grad_keys, grad_values), grad_blocks = lax.scan(
        one_block, (zeros, zeros), jnp.arange(length // block_rows, dtype=jnp.int32)
    )
    grad_query = jnp.moveaxis(grad_blocks, 0, 1).reshape(query_rows.shape)
    return (grad_query, grad_keys, grad_values)


def text_allowed(text_len, text_mask):
    slots = jnp.arange(text_mask.shape[1], dtype=jnp.int32)
    allowed = (slots[None, :] < text_len[:, None]) & ((text_mask > 0) | (slots[None, :] == 0))
    return allowed[:, None, None, :]


def cross_forward(query_rows, key_rows, value_rows, allowed):
    score_scale = query_rows.shape[3] ** (-0.5)
    raw_scores = jnp.einsum(
        "cqhd,ckhd->chqk", query_rows, key_rows, preferred_element_type=jnp.float32
    )
    logits = jnp.where(allowed, raw_scores * score_scale, MASKED)
    row_max = jnp.max(logits, axis=-1, keepdims=True)
    exponent = jnp.exp(logits - row_max)
    row_sum = jnp.sum(exponent, axis=-1, keepdims=True)
    weights = (exponent / row_sum).astype(jnp.bfloat16)
    crossed = jnp.einsum("chqk,ckhd->cqhd", weights, value_rows, preferred_element_type=jnp.float32)
    return (crossed.astype(jnp.bfloat16), row_max + jnp.log(row_sum))


def cross_backward(query_rows, key_rows, value_rows, grad_rows, log_sums, allowed):
    score_scale = query_rows.shape[3] ** (-0.5)
    raw_scores = jnp.einsum(
        "cqhd,ckhd->chqk", query_rows, key_rows, preferred_element_type=jnp.float32
    )
    logits = jnp.where(allowed, raw_scores * score_scale, MASKED)
    probs = jnp.exp(logits - log_sums)
    weights = probs.astype(jnp.bfloat16)
    grad_probs = jnp.einsum(
        "cqhd,ckhd->chqk", grad_rows, value_rows, preferred_element_type=jnp.float32
    )
    row_dot = jnp.sum(probs * grad_probs, axis=-1, keepdims=True)
    grad_scores = (probs * (grad_probs - row_dot)).astype(jnp.bfloat16)
    grad_query = (
        jnp.einsum("chqk,ckhd->cqhd", grad_scores, key_rows, preferred_element_type=jnp.float32)
        * score_scale
    )
    grad_keys = (
        jnp.einsum("chqk,cqhd->ckhd", grad_scores, query_rows, preferred_element_type=jnp.float32)
        * score_scale
    )
    grad_values = jnp.einsum(
        "chqk,cqhd->ckhd", weights, grad_rows, preferred_element_type=jnp.float32
    )
    return (grad_query, grad_keys, grad_values)


def sum_ffn(grad_ffn_in, grad_ffn_out):
    return (
        lax.psum_scatter(grad_ffn_in, ("clip", "frame"), scatter_dimension=0, tiled=True),
        lax.psum_scatter(grad_ffn_out, ("clip", "frame"), scatter_dimension=0, tiled=True),
    )


def sum_attention(
    grad_self_qkv, grad_self_out, grad_cross_qkv, grad_cross_out, grad_gains, grad_shifts
):
    return (
        lax.psum_scatter(grad_self_qkv, ("clip", "frame"), scatter_dimension=0, tiled=True),
        lax.psum_scatter(grad_self_out, ("clip", "frame"), scatter_dimension=0, tiled=True),
        lax.psum_scatter(grad_cross_qkv, ("clip", "frame"), scatter_dimension=0, tiled=True),
        lax.psum_scatter(grad_cross_out, ("clip", "frame"), scatter_dimension=0, tiled=True),
        lax.psum_scatter(grad_gains, ("clip", "frame"), scatter_dimension=1, tiled=True),
        lax.psum_scatter(grad_shifts, ("clip", "frame"), scatter_dimension=1, tiled=True),
    )


def on_device_any(
    hidden_in,
    text_states,
    out_grad,
    self_qkv,
    self_out,
    cross_qkv,
    cross_out,
    ffn_in,
    ffn_out,
    ln_gain,
    ln_bias,
    clip_len,
    frame_mask,
    text_len,
    text_mask,
):
    clip_count, frames, model_width = hidden_in.shape
    text_slots = text_states.shape[1]
    group_count = lax.axis_size("frame")
    columns_here = model_width // group_count
    heads_here = columns_here // HD
    length = frames * group_count
    frame_index = lax.axis_index("frame")
    full_qkv, full_out, full_cross, full_cross_out, gains_low, shifts_low = fetch_attention(
        self_qkv, self_out, cross_qkv, cross_out, ln_gain, ln_bias
    )
    gains = gains_low.astype(jnp.float32)
    shifts = shifts_low.astype(jnp.float32)
    hidden = hidden_in.astype(jnp.float32)
    first_norm, first_pull = jax.vjp(layer_norm, hidden, gains[0], shifts[0])
    first_low = first_norm.astype(jnp.bfloat16)
    query_low = project(first_low, full_qkv[:, 0]).astype(jnp.bfloat16)
    key_low = project(first_low, full_qkv[:, 1]).astype(jnp.bfloat16)
    value_low = project(first_low, full_qkv[:, 2]).astype(jnp.bfloat16)
    query_heads, key_heads, value_heads = (
        lax.all_to_all(query_low, "frame", split_axis=2, concat_axis=1, tiled=True),
        lax.all_to_all(key_low, "frame", split_axis=2, concat_axis=1, tiled=True),
        lax.all_to_all(value_low, "frame", split_axis=2, concat_axis=1, tiled=True),
    )
    head_shape = (clip_count, length, heads_here, HD)
    query_heads = query_heads.reshape(head_shape)
    key_heads = key_heads.reshape(head_shape)
    value_heads = value_heads.reshape(head_shape)
    columns = jnp.arange(length, dtype=jnp.int32)
    key_valid = (columns[None, :] < clip_len[:, None]) & (frame_mask > 0)
    attended_heads, self_sums = self_forward(
        query_heads, key_heads, value_heads, clip_len, key_valid
    )
    attended = lax.all_to_all(
        attended_heads.reshape(clip_count, length, columns_here),
        "frame",
        split_axis=1,
        concat_axis=2,
        tiled=True,
    )
    after_self = hidden + project(attended, full_out)
    second_norm, second_pull = jax.vjp(layer_norm, after_self, gains[1], shifts[1])
    second_low = second_norm.astype(jnp.bfloat16)
    cross_query = project(second_low, full_cross[:, 0]).astype(jnp.bfloat16)
    cross_query_heads = lax.all_to_all(
        cross_query, "frame", split_axis=2, concat_axis=1, tiled=True
    ).reshape(head_shape)
    key_columns = lax.dynamic_slice_in_dim(
        full_cross[:, 1], frame_index * columns_here, columns_here, 1
    )
    value_columns = lax.dynamic_slice_in_dim(
        full_cross[:, 2], frame_index * columns_here, columns_here, 1
    )
    text_shape = (clip_count, text_slots, heads_here, HD)
    text_keys = project(text_states, key_columns).astype(jnp.bfloat16).reshape(text_shape)
    text_values = project(text_states, value_columns).astype(jnp.bfloat16).reshape(text_shape)
    allowed_text = text_allowed(text_len, text_mask)
    crossed_heads, cross_sums = cross_forward(
        cross_query_heads, text_keys, text_values, allowed_text
    )
    crossed = lax.all_to_all(
        crossed_heads.reshape(clip_count, length, columns_here),
        "frame",
        split_axis=1,
        concat_axis=2,
        tiled=True,
    )
    after_cross = after_self + project(crossed, full_cross_out)
    ffn_weight_in, ffn_weight_out = fetch_ffn(ffn_in, ffn_out)
    third_norm, third_pull = jax.vjp(layer_norm, after_cross, gains[2], shifts[2])
    third_low = third_norm.astype(jnp.bfloat16)
    pre_act = project(third_low, ffn_weight_in)
    activated, gelu_pull = jax.vjp(activate, pre_act)
    inner_low = activated.astype(jnp.bfloat16)
    output = (after_cross + project(inner_low, ffn_weight_out)).astype(jnp.bfloat16)
    ffn_weight_in, ffn_weight_out = fetch_ffn(ffn_in, ffn_out)
    grad_ffn_out = weight_grad(inner_low, out_grad)
    (grad_pre,) = gelu_pull(project_back(out_grad, ffn_weight_out))
    grad_pre_low = grad_pre.astype(jnp.bfloat16)
    grad_ffn_in = weight_grad(third_low, grad_pre_low)
    ffn_sums = sum_ffn(grad_ffn_in, grad_ffn_out)
    grad_third, gain_third, shift_third = third_pull(project_back(grad_pre_low, ffn_weight_in))
    grad_after_cross = out_grad.astype(jnp.float32) + grad_third
    full_qkv, full_out, full_cross, full_cross_out, gains_low, shifts_low = fetch_attention(
        self_qkv, self_out, cross_qkv, cross_out, ln_gain, ln_bias
    )
    key_columns = lax.dynamic_slice_in_dim(
        full_cross[:, 1], frame_index * columns_here, columns_here, 1
    )
    value_columns = lax.dynamic_slice_in_dim(
        full_cross[:, 2], frame_index * columns_here, columns_here, 1
    )
    cross_branch = grad_after_cross.astype(jnp.bfloat16)
    grad_cross_out = weight_grad(crossed, cross_branch)
    grad_crossed = project_back(cross_branch, full_cross_out).astype(jnp.bfloat16)
    grad_crossed_heads = lax.all_to_all(
        grad_crossed, "frame", split_axis=2, concat_axis=1, tiled=True
    ).reshape(head_shape)
    grad_cq, grad_tk, grad_tv = cross_backward(
        cross_query_heads, text_keys, text_values, grad_crossed_heads, cross_sums, allowed_text
    )
    grad_tk_low = grad_tk.astype(jnp.bfloat16).reshape(clip_count, text_slots, columns_here)
    grad_tv_low = grad_tv.astype(jnp.bfloat16).reshape(clip_count, text_slots, columns_here)
    text_terms = project_back(grad_tk_low, key_columns) + project_back(grad_tv_low, value_columns)
    grad_text = lax.psum_scatter(
        text_terms.astype(jnp.bfloat16), "frame", scatter_dimension=1, tiled=True
    )
    empty_square = jnp.zeros((model_width, model_width), jnp.float32)
    grad_cross_key = lax.dynamic_update_slice_in_dim(
        empty_square, weight_grad(text_states, grad_tk_low), frame_index * columns_here, 1
    )
    grad_cross_value = lax.dynamic_update_slice_in_dim(
        empty_square, weight_grad(text_states, grad_tv_low), frame_index * columns_here, 1
    )
    grad_cq_low = grad_cq.astype(jnp.bfloat16).reshape(clip_count, length, columns_here)
    grad_cross_query = lax.all_to_all(grad_cq_low, "frame", split_axis=1, concat_axis=2, tiled=True)
    grad_cross_qw = weight_grad(second_low, grad_cross_query)
    grad_second, gain_second, shift_second = second_pull(
        project_back(grad_cross_query, full_cross[:, 0])
    )
    grad_after_self = grad_after_cross + grad_second
    self_branch = grad_after_self.astype(jnp.bfloat16)
    grad_self_out = weight_grad(attended, self_branch)
    grad_attended = project_back(self_branch, full_out).astype(jnp.bfloat16)
    grad_attended_heads = lax.all_to_all(
        grad_attended, "frame", split_axis=2, concat_axis=1, tiled=True
    ).reshape(head_shape)
    grad_query, grad_keys, grad_values = self_backward(
        query_heads, key_heads, value_heads, grad_attended_heads, self_sums, clip_len, key_valid
    )
    flat_shape = (clip_count, length, columns_here)
    grad_query, grad_keys, grad_values = (
        lax.all_to_all(
            grad_query.astype(jnp.bfloat16).reshape(flat_shape),
            "frame",
            split_axis=1,
            concat_axis=2,
            tiled=True,
        ),
        lax.all_to_all(
            grad_keys.astype(jnp.bfloat16).reshape(flat_shape),
            "frame",
            split_axis=1,
            concat_axis=2,
            tiled=True,
        ),
        lax.all_to_all(
            grad_values.astype(jnp.bfloat16).reshape(flat_shape),
            "frame",
            split_axis=1,
            concat_axis=2,
            tiled=True,
        ),
    )
    grad_self_qkv = jnp.stack(
        [
            weight_grad(first_low, grad_query),
            weight_grad(first_low, grad_keys),
            weight_grad(first_low, grad_values),
        ],
        axis=1,
    )
    grad_first_norm = (
        project_back(grad_query, full_qkv[:, 0])
        + project_back(grad_keys, full_qkv[:, 1])
        + project_back(grad_values, full_qkv[:, 2])
    )
    grad_first, gain_first, shift_first = first_pull(grad_first_norm)
    grad_hidden = (grad_after_self + grad_first).astype(jnp.bfloat16)
    grad_cross_qkv = jnp.stack([grad_cross_qw, grad_cross_key, grad_cross_value], axis=1)
    grad_gains = jnp.stack([gain_first, gain_second, gain_third])
    grad_shifts = jnp.stack([shift_first, shift_second, shift_third])
    attn_sums = sum_attention(
        grad_self_qkv, grad_self_out, grad_cross_qkv, grad_cross_out, grad_gains, grad_shifts
    )
    return (
        output,
        grad_hidden,
        grad_text,
        attn_sums[0],
        attn_sums[1],
        attn_sums[2],
        attn_sums[3],
        ffn_sums[0],
        ffn_sums[1],
        attn_sums[4],
        attn_sums[5],
    )


MESH = pl.DeviceIdType.MESH
HBM = pl.BlockSpec(memory_space=pl.ANY)
VMEM = pl.BlockSpec(memory_space=pltpu.VMEM)
SMEM = pl.BlockSpec(memory_space=pltpu.SMEM)
NEG = -1e30
F32 = jnp.float32
BF16 = jnp.bfloat16


def fits(mesh):
    return mesh.shape["clip"] == 4 and mesh.shape["frame"] == 8


class Here:
    def __init__(self):
        self.c = lax.axis_index("clip")
        self.f = lax.axis_index("frame")
        self.core = lax.rem(self.f, 2)
        self.z = lax.div(self.f, 2)
        self.pair = lax.div(self.z, 2)
        self.role = lax.rem(self.z, 2)
        self.group = lax.rem(self.f, 4)
        self.cx = self.c + 1 - 2 * lax.rem(self.c, 2)
        self.cy = lax.rem(self.c + 2, 4)
        self.cd = 3 - self.c
        self.sib = self.f + 1 - 2 * self.core
        self.partner = self.f + 2 - 4 * self.role
        self.far_gate = 2 * (2 - self.pair) + self.core
        self.is_gate = self.role + self.pair == 1
        self.far = [2 * (2 * (1 - self.pair) + j) + self.core for j in range(2)]

    def step(self, d):
        return lax.rem(self.f + d, 8)

    def zstep(self, d):
        return lax.rem(self.f + 2 * d, 8)


class Wire:
    def __init__(self, here, send_sem, recv_sem):
        self.here, self.send_sem, self.recv_sem = here, send_sem, recv_sem
        self.used = 0
        self.open = []

    def copy(self, src, dst, tag, c, f):
        self.used += 1
        return pltpu.make_async_remote_copy(
            src_ref=src,
            dst_ref=dst,
            send_sem=self.send_sem.at[self.used - 1],
            recv_sem=self.recv_sem.at[tag],
            device_id=(c, f),
            device_id_type=MESH,
        )

    def send(self, src, dst, tag, c, f):
        copy = self.copy(src, dst, tag, c, f)
        copy.start()
        self.open.append(copy)

    def arrived(self, dst, tag):
        pltpu.make_async_remote_copy(
            src_ref=dst,
            dst_ref=dst,
            send_sem=self.send_sem.at[0],
            recv_sem=self.recv_sem.at[tag],
            device_id=(self.here.c, self.here.sib),
            device_id_type=MESH,
        ).wait_recv()

    def drain(self):
        for copy in self.open:
            copy.wait_send()
        self.open = []


def call_out(devices):
    barrier = pltpu.get_barrier_semaphore()
    for device in devices:
        pl.semaphore_signal(barrier, inc=1, device_id=device, device_id_type=MESH)


def hear_all(devices):
    pl.semaphore_wait(pltpu.get_barrier_semaphore(), len(devices))


def frame_others(here):
    return [(here.c, here.step(d)) for d in range(1, 8)]


def clip_others(here):
    return [(here.cx, here.f), (here.cy, here.f), (here.cd, here.f)]


class ClipGather:
    def __init__(self, wire, block, tag, own=None):
        self.wire, self.block, self.tag = wire, block, tag
        self.own = own or (lambda half: block(wire.here.c, half))

    def begin(self):
        h, w, b, t, own = self.wire.here, self.wire, self.block, self.tag, self.own
        w.send(own(0), b(h.c, 0), t, h.cx, h.f)
        w.send(own(1), b(h.c, 1), t + 2, h.cy, h.f)
        w.send(own(1), b(h.c, 1), t + 1, h.cx, h.f)
        w.send(own(0), b(h.c, 0), t + 3, h.cy, h.f)

    def middle(self):
        h, w, b, t = self.wire.here, self.wire, self.block, self.tag
        w.arrived(b(h.cx, 0), t)
        w.send(b(h.cx, 0), b(h.cx, 0), t + 4, h.cy, h.f)
        w.arrived(b(h.cy, 1), t + 2)
        w.send(b(h.cy, 1), b(h.cy, 1), t + 5, h.cx, h.f)

    def near(self):
        h, w, b, t = self.wire.here, self.wire, self.block, self.tag
        w.arrived(b(h.cx, 1), t + 1)
        w.arrived(b(h.cy, 0), t + 3)

    def end(self):
        h, w, b, t = self.wire.here, self.wire, self.block, self.tag
        w.arrived(b(h.cd, 0), t + 4)
        w.arrived(b(h.cd, 1), t + 5)


class ZGather:
    def __init__(self, wire, slot, tag, own=None):
        self.wire, self.slot, self.tag = wire, slot, tag
        self.own = own if own is not None else slot(wire.here.f)
        self.open = []

    def step(self, s):
        h, w = self.wire.here, self.wire
        left, right = h.f - 2 * (s - 1), h.f + 2 * (s - 1)
        if s > 1:

            @pl.when(left >= 0)
            def _():
                w.arrived(self.slot(left), self.tag + s - 2)

            @pl.when(right <= 7)
            def _():
                w.arrived(self.slot(right), self.tag + 3 + s - 2)

        if s > 3:
            return
        for block, tag, go, to in (
            (left, self.tag, (left >= 0) & (h.z <= 2), h.f + 2),
            (right, self.tag + 3, (right <= 7) & (h.z >= 1), h.f - 2),
        ):
            src = self.own if s == 1 else self.slot(block)
            copy = w.copy(src, self.slot(block), tag + s - 1, h.c, to)
            pl.when(go)(copy.start)
            self.open.append((go, copy))

    def relay(self, d):
        h, w = self.wire.here, self.wire
        f = h.zstep(d)
        w.send(self.own if d == 0 else self.slot(f), self.slot(f), self.tag + 6 + d, h.c, h.sib)

    def end(self):
        h, w = self.wire.here, self.wire
        for d in range(4):
            w.arrived(self.slot(h.zstep(d) + h.sib - h.f), self.tag + 6 + d)

    def drain(self):
        for go, copy in self.open:
            pl.when(go)(copy.wait_send)


class MatrixGather:
    def __init__(self, wire, block, rows, tag):
        h = wire.here
        self.wire, self.block, self.tag = wire, block, tag
        self.z = ZGather(wire, lambda f: block(h.c, f), tag)
        toward = 2 - 4 * h.pair
        at_end = jnp.logical_not(h.is_gate)
        self.order = [
            h.f,
            h.f + toward,
            jnp.where(at_end, h.f + 2 * toward, h.f - toward),
            jnp.where(at_end, h.f + 3 * toward, h.f + 2 * toward),
        ]
        self.clip = [
            ClipGather(
                wire,
                lambda c, half, f=f: block(c, f).at[pl.ds(rows // 2 * half, rows // 2), :],
                tag + 10 + 6 * d,
            )
            for d, f in enumerate(self.order)
        ]

    def step(self, s):
        self.z.step(s)
        self.clip[s - 1].begin()
        self.z.relay(s - 1) if s == 1 else None
        if s == 4:
            for d in range(1, 4):
                self.z.relay(d)

    def _relay(self, d, i, c):
        h, w = self.wire.here, self.wire
        block = self.block(c, self.order[d])
        w.send(block, block, self.tag + 34 + 3 * d + i, h.c, h.sib)

    def middle(self, d):
        self.clip[d].middle()

    def near(self, d):
        h = self.wire.here
        self.clip[d].near()
        self._relay(d, 0, h.cx)
        self._relay(d, 1, h.cy)

    def last(self, d):
        self.clip[d].end()
        self._relay(d, 2, self.wire.here.cd)

    def end(self):
        h, w = self.wire.here, self.wire
        self.z.end()
        for d in range(4):
            f = self.order[d] + h.sib - h.f
            for i, c in enumerate((h.cx, h.cy, h.cd)):
                w.arrived(self.block(c, f), self.tag + 34 + 3 * d + i)


class ClipScatter:
    def __init__(self, wire, parts, slots, tag):
        self.wire, self.parts, self.slots, self.tag = wire, parts, slots, tag

    def begin(self, which=None):
        h, w, p, s, t = self.wire.here, self.wire, self.parts, self.slots, self.tag
        if which != 1:
            w.send(p(h.cd, 0), s[0], t, h.cx, h.f)
            w.send(p(h.cd, 1), s[1], t + 1, h.cy, h.f)
        if which != 0:
            w.send(p(h.cx, 0), s[2], t + 2, h.cx, h.f)
            w.send(p(h.cy, 1), s[3], t + 3, h.cy, h.f)

    def middle(self):
        h, w, p, s, t = self.wire.here, self.wire, self.parts, self.slots, self.tag
        w.arrived(s[0], t)
        add_into(s[0], p(h.cy, 0))
        w.send(s[0], s[4], t + 4, h.cy, h.f)
        w.arrived(s[1], t + 1)
        add_into(s[1], p(h.cx, 1))
        w.send(s[1], s[5], t + 5, h.cx, h.f)

    def end(self):
        w, s, t = self.wire, self.slots, self.tag
        for i in range(2, 6):
            w.arrived(s[i], t + i)

    def total(self, half):
        s = self.slots
        first, second = (s[2], s[4]) if half == 0 else (s[5], s[3])
        own = self.parts(self.wire.here.c, half)
        return own[...].astype(F32) + first[...].astype(F32) + second[...].astype(F32)


class ZScatter:
    def __init__(self, wire, terms, near, far, tag):
        self.wire, self.terms, self.near, self.far, self.tag = wire, terms, near, far, tag
        self.open = []

    def term(self, m):
        pair = self.wire.here.pair
        return self.terms.at[m + pair * (3 - 2 * m)]

    def _start(self, go, src, dst, tag, f):
        copy = self.wire.copy(src, dst, self.tag + tag, self.wire.here.c, f)
        pl.when(go)(copy.start)
        self.open.append((go, copy))

    def begin(self):
        h = self.wire.here
        for i, m in enumerate((3, 2, 1)):
            self._start(jnp.logical_not(h.is_gate), self.term(m), self.near.at[i], i, h.partner)

    def step(self, s):
        h, w = self.wire.here, self.wire
        block, m, tag, to, f = (
            (self.near.at[0], 3, 0, 0, h.far_gate),
            (self.near.at[1], 2, 1, 1, h.far_gate),
            (self.far.at[0], 0, 3, 0, h.partner),
        )[s - 1]

        @pl.when(h.is_gate)
        def _():
            w.arrived(block, self.tag + tag)
            add_into(block, self.term(m))

        self._start(h.is_gate, block, self.far.at[to], 3 + to, f)

    def end(self):
        h, w = self.wire.here, self.wire

        @pl.when(h.is_gate)
        def _():
            w.arrived(self.near.at[2], self.tag + 2)
            w.arrived(self.far.at[1], self.tag + 4)

        @pl.when(jnp.logical_not(h.is_gate))
        def _():
            w.arrived(self.far.at[0], self.tag + 3)

    def total(self, out):
        h = self.wire.here
        self.end()

        @pl.when(h.is_gate)
        def _():
            others = self.near[2].astype(F32) + self.far[1].astype(F32)
            out[...] = (self.terms[h.z].astype(F32) + others).astype(out.dtype)

        @pl.when(jnp.logical_not(h.is_gate))
        def _():
            out[...] = (self.terms[h.z].astype(F32) + self.far[0].astype(F32)).astype(out.dtype)

    def drain(self):
        for go, copy in self.open:
            pl.when(go)(copy.wait_send)


class SiblingSum:
    def __init__(self, wire, terms, inbox, sums, tag):
        self.wire, self.terms, self.inbox, self.sums, self.tag = wire, terms, inbox, sums, tag

    def begin(self):
        h, w = self.wire.here, self.wire
        for z in range(4):
            w.send(self.terms(2 * z + 1 - h.core), self.inbox(z), self.tag + z, h.c, h.sib)

    def end(self):
        h, w = self.wire.here, self.wire
        for z in range(4):
            w.arrived(self.inbox(z), self.tag + z)
            own, other = self.terms(2 * z + h.core), self.inbox(z)
            self.sums(z)[...] = (own[...].astype(F32) + other[...].astype(F32)).astype(BF16)


def add_into(into, other):
    into[...] = (into[...].astype(F32) + other[...].astype(F32)).astype(BF16)


class LocalCopy:
    def __init__(self, src, through, dst, sem):
        self.a = pltpu.make_async_copy(src, through, sem)
        self.b = pltpu.make_async_copy(through, dst, sem)
        self.a.start()

    def turn(self):
        self.a.wait()
        self.b.start()

    def wait(self):
        self.b.wait()


def comm_call(body, out_shape, in_specs, out_specs, scratch, copies, tags, collective_id, cost=None):
    return pl.pallas_call(
        body,
        out_shape=out_shape,
        in_specs=in_specs,
        out_specs=out_specs,
        scratch_shapes=list(scratch)
        + [pltpu.SemaphoreType.DMA((copies,)), pltpu.SemaphoreType.DMA((tags,))],
        compiler_params=pltpu.CompilerParams(
            collective_id=collective_id, has_side_effects=True, vmem_limit_bytes=60 * 2**20
        ),
    )


def shape(dims, dtype=BF16):
    return jax.ShapeDtypeStruct(dims, dtype)


ROWS = 256


def dot(left, right, contract):
    return lax.dot_general(left, right, ((contract[:1], contract[1:]), ((), ())), preferred_element_type=F32)


def fill_key_bias(bias, clip_len, frame_mask, clip):
    column = lax.broadcasted_iota(jnp.int32, (1, 1024), 1)
    valid = (column < clip_len[clip]) & (frame_mask[pl.ds(clip, 1), :] > 0)
    row = jnp.where(valid, 0.0, NEG).astype(F32)
    bias[...] = jnp.broadcast_to(row, (128, 1024)).T


def text_bias_rows(text_len, text_mask):
    slot = lax.broadcasted_iota(jnp.int32, (1, 128), 1)
    rows = []
    for clip in range(2):
        valid = (slot < text_len[clip]) & ((text_mask[clip : clip + 1, :] > 0) | (slot == 0))
        rows.append(jnp.where(valid, 0.0, NEG).astype(F32))
    return rows


def mask_scores(scores, bias_ref, first, rows):
    low = scores[first:] + bias_ref[first : first + rows, 0:1]
    key = lax.broadcasted_iota(jnp.int32, (rows, rows), 0)
    query = lax.broadcasted_iota(jnp.int32, (rows, rows), 1)
    low = jnp.where(key < query, low, jnp.where(key == query, scores[first:], NEG))
    if first == 0:
        return low
    return jnp.concatenate([scores[:first] + bias_ref[0:first, 0:1], low], axis=0)


def norm_parts(value):
    centered = value - jnp.mean(value, axis=-1, keepdims=True)
    scale = lax.rsqrt(jnp.mean(centered * centered, axis=-1, keepdims=True) + EPSILON)
    return centered * scale, scale


def column_weight(cols, j):
    return cols[:, :, 32 * j : 32 * j + 32, :].reshape(1024, 256)


def attend_rows(i, length, bias, q_ref, k_ref, v_t, o_ref, lse_ref, out_t):
    lane_head = lax.broadcasted_iota(jnp.int32, (ROWS, 256), 1) // HD
    first, n = i * ROWS, (i + 1) * ROWS
    q = q_ref[first:n, :]

    def head(j, _):
        q_head = jnp.where(lane_head == j, q, 0) * jnp.asarray(HD**-0.5, BF16)
        scores = mask_scores(dot(k_ref[0:n, :], q_head, (1, 1)), bias, first, ROWS)
        top = jnp.max(scores, axis=0, keepdims=True)
        weight = jnp.exp(scores - top)
        total = jnp.sum(weight, axis=0, keepdims=True)
        at = pl.ds(pl.multiple_of(j * HD, HD), HD)
        out_t[at, :] = dot(v_t[at, 0:n], weight.astype(BF16), (1, 0)) / total
        lse_ref[pl.ds(j, 1), first:n] = top + jnp.log(total)
        return 0

    lax.fori_loop(0, 4, head, 0)
    live = first + lax.broadcasted_iota(jnp.int32, (ROWS, 256), 0) < length
    o_ref[first:n, :] = jnp.where(live, out_t[...].T, 0).astype(BF16)


def square_of(square, which):
    return square[:, :, 32 * which : 32 * which + 32, :].reshape(1024, 1024)


def text_probs(query, keys, bias, lane_head):
    heads = [jnp.where(lane_head == j, query, 0) for j in range(4)]
    stacked = jnp.concatenate(heads, axis=0)
    scores = dot(stacked, keys, (1, 1)) + bias
    weight = jnp.exp(scores - jnp.max(scores, axis=1, keepdims=True))
    return weight / jnp.sum(weight, axis=1, keepdims=True), stacked


def pick_heads(stacked, lane_head):
    return sum(jnp.where(lane_head == j, stacked[128 * j : 128 * j + 128], 0) for j in range(4))


def forward_body(
    clip_len, text_len, frame_mask, text_mask, gain, shift, self_qkv, cross_qkv, self_out, cross_out,
    text, hid, fin, fout, grad,
    o_hid, o_first, o_q, o_k, o_v, o_heads, o_lse, o_w_a, o_w_b, o_params, o_att, o_tkv, o_square,
    o_second, o_query, o_crossed, o_self, o_cross, o_out, o_in, o_third, o_sum,
    hid_all, first, q_ref, k_ref, v_ref, heads, lse, w_a, w_b, params, att, tkv, sq_self, sq_cross,
    second, query_ref, crossed, after_self, after_cross, out_ref, in_ref,
    out_t, v_t, own_tkv, own_text, own_hid, fin_in, grad_all, win, wout,
    tokens, inner, slope, g_pre, terms, slots, out_w, inbox, sums, near, far,
    bias, cols_a, cols_b, square, placed, local, saved, send_sem, recv_sem,
):
    h = Here()
    w = Wire(h, send_sem, recv_sem)
    partners = frame_others(h) + clip_others(h)
    call_out(partners)
    length = clip_len[h.pair]
    tag = [0]

    def tags(n):
        tag[0] += n
        return tag[0] - n

    T_HID, T_A, T_B, T_FIN, T_AXY, T_BXY = tags(10), tags(7), tags(7), tags(3), tags(6), tags(6)
    T_SELF, T_CROSS, T_ATT, T_TKV, T_WIN, T_GRAD = tags(46), tags(46), tags(8), tags(3), tags(10), tags(6)
    T_TOK, T_WOUT, T_TERM, T_OSIB, T_OZ = tags(6), tags(10), tags(6), tags(4), tags(5)

    def my_columns(f):
        return pl.ds(pl.multiple_of(lax.rem(f, 4) * 256, 256), 256)

    def fin_part(c):
        return fin.at[:, pl.ds(pl.multiple_of(c * 1024, 1024), 1024)]

    spread = lax.broadcasted_iota(jnp.int32, (32, 128), 0) + 32 * lax.rem(h.f, 4)
    spread = jnp.where(spread == lax.broadcasted_iota(jnp.int32, (32, 128), 1), 1.0, 0.0).astype(BF16)
    placed[...] = jnp.zeros_like(placed)
    placed[0:3, :] = dot(gain[...], spread, (1, 0))
    placed[3:6, :] = dot(shift[...], spread, (1, 0))
    for q in range(8):
        group = placed[...] if q % 2 == 0 else jnp.zeros((16, 128), F32)
        cols_a[96:112, 128 * q : 128 * q + 128] = group.astype(BF16)
    for j in range(3):
        cols_a[32 * j : 32 * j + 32, :] = self_qkv[j]
    for j in range(2):
        cols_b[32 * j : 32 * j + 32, :] = cross_qkv[1 + j]
    square[0:32, :] = self_out[...]
    square[32:64, :] = cross_qkv[0]
    square[64:96, :] = cross_out[...]
    own = [
        pltpu.make_async_copy(src, dst, local.at[i])
        for i, (src, dst) in enumerate(
            (
                (cols_a.at[:, my_columns(h.f)], w_a.at[h.c, h.f]),
                (cols_b.at[:, my_columns(h.f)], w_b.at[h.c, h.f]),
                (hid.at[h.pair], hid_all.at[h.f]),
                (square.at[pl.ds(0, 32)], sq_self.at[h.c, h.f]),
                (fin_part(h.c), fin_in.at[h.c]),
                (text, own_text),
                (hid, own_hid),
                (grad, grad_all.at[h.c]),
                (fout, wout.at[h.f]),
                (square.at[pl.ds(32, 64)], sq_cross.at[h.c, h.f]),
            )
        )
    ]
    for copy in own:
        copy.start()
    saves = []

    def save(src, dst):
        copy = pltpu.make_async_copy(src, dst, saved.at[len(saves)])
        copy.start()
        saves.append(copy)

    hear_all(partners)

    own[0].wait()
    for d in (2, 6, 4, 3, 5, 1, 7):
        f = h.step(d)
        w.send(cols_a.at[:, my_columns(f)], w_a.at[h.c, h.f], T_A + d - 1, h.c, f)
    own[7].wait()
    grad_gather = ClipGather(w, lambda c, half: grad_all.at[c, pl.ds(128 * half, 128), :], T_GRAD)
    grad_gather.begin()
    for i, (c, f) in enumerate(clip_others(h)):
        w.send(fin_part(c), fin_in.at[h.c], T_FIN + i, c, f)
    w.send(hid.at[h.pair], hid_all.at[h.f], T_HID, h.c, h.sib)

    def half_of(ref, part):
        return ref.at[pl.ds(64 * part, 64), :]

    for d in range(1, 8):
        w.arrived(w_a.at[h.c, lax.rem(h.f + 8 - d, 8)], T_A + d - 1)
    a_gather = ClipGather(w, lambda c, half: w_a.at[c, pl.ds(4 * half, 4)], T_AXY)
    a_gather.begin()
    for part in range(2):
        w.send(
            half_of(hid.at[1 - h.pair], part),
            half_of(hid_all.at[h.f], part),
            T_HID + 3 + 2 * h.role + part,
            h.c,
            h.far_gate,
        )
        w.send(half_of(hid.at[h.pair], part), half_of(hid_all.at[h.f], part), T_HID + 1 + part, h.c, h.partner)
    own[3].wait()
    self_gather = MatrixGather(w, lambda c, f: sq_self.at[c, f], 32, T_SELF)
    self_gather.step(1)
    forwards = []
    for part in range(2):
        for j in range(2):
            block = half_of(hid_all.at[h.far[j]], part)
            w.arrived(block, T_HID + 3 + 2 * j + part)
            forward = w.copy(block, block, T_HID + 3 + 2 * j + part, h.c, h.partner)
            pl.when(h.is_gate)(forward.start)
            forwards.append(forward)
    self_gather.step(2)
    a_gather.middle()
    for part in range(2):
        w.arrived(half_of(hid_all.at[h.partner], part), T_HID + 1 + part)
    w.send(hid_all.at[h.partner], hid_all.at[h.partner], T_HID + 7, h.c, h.sib)
    for j in range(2):
        w.send(hid_all.at[h.far[j]], hid_all.at[h.far[j]], T_HID + 8 + j, h.c, h.sib)
    self_gather.step(3)
    own[1].wait()
    for d in (2, 6, 4, 3, 5, 1, 7):
        f = h.step(d)
        w.send(cols_b.at[:, my_columns(f)], w_b.at[h.c, h.f], T_B + d - 1, h.c, f)
    fill_key_bias(bias, clip_len, frame_mask, h.pair)
    text_bias = text_bias_rows(text_len, text_mask)
    self_gather.middle(0)
    self_gather.step(4)
    self_gather.middle(1)
    own[9].wait()
    cross_gather = MatrixGather(w, lambda c, f: sq_cross.at[c, f], 64, T_CROSS)
    a_gather.near()
    a_gather.end()
    grad_gather.middle()
    cross_gather.step(1)
    own[4].wait()
    for i, (c, f) in enumerate(clip_others(h)):
        w.arrived(fin_in.at[c], T_FIN + i)
    win_gather = ZGather(w, lambda f: win.at[:, f], T_WIN, fin_in)
    win_copy = pltpu.make_async_copy(fin_in, win.at[:, h.f], local.at[11])
    win_copy.start()
    win_gather.step(1)
    win_gather.relay(0)
    for g in range(8):
        group = sum(w_a[g // 2, 4 * (g % 2) + i, 96:104, 0:128].astype(F32) for i in range(4))
        params[:, 128 * g : 128 * g + 128] = group
    own[2].wait()
    w.arrived(hid_all.at[h.sib], T_HID)
    w.arrived(hid_all.at[h.partner + h.sib - h.f], T_HID + 7)
    for j in range(2):
        w.arrived(hid_all.at[h.far[j] + h.sib - h.f], T_HID + 8 + j)

    def project_rows(i, _):
        at = pl.ds(pl.multiple_of(i * 256, 256), 256)
        rows = hid_all[pl.ds(2 * i, 2)].reshape(256, 1024).astype(F32)
        xhat, _ = norm_parts(rows)
        low = (xhat * params[0:1, :] + params[3:4, :]).astype(BF16)
        first[at, :] = low
        for j, out in enumerate((q_ref, k_ref, v_ref)):
            out[at, :] = dot(low, column_weight(w_a, j), (1, 0)).astype(BF16)
        return 0

    lax.fori_loop(0, 2, project_rows, 0)
    self_gather.middle(2)
    for d in range(1, 8):
        w.arrived(w_b.at[h.c, lax.rem(h.f + 8 - d, 8)], T_B + d - 1)
    b_gather = ClipGather(w, lambda c, half: w_b.at[c, pl.ds(4 * half, 4)], T_BXY)
    b_gather.begin()
    cross_gather.step(2)
    lax.fori_loop(2, 4, project_rows, 0)
    v_t[...] = v_ref[...].T
    win_gather.step(2)
    self_gather.middle(3)
    cross_gather.step(3)
    b_gather.middle()

    def att_slot(f):
        return att.at[lax.div(f, 4), :, my_columns(f)]

    att_sends = []

    def attend_and_send(i):
        attend_rows(i, length, bias, q_ref, k_ref, v_t, heads, lse, out_t)
        for f in (2 * i, 2 * i + 1):
            block = heads.at[pl.ds(128 * f, 128), :]
            away = h.f != f
            copy = w.copy(block, att_slot(h.f), T_ATT + h.f, h.c, f)
            stay = pltpu.make_async_copy(block, att_slot(h.f), local.at[12])
            pl.when(away)(copy.start)
            pl.when(jnp.logical_not(away))(stay.start)
            att_sends.append((away, copy, stay))

    attend_and_send(3)
    def text_slot(f):
        return tkv.at[:, :, :, my_columns(f)]

    b_gather.near()
    b_gather.end()
    own[5].wait()
    for clip in range(2):
        for j in range(2):
            own_tkv[clip, j] = dot(own_text[clip], column_weight(w_b, j), (1, 0)).astype(BF16)
    w.send(own_tkv, text_slot(h.f), T_TKV, h.c, h.partner)
    w.send(own_tkv, text_slot(h.f), T_TKV + 1, h.c, h.sib)
    text_copy = pltpu.make_async_copy(own_tkv, text_slot(h.f), local.at[10])
    text_copy.start()
    cross_gather.step(4)
    win_gather.step(3)
    cross_gather.middle(0)
    attend_and_send(2)
    for d in range(4):
        self_gather.near(d)
        self_gather.last(d)
    cross_gather.middle(1)
    w.arrived(text_slot(h.partner), T_TKV)
    w.send(text_slot(h.partner), text_slot(h.partner), T_TKV + 2, h.c, h.sib)
    attend_and_send(1)
    win_gather.step(4)
    for d in range(1, 4):
        win_gather.relay(d)
    cross_gather.middle(2)
    attend_and_send(0)
    cross_gather.middle(3)
    for src, dst in (
        (hid_all, o_hid), (first, o_first), (q_ref, o_q), (k_ref, o_k), (v_ref, o_v), (heads, o_heads), (lse, o_lse),
        (w_a, o_w_a), (w_b, o_w_b), (params, o_params),
    ):
        save(src, dst)
    self_gather.end()
    for d in range(1, 8):
        f = lax.rem(h.f + 8 - d, 8)
        w.arrived(att_slot(f), T_ATT + f)
    for away, _, stay in att_sends:
        pl.when(jnp.logical_not(away))(stay.wait)

    own[6].wait()
    value = own_hid[...].reshape(256, 1024).astype(F32) + dot(
        att[...].reshape(256, 1024), square_of(sq_self, 0), (1, 0)
    )
    after_self[...] = value
    xhat, _ = norm_parts(value)
    second[...] = (xhat * params[1:2, :] + params[4:5, :]).astype(BF16)
    for d in range(4):
        cross_gather.near(d)
        cross_gather.last(d)
    cross_gather.end()
    query_ref[...] = dot(second[...], square_of(sq_cross, 0), (1, 0)).astype(BF16)
    w.arrived(text_slot(h.sib), T_TKV + 1)
    w.arrived(text_slot(h.partner + h.sib - h.f), T_TKV + 2)
    text_copy.wait()
    lane_head = lax.broadcasted_iota(jnp.int32, (128, 256), 1) // HD
    for clip in range(2):
        for group in range(4):
            rows, columns = pl.ds(128 * clip, 128), pl.ds(256 * group, 256)
            query = query_ref[rows, columns] * jnp.asarray(HD**-0.5, BF16)
            probs, _ = text_probs(query, tkv[clip, 0, :, columns], text_bias[clip], lane_head)
            part = dot(probs.astype(BF16), tkv[clip, 1, :, columns], (1, 0))
            crossed[rows, columns] = pick_heads(part, lane_head).astype(BF16)
    own[8].wait()
    out_gather = ZGather(w, lambda f: wout.at[f], T_WOUT)
    out_gather.step(1)
    out_gather.relay(0)
    value = after_self[...] + dot(crossed[...], square_of(sq_cross, 1), (1, 0))
    after_cross[...] = value
    xhat, _ = norm_parts(value)
    tokens[h.c] = (xhat * params[2:3, :] + params[5:6, :]).astype(BF16)

    token_gather = ClipGather(w, lambda c, half: tokens.at[c, pl.ds(128 * half, 128), :], T_TOK)
    token_gather.begin()
    for src, dst in (
        (att, o_att), (tkv, o_tkv), (second, o_second), (query_ref, o_query), (crossed, o_crossed),
        (after_self, o_self), (after_cross, o_cross),
    ):
        save(src, dst)
    save(sq_self, o_square.at[0])
    for which in range(2):
        save(sq_cross.at[:, :, pl.ds(32 * which, 32), :], o_square.at[1 + which])
    win_copy.wait()
    win_gather.end()

    def hidden(c):
        def part(i, _):
            rows = pl.ds(pl.multiple_of(128 * i, 128), 128)
            pre = dot(tokens[c, rows, :], win[...].reshape(1024, 1024), (1, 0))
            cdf = 0.5 * (1.0 + lax.erf(pre * (0.5**0.5)))
            inner[c, rows, :] = (pre * cdf).astype(BF16)
            slope[c, rows, :] = cdf + pre * jnp.exp(-0.5 * pre * pre) * 0.3989422804014327
            return 0

        lax.fori_loop(0, 2, part, 0)

    def hidden_back(c):
        g_inner = dot(grad_all[c], wout[...].reshape(1024, 1024), (1, 1))
        g_pre[c] = (g_inner * slope[c]).astype(BF16)
        terms[c] = dot(g_pre[c], win[...].reshape(1024, 1024), (1, 1)).astype(BF16)

    def out_terms(c):
        out_ref[c] = dot(inner[c], wout[...].reshape(1024, 1024), (1, 0)).astype(BF16)

    sibling = SiblingSum(w, lambda f: out_w.at[f], lambda z: inbox.at[z], lambda z: sums.at[z], T_OSIB)
    z_scatter = ZScatter(w, sums, near, far, T_OZ)
    tall = (1024, 1024)

    def out_weight(i, _):
        columns = pl.ds(pl.multiple_of(i * 256, 256), 256)
        out = dot(inner[:, :, columns].reshape(1024, 256), grad_all[...].reshape(tall), (0, 0))
        out_w[pl.ds(2 * i, 2)] = out.astype(BF16).reshape(2, 128, 1024)
        return 0

    def in_weight(i, _):
        columns = pl.ds(pl.multiple_of(i * 256, 256), 256)
        out = dot(tokens[:, :, columns].reshape(1024, 256), g_pre[...].reshape(tall), (0, 0))
        in_ref[:, pl.ds(pl.multiple_of(32 * i, 32), 32), :] = out.astype(BF16).reshape(8, 32, 1024)
        return 0

    hidden(h.c)
    out_gather.step(2)
    grad_gather.near()
    grad_gather.end()
    token_gather.middle()
    token_gather.near()
    out_gather.step(3)

    def both(i, _):
        hidden(jnp.where(i == 0, h.cx, h.cy))
        return 0

    lax.fori_loop(0, 2, both, 0)
    out_gather.step(4)
    for d in range(1, 4):
        out_gather.relay(d)
    token_gather.end()
    hidden(h.cd)
    lax.fori_loop(0, 4, out_weight, 0)
    sibling.begin()
    out_gather.end()
    scatter = ClipScatter(
        w, lambda c, half: terms.at[c, pl.ds(128 * half, 128), :], [slots.at[i] for i in range(6)], T_TERM
    )
    hidden_back(h.cd)
    scatter.begin(0)
    sibling.end()
    z_scatter.begin()

    def others_back(i, _):
        hidden_back(jnp.where(i == 0, h.cx, h.cy))
        return 0

    lax.fori_loop(0, 2, others_back, 0)
    scatter.begin(1)
    hidden_back(h.c)
    scatter.middle()
    z_scatter.step(1)
    lax.fori_loop(0, 2, in_weight, 0)
    lax.fori_loop(2, 4, in_weight, 0)
    save(in_ref, o_in)
    z_scatter.step(2)
    z_scatter.step(3)

    def out_term(i, _):
        out_terms(i)
        return 0

    lax.fori_loop(0, 4, out_term, 0)
    save(out_ref, o_out)
    scatter.end()
    for half in range(2):
        o_third[128 * half : 128 * half + 128, :] = scatter.total(half)
    z_scatter.total(o_sum)
    w.drain()
    for copy in forwards:
        pl.when(h.is_gate)(copy.wait_send)
    for away, copy, _ in att_sends:
        pl.when(away)(copy.wait_send)
    for one in (self_gather.z, cross_gather.z, win_gather, out_gather, z_scatter):
        one.drain()
    for copy in saves:
        copy.wait()


def forward(*args):
    column, rows, full, quarter = (1024, 256), (256, 1024), (4, 256, 1024), (4, 128, 1024)
    kept = [
        shape((8, 128, 1024)),
        shape((1024, 1024)),
        shape(column),
        shape(column),
        shape(column),
        shape(column),
        shape((8, 1024), F32),
        shape((4, 8, 112, 256)),
        shape((4, 8, 64, 256)),
        shape((8, 1024), F32),
        shape((2, 128, 1024)),
        shape((2, 2, 128, 1024)),
        shape((4, 8, 96, 1024)),
        shape(rows),
        shape(rows),
        shape(rows),
        shape(rows, F32),
        shape(rows, F32),
        shape(full),
        shape((8, 128, 1024)),
    ]
    scratch = [pltpu.VMEM(one.shape, one.dtype) for one in kept]
    scratch[12:13] = [pltpu.VMEM((4, 8, rows, 1024), BF16) for rows in (32, 64)]
    kept[12] = shape((3, 4, 8, 32, 1024))
    return comm_call(
        forward_body,
        tuple(kept) + (shape(rows, F32), shape((128, 1024), F32)),
        [SMEM] * 2 + [VMEM] * 8 + [HBM] * 5,
        (HBM,) * len(kept) + (VMEM,) * 2,
        scratch
        + [
            pltpu.VMEM((256, ROWS), F32),
            pltpu.VMEM((256, 1024), BF16),
            pltpu.VMEM((2, 2, 128, 256), BF16),
            pltpu.VMEM((2, 128, 1024), BF16),
            pltpu.VMEM((2, 128, 1024), BF16),
            pltpu.VMEM((4, 32, 1024), BF16),
            pltpu.VMEM(full, BF16),
            pltpu.VMEM((4, 8, 32, 1024), BF16),
            pltpu.VMEM((8, 128, 1024), BF16),
            pltpu.VMEM(full, BF16),
            pltpu.VMEM(full, BF16),
            pltpu.VMEM(full, F32),
            pltpu.VMEM(full, BF16),
            pltpu.VMEM(full, BF16),
            pltpu.VMEM((6, 128, 1024), BF16),
            pltpu.VMEM((8, 128, 1024), BF16),
            pltpu.VMEM(quarter, BF16),
            pltpu.VMEM(quarter, BF16),
            pltpu.VMEM((3, 128, 1024), BF16),
            pltpu.VMEM((2, 128, 1024), BF16),
            pltpu.VMEM((1024, 128), F32),
            pltpu.VMEM((112, 1024), BF16),
            pltpu.VMEM((64, 1024), BF16),
            pltpu.VMEM((96, 1024), BF16),
            pltpu.VMEM((16, 128), F32),
            pltpu.SemaphoreType.DMA((13,)),
            pltpu.SemaphoreType.DMA((24,)),
        ],
        216,
        192,
        1,
    )(*args)


def attend_back_rows(i, length, bias, q_ref, k_ref, v_ref, o_ref, lse_ref, g_ref, dq_ref, dq_t, k_t, dk, dv):
    lane_head = lax.broadcasted_iota(jnp.int32, (ROWS, 256), 1) // HD
    first, n = i * ROWS, (i + 1) * ROWS
    q = q_ref[first:n, :] * jnp.asarray(HD**-0.5, BF16)
    live = first + lax.broadcasted_iota(jnp.int32, (ROWS, 256), 0) < length
    g = jnp.where(live, g_ref[first:n, :], 0)
    both = (g.astype(F32) * o_ref[first:n, :].astype(F32)).T
    row_dots = jnp.concatenate(
        [jnp.sum(both[HD * j : HD * j + HD], axis=0, keepdims=True) for j in range(4)], axis=0
    )
    lse = lse_ref[0:4, first:n]

    def pick(rows, j):
        at = lax.broadcasted_iota(jnp.int32, rows.shape, 0) == j
        return jnp.sum(jnp.where(at, rows, 0), axis=0, keepdims=True)

    def head(j, _):
        q_head = jnp.where(lane_head == j, q, 0)
        g_head = jnp.where(lane_head == j, g, 0)
        scores = mask_scores(dot(k_ref[0:n, :], q_head, (1, 1)), bias, first, ROWS)
        probs = jnp.exp(scores - pick(lse, j))
        grads = dot(v_ref[0:n, :], g_head, (1, 1))
        dlogits = (probs * (grads - pick(row_dots, j))).astype(BF16)
        dv[0:n, :] += dot(probs.astype(BF16), g_head, (1, 0))
        dk[0:n, :] += dot(dlogits, q_head, (1, 0))
        at = pl.ds(pl.multiple_of(j * HD, HD), HD)
        dq_t[at, :] = dot(k_t[at, 0:n], dlogits, (1, 0))
        return 0

    lax.fori_loop(0, 4, head, 0)
    dq_ref[first:n, :] = (dq_t[...].T * (HD**-0.5)).astype(BF16)


def norm_back(xhat, scale, grad, gain):
    h = grad * gain
    return scale * (
        h
        - jnp.mean(h, axis=-1, keepdims=True)
        - xhat * jnp.mean(h * xhat, axis=-1, keepdims=True)
    )


def backward_body(
    clip_len, text_len, frame_mask, text_mask, norms_in,
    h_third, h_out, h_cross, h_self, h_second, h_query, h_crossed, h_att, h_square, h_tkv, h_out_terms, h_in_terms,
    h_q, h_k, h_v, h_o, h_lse, h_hid, h_first, h_wa, h_wb, h_text, h_own,
    o_output, o_in, o_hidden, o_square, o_qkv, o_ckv, o_norm, o_text,
    v_third, v_out, after_cross, query_ref, crossed, att, mats, tkv, out_terms,
    q_ref, k_ref, v_ref, o_ref, lse, w_a, w_b, text_in,
    g_crossed, g_att, g_after, slots, t_inbox, t_near, t_far, t_total,
    i_inbox, i_near, i_far, i_out, i_in,
    g_square, s_inbox, s_slots, s_part, y_part, z_near, z_far, y_near, y_far,
    g_heads, dq_t, k_t, dk, dv, d_cols, f_inbox, f_in,
    a_terms, a_slots, a_sum, a_in, b_terms, b_slots, b_sum, b_in,
    t_terms, tt_in, n_row, n_terms, n_slots, n_sum, n_in,
    bias, loaded, local, send_sem, recv_sem,
):
    h = Here()
    w = Wire(h, send_sem, recv_sem)
    partners = frame_others(h) + clip_others(h)
    call_out(partners)
    length = clip_len[h.pair]
    tag = [0]

    def tags(n):
        tag[0] += n
        return tag[0] - n

    loads = []

    def load(src, dst):
        copy = pltpu.make_async_copy(src, dst, loaded.at[len(loads)])
        copy.start()
        loads.append(copy)
        return copy

    l_terms = load(h_out_terms, out_terms)
    own_terms = [mats.at[0, z, pl.ds(0, 4)] for z in range(4)]
    l_own = [load(h_in_terms.at[2 * z + h.core], own_terms[z]) for z in range(4)]
    l_third, l_cross = load(h_third, v_third), load(h_cross, after_cross)
    l_out, l_m2 = load(h_out, v_out), load(h_square.at[2], mats.at[2])
    l_middle = [load(*pair) for pair in ((h_crossed, crossed), (h_query, query_ref), (h_tkv, tkv))]
    l_m1 = load(h_square.at[1], mats.at[1])
    l_att = load(h_att, att)
    l_heads = [
        load(*pair)
        for pair in (
            (h_q, q_ref), (h_k, k_ref), (h_v, v_ref), (h_o, o_ref), (h_lse, lse), (h_wb, w_b), (h_text, text_in),
            (h_wa, w_a),
        )
    ]
    fill_key_bias(bias, clip_len, frame_mask, h.pair)
    text_bias = text_bias_rows(text_len, text_mask)
    hear_all(partners)

    def matrix(which):
        return mats[which].reshape(1024, 1024)

    out_scatter = ClipScatter(
        w,
        lambda c, half: out_terms.at[c, pl.ds(128 * half, 128), :],
        [slots.at[i] for i in range(6)],
        tags(6),
    )
    in_tag = tags(4)
    for z in range(4):
        w.send(h_in_terms.at[2 * z + 1 - h.core], i_inbox.at[z], in_tag + z, h.c, h.sib)
    in_scatter = ZScatter(w, i_inbox, i_near, i_far, tags(5))
    l_terms.wait()
    out_scatter.begin()

    def square_sums(which):
        sibling = SiblingSum(
            w,
            lambda f: g_square.at[which, :, f],
            lambda z: s_inbox.at[which, z],
            lambda z: s_inbox.at[which, z],
            tags(4),
        )
        clip = ClipScatter(
            w,
            lambda c, half: s_inbox.at[which, :, c, pl.ds(16 * half, 16), :],
            [s_slots.at[which, i] for i in range(6)],
            tags(6),
        )
        return sibling, clip

    squares = [square_sums(which) for which in range(3)]

    def put(which, value):
        g_square[which] = value.astype(BF16).reshape(4, 8, 32, 1024)

    def columns_of(f):
        return pl.ds(pl.multiple_of(lax.rem(f, 4) * 256, 256), 256)

    def part_of(f):
        return g_att.at[lax.div(f, 4), :, columns_of(f)]

    def text_part(f):
        return g_text.at[lax.div(f, 4), :, :, columns_of(f)]

    for copy in (l_third, l_cross, l_out):
        copy.wait()
    xhat, scale = norm_parts(after_cross[...])
    grad = v_third[...]
    gain_third = jnp.sum(grad * xhat, axis=0, keepdims=True)
    shift_third = jnp.sum(grad, axis=0, keepdims=True)
    n_row[...] = jnp.zeros_like(n_row)
    n_row[2:3, :] = gain_third
    n_row[5:6, :] = shift_third
    g_after_cross = v_out[...].reshape(256, 1024).astype(F32) + norm_back(xhat, scale, grad, norms_in[2:3, :])
    g_after[...] = g_after_cross
    after_self, own_hid = v_third, v_out
    l_self, l_own_hid = load(h_self, after_self), load(h_own, own_hid)
    branch = g_after_cross.astype(BF16)
    l_m2.wait()
    g_crossed[...] = dot(branch, matrix(2), (1, 1)).astype(BF16)
    l_first = load(h_first, mats.at[2])
    for copy in l_middle + l_own:
        copy.wait()
    put(2, dot(crossed[...], branch, (0, 0)))
    squares[2][0].begin()
    second = crossed
    l_second = load(h_second, second)
    for z in range(4):
        w.arrived(i_inbox.at[z], in_tag + z)
        add_into(i_inbox.at[z], own_terms[z])
    in_scatter.begin()
    l_m0 = load(h_square.at[0], mats.at[0])
    g_query, g_text = query_ref, tkv
    lane_head = lax.broadcasted_iota(jnp.int32, (128, 256), 1) // HD
    for clip in range(2):
        for group in range(4):
            rows, columns = pl.ds(128 * clip, 128), pl.ds(256 * group, 256)
            keys, values = tkv[clip, 0, :, columns], tkv[clip, 1, :, columns]
            query = query_ref[rows, columns] * jnp.asarray(HD**-0.5, BF16)
            probs, stacked = text_probs(query, keys, text_bias[clip], lane_head)
            grads = g_crossed[rows, columns]
            g_stacked = jnp.concatenate([jnp.where(lane_head == j, grads, 0) for j in range(4)], axis=0)
            g_probs = dot(g_stacked, values, (1, 1))
            row_dot = jnp.sum(probs * g_probs, axis=1, keepdims=True)
            g_logits = (probs * (g_probs - row_dot)).astype(BF16)
            part = dot(g_logits, keys, (1, 0))
            g_query[rows, columns] = (pick_heads(part, lane_head) * (HD**-0.5)).astype(BF16)
            g_text[clip, 0, :, columns] = dot(g_logits, stacked, (0, 0)).astype(BF16)
            g_text[clip, 1, :, columns] = dot(probs.astype(BF16), g_stacked, (0, 0)).astype(BF16)
        if clip == 0:
            out_scatter.middle()
            in_scatter.step(1)
            squares[2][0].end()
            squares[2][1].begin()
    text_sibling = SiblingSum(w, text_part, lambda z: t_inbox.at[z], lambda z: t_inbox.at[z], tags(4))
    text_sibling.begin()
    l_m1.wait()
    grad = dot(g_query[...], matrix(1), (1, 1))
    l_hid = load(h_hid, mats.at[1])
    l_self.wait()
    xhat, scale = norm_parts(after_self[...])
    n_row[1:2, :] = jnp.sum(grad * xhat, axis=0, keepdims=True)
    n_row[4:5, :] = jnp.sum(grad, axis=0, keepdims=True)
    g_after_self = g_after[...] + norm_back(xhat, scale, grad, norms_in[1:2, :])
    g_after[...] = g_after_self
    branch = g_after_self.astype(BF16)
    l_m0.wait()
    g_att[...] = dot(branch, matrix(0), (1, 1)).astype(BF16).reshape(2, 128, 1024)
    heads_tag = tags(7)
    for d in (4, 2, 6, 3, 5, 1, 7):
        f = h.step(d)
        w.send(part_of(f), g_heads.at[h.f], heads_tag + d - 1, h.c, f)
    own_part = pltpu.make_async_copy(part_of(h.f), g_heads.at[h.f], local.at[0])
    own_part.start()
    in_scatter.step(2)
    in_scatter.step(3)
    l_second.wait()
    l_att.wait()
    put(1, dot(second[...], g_query[...], (0, 0)))
    squares[1][0].begin()
    put(0, dot(att[...].reshape(256, 1024), branch, (0, 0)))
    squares[0][0].begin()
    text_sibling.end()
    text_scatter = ZScatter(w, t_inbox, t_near, t_far, tags(5))
    text_scatter.begin()
    squares[2][1].middle()
    squares[1][0].end()
    squares[1][1].begin()
    out_scatter.end()
    for half in range(2):
        rows = pl.ds(128 * half, 128)
        o_output[rows, :] = (after_cross[rows, :] + out_scatter.total(half)).astype(BF16)
    squares[0][0].end()
    squares[0][1].begin()
    in_scatter.total(i_out)
    i_tag = tags(3)
    for i, (c, f) in enumerate(clip_others(h)):
        w.send(i_out.at[c], i_in.at[h.c], i_tag + i, c, f)
    i_in[h.c] = i_out[h.c]
    squares[1][1].middle()

    def square_part(which, out, row):
        squares[which][1].end()
        for half in range(2):
            total = squares[which][1].total(half)
            out[:, row + 16 * half : row + 16 * half + 16, :] = total.astype(BF16)

    text_scatter.step(1)
    for copy in l_heads:
        copy.wait()
    k_t[...] = k_ref[...].T
    dk[...] = jnp.zeros_like(dk)
    dv[...] = jnp.zeros_like(dv)
    for d in range(1, 8):
        w.arrived(g_heads.at[lax.rem(h.f + 8 - d, 8)], heads_tag + d - 1)
    own_part.wait()
    g_rows = g_heads[...].reshape(1024, 256)

    def rows_back(i):
        attend_back_rows(
            i, length, bias, q_ref, k_ref, v_ref, o_ref, lse, g_rows, d_cols.at[0], dq_t, k_t, dk, dv
        )

    text_scatter.step(2)
    text_scatter.step(3)
    squares[0][1].middle()
    rows_back(0)
    square_part(2, s_part, 32)
    square_part(1, s_part, 0)
    z_scatter = ZScatter(w, s_part, z_near, z_far, tags(5))
    z_scatter.begin()
    rows_back(1)

    class Columns:
        def __init__(self, terms, slots, sums, inbox):
            self.sums, self.inbox, self.tag = sums, inbox, tags(13)
            self.clip = ClipScatter(
                w,
                lambda c, half: terms.at[c, pl.ds(4 * half, 4)],
                [slots.at[i] for i in range(6)],
                self.tag,
            )

        def spread(self):
            self.clip.end()
            for half in range(2):
                self.sums[4 * half : 4 * half + 4] = self.clip.total(half).astype(BF16)
            for d in (4, 2, 6, 3, 5, 1, 7):
                f = h.step(d)
                w.send(self.sums.at[f], self.inbox.at[h.f], self.tag + 5 + d, h.c, f)
            self.inbox[h.f] = self.sums[h.f]

        def wait(self):
            for d in range(1, 8):
                w.arrived(self.inbox.at[lax.rem(h.f + 8 - d, 8)], self.tag + 5 + d)

    text_scatter.total(t_total)
    g_tkv = [t_total[j].astype(BF16) for j in range(2)]
    text = text_in[h.pair]
    for j in range(2):
        b_terms[:, :, 32 * j : 32 * j + 32, :] = (
            dot(text, g_tkv[j], (0, 0)).astype(BF16).reshape(4, 8, 32, 256)
        )
    b_columns = Columns(b_terms, b_slots, b_sum, b_in)
    b_columns.clip.begin()
    t_terms[...] = (
        dot(g_tkv[0], column_weight(w_b, 0), (1, 1)) + dot(g_tkv[1], column_weight(w_b, 1), (1, 1))
    ).astype(BF16)
    tt_tag = tags(7)
    for d in range(1, 8):
        f = h.step(d)
        w.send(
            t_terms.at[pl.ds(pl.multiple_of(f * 16, 16), 16), :], tt_in.at[h.f], tt_tag + d - 1, h.c, f
        )
    tt_in[h.f] = t_terms[pl.ds(pl.multiple_of(h.f * 16, 16), 16), :]
    z_scatter.step(1)
    rows_back(2)
    square_part(0, y_part, 0)
    y_scatter = ZScatter(w, y_part, y_near, y_far, tags(5))
    y_scatter.begin()
    z_scatter.step(2)
    z_scatter.step(3)
    b_columns.clip.middle()
    rows_back(3)
    d_cols[1] = dk[...].astype(BF16)
    d_cols[2] = dv[...].astype(BF16)
    l_first.wait()
    a_columns = [Columns(a_terms.at[j], a_slots.at[j], a_sum.at[j], a_in.at[j]) for j in range(3)]
    for j in range(3):
        a_terms[j] = dot(mats[2].reshape(1024, 1024), d_cols[j], (0, 0)).astype(BF16).reshape(4, 8, 32, 256)
        a_columns[j].clip.begin()
    y_scatter.step(1)

    f_terms = mats.at[0]
    f_sibling = SiblingSum(
        w,
        lambda f: f_terms.at[lax.div(f, 2), pl.ds(pl.multiple_of(lax.rem(f, 2) * 4, 4), 4)],
        lambda z: f_inbox.at[z],
        lambda z: f_inbox.at[z],
        tags(4),
    )
    l_hid.wait()

    def frame_terms(i, _):
        rows = pl.ds(pl.multiple_of(i * 256, 256), 256)
        grad = sum(dot(d_cols[j, rows, :], column_weight(w_a, j), (1, 1)) for j in range(3))
        f_terms[i] = grad.astype(BF16).reshape(8, 32, 1024)
        xhat, _ = norm_parts(mats[1, i].reshape(256, 1024).astype(F32))
        n_row[0:1, :] += jnp.sum(grad * xhat, axis=0, keepdims=True)
        n_row[3:4, :] += jnp.sum(grad, axis=0, keepdims=True)
        return 0

    lax.fori_loop(0, 4, frame_terms, 0)
    f_sibling.begin()
    y_scatter.step(2)
    a_columns[0].clip.middle()
    f_sibling.end()
    f_tag = tags(4)
    other = 2 * (1 - h.pair)
    is_end = jnp.logical_not(h.is_gate)
    to_gate, to_far = [], []
    for j in range(2):
        to_gate.append(w.copy(f_inbox.at[other + j], f_in.at[1 + j], f_tag + 1 + j, h.c, h.partner))
        pl.when(is_end)(to_gate[j].start)
    w.send(f_inbox.at[lax.div(h.partner, 2)], f_in.at[0], f_tag, h.c, h.partner)
    for c in range(4):
        for f in range(8):
            group = 2 * c + f // 4
            n_terms[c, f] = n_row[:, 128 * group : 128 * group + 128].astype(BF16)
    n_columns = Columns(n_terms, n_slots, n_sum, n_in)
    n_columns.clip.begin()
    a_columns[1].clip.middle()
    a_columns[0].spread()
    for j in range(2):

        @pl.when(h.is_gate)
        def _():
            w.arrived(f_in.at[1 + j], f_tag + 1 + j)
            add_into(f_inbox.at[other + j], f_in.at[1 + j])

        to_far.append(w.copy(f_inbox.at[other + j], f_in.at[3], f_tag + 3, h.c, h.far[j]))
        pl.when(h.is_gate)(to_far[j].start)
    a_columns[2].clip.middle()
    a_columns[1].spread()
    n_columns.clip.middle()
    y_scatter.step(3)
    a_columns[2].spread()
    n_columns.spread()
    b_columns.spread()
    z_scatter.total(o_square.at[pl.ds(32, 64), :])
    for i, (c, f) in enumerate(clip_others(h)):
        w.arrived(i_in.at[c], i_tag + i)
    for c in range(4):
        o_in[:, 1024 * c : 1024 * c + 1024] = i_in[c].astype(F32)
    for d in range(1, 8):
        w.arrived(tt_in.at[lax.rem(h.f + 8 - d, 8)], tt_tag + d - 1)
    for p in range(2):
        o_text[p] = sum(tt_in[4 * p + q].astype(F32) for q in range(4)).astype(BF16)
    y_scatter.total(o_square.at[pl.ds(0, 32), :])
    w.arrived(f_in.at[0], f_tag)
    w.arrived(f_in.at[3], f_tag + 3)

    def hidden_out(clip, total):
        xhat, scale = norm_parts(own_hid[clip].astype(F32))
        rows = pl.ds(pl.multiple_of(clip * 128, 128), 128)
        o_hidden[clip] = (g_after[rows, :] + norm_back(xhat, scale, total, norms_in[0:1, :])).astype(BF16)

    l_own_hid.wait()
    hidden_out(h.pair, (f_inbox[h.z].astype(F32) + f_in[0].astype(F32)).reshape(128, 1024))
    hidden_out(1 - h.pair, f_in[3].astype(F32).reshape(128, 1024))
    for j in range(3):
        a_columns[j].wait()
        for q in range(4):
            o_qkv[j, :, 256 * q : 256 * q + 256] = a_in[j, q].astype(F32) + a_in[j, 4 + q].astype(F32)
    b_columns.wait()
    for j in range(2):
        for q in range(4):
            at = pl.ds(32 * j, 32)
            o_ckv[j, :, 256 * q : 256 * q + 256] = b_in[q, at, :].astype(F32) + b_in[4 + q, at, :].astype(F32)
    n_columns.wait()
    o_norm[...] = sum(n_in[f].astype(F32) for f in range(8))
    w.drain()
    for one in (in_scatter, text_scatter, z_scatter, y_scatter):
        one.drain()
    for j in range(2):
        pl.when(is_end)(to_gate[j].wait_send)
        pl.when(h.is_gate)(to_far[j].wait_send)


def backward(*args):
    def buffer(*dims):
        return pltpu.VMEM(dims, BF16)

    def full(*dims):
        return pltpu.VMEM(dims, F32)

    return comm_call(
        backward_body,
        (
            shape((256, 1024)),
            shape((32, 4096), F32),
            shape((2, 128, 1024)),
            shape((96, 1024), F32),
            shape((3, 32, 1024), F32),
            shape((2, 32, 1024), F32),
            shape((16, 128), F32),
            shape((2, 16, 1024)),
        ),
        [SMEM] * 2 + [VMEM] * 3 + [HBM] * 23,
        (VMEM,) * 8,
        [
            full(256, 1024), buffer(2, 128, 1024), full(256, 1024), buffer(256, 1024), buffer(256, 1024),
            buffer(2, 128, 1024), buffer(3, 4, 8, 32, 1024), buffer(2, 2, 128, 1024), buffer(4, 256, 1024),
            buffer(1024, 256), buffer(1024, 256), buffer(1024, 256), buffer(1024, 256), full(8, 1024),
            buffer(4, 8, 112, 256), buffer(4, 8, 64, 256), buffer(2, 128, 1024),
            buffer(256, 1024), buffer(2, 128, 1024), full(256, 1024),
            buffer(6, 128, 1024), buffer(4, 2, 128, 256), buffer(3, 2, 128, 256), buffer(2, 2, 128, 256),
            full(2, 128, 256),
            buffer(4, 4, 32, 1024), buffer(3, 4, 32, 1024), buffer(2, 4, 32, 1024),
            buffer(4, 32, 1024), buffer(4, 32, 1024),
            buffer(3, 4, 8, 32, 1024), buffer(3, 4, 4, 32, 1024), buffer(3, 6, 4, 16, 1024),
            buffer(4, 64, 1024), buffer(4, 32, 1024), buffer(3, 64, 1024), buffer(2, 64, 1024),
            buffer(3, 32, 1024), buffer(2, 32, 1024),
            buffer(8, 128, 256), full(256, ROWS), buffer(256, 1024), full(1024, 256), full(1024, 256),
            buffer(3, 1024, 256), buffer(4, 4, 32, 1024), buffer(4, 4, 32, 1024),
            buffer(3, 4, 8, 32, 256), buffer(3, 6, 4, 32, 256), buffer(3, 8, 32, 256), buffer(3, 8, 32, 256),
            buffer(4, 8, 64, 256), buffer(6, 4, 64, 256), buffer(8, 64, 256), buffer(8, 64, 256),
            buffer(128, 1024), buffer(8, 16, 1024), full(16, 1024), buffer(4, 8, 16, 128), buffer(6, 4, 16, 128),
            buffer(8, 16, 128), buffer(8, 16, 128), full(1024, 128),
            pltpu.SemaphoreType.DMA((32,)),
            pltpu.SemaphoreType.DMA((1,)),
        ],
        208,
        160,
        2,
    )(*args)


def finish_body(*refs):
    ins, outs = refs[:9], refs[9:]
    output, hidden, text, qkv, square, ckv, fin, fout, norm = ins
    o_output, o_hidden, o_text, o_qkv, o_self_out, o_cross, o_cross_out, o_fin, o_fout, o_gain, o_shift = outs
    o_fout[...] = fout[...]
    o_output[...] = output[...].reshape(2, 128, 1024)
    o_hidden[...] = hidden[...]
    o_text[...] = text[...]
    o_fin[...] = fin[...]
    o_qkv[...] = qkv[...]
    o_self_out[...] = square[0:32, :]
    o_cross[0] = square[32:64, :]
    o_cross[1:3] = ckv[...]
    o_cross_out[...] = square[64:96, :]
    place = lax.rem(lax.axis_index("frame"), 4)
    for row, out in ((0, o_gain), (3, o_shift)):
        out[...] = sum(
            jnp.where(place == i, norm[row : row + 3, 32 * i : 32 * i + 32], 0) for i in range(4)
        )


def finish(*args):
    return pl.pallas_call(
        finish_body,
        out_shape=(
            shape((2, 128, 1024)),
            shape((2, 128, 1024)),
            shape((2, 16, 1024)),
            shape((3, 32, 1024), F32),
            shape((32, 1024), F32),
            shape((3, 32, 1024), F32),
            shape((32, 1024), F32),
            shape((32, 4096), F32),
            shape((128, 1024), F32),
            shape((3, 32), F32),
            shape((3, 32), F32),
        ),
        in_specs=[VMEM] * 9,
        out_specs=(VMEM,) * 11,
        compiler_params=pltpu.CompilerParams(vmem_limit_bytes=60 * 2**20),
    )(*args)


def on_device_fast(
    hidden_in,
    text_states,
    out_grad,
    self_qkv,
    self_out,
    cross_qkv,
    cross_out,
    ffn_in,
    ffn_out,
    ln_gain,
    ln_bias,
    clip_len,
    frame_mask,
    text_len,
    text_mask,
):
    (
        hid_all, first_low, query, key, value, att_heads, lse, w_a, w_b, params, att, tkv, square,
        second, cross_query, crossed, after_self, after_cross, out_terms, in_terms, third_sum, grad_ffn_out,
    ) = forward(
        clip_len, text_len, frame_mask, text_mask, ln_gain, ln_bias, jnp.moveaxis(self_qkv, 1, 0),
        jnp.moveaxis(cross_qkv, 1, 0), self_out, cross_out, text_states, hidden_in, ffn_in, ffn_out, out_grad.reshape(256, 1024),
    )
    output, grad_ffn_in, grad_hidden, square_sum, qkv_sum, ckv_sum, norm_sum, grad_text = backward(
        clip_len, text_len, frame_mask, text_mask, params,
        third_sum, out_grad, after_cross, after_self, second, cross_query, crossed, att, square, tkv,
        out_terms, in_terms.reshape(8, 4, 32, 1024), query, key, value, att_heads, lse,
        hid_all.reshape(4, 8, 32, 1024), first_low.reshape(4, 8, 32, 1024), w_a, w_b, text_states, hidden_in,
    )
    results = finish(output, grad_hidden, grad_text, qkv_sum, square_sum, ckv_sum, grad_ffn_in, grad_ffn_out, norm_sum)
    output, grad_hidden, grad_text, qkv, g_self_out, cross, g_cross_out, grad_ffn_in, grad_ffn_out, gains, shifts = results
    return (
        output,
        grad_hidden,
        grad_text,
        jnp.moveaxis(qkv, 0, 1),
        g_self_out,
        jnp.moveaxis(cross, 0, 1),
        g_cross_out,
        grad_ffn_in,
        grad_ffn_out,
        gains,
        shifts,
    )


def solution(mesh):
    return jax.shard_map(
        on_device_fast if fits(mesh) else on_device_any,
        mesh=mesh,
        in_specs=(
            P("clip", "frame", None),
            P("clip", None, None),
            P("clip", "frame", None),
            P(("clip", "frame"), None, None),
            P(("clip", "frame"), None),
            P(("clip", "frame"), None, None),
            P(("clip", "frame"), None),
            P(("clip", "frame"), None),
            P(("clip", "frame"), None),
            P(None, ("clip", "frame")),
            P(None, ("clip", "frame")),
            P("clip"),
            P("clip", None),
            P("clip"),
            P("clip", None),
        ),
        out_specs=(
            P("clip", "frame", None),
            P("clip", "frame", None),
            P("clip", "frame", None),
            P(("clip", "frame"), None, None),
            P(("clip", "frame"), None),
            P(("clip", "frame"), None, None),
            P(("clip", "frame"), None),
            P(("clip", "frame"), None),
            P(("clip", "frame"), None),
            P(None, ("clip", "frame")),
            P(None, ("clip", "frame")),
        ),
        check_vma=False,
    )
```

```python
import functools

import jax
import jax.numpy as jnp
from jax import lax
from jax.experimental import pallas as pl
from jax.experimental.pallas import tpu as pltpu
from jax.sharding import PartitionSpec as P

HD = 64


MASKED = -1000000000.0
EPSILON = 1e-05


def layer_norm(value, gain, shift):
    average = jnp.mean(value, axis=-1, keepdims=True)
    centered = value - average
    variance = jnp.mean(centered * centered, axis=-1, keepdims=True)
    return centered * lax.rsqrt(variance + EPSILON) * gain + shift


def activate(value):
    return jax.nn.gelu(value, approximate=False)


def project(left, right):
    return jnp.einsum("cnd,de->cne", left, right, preferred_element_type=jnp.float32)


def project_back(grad_rows, weight):
    return jnp.einsum("cne,de->cnd", grad_rows, weight, preferred_element_type=jnp.float32)


def weight_grad(left, right):
    return jnp.einsum("cnd,cne->de", left, right, preferred_element_type=jnp.float32)


def fetch_attention(self_qkv, self_out, cross_qkv, cross_out, ln_gain, ln_bias):
    return (
        lax.all_gather(self_qkv, ("clip", "frame"), axis=0, tiled=True),
        lax.all_gather(self_out, ("clip", "frame"), axis=0, tiled=True),
        lax.all_gather(cross_qkv, ("clip", "frame"), axis=0, tiled=True),
        lax.all_gather(cross_out, ("clip", "frame"), axis=0, tiled=True),
        lax.all_gather(ln_gain, ("clip", "frame"), axis=1, tiled=True),
        lax.all_gather(ln_bias, ("clip", "frame"), axis=1, tiled=True),
    )


def fetch_ffn(ffn_in, ffn_out):
    return (
        lax.all_gather(ffn_in, ("clip", "frame"), axis=0, tiled=True),
        lax.all_gather(ffn_out, ("clip", "frame"), axis=0, tiled=True),
    )


def self_masks(first_row, block_rows, clip_len, key_valid):
    columns = jnp.arange(key_valid.shape[1], dtype=jnp.int32)
    row_ids = first_row + jnp.arange(block_rows, dtype=jnp.int32)
    diagonal = columns[None, :] == row_ids[:, None]
    allowed = (columns[None, :] <= row_ids[:, None])[None] & (
        key_valid[:, None, :] | diagonal[None]
    )
    live_rows = (row_ids[None, :] < clip_len[:, None]).astype(jnp.float32)
    return (allowed[:, None], live_rows[:, None, :, None])


def self_forward(query_rows, key_rows, value_rows, clip_len, key_valid):
    length = query_rows.shape[1]
    block_rows = min(512, length)
    score_scale = query_rows.shape[3] ** (-0.5)

    def one_block(block_index):
        first_row = block_index * block_rows
        query_block = lax.dynamic_slice_in_dim(query_rows, first_row, block_rows, 1)
        raw_scores = jnp.einsum(
            "cqhd,ckhd->chqk", query_block, key_rows, preferred_element_type=jnp.float32
        )
        allowed, live_rows = self_masks(first_row, block_rows, clip_len, key_valid)
        logits = jnp.where(allowed, raw_scores * score_scale, MASKED)
        row_max = jnp.max(logits, axis=-1, keepdims=True)
        exponent = jnp.exp(logits - row_max)
        row_sum = jnp.sum(exponent, axis=-1, keepdims=True)
        weights = (exponent / row_sum * live_rows).astype(jnp.bfloat16)
        attended = jnp.einsum(
            "chqk,ckhd->cqhd", weights, value_rows, preferred_element_type=jnp.float32
        )
        return (attended.astype(jnp.bfloat16), row_max + jnp.log(row_sum))

    blocks, log_sums = lax.map(one_block, jnp.arange(length // block_rows, dtype=jnp.int32))
    return (jnp.moveaxis(blocks, 0, 1).reshape(query_rows.shape), log_sums)


def self_backward(query_rows, key_rows, value_rows, grad_rows, log_sums, clip_len, key_valid):
    length = query_rows.shape[1]
    block_rows = min(512, length)
    score_scale = query_rows.shape[3] ** (-0.5)

    def one_block(totals, block_index):
        grad_keys, grad_values = totals
        first_row = block_index * block_rows
        query_block = lax.dynamic_slice_in_dim(query_rows, first_row, block_rows, 1)
        grad_block = lax.dynamic_slice_in_dim(grad_rows, first_row, block_rows, 1)
        raw_scores = jnp.einsum(
            "cqhd,ckhd->chqk", query_block, key_rows, preferred_element_type=jnp.float32
        )
        allowed, live_rows = self_masks(first_row, block_rows, clip_len, key_valid)
        logits = jnp.where(allowed, raw_scores * score_scale, MASKED)
        probs = jnp.exp(logits - log_sums[block_index])
        weights = (probs * live_rows).astype(jnp.bfloat16)
        grad_probs = (
            jnp.einsum(
                "cqhd,ckhd->chqk", grad_block, value_rows, preferred_element_type=jnp.float32
            )
            * live_rows
        )
        row_dot = jnp.sum(probs * grad_probs, axis=-1, keepdims=True)
        grad_scores = (probs * (grad_probs - row_dot)).astype(jnp.bfloat16)
        grad_query = (
            jnp.einsum("chqk,ckhd->cqhd", grad_scores, key_rows, preferred_element_type=jnp.float32)
            * score_scale
        )
        grad_keys = (
            grad_keys
            + jnp.einsum(
                "chqk,cqhd->ckhd", grad_scores, query_block, preferred_element_type=jnp.float32
            )
            * score_scale
        )
        grad_values = grad_values + jnp.einsum(
            "chqk,cqhd->ckhd", weights, grad_block, preferred_element_type=jnp.float32
        )
        return ((grad_keys, grad_values), grad_query)

    zeros = jnp.zeros(key_rows.shape, jnp.float32)
    (grad_keys, grad_values), grad_blocks = lax.scan(
        one_block, (zeros, zeros), jnp.arange(length // block_rows, dtype=jnp.int32)
    )
    grad_query = jnp.moveaxis(grad_blocks, 0, 1).reshape(query_rows.shape)
    return (grad_query, grad_keys, grad_values)


def text_allowed(text_len, text_mask):
    slots = jnp.arange(text_mask.shape[1], dtype=jnp.int32)
    allowed = (slots[None, :] < text_len[:, None]) & ((text_mask > 0) | (slots[None, :] == 0))
    return allowed[:, None, None, :]


def cross_forward(query_rows, key_rows, value_rows, allowed):
    score_scale = query_rows.shape[3] ** (-0.5)
    raw_scores = jnp.einsum(
        "cqhd,ckhd->chqk", query_rows, key_rows, preferred_element_type=jnp.float32
    )
    logits = jnp.where(allowed, raw_scores * score_scale, MASKED)
    row_max = jnp.max(logits, axis=-1, keepdims=True)
    exponent = jnp.exp(logits - row_max)
    row_sum = jnp.sum(exponent, axis=-1, keepdims=True)
    weights = (exponent / row_sum).astype(jnp.bfloat16)
    crossed = jnp.einsum("chqk,ckhd->cqhd", weights, value_rows, preferred_element_type=jnp.float32)
    return (crossed.astype(jnp.bfloat16), row_max + jnp.log(row_sum))


def cross_backward(query_rows, key_rows, value_rows, grad_rows, log_sums, allowed):
    score_scale = query_rows.shape[3] ** (-0.5)
    raw_scores = jnp.einsum(
        "cqhd,ckhd->chqk", query_rows, key_rows, preferred_element_type=jnp.float32
    )
    logits = jnp.where(allowed, raw_scores * score_scale, MASKED)
    probs = jnp.exp(logits - log_sums)
    weights = probs.astype(jnp.bfloat16)
    grad_probs = jnp.einsum(
        "cqhd,ckhd->chqk", grad_rows, value_rows, preferred_element_type=jnp.float32
    )
    row_dot = jnp.sum(probs * grad_probs, axis=-1, keepdims=True)
    grad_scores = (probs * (grad_probs - row_dot)).astype(jnp.bfloat16)
    grad_query = (
        jnp.einsum("chqk,ckhd->cqhd", grad_scores, key_rows, preferred_element_type=jnp.float32)
        * score_scale
    )
    grad_keys = (
        jnp.einsum("chqk,cqhd->ckhd", grad_scores, query_rows, preferred_element_type=jnp.float32)
        * score_scale
    )
    grad_values = jnp.einsum(
        "chqk,cqhd->ckhd", weights, grad_rows, preferred_element_type=jnp.float32
    )
    return (grad_query, grad_keys, grad_values)


def sum_ffn(grad_ffn_in, grad_ffn_out):
    return (
        lax.psum_scatter(grad_ffn_in, ("clip", "frame"), scatter_dimension=0, tiled=True),
        lax.psum_scatter(grad_ffn_out, ("clip", "frame"), scatter_dimension=0, tiled=True),
    )


def sum_attention(
    grad_self_qkv, grad_self_out, grad_cross_qkv, grad_cross_out, grad_gains, grad_shifts
):
    return (
        lax.psum_scatter(grad_self_qkv, ("clip", "frame"), scatter_dimension=0, tiled=True),
        lax.psum_scatter(grad_self_out, ("clip", "frame"), scatter_dimension=0, tiled=True),
        lax.psum_scatter(grad_cross_qkv, ("clip", "frame"), scatter_dimension=0, tiled=True),
        lax.psum_scatter(grad_cross_out, ("clip", "frame"), scatter_dimension=0, tiled=True),
        lax.psum_scatter(grad_gains, ("clip", "frame"), scatter_dimension=1, tiled=True),
        lax.psum_scatter(grad_shifts, ("clip", "frame"), scatter_dimension=1, tiled=True),
    )


def on_device_any(
    hidden_in,
    text_states,
    out_grad,
    self_qkv,
    self_out,
    cross_qkv,
    cross_out,
    ffn_in,
    ffn_out,
    ln_gain,
    ln_bias,
    clip_len,
    frame_mask,
    text_len,
    text_mask,
):
    clip_count, frames, model_width = hidden_in.shape
    text_slots = text_states.shape[1]
    group_count = lax.axis_size("frame")
    columns_here = model_width // group_count
    heads_here = columns_here // HD
    length = frames * group_count
    frame_index = lax.axis_index("frame")
    full_qkv, full_out, full_cross, full_cross_out, gains_low, shifts_low = fetch_attention(
        self_qkv, self_out, cross_qkv, cross_out, ln_gain, ln_bias
    )
    gains = gains_low.astype(jnp.float32)
    shifts = shifts_low.astype(jnp.float32)
    hidden = hidden_in.astype(jnp.float32)
    first_norm, first_pull = jax.vjp(layer_norm, hidden, gains[0], shifts[0])
    first_low = first_norm.astype(jnp.bfloat16)
    query_low = project(first_low, full_qkv[:, 0]).astype(jnp.bfloat16)
    key_low = project(first_low, full_qkv[:, 1]).astype(jnp.bfloat16)
    value_low = project(first_low, full_qkv[:, 2]).astype(jnp.bfloat16)
    query_heads, key_heads, value_heads = (
        lax.all_to_all(query_low, "frame", split_axis=2, concat_axis=1, tiled=True),
        lax.all_to_all(key_low, "frame", split_axis=2, concat_axis=1, tiled=True),
        lax.all_to_all(value_low, "frame", split_axis=2, concat_axis=1, tiled=True),
    )
    head_shape = (clip_count, length, heads_here, HD)
    query_heads = query_heads.reshape(head_shape)
    key_heads = key_heads.reshape(head_shape)
    value_heads = value_heads.reshape(head_shape)
    columns = jnp.arange(length, dtype=jnp.int32)
    key_valid = (columns[None, :] < clip_len[:, None]) & (frame_mask > 0)
    attended_heads, self_sums = self_forward(
        query_heads, key_heads, value_heads, clip_len, key_valid
    )
    attended = lax.all_to_all(
        attended_heads.reshape(clip_count, length, columns_here),
        "frame",
        split_axis=1,
        concat_axis=2,
        tiled=True,
    )
    after_self = hidden + project(attended, full_out)
    second_norm, second_pull = jax.vjp(layer_norm, after_self, gains[1], shifts[1])
    second_low = second_norm.astype(jnp.bfloat16)
    cross_query = project(second_low, full_cross[:, 0]).astype(jnp.bfloat16)
    cross_query_heads = lax.all_to_all(
        cross_query, "frame", split_axis=2, concat_axis=1, tiled=True
    ).reshape(head_shape)
    key_columns = lax.dynamic_slice_in_dim(
        full_cross[:, 1], frame_index * columns_here, columns_here, 1
    )
    value_columns = lax.dynamic_slice_in_dim(
        full_cross[:, 2], frame_index * columns_here, columns_here, 1
    )
    text_shape = (clip_count, text_slots, heads_here, HD)
    text_keys = project(text_states, key_columns).astype(jnp.bfloat16).reshape(text_shape)
    text_values = project(text_states, value_columns).astype(jnp.bfloat16).reshape(text_shape)
    allowed_text = text_allowed(text_len, text_mask)
    crossed_heads, cross_sums = cross_forward(
        cross_query_heads, text_keys, text_values, allowed_text
    )
    crossed = lax.all_to_all(
        crossed_heads.reshape(clip_count, length, columns_here),
        "frame",
        split_axis=1,
        concat_axis=2,
        tiled=True,
    )
    after_cross = after_self + project(crossed, full_cross_out)
    ffn_weight_in, ffn_weight_out = fetch_ffn(ffn_in, ffn_out)
    third_norm, third_pull = jax.vjp(layer_norm, after_cross, gains[2], shifts[2])
    third_low = third_norm.astype(jnp.bfloat16)
    pre_act = project(third_low, ffn_weight_in)
    activated, gelu_pull = jax.vjp(activate, pre_act)
    inner_low = activated.astype(jnp.bfloat16)
    output = (after_cross + project(inner_low, ffn_weight_out)).astype(jnp.bfloat16)
    ffn_weight_in, ffn_weight_out = fetch_ffn(ffn_in, ffn_out)
    grad_ffn_out = weight_grad(inner_low, out_grad)
    (grad_pre,) = gelu_pull(project_back(out_grad, ffn_weight_out))
    grad_pre_low = grad_pre.astype(jnp.bfloat16)
    grad_ffn_in = weight_grad(third_low, grad_pre_low)
    ffn_sums = sum_ffn(grad_ffn_in, grad_ffn_out)
    grad_third, gain_third, shift_third = third_pull(project_back(grad_pre_low, ffn_weight_in))
    grad_after_cross = out_grad.astype(jnp.float32) + grad_third
    full_qkv, full_out, full_cross, full_cross_out, gains_low, shifts_low = fetch_attention(
        self_qkv, self_out, cross_qkv, cross_out, ln_gain, ln_bias
    )
    key_columns = lax.dynamic_slice_in_dim(
        full_cross[:, 1], frame_index * columns_here, columns_here, 1
    )
    value_columns = lax.dynamic_slice_in_dim(
        full_cross[:, 2], frame_index * columns_here, columns_here, 1
    )
    cross_branch = grad_after_cross.astype(jnp.bfloat16)
    grad_cross_out = weight_grad(crossed, cross_branch)
    grad_crossed = project_back(cross_branch, full_cross_out).astype(jnp.bfloat16)
    grad_crossed_heads = lax.all_to_all(
        grad_crossed, "frame", split_axis=2, concat_axis=1, tiled=True
    ).reshape(head_shape)
    grad_cq, grad_tk, grad_tv = cross_backward(
        cross_query_heads, text_keys, text_values, grad_crossed_heads, cross_sums, allowed_text
    )
    grad_tk_low = grad_tk.astype(jnp.bfloat16).reshape(clip_count, text_slots, columns_here)
    grad_tv_low = grad_tv.astype(jnp.bfloat16).reshape(clip_count, text_slots, columns_here)
    text_terms = project_back(grad_tk_low, key_columns) + project_back(grad_tv_low, value_columns)
    grad_text = lax.psum_scatter(
        text_terms.astype(jnp.bfloat16), "frame", scatter_dimension=1, tiled=True
    )
    empty_square = jnp.zeros((model_width, model_width), jnp.float32)
    grad_cross_key = lax.dynamic_update_slice_in_dim(
        empty_square, weight_grad(text_states, grad_tk_low), frame_index * columns_here, 1
    )
    grad_cross_value = lax.dynamic_update_slice_in_dim(
        empty_square, weight_grad(text_states, grad_tv_low), frame_index * columns_here, 1
    )
    grad_cq_low = grad_cq.astype(jnp.bfloat16).reshape(clip_count, length, columns_here)
    grad_cross_query = lax.all_to_all(grad_cq_low, "frame", split_axis=1, concat_axis=2, tiled=True)
    grad_cross_qw = weight_grad(second_low, grad_cross_query)
    grad_second, gain_second, shift_second = second_pull(
        project_back(grad_cross_query, full_cross[:, 0])
    )
    grad_after_self = grad_after_cross + grad_second
    self_branch = grad_after_self.astype(jnp.bfloat16)
    grad_self_out = weight_grad(attended, self_branch)
    grad_attended = project_back(self_branch, full_out).astype(jnp.bfloat16)
    grad_attended_heads = lax.all_to_all(
        grad_attended, "frame", split_axis=2, concat_axis=1, tiled=True
    ).reshape(head_shape)
    grad_query, grad_keys, grad_values = self_backward(
        query_heads, key_heads, value_heads, grad_attended_heads, self_sums, clip_len, key_valid
    )
    flat_shape = (clip_count, length, columns_here)
    grad_query, grad_keys, grad_values = (
        lax.all_to_all(
            grad_query.astype(jnp.bfloat16).reshape(flat_shape),
            "frame",
            split_axis=1,
            concat_axis=2,
            tiled=True,
        ),
        lax.all_to_all(
            grad_keys.astype(jnp.bfloat16).reshape(flat_shape),
            "frame",
            split_axis=1,
            concat_axis=2,
            tiled=True,
        ),
        lax.all_to_all(
            grad_values.astype(jnp.bfloat16).reshape(flat_shape),
            "frame",
            split_axis=1,
            concat_axis=2,
            tiled=True,
        ),
    )
    grad_self_qkv = jnp.stack(
        [
            weight_grad(first_low, grad_query),
            weight_grad(first_low, grad_keys),
            weight_grad(first_low, grad_values),
        ],
        axis=1,
    )
    grad_first_norm = (
        project_back(grad_query, full_qkv[:, 0])
        + project_back(grad_keys, full_qkv[:, 1])
        + project_back(grad_values, full_qkv[:, 2])
    )
    grad_first, gain_first, shift_first = first_pull(grad_first_norm)
    grad_hidden = (grad_after_self + grad_first).astype(jnp.bfloat16)
    grad_cross_qkv = jnp.stack([grad_cross_qw, grad_cross_key, grad_cross_value], axis=1)
    grad_gains = jnp.stack([gain_first, gain_second, gain_third])
    grad_shifts = jnp.stack([shift_first, shift_second, shift_third])
    attn_sums = sum_attention(
        grad_self_qkv, grad_self_out, grad_cross_qkv, grad_cross_out, grad_gains, grad_shifts
    )
    return (
        output,
        grad_hidden,
        grad_text,
        attn_sums[0],
        attn_sums[1],
        attn_sums[2],
        attn_sums[3],
        ffn_sums[0],
        ffn_sums[1],
        attn_sums[4],
        attn_sums[5],
    )


MESH = pl.DeviceIdType.MESH
HBM = pl.BlockSpec(memory_space=pl.ANY)
VMEM = pl.BlockSpec(memory_space=pltpu.VMEM)
SMEM = pl.BlockSpec(memory_space=pltpu.SMEM)
NEG = -1e30
F32 = jnp.float32
BF16 = jnp.bfloat16


def fits(mesh):
    return mesh.shape["clip"] == 4 and mesh.shape["frame"] == 8


class Here:
    def __init__(self):
        self.c = lax.axis_index("clip")
        self.f = lax.axis_index("frame")
        self.core = lax.rem(self.f, 2)
        self.z = lax.div(self.f, 2)
        self.pair = lax.div(self.z, 2)
        self.role = lax.rem(self.z, 2)
        self.group = lax.rem(self.f, 4)
        self.cx = self.c + 1 - 2 * lax.rem(self.c, 2)
        self.cy = lax.rem(self.c + 2, 4)
        self.cd = 3 - self.c
        self.sib = self.f + 1 - 2 * self.core
        self.partner = self.f + 2 - 4 * self.role
        self.far_gate = 2 * (2 - self.pair) + self.core
        self.is_gate = self.role + self.pair == 1
        self.far = [2 * (2 * (1 - self.pair) + j) + self.core for j in range(2)]

    def step(self, d):
        return lax.rem(self.f + d, 8)

    def zstep(self, d):
        return lax.rem(self.f + 2 * d, 8)


class Wire:
    def __init__(self, here, send_sem, recv_sem):
        self.here, self.send_sem, self.recv_sem = here, send_sem, recv_sem
        self.used = 0
        self.open = []

    def copy(self, src, dst, tag, c, f):
        self.used += 1
        return pltpu.make_async_remote_copy(
            src_ref=src,
            dst_ref=dst,
            send_sem=self.send_sem.at[self.used - 1],
            recv_sem=self.recv_sem.at[tag],
            device_id=(c, f),
            device_id_type=MESH,
        )

    def send(self, src, dst, tag, c, f):
        copy = self.copy(src, dst, tag, c, f)
        copy.start()
        self.open.append(copy)

    def arrived(self, dst, tag):
        pltpu.make_async_remote_copy(
            src_ref=dst,
            dst_ref=dst,
            send_sem=self.send_sem.at[0],
            recv_sem=self.recv_sem.at[tag],
            device_id=(self.here.c, self.here.sib),
            device_id_type=MESH,
        ).wait_recv()

    def drain(self):
        for copy in self.open:
            copy.wait_send()
        self.open = []


def call_out(devices):
    barrier = pltpu.get_barrier_semaphore()
    for device in devices:
        pl.semaphore_signal(barrier, inc=1, device_id=device, device_id_type=MESH)


def hear_all(devices):
    pl.semaphore_wait(pltpu.get_barrier_semaphore(), len(devices))


def frame_others(here):
    return [(here.c, here.step(d)) for d in range(1, 8)]


def clip_others(here):
    return [(here.cx, here.f), (here.cy, here.f), (here.cd, here.f)]


class ClipGather:
    def __init__(self, wire, block, tag, own=None):
        self.wire, self.block, self.tag = wire, block, tag
        self.own = own or (lambda half: block(wire.here.c, half))

    def begin(self):
        h, w, b, t, own = self.wire.here, self.wire, self.block, self.tag, self.own
        w.send(own(0), b(h.c, 0), t, h.cx, h.f)
        w.send(own(1), b(h.c, 1), t + 2, h.cy, h.f)
        w.send(own(1), b(h.c, 1), t + 1, h.cx, h.f)
        w.send(own(0), b(h.c, 0), t + 3, h.cy, h.f)

    def middle(self):
        h, w, b, t = self.wire.here, self.wire, self.block, self.tag
        w.arrived(b(h.cx, 0), t)
        w.send(b(h.cx, 0), b(h.cx, 0), t + 4, h.cy, h.f)
        w.arrived(b(h.cy, 1), t + 2)
        w.send(b(h.cy, 1), b(h.cy, 1), t + 5, h.cx, h.f)

    def near(self):
        h, w, b, t = self.wire.here, self.wire, self.block, self.tag
        w.arrived(b(h.cx, 1), t + 1)
        w.arrived(b(h.cy, 0), t + 3)

    def end(self):
        h, w, b, t = self.wire.here, self.wire, self.block, self.tag
        w.arrived(b(h.cd, 0), t + 4)
        w.arrived(b(h.cd, 1), t + 5)


class ZGather:
    def __init__(self, wire, slot, tag, own=None):
        self.wire, self.slot, self.tag = wire, slot, tag
        self.own = own if own is not None else slot(wire.here.f)
        self.open = []

    def step(self, s):
        h, w = self.wire.here, self.wire
        left, right = h.f - 2 * (s - 1), h.f + 2 * (s - 1)
        if s > 1:

            @pl.when(left >= 0)
            def _():
                w.arrived(self.slot(left), self.tag + s - 2)

            @pl.when(right <= 7)
            def _():
                w.arrived(self.slot(right), self.tag + 3 + s - 2)

        if s > 3:
            return
        for block, tag, go, to in (
            (left, self.tag, (left >= 0) & (h.z <= 2), h.f + 2),
            (right, self.tag + 3, (right <= 7) & (h.z >= 1), h.f - 2),
        ):
            src = self.own if s == 1 else self.slot(block)
            copy = w.copy(src, self.slot(block), tag + s - 1, h.c, to)
            pl.when(go)(copy.start)
            self.open.append((go, copy))

    def relay(self, d):
        h, w = self.wire.here, self.wire
        f = h.zstep(d)
        w.send(self.own if d == 0 else self.slot(f), self.slot(f), self.tag + 6 + d, h.c, h.sib)

    def end(self):
        h, w = self.wire.here, self.wire
        for d in range(4):
            w.arrived(self.slot(h.zstep(d) + h.sib - h.f), self.tag + 6 + d)

    def drain(self):
        for go, copy in self.open:
            pl.when(go)(copy.wait_send)


class MatrixGather:
    def __init__(self, wire, block, rows, tag):
        h = wire.here
        self.wire, self.block, self.tag = wire, block, tag
        self.z = ZGather(wire, lambda f: block(h.c, f), tag)
        toward = 2 - 4 * h.pair
        at_end = jnp.logical_not(h.is_gate)
        self.order = [
            h.f,
            h.f + toward,
            jnp.where(at_end, h.f + 2 * toward, h.f - toward),
            jnp.where(at_end, h.f + 3 * toward, h.f + 2 * toward),
        ]
        self.clip = [
            ClipGather(
                wire,
                lambda c, half, f=f: block(c, f).at[pl.ds(rows // 2 * half, rows // 2), :],
                tag + 10 + 6 * d,
            )
            for d, f in enumerate(self.order)
        ]

    def step(self, s):
        self.z.step(s)
        self.clip[s - 1].begin()
        self.z.relay(s - 1) if s == 1 else None
        if s == 4:
            for d in range(1, 4):
                self.z.relay(d)

    def _relay(self, d, i, c):
        h, w = self.wire.here, self.wire
        block = self.block(c, self.order[d])
        w.send(block, block, self.tag + 34 + 3 * d + i, h.c, h.sib)

    def middle(self, d):
        self.clip[d].middle()

    def near(self, d):
        h = self.wire.here
        self.clip[d].near()
        self._relay(d, 0, h.cx)
        self._relay(d, 1, h.cy)

    def last(self, d):
        self.clip[d].end()
        self._relay(d, 2, self.wire.here.cd)

    def end(self):
        h, w = self.wire.here, self.wire
        self.z.end()
        for d in range(4):
            f = self.order[d] + h.sib - h.f
            for i, c in enumerate((h.cx, h.cy, h.cd)):
                w.arrived(self.block(c, f), self.tag + 34 + 3 * d + i)


class ClipScatter:
    def __init__(self, wire, parts, slots, tag):
        self.wire, self.parts, self.slots, self.tag = wire, parts, slots, tag

    def begin(self, which=None):
        h, w, p, s, t = self.wire.here, self.wire, self.parts, self.slots, self.tag
        if which != 1:
            w.send(p(h.cd, 0), s[0], t, h.cx, h.f)
            w.send(p(h.cd, 1), s[1], t + 1, h.cy, h.f)
        if which != 0:
            w.send(p(h.cx, 0), s[2], t + 2, h.cx, h.f)
            w.send(p(h.cy, 1), s[3], t + 3, h.cy, h.f)

    def middle(self):
        h, w, p, s, t = self.wire.here, self.wire, self.parts, self.slots, self.tag
        w.arrived(s[0], t)
        add_into(s[0], p(h.cy, 0))
        w.send(s[0], s[4], t + 4, h.cy, h.f)
        w.arrived(s[1], t + 1)
        add_into(s[1], p(h.cx, 1))
        w.send(s[1], s[5], t + 5, h.cx, h.f)

    def end(self):
        w, s, t = self.wire, self.slots, self.tag
        for i in range(2, 6):
            w.arrived(s[i], t + i)

    def total(self, half):
        s = self.slots
        first, second = (s[2], s[4]) if half == 0 else (s[5], s[3])
        own = self.parts(self.wire.here.c, half)
        return own[...].astype(F32) + first[...].astype(F32) + second[...].astype(F32)


class ZScatter:
    def __init__(self, wire, terms, near, far, tag):
        self.wire, self.terms, self.near, self.far, self.tag = wire, terms, near, far, tag
        self.open = []

    def term(self, m):
        pair = self.wire.here.pair
        return self.terms.at[m + pair * (3 - 2 * m)]

    def _start(self, go, src, dst, tag, f):
        copy = self.wire.copy(src, dst, self.tag + tag, self.wire.here.c, f)
        pl.when(go)(copy.start)
        self.open.append((go, copy))

    def begin(self):
        h = self.wire.here
        for i, m in enumerate((3, 2, 1)):
            self._start(jnp.logical_not(h.is_gate), self.term(m), self.near.at[i], i, h.partner)

    def step(self, s):
        h, w = self.wire.here, self.wire
        block, m, tag, to, f = (
            (self.near.at[0], 3, 0, 0, h.far_gate),
            (self.near.at[1], 2, 1, 1, h.far_gate),
            (self.far.at[0], 0, 3, 0, h.partner),
        )[s - 1]

        @pl.when(h.is_gate)
        def _():
            w.arrived(block, self.tag + tag)
            add_into(block, self.term(m))

        self._start(h.is_gate, block, self.far.at[to], 3 + to, f)

    def end(self):
        h, w = self.wire.here, self.wire

        @pl.when(h.is_gate)
        def _():
            w.arrived(self.near.at[2], self.tag + 2)
            w.arrived(self.far.at[1], self.tag + 4)

        @pl.when(jnp.logical_not(h.is_gate))
        def _():
            w.arrived(self.far.at[0], self.tag + 3)

    def total(self, out):
        h = self.wire.here
        self.end()

        @pl.when(h.is_gate)
        def _():
            others = self.near[2].astype(F32) + self.far[1].astype(F32)
            out[...] = (self.terms[h.z].astype(F32) + others).astype(out.dtype)

        @pl.when(jnp.logical_not(h.is_gate))
        def _():
            out[...] = (self.terms[h.z].astype(F32) + self.far[0].astype(F32)).astype(out.dtype)

    def drain(self):
        for go, copy in self.open:
            pl.when(go)(copy.wait_send)


class SiblingSum:
    def __init__(self, wire, terms, inbox, sums, tag):
        self.wire, self.terms, self.inbox, self.sums, self.tag = wire, terms, inbox, sums, tag

    def begin(self):
        h, w = self.wire.here, self.wire
        for z in range(4):
            w.send(self.terms(2 * z + 1 - h.core), self.inbox(z), self.tag + z, h.c, h.sib)

    def end(self):
        h, w = self.wire.here, self.wire
        for z in range(4):
            w.arrived(self.inbox(z), self.tag + z)
            own, other = self.terms(2 * z + h.core), self.inbox(z)
            self.sums(z)[...] = (own[...].astype(F32) + other[...].astype(F32)).astype(BF16)


def add_into(into, other):
    into[...] = (into[...].astype(F32) + other[...].astype(F32)).astype(BF16)


class LocalCopy:
    def __init__(self, src, through, dst, sem):
        self.a = pltpu.make_async_copy(src, through, sem)
        self.b = pltpu.make_async_copy(through, dst, sem)
        self.a.start()

    def turn(self):
        self.a.wait()
        self.b.start()

    def wait(self):
        self.b.wait()


def comm_call(body, out_shape, in_specs, out_specs, scratch, copies, tags, collective_id, cost=None):
    return pl.pallas_call(
        body,
        out_shape=out_shape,
        in_specs=in_specs,
        out_specs=out_specs,
        scratch_shapes=list(scratch)
        + [pltpu.SemaphoreType.DMA((copies,)), pltpu.SemaphoreType.DMA((tags,))],
        compiler_params=pltpu.CompilerParams(
            collective_id=collective_id, has_side_effects=True, vmem_limit_bytes=60 * 2**20
        ),
    )


def shape(dims, dtype=BF16):
    return jax.ShapeDtypeStruct(dims, dtype)


ROWS = 256


def dot(left, right, contract):
    return lax.dot_general(left, right, ((contract[:1], contract[1:]), ((), ())), preferred_element_type=F32)


def fill_key_bias(bias, clip_len, frame_mask, clip):
    column = lax.broadcasted_iota(jnp.int32, (1, 1024), 1)
    valid = (column < clip_len[clip]) & (frame_mask[pl.ds(clip, 1), :] > 0)
    row = jnp.where(valid, 0.0, NEG).astype(F32)
    bias[...] = jnp.broadcast_to(row, (128, 1024)).T


def text_bias_rows(text_len, text_mask):
    slot = lax.broadcasted_iota(jnp.int32, (1, 128), 1)
    rows = []
    for clip in range(2):
        valid = (slot < text_len[clip]) & ((text_mask[clip : clip + 1, :] > 0) | (slot == 0))
        rows.append(jnp.where(valid, 0.0, NEG).astype(F32))
    return rows


def mask_scores(scores, bias_ref, first, rows):
    low = scores[first:] + bias_ref[first : first + rows, 0:1]
    key = lax.broadcasted_iota(jnp.int32, (rows, rows), 0)
    query = lax.broadcasted_iota(jnp.int32, (rows, rows), 1)
    low = jnp.where(key < query, low, jnp.where(key == query, scores[first:], NEG))
    if first == 0:
        return low
    return jnp.concatenate([scores[:first] + bias_ref[0:first, 0:1], low], axis=0)


def norm_parts(value):
    centered = value - jnp.mean(value, axis=-1, keepdims=True)
    scale = lax.rsqrt(jnp.mean(centered * centered, axis=-1, keepdims=True) + EPSILON)
    return centered * scale, scale


def column_weight(cols, j):
    return cols[:, :, 32 * j : 32 * j + 32, :].reshape(1024, 256)


def attend_rows(i, length, bias, q_ref, k_ref, v_t, o_ref, lse_ref, out_t):
    lane_head = lax.broadcasted_iota(jnp.int32, (ROWS, 256), 1) // HD
    first, n = i * ROWS, (i + 1) * ROWS
    q = q_ref[first:n, :]

    def head(j, _):
        q_head = jnp.where(lane_head == j, q, 0) * jnp.asarray(HD**-0.5, BF16)
        scores = mask_scores(dot(k_ref[0:n, :], q_head, (1, 1)), bias, first, ROWS)
        top = jnp.max(scores, axis=0, keepdims=True)
        weight = jnp.exp(scores - top)
        total = jnp.sum(weight, axis=0, keepdims=True)
        at = pl.ds(pl.multiple_of(j * HD, HD), HD)
        out_t[at, :] = dot(v_t[at, 0:n], weight.astype(BF16), (1, 0)) / total
        lse_ref[pl.ds(j, 1), first:n] = top + jnp.log(total)
        return 0

    lax.fori_loop(0, 4, head, 0)
    live = first + lax.broadcasted_iota(jnp.int32, (ROWS, 256), 0) < length
    o_ref[first:n, :] = jnp.where(live, out_t[...].T, 0).astype(BF16)


def square_of(square, which):
    return square[:, :, 32 * which : 32 * which + 32, :].reshape(1024, 1024)


def text_probs(query, keys, bias, lane_head):
    heads = [jnp.where(lane_head == j, query, 0) for j in range(4)]
    stacked = jnp.concatenate(heads, axis=0)
    scores = dot(stacked, keys, (1, 1)) + bias
    weight = jnp.exp(scores - jnp.max(scores, axis=1, keepdims=True))
    return weight / jnp.sum(weight, axis=1, keepdims=True), stacked


def pick_heads(stacked, lane_head):
    return sum(jnp.where(lane_head == j, stacked[128 * j : 128 * j + 128], 0) for j in range(4))


def forward_body(
    clip_len, text_len, frame_mask, text_mask, gain, shift, self_qkv, cross_qkv, self_out, cross_out,
    text, hid, fin, fout, grad,
    o_hid, o_first, o_q, o_k, o_v, o_heads, o_lse, o_w_a, o_w_b, o_params, o_att, o_tkv, o_square,
    o_second, o_query, o_crossed, o_self, o_cross, o_out, o_in, o_third, o_sum,
    hid_all, first, q_ref, k_ref, v_ref, heads, lse, w_a, w_b, params, att, tkv, sq_self, sq_cross,
    second, query_ref, crossed, after_self, after_cross, out_ref, in_ref,
    out_t, v_t, own_tkv, own_text, own_hid, fin_in, grad_all, win, wout,
    tokens, inner, slope, g_pre, terms, slots, out_w, inbox, sums, near, far,
    bias, cols_a, cols_b, square, placed, local, saved, send_sem, recv_sem,
):
    h = Here()
    w = Wire(h, send_sem, recv_sem)
    partners = frame_others(h) + clip_others(h)
    call_out(partners)
    length = clip_len[h.pair]
    tag = [0]

    def tags(n):
        tag[0] += n
        return tag[0] - n

    T_HID, T_A, T_B, T_FIN, T_AXY, T_BXY = tags(10), tags(7), tags(7), tags(3), tags(6), tags(6)
    T_SELF, T_CROSS, T_ATT, T_TKV, T_WIN, T_GRAD = tags(46), tags(46), tags(8), tags(3), tags(10), tags(6)
    T_TOK, T_WOUT, T_TERM, T_OSIB, T_OZ = tags(6), tags(10), tags(6), tags(4), tags(5)

    def my_columns(f):
        return pl.ds(pl.multiple_of(lax.rem(f, 4) * 256, 256), 256)

    def fin_part(c):
        return fin.at[:, pl.ds(pl.multiple_of(c * 1024, 1024), 1024)]

    spread = lax.broadcasted_iota(jnp.int32, (32, 128), 0) + 32 * lax.rem(h.f, 4)
    spread = jnp.where(spread == lax.broadcasted_iota(jnp.int32, (32, 128), 1), 1.0, 0.0).astype(BF16)
    placed[...] = jnp.zeros_like(placed)
    placed[0:3, :] = dot(gain[...], spread, (1, 0))
    placed[3:6, :] = dot(shift[...], spread, (1, 0))
    for q in range(8):
        group = placed[...] if q % 2 == 0 else jnp.zeros((16, 128), F32)
        cols_a[96:112, 128 * q : 128 * q + 128] = group.astype(BF16)
    for j in range(3):
        cols_a[32 * j : 32 * j + 32, :] = self_qkv[j]
    for j in range(2):
        cols_b[32 * j : 32 * j + 32, :] = cross_qkv[1 + j]
    square[0:32, :] = self_out[...]
    square[32:64, :] = cross_qkv[0]
    square[64:96, :] = cross_out[...]
    own = [
        pltpu.make_async_copy(src, dst, local.at[i])
        for i, (src, dst) in enumerate(
            (
                (cols_a.at[:, my_columns(h.f)], w_a.at[h.c, h.f]),
                (cols_b.at[:, my_columns(h.f)], w_b.at[h.c, h.f]),
                (hid.at[h.pair], hid_all.at[h.f]),
                (square.at[pl.ds(0, 32)], sq_self.at[h.c, h.f]),
                (fin_part(h.c), fin_in.at[h.c]),
                (text, own_text),
                (hid, own_hid),
                (grad, grad_all.at[h.c]),
                (fout, wout.at[h.f]),
                (square.at[pl.ds(32, 64)], sq_cross.at[h.c, h.f]),
            )
        )
    ]
    for copy in own:
        copy.start()
    saves = []

    def save(src, dst):
        copy = pltpu.make_async_copy(src, dst, saved.at[len(saves)])
        copy.start()
        saves.append(copy)

    hear_all(partners)

    own[0].wait()
    for d in (2, 6, 4, 3, 5, 1, 7):
        f = h.step(d)
        w.send(cols_a.at[:, my_columns(f)], w_a.at[h.c, h.f], T_A + d - 1, h.c, f)
    own[7].wait()
    grad_gather = ClipGather(w, lambda c, half: grad_all.at[c, pl.ds(128 * half, 128), :], T_GRAD)
    grad_gather.begin()
    for i, (c, f) in enumerate(clip_others(h)):
        w.send(fin_part(c), fin_in.at[h.c], T_FIN + i, c, f)
    w.send(hid.at[h.pair], hid_all.at[h.f], T_HID, h.c, h.sib)

    def half_of(ref, part):
        return ref.at[pl.ds(64 * part, 64), :]

    for d in range(1, 8):
        w.arrived(w_a.at[h.c, lax.rem(h.f + 8 - d, 8)], T_A + d - 1)
    a_gather = ClipGather(w, lambda c, half: w_a.at[c, pl.ds(4 * half, 4)], T_AXY)
    a_gather.begin()
    for part in range(2):
        w.send(
            half_of(hid.at[1 - h.pair], part),
            half_of(hid_all.at[h.f], part),
            T_HID + 3 + 2 * h.role + part,
            h.c,
            h.far_gate,
        )
        w.send(half_of(hid.at[h.pair], part), half_of(hid_all.at[h.f], part), T_HID + 1 + part, h.c, h.partner)
    own[3].wait()
    self_gather = MatrixGather(w, lambda c, f: sq_self.at[c, f], 32, T_SELF)
    self_gather.step(1)
    forwards = []
    for part in range(2):
        for j in range(2):
            block = half_of(hid_all.at[h.far[j]], part)
            w.arrived(block, T_HID + 3 + 2 * j + part)
            forward = w.copy(block, block, T_HID + 3 + 2 * j + part, h.c, h.partner)
            pl.when(h.is_gate)(forward.start)
            forwards.append(forward)
    self_gather.step(2)
    a_gather.middle()
    for part in range(2):
        w.arrived(half_of(hid_all.at[h.partner], part), T_HID + 1 + part)
    w.send(hid_all.at[h.partner], hid_all.at[h.partner], T_HID + 7, h.c, h.sib)
    for j in range(2):
        w.send(hid_all.at[h.far[j]], hid_all.at[h.far[j]], T_HID + 8 + j, h.c, h.sib)
    self_gather.step(3)
    own[1].wait()
    for d in (2, 6, 4, 3, 5, 1, 7):
        f = h.step(d)
        w.send(cols_b.at[:, my_columns(f)], w_b.at[h.c, h.f], T_B + d - 1, h.c, f)
    fill_key_bias(bias, clip_len, frame_mask, h.pair)
    text_bias = text_bias_rows(text_len, text_mask)
    self_gather.middle(0)
    self_gather.step(4)
    self_gather.middle(1)
    own[9].wait()
    cross_gather = MatrixGather(w, lambda c, f: sq_cross.at[c, f], 64, T_CROSS)
    a_gather.near()
    a_gather.end()
    grad_gather.middle()
    cross_gather.step(1)
    own[4].wait()
    for i, (c, f) in enumerate(clip_others(h)):
        w.arrived(fin_in.at[c], T_FIN + i)
    win_gather = ZGather(w, lambda f: win.at[:, f], T_WIN, fin_in)
    win_copy = pltpu.make_async_copy(fin_in, win.at[:, h.f], local.at[11])
    win_copy.start()
    win_gather.step(1)
    win_gather.relay(0)
    for g in range(8):
        group = sum(w_a[g // 2, 4 * (g % 2) + i, 96:104, 0:128].astype(F32) for i in range(4))
        params[:, 128 * g : 128 * g + 128] = group
    own[2].wait()
    w.arrived(hid_all.at[h.sib], T_HID)
    w.arrived(hid_all.at[h.partner + h.sib - h.f], T_HID + 7)
    for j in range(2):
        w.arrived(hid_all.at[h.far[j] + h.sib - h.f], T_HID + 8 + j)

    def project_rows(i, _):
        at = pl.ds(pl.multiple_of(i * 256, 256), 256)
        rows = hid_all[pl.ds(2 * i, 2)].reshape(256, 1024).astype(F32)
        xhat, _ = norm_parts(rows)
        low = (xhat * params[0:1, :] + params[3:4, :]).astype(BF16)
        first[at, :] = low
        for j, out in enumerate((q_ref, k_ref, v_ref)):
            out[at, :] = dot(low, column_weight(w_a, j), (1, 0)).astype(BF16)
        return 0

    lax.fori_loop(0, 2, project_rows, 0)
    self_gather.middle(2)
    for d in range(1, 8):
        w.arrived(w_b.at[h.c, lax.rem(h.f + 8 - d, 8)], T_B + d - 1)
    b_gather = ClipGather(w, lambda c, half: w_b.at[c, pl.ds(4 * half, 4)], T_BXY)
    b_gather.begin()
    cross_gather.step(2)
    lax.fori_loop(2, 4, project_rows, 0)
    v_t[...] = v_ref[...].T
    win_gather.step(2)
    self_gather.middle(3)
    cross_gather.step(3)
    b_gather.middle()

    def att_slot(f):
        return att.at[lax.div(f, 4), :, my_columns(f)]

    att_sends = []

    def attend_and_send(i):
        attend_rows(i, length, bias, q_ref, k_ref, v_t, heads, lse, out_t)
        for f in (2 * i, 2 * i + 1):
            block = heads.at[pl.ds(128 * f, 128), :]
            away = h.f != f
            copy = w.copy(block, att_slot(h.f), T_ATT + h.f, h.c, f)
            stay = pltpu.make_async_copy(block, att_slot(h.f), local.at[12])
            pl.when(away)(copy.start)
            pl.when(jnp.logical_not(away))(stay.start)
            att_sends.append((away, copy, stay))

    attend_and_send(3)
    def text_slot(f):
        return tkv.at[:, :, :, my_columns(f)]

    b_gather.near()
    b_gather.end()
    own[5].wait()
    for clip in range(2):
        for j in range(2):
            own_tkv[clip, j] = dot(own_text[clip], column_weight(w_b, j), (1, 0)).astype(BF16)
    w.send(own_tkv, text_slot(h.f), T_TKV, h.c, h.partner)
    w.send(own_tkv, text_slot(h.f), T_TKV + 1, h.c, h.sib)
    text_copy = pltpu.make_async_copy(own_tkv, text_slot(h.f), local.at[10])
    text_copy.start()
    cross_gather.step(4)
    win_gather.step(3)
    cross_gather.middle(0)
    attend_and_send(2)
    for d in range(4):
        self_gather.near(d)
        self_gather.last(d)
    cross_gather.middle(1)
    w.arrived(text_slot(h.partner), T_TKV)
    w.send(text_slot(h.partner), text_slot(h.partner), T_TKV + 2, h.c, h.sib)
    attend_and_send(1)
    win_gather.step(4)
    for d in range(1, 4):
        win_gather.relay(d)
    cross_gather.middle(2)
    attend_and_send(0)
    cross_gather.middle(3)
    for src, dst in (
        (hid_all, o_hid), (first, o_first), (q_ref, o_q), (k_ref, o_k), (v_ref, o_v), (heads, o_heads), (lse, o_lse),
        (w_a, o_w_a), (w_b, o_w_b), (params, o_params),
    ):
        save(src, dst)
    self_gather.end()
    for d in range(1, 8):
        f = lax.rem(h.f + 8 - d, 8)
        w.arrived(att_slot(f), T_ATT + f)
    for away, _, stay in att_sends:
        pl.when(jnp.logical_not(away))(stay.wait)

    own[6].wait()
    value = own_hid[...].reshape(256, 1024).astype(F32) + dot(
        att[...].reshape(256, 1024), square_of(sq_self, 0), (1, 0)
    )
    after_self[...] = value
    xhat, _ = norm_parts(value)
    second[...] = (xhat * params[1:2, :] + params[4:5, :]).astype(BF16)
    for d in range(4):
        cross_gather.near(d)
        cross_gather.last(d)
    cross_gather.end()
    query_ref[...] = dot(second[...], square_of(sq_cross, 0), (1, 0)).astype(BF16)
    w.arrived(text_slot(h.sib), T_TKV + 1)
    w.arrived(text_slot(h.partner + h.sib - h.f), T_TKV + 2)
    text_copy.wait()
    lane_head = lax.broadcasted_iota(jnp.int32, (128, 256), 1) // HD
    for clip in range(2):
        for group in range(4):
            rows, columns = pl.ds(128 * clip, 128), pl.ds(256 * group, 256)
            query = query_ref[rows, columns] * jnp.asarray(HD**-0.5, BF16)
            probs, _ = text_probs(query, tkv[clip, 0, :, columns], text_bias[clip], lane_head)
            part = dot(probs.astype(BF16), tkv[clip, 1, :, columns], (1, 0))
            crossed[rows, columns] = pick_heads(part, lane_head).astype(BF16)
    own[8].wait()
    out_gather = ZGather(w, lambda f: wout.at[f], T_WOUT)
    out_gather.step(1)
    out_gather.relay(0)
    value = after_self[...] + dot(crossed[...], square_of(sq_cross, 1), (1, 0))
    after_cross[...] = value
    xhat, _ = norm_parts(value)
    tokens[h.c] = (xhat * params[2:3, :] + params[5:6, :]).astype(BF16)

    token_gather = ClipGather(w, lambda c, half: tokens.at[c, pl.ds(128 * half, 128), :], T_TOK)
    token_gather.begin()
    for src, dst in (
        (att, o_att), (tkv, o_tkv), (second, o_second), (query_ref, o_query), (crossed, o_crossed),
        (after_self, o_self), (after_cross, o_cross),
    ):
        save(src, dst)
    save(sq_self, o_square.at[0])
    for which in range(2):
        save(sq_cross.at[:, :, pl.ds(32 * which, 32), :], o_square.at[1 + which])
    win_copy.wait()
    win_gather.end()

    def hidden(c):
        def part(i, _):
            rows = pl.ds(pl.multiple_of(128 * i, 128), 128)
            pre = dot(tokens[c, rows, :], win[...].reshape(1024, 1024), (1, 0))
            cdf = 0.5 * (1.0 + lax.erf(pre * (0.5**0.5)))
            inner[c, rows, :] = (pre * cdf).astype(BF16)
            slope[c, rows, :] = cdf + pre * jnp.exp(-0.5 * pre * pre) * 0.3989422804014327
            return 0

        lax.fori_loop(0, 2, part, 0)

    def hidden_back(c):
        g_inner = dot(grad_all[c], wout[...].reshape(1024, 1024), (1, 1))
        g_pre[c] = (g_inner * slope[c]).astype(BF16)
        terms[c] = dot(g_pre[c], win[...].reshape(1024, 1024), (1, 1)).astype(BF16)

    def out_terms(c):
        out_ref[c] = dot(inner[c], wout[...].reshape(1024, 1024), (1, 0)).astype(BF16)

    sibling = SiblingSum(w, lambda f: out_w.at[f], lambda z: inbox.at[z], lambda z: sums.at[z], T_OSIB)
    z_scatter = ZScatter(w, sums, near, far, T_OZ)
    tall = (1024, 1024)

    def out_weight(i, _):
        columns = pl.ds(pl.multiple_of(i * 256, 256), 256)
        out = dot(inner[:, :, columns].reshape(1024, 256), grad_all[...].reshape(tall), (0, 0))
        out_w[pl.ds(2 * i, 2)] = out.astype(BF16).reshape(2, 128, 1024)
        return 0

    def in_weight(i, _):
        columns = pl.ds(pl.multiple_of(i * 256, 256), 256)
        out = dot(tokens[:, :, columns].reshape(1024, 256), g_pre[...].reshape(tall), (0, 0))
        in_ref[:, pl.ds(pl.multiple_of(32 * i, 32), 32), :] = out.astype(BF16).reshape(8, 32, 1024)
        return 0

    hidden(h.c)
    out_gather.step(2)
    grad_gather.near()
    grad_gather.end()
    token_gather.middle()
    token_gather.near()
    out_gather.step(3)

    def both(i, _):
        hidden(jnp.where(i == 0, h.cx, h.cy))
        return 0

    lax.fori_loop(0, 2, both, 0)
    out_gather.step(4)
    for d in range(1, 4):
        out_gather.relay(d)
    token_gather.end()
    hidden(h.cd)
    lax.fori_loop(0, 4, out_weight, 0)
    sibling.begin()
    out_gather.end()
    scatter = ClipScatter(
        w, lambda c, half: terms.at[c, pl.ds(128 * half, 128), :], [slots.at[i] for i in range(6)], T_TERM
    )
    hidden_back(h.cd)
    scatter.begin(0)
    sibling.end()
    z_scatter.begin()

    def others_back(i, _):
        hidden_back(jnp.where(i == 0, h.cx, h.cy))
        return 0

    lax.fori_loop(0, 2, others_back, 0)
    scatter.begin(1)
    hidden_back(h.c)
    scatter.middle()
    z_scatter.step(1)
    lax.fori_loop(0, 2, in_weight, 0)
    lax.fori_loop(2, 4, in_weight, 0)
    save(in_ref, o_in)
    z_scatter.step(2)
    z_scatter.step(3)

    def out_term(i, _):
        out_terms(i)
        return 0

    lax.fori_loop(0, 4, out_term, 0)
    save(out_ref, o_out)
    scatter.end()
    for half in range(2):
        o_third[128 * half : 128 * half + 128, :] = scatter.total(half)
    z_scatter.total(o_sum)
    w.drain()
    for copy in forwards:
        pl.when(h.is_gate)(copy.wait_send)
    for away, copy, _ in att_sends:
        pl.when(away)(copy.wait_send)
    for one in (self_gather.z, cross_gather.z, win_gather, out_gather, z_scatter):
        one.drain()
    for copy in saves:
        copy.wait()


def forward(*args):
    column, rows, full, quarter = (1024, 256), (256, 1024), (4, 256, 1024), (4, 128, 1024)
    kept = [
        shape((8, 128, 1024)),
        shape((1024, 1024)),
        shape(column),
        shape(column),
        shape(column),
        shape(column),
        shape((8, 1024), F32),
        shape((4, 8, 112, 256)),
        shape((4, 8, 64, 256)),
        shape((8, 1024), F32),
        shape((2, 128, 1024)),
        shape((2, 2, 128, 1024)),
        shape((4, 8, 96, 1024)),
        shape(rows),
        shape(rows),
        shape(rows),
        shape(rows, F32),
        shape(rows, F32),
        shape(full),
        shape((8, 128, 1024)),
    ]
    scratch = [pltpu.VMEM(one.shape, one.dtype) for one in kept]
    scratch[12:13] = [pltpu.VMEM((4, 8, rows, 1024), BF16) for rows in (32, 64)]
    kept[12] = shape((3, 4, 8, 32, 1024))
    return comm_call(
        forward_body,
        tuple(kept) + (shape(rows, F32), shape((128, 1024), F32)),
        [SMEM] * 2 + [VMEM] * 8 + [HBM] * 5,
        (HBM,) * len(kept) + (VMEM,) * 2,
        scratch
        + [
            pltpu.VMEM((256, ROWS), F32),
            pltpu.VMEM((256, 1024), BF16),
            pltpu.VMEM((2, 2, 128, 256), BF16),
            pltpu.VMEM((2, 128, 1024), BF16),
            pltpu.VMEM((2, 128, 1024), BF16),
            pltpu.VMEM((4, 32, 1024), BF16),
            pltpu.VMEM(full, BF16),
            pltpu.VMEM((4, 8, 32, 1024), BF16),
            pltpu.VMEM((8, 128, 1024), BF16),
            pltpu.VMEM(full, BF16),
            pltpu.VMEM(full, BF16),
            pltpu.VMEM(full, F32),
            pltpu.VMEM(full, BF16),
            pltpu.VMEM(full, BF16),
            pltpu.VMEM((6, 128, 1024), BF16),
            pltpu.VMEM((8, 128, 1024), BF16),
            pltpu.VMEM(quarter, BF16),
            pltpu.VMEM(quarter, BF16),
            pltpu.VMEM((3, 128, 1024), BF16),
            pltpu.VMEM((2, 128, 1024), BF16),
            pltpu.VMEM((1024, 128), F32),
            pltpu.VMEM((112, 1024), BF16),
            pltpu.VMEM((64, 1024), BF16),
            pltpu.VMEM((96, 1024), BF16),
            pltpu.VMEM((16, 128), F32),
            pltpu.SemaphoreType.DMA((13,)),
            pltpu.SemaphoreType.DMA((24,)),
        ],
        216,
        192,
        1,
    )(*args)


def attend_back_rows(i, length, bias, q_ref, k_ref, v_ref, o_ref, lse_ref, g_ref, dq_ref, dq_t, k_t, dk, dv):
    lane_head = lax.broadcasted_iota(jnp.int32, (ROWS, 256), 1) // HD
    first, n = i * ROWS, (i + 1) * ROWS
    q = q_ref[first:n, :] * jnp.asarray(HD**-0.5, BF16)
    live = first + lax.broadcasted_iota(jnp.int32, (ROWS, 256), 0) < length
    g = jnp.where(live, g_ref[first:n, :], 0)
    both = (g.astype(F32) * o_ref[first:n, :].astype(F32)).T
    row_dots = jnp.concatenate(
        [jnp.sum(both[HD * j : HD * j + HD], axis=0, keepdims=True) for j in range(4)], axis=0
    )
    lse = lse_ref[0:4, first:n]

    def pick(rows, j):
        at = lax.broadcasted_iota(jnp.int32, rows.shape, 0) == j
        return jnp.sum(jnp.where(at, rows, 0), axis=0, keepdims=True)

    def head(j, _):
        q_head = jnp.where(lane_head == j, q, 0)
        g_head = jnp.where(lane_head == j, g, 0)
        scores = mask_scores(dot(k_ref[0:n, :], q_head, (1, 1)), bias, first, ROWS)
        probs = jnp.exp(scores - pick(lse, j))
        grads = dot(v_ref[0:n, :], g_head, (1, 1))
        dlogits = (probs * (grads - pick(row_dots, j))).astype(BF16)
        dv[0:n, :] += dot(probs.astype(BF16), g_head, (1, 0))
        dk[0:n, :] += dot(dlogits, q_head, (1, 0))
        at = pl.ds(pl.multiple_of(j * HD, HD), HD)
        dq_t[at, :] = dot(k_t[at, 0:n], dlogits, (1, 0))
        return 0

    lax.fori_loop(0, 4, head, 0)
    dq_ref[first:n, :] = (dq_t[...].T * (HD**-0.5)).astype(BF16)


def norm_back(xhat, scale, grad, gain):
    h = grad * gain
    return scale * (
        h
        - jnp.mean(h, axis=-1, keepdims=True)
        - xhat * jnp.mean(h * xhat, axis=-1, keepdims=True)
    )


def backward_body(
    clip_len, text_len, frame_mask, text_mask, norms_in,
    h_third, h_out, h_cross, h_self, h_second, h_query, h_crossed, h_att, h_square, h_tkv, h_out_terms, h_in_terms,
    h_q, h_k, h_v, h_o, h_lse, h_hid, h_first, h_wa, h_wb, h_text, h_own,
    o_output, o_in, o_hidden, o_square, o_qkv, o_ckv, o_norm, o_text,
    v_third, v_out, after_cross, query_ref, crossed, att, mats, tkv, out_terms,
    q_ref, k_ref, v_ref, o_ref, lse, w_a, w_b, text_in,
    g_crossed, g_att, g_after, slots, t_inbox, t_near, t_far, t_total,
    i_inbox, i_near, i_far, i_out, i_in,
    g_square, s_inbox, s_slots, s_part, y_part, z_near, z_far, y_near, y_far,
    g_heads, dq_t, k_t, dk, dv, d_cols, f_inbox, f_in,
    a_terms, a_slots, a_sum, a_in, b_terms, b_slots, b_sum, b_in,
    t_terms, tt_in, n_row, n_terms, n_slots, n_sum, n_in,
    bias, loaded, local, send_sem, recv_sem,
):
    h = Here()
    w = Wire(h, send_sem, recv_sem)
    partners = frame_others(h) + clip_others(h)
    call_out(partners)
    length = clip_len[h.pair]
    tag = [0]

    def tags(n):
        tag[0] += n
        return tag[0] - n

    loads = []

    def load(src, dst):
        copy = pltpu.make_async_copy(src, dst, loaded.at[len(loads)])
        copy.start()
        loads.append(copy)
        return copy

    l_terms = load(h_out_terms, out_terms)
    own_terms = [mats.at[0, z, pl.ds(0, 4)] for z in range(4)]
    l_own = [load(h_in_terms.at[2 * z + h.core], own_terms[z]) for z in range(4)]
    l_third, l_cross = load(h_third, v_third), load(h_cross, after_cross)
    l_out, l_m2 = load(h_out, v_out), load(h_square.at[2], mats.at[2])
    l_middle = [load(*pair) for pair in ((h_crossed, crossed), (h_query, query_ref), (h_tkv, tkv))]
    l_m1 = load(h_square.at[1], mats.at[1])
    l_att = load(h_att, att)
    l_heads = [
        load(*pair)
        for pair in (
            (h_q, q_ref), (h_k, k_ref), (h_v, v_ref), (h_o, o_ref), (h_lse, lse), (h_wb, w_b), (h_text, text_in),
            (h_wa, w_a),
        )
    ]
    fill_key_bias(bias, clip_len, frame_mask, h.pair)
    text_bias = text_bias_rows(text_len, text_mask)
    hear_all(partners)

    def matrix(which):
        return mats[which].reshape(1024, 1024)

    out_scatter = ClipScatter(
        w,
        lambda c, half: out_terms.at[c, pl.ds(128 * half, 128), :],
        [slots.at[i] for i in range(6)],
        tags(6),
    )
    in_tag = tags(4)
    for z in range(4):
        w.send(h_in_terms.at[2 * z + 1 - h.core], i_inbox.at[z], in_tag + z, h.c, h.sib)
    in_scatter = ZScatter(w, i_inbox, i_near, i_far, tags(5))
    l_terms.wait()
    out_scatter.begin()

    def square_sums(which):
        sibling = SiblingSum(
            w,
            lambda f: g_square.at[which, :, f],
            lambda z: s_inbox.at[which, z],
            lambda z: s_inbox.at[which, z],
            tags(4),
        )
        clip = ClipScatter(
            w,
            lambda c, half: s_inbox.at[which, :, c, pl.ds(16 * half, 16), :],
            [s_slots.at[which, i] for i in range(6)],
            tags(6),
        )
        return sibling, clip

    squares = [square_sums(which) for which in range(3)]

    def put(which, value):
        g_square[which] = value.astype(BF16).reshape(4, 8, 32, 1024)

    def columns_of(f):
        return pl.ds(pl.multiple_of(lax.rem(f, 4) * 256, 256), 256)

    def part_of(f):
        return g_att.at[lax.div(f, 4), :, columns_of(f)]

    def text_part(f):
        return g_text.at[lax.div(f, 4), :, :, columns_of(f)]

    for copy in (l_third, l_cross, l_out):
        copy.wait()
    xhat, scale = norm_parts(after_cross[...])
    grad = v_third[...]
    gain_third = jnp.sum(grad * xhat, axis=0, keepdims=True)
    shift_third = jnp.sum(grad, axis=0, keepdims=True)
    n_row[...] = jnp.zeros_like(n_row)
    n_row[2:3, :] = gain_third
    n_row[5:6, :] = shift_third
    g_after_cross = v_out[...].reshape(256, 1024).astype(F32) + norm_back(xhat, scale, grad, norms_in[2:3, :])
    g_after[...] = g_after_cross
    after_self, own_hid = v_third, v_out
    l_self, l_own_hid = load(h_self, after_self), load(h_own, own_hid)
    branch = g_after_cross.astype(BF16)
    l_m2.wait()
    g_crossed[...] = dot(branch, matrix(2), (1, 1)).astype(BF16)
    l_first = load(h_first, mats.at[2])
    for copy in l_middle + l_own:
        copy.wait()
    put(2, dot(crossed[...], branch, (0, 0)))
    squares[2][0].begin()
    second = crossed
    l_second = load(h_second, second)
    for z in range(4):
        w.arrived(i_inbox.at[z], in_tag + z)
        add_into(i_inbox.at[z], own_terms[z])
    in_scatter.begin()
    l_m0 = load(h_square.at[0], mats.at[0])
    g_query, g_text = query_ref, tkv
    lane_head = lax.broadcasted_iota(jnp.int32, (128, 256), 1) // HD
    for clip in range(2):
        for group in range(4):
            rows, columns = pl.ds(128 * clip, 128), pl.ds(256 * group, 256)
            keys, values = tkv[clip, 0, :, columns], tkv[clip, 1, :, columns]
            query = query_ref[rows, columns] * jnp.asarray(HD**-0.5, BF16)
            probs, stacked = text_probs(query, keys, text_bias[clip], lane_head)
            grads = g_crossed[rows, columns]
            g_stacked = jnp.concatenate([jnp.where(lane_head == j, grads, 0) for j in range(4)], axis=0)
            g_probs = dot(g_stacked, values, (1, 1))
            row_dot = jnp.sum(probs * g_probs, axis=1, keepdims=True)
            g_logits = (probs * (g_probs - row_dot)).astype(BF16)
            part = dot(g_logits, keys, (1, 0))
            g_query[rows, columns] = (pick_heads(part, lane_head) * (HD**-0.5)).astype(BF16)
            g_text[clip, 0, :, columns] = dot(g_logits, stacked, (0, 0)).astype(BF16)
            g_text[clip, 1, :, columns] = dot(probs.astype(BF16), g_stacked, (0, 0)).astype(BF16)
        if clip == 0:
            out_scatter.middle()
            in_scatter.step(1)
            squares[2][0].end()
            squares[2][1].begin()
    text_sibling = SiblingSum(w, text_part, lambda z: t_inbox.at[z], lambda z: t_inbox.at[z], tags(4))
    text_sibling.begin()
    l_m1.wait()
    grad = dot(g_query[...], matrix(1), (1, 1))
    l_hid = load(h_hid, mats.at[1])
    l_self.wait()
    xhat, scale = norm_parts(after_self[...])
    n_row[1:2, :] = jnp.sum(grad * xhat, axis=0, keepdims=True)
    n_row[4:5, :] = jnp.sum(grad, axis=0, keepdims=True)
    g_after_self = g_after[...] + norm_back(xhat, scale, grad, norms_in[1:2, :])
    g_after[...] = g_after_self
    branch = g_after_self.astype(BF16)
    l_m0.wait()
    g_att[...] = dot(branch, matrix(0), (1, 1)).astype(BF16).reshape(2, 128, 1024)
    heads_tag = tags(7)
    for d in (4, 2, 6, 3, 5, 1, 7):
        f = h.step(d)
        w.send(part_of(f), g_heads.at[h.f], heads_tag + d - 1, h.c, f)
    own_part = pltpu.make_async_copy(part_of(h.f), g_heads.at[h.f], local.at[0])
    own_part.start()
    in_scatter.step(2)
    in_scatter.step(3)
    l_second.wait()
    l_att.wait()
    put(1, dot(second[...], g_query[...], (0, 0)))
    squares[1][0].begin()
    put(0, dot(att[...].reshape(256, 1024), branch, (0, 0)))
    squares[0][0].begin()
    text_sibling.end()
    text_scatter = ZScatter(w, t_inbox, t_near, t_far, tags(5))
    text_scatter.begin()
    squares[2][1].middle()
    squares[1][0].end()
    squares[1][1].begin()
    out_scatter.end()
    for half in range(2):
        rows = pl.ds(128 * half, 128)
        o_output[rows, :] = (after_cross[rows, :] + out_scatter.total(half)).astype(BF16)
    squares[0][0].end()
    squares[0][1].begin()
    in_scatter.total(i_out)
    i_tag = tags(3)
    for i, (c, f) in enumerate(clip_others(h)):
        w.send(i_out.at[c], i_in.at[h.c], i_tag + i, c, f)
    i_in[h.c] = i_out[h.c]
    squares[1][1].middle()

    def square_part(which, out, row):
        squares[which][1].end()
        for half in range(2):
            total = squares[which][1].total(half)
            out[:, row + 16 * half : row + 16 * half + 16, :] = total.astype(BF16)

    text_scatter.step(1)
    for copy in l_heads:
        copy.wait()
    k_t[...] = k_ref[...].T
    dk[...] = jnp.zeros_like(dk)
    dv[...] = jnp.zeros_like(dv)
    for d in range(1, 8):
        w.arrived(g_heads.at[lax.rem(h.f + 8 - d, 8)], heads_tag + d - 1)
    own_part.wait()
    g_rows = g_heads[...].reshape(1024, 256)

    def rows_back(i):
        attend_back_rows(
            i, length, bias, q_ref, k_ref, v_ref, o_ref, lse, g_rows, d_cols.at[0], dq_t, k_t, dk, dv
        )

    text_scatter.step(2)
    text_scatter.step(3)
    squares[0][1].middle()
    rows_back(0)
    square_part(2, s_part, 32)
    square_part(1, s_part, 0)
    z_scatter = ZScatter(w, s_part, z_near, z_far, tags(5))
    z_scatter.begin()
    rows_back(1)

    class Columns:
        def __init__(self, terms, slots, sums, inbox):
            self.sums, self.inbox, self.tag = sums, inbox, tags(13)
            self.clip = ClipScatter(
                w,
                lambda c, half: terms.at[c, pl.ds(4 * half, 4)],
                [slots.at[i] for i in range(6)],
                self.tag,
            )

        def spread(self):
            self.clip.end()
            for half in range(2):
                self.sums[4 * half : 4 * half + 4] = self.clip.total(half).astype(BF16)
            for d in (4, 2, 6, 3, 5, 1, 7):
                f = h.step(d)
                w.send(self.sums.at[f], self.inbox.at[h.f], self.tag + 5 + d, h.c, f)
            self.inbox[h.f] = self.sums[h.f]

        def wait(self):
            for d in range(1, 8):
                w.arrived(self.inbox.at[lax.rem(h.f + 8 - d, 8)], self.tag + 5 + d)

    text_scatter.total(t_total)
    g_tkv = [t_total[j].astype(BF16) for j in range(2)]
    text = text_in[h.pair]
    for j in range(2):
        b_terms[:, :, 32 * j : 32 * j + 32, :] = (
            dot(text, g_tkv[j], (0, 0)).astype(BF16).reshape(4, 8, 32, 256)
        )
    b_columns = Columns(b_terms, b_slots, b_sum, b_in)
    b_columns.clip.begin()
    t_terms[...] = (
        dot(g_tkv[0], column_weight(w_b, 0), (1, 1)) + dot(g_tkv[1], column_weight(w_b, 1), (1, 1))
    ).astype(BF16)
    tt_tag = tags(7)
    for d in range(1, 8):
        f = h.step(d)
        w.send(
            t_terms.at[pl.ds(pl.multiple_of(f * 16, 16), 16), :], tt_in.at[h.f], tt_tag + d - 1, h.c, f
        )
    tt_in[h.f] = t_terms[pl.ds(pl.multiple_of(h.f * 16, 16), 16), :]
    z_scatter.step(1)
    rows_back(2)
    square_part(0, y_part, 0)
    y_scatter = ZScatter(w, y_part, y_near, y_far, tags(5))
    y_scatter.begin()
    z_scatter.step(2)
    z_scatter.step(3)
    b_columns.clip.middle()
    rows_back(3)
    b_columns.spread()
    d_cols[1] = dk[...].astype(BF16)
    d_cols[2] = dv[...].astype(BF16)
    l_first.wait()
    a_columns = [Columns(a_terms.at[j], a_slots.at[j], a_sum.at[j], a_in.at[j]) for j in range(3)]
    for j in range(3):
        a_terms[j] = dot(mats[2].reshape(1024, 1024), d_cols[j], (0, 0)).astype(BF16).reshape(4, 8, 32, 256)
        a_columns[j].clip.begin()
    y_scatter.step(1)

    f_terms = mats.at[0]
    f_sibling = SiblingSum(
        w,
        lambda f: f_terms.at[lax.div(f, 2), pl.ds(pl.multiple_of(lax.rem(f, 2) * 4, 4), 4)],
        lambda z: f_inbox.at[z],
        lambda z: f_inbox.at[z],
        tags(4),
    )
    l_hid.wait()

    def frame_terms(i, _):
        rows = pl.ds(pl.multiple_of(i * 256, 256), 256)
        grad = sum(dot(d_cols[j, rows, :], column_weight(w_a, j), (1, 1)) for j in range(3))
        f_terms[i] = grad.astype(BF16).reshape(8, 32, 1024)
        xhat, _ = norm_parts(mats[1, i].reshape(256, 1024).astype(F32))
        n_row[0:1, :] += jnp.sum(grad * xhat, axis=0, keepdims=True)
        n_row[3:4, :] += jnp.sum(grad, axis=0, keepdims=True)
        return 0

    lax.fori_loop(0, 4, frame_terms, 0)
    f_sibling.begin()
    y_scatter.step(2)
    a_columns[0].clip.middle()
    f_sibling.end()
    f_tag = tags(4)
    other = 2 * (1 - h.pair)
    is_end = jnp.logical_not(h.is_gate)
    to_gate, to_far = [], []
    for j in range(2):
        to_gate.append(w.copy(f_inbox.at[other + j], f_in.at[1 + j], f_tag + 1 + j, h.c, h.partner))
        pl.when(is_end)(to_gate[j].start)
    w.send(f_inbox.at[lax.div(h.partner, 2)], f_in.at[0], f_tag, h.c, h.partner)
    for c in range(4):
        for f in range(8):
            group = 2 * c + f // 4
            n_terms[c, f] = n_row[:, 128 * group : 128 * group + 128].astype(BF16)
    n_columns = Columns(n_terms, n_slots, n_sum, n_in)
    n_columns.clip.begin()
    a_columns[1].clip.middle()
    a_columns[0].spread()
    for j in range(2):

        @pl.when(h.is_gate)
        def _():
            w.arrived(f_in.at[1 + j], f_tag + 1 + j)
            add_into(f_inbox.at[other + j], f_in.at[1 + j])

        to_far.append(w.copy(f_inbox.at[other + j], f_in.at[3], f_tag + 3, h.c, h.far[j]))
        pl.when(h.is_gate)(to_far[j].start)
    a_columns[2].clip.middle()
    a_columns[1].spread()
    n_columns.clip.middle()
    y_scatter.step(3)
    a_columns[2].spread()
    n_columns.spread()
    z_scatter.total(o_square.at[pl.ds(32, 64), :])
    for i, (c, f) in enumerate(clip_others(h)):
        w.arrived(i_in.at[c], i_tag + i)
    for c in range(4):
        o_in[:, 1024 * c : 1024 * c + 1024] = i_in[c].astype(F32)
    for d in range(1, 8):
        w.arrived(tt_in.at[lax.rem(h.f + 8 - d, 8)], tt_tag + d - 1)
    for p in range(2):
        o_text[p] = sum(tt_in[4 * p + q].astype(F32) for q in range(4)).astype(BF16)
    y_scatter.total(o_square.at[pl.ds(0, 32), :])
    w.arrived(f_in.at[0], f_tag)
    w.arrived(f_in.at[3], f_tag + 3)

    def hidden_out(clip, total):
        xhat, scale = norm_parts(own_hid[clip].astype(F32))
        rows = pl.ds(pl.multiple_of(clip * 128, 128), 128)
        o_hidden[clip] = (g_after[rows, :] + norm_back(xhat, scale, total, norms_in[0:1, :])).astype(BF16)

    l_own_hid.wait()
    hidden_out(h.pair, (f_inbox[h.z].astype(F32) + f_in[0].astype(F32)).reshape(128, 1024))
    hidden_out(1 - h.pair, f_in[3].astype(F32).reshape(128, 1024))
    for j in range(3):
        a_columns[j].wait()
        for q in range(4):
            o_qkv[j, :, 256 * q : 256 * q + 256] = a_in[j, q].astype(F32) + a_in[j, 4 + q].astype(F32)
    b_columns.wait()
    for j in range(2):
        for q in range(4):
            at = pl.ds(32 * j, 32)
            o_ckv[j, :, 256 * q : 256 * q + 256] = b_in[q, at, :].astype(F32) + b_in[4 + q, at, :].astype(F32)
    n_columns.wait()
    o_norm[...] = sum(n_in[f].astype(F32) for f in range(8))
    w.drain()
    for one in (in_scatter, text_scatter, z_scatter, y_scatter):
        one.drain()
    for j in range(2):
        pl.when(is_end)(to_gate[j].wait_send)
        pl.when(h.is_gate)(to_far[j].wait_send)


def backward(*args):
    def buffer(*dims):
        return pltpu.VMEM(dims, BF16)

    def full(*dims):
        return pltpu.VMEM(dims, F32)

    return comm_call(
        backward_body,
        (
            shape((256, 1024)),
            shape((32, 4096), F32),
            shape((2, 128, 1024)),
            shape((96, 1024), F32),
            shape((3, 32, 1024), F32),
            shape((2, 32, 1024), F32),
            shape((16, 128), F32),
            shape((2, 16, 1024)),
        ),
        [SMEM] * 2 + [VMEM] * 3 + [HBM] * 23,
        (VMEM,) * 8,
        [
            full(256, 1024), buffer(2, 128, 1024), full(256, 1024), buffer(256, 1024), buffer(256, 1024),
            buffer(2, 128, 1024), buffer(3, 4, 8, 32, 1024), buffer(2, 2, 128, 1024), buffer(4, 256, 1024),
            buffer(1024, 256), buffer(1024, 256), buffer(1024, 256), buffer(1024, 256), full(8, 1024),
            buffer(4, 8, 112, 256), buffer(4, 8, 64, 256), buffer(2, 128, 1024),
            buffer(256, 1024), buffer(2, 128, 1024), full(256, 1024),
            buffer(6, 128, 1024), buffer(4, 2, 128, 256), buffer(3, 2, 128, 256), buffer(2, 2, 128, 256),
            full(2, 128, 256),
            buffer(4, 4, 32, 1024), buffer(3, 4, 32, 1024), buffer(2, 4, 32, 1024),
            buffer(4, 32, 1024), buffer(4, 32, 1024),
            buffer(3, 4, 8, 32, 1024), buffer(3, 4, 4, 32, 1024), buffer(3, 6, 4, 16, 1024),
            buffer(4, 64, 1024), buffer(4, 32, 1024), buffer(3, 64, 1024), buffer(2, 64, 1024),
            buffer(3, 32, 1024), buffer(2, 32, 1024),
            buffer(8, 128, 256), full(256, ROWS), buffer(256, 1024), full(1024, 256), full(1024, 256),
            buffer(3, 1024, 256), buffer(4, 4, 32, 1024), buffer(4, 4, 32, 1024),
            buffer(3, 4, 8, 32, 256), buffer(3, 6, 4, 32, 256), buffer(3, 8, 32, 256), buffer(3, 8, 32, 256),
            buffer(4, 8, 64, 256), buffer(6, 4, 64, 256), buffer(8, 64, 256), buffer(8, 64, 256),
            buffer(128, 1024), buffer(8, 16, 1024), full(16, 1024), buffer(4, 8, 16, 128), buffer(6, 4, 16, 128),
            buffer(8, 16, 128), buffer(8, 16, 128), full(1024, 128),
            pltpu.SemaphoreType.DMA((32,)),
            pltpu.SemaphoreType.DMA((1,)),
        ],
        208,
        160,
        2,
    )(*args)


def finish_body(*refs):
    ins, outs = refs[:9], refs[9:]
    output, hidden, text, qkv, square, ckv, fin, fout, norm = ins
    o_output, o_hidden, o_text, o_qkv, o_self_out, o_cross, o_cross_out, o_fin, o_fout, o_gain, o_shift = outs
    o_fout[...] = fout[...]
    o_output[...] = output[...].reshape(2, 128, 1024)
    o_hidden[...] = hidden[...]
    o_text[...] = text[...]
    o_fin[...] = fin[...]
    o_qkv[...] = qkv[...]
    o_self_out[...] = square[0:32, :]
    o_cross[0] = square[32:64, :]
    o_cross[1:3] = ckv[...]
    o_cross_out[...] = square[64:96, :]
    place = lax.rem(lax.axis_index("frame"), 4)
    for row, out in ((0, o_gain), (3, o_shift)):
        out[...] = sum(
            jnp.where(place == i, norm[row : row + 3, 32 * i : 32 * i + 32], 0) for i in range(4)
        )


def finish(*args):
    return pl.pallas_call(
        finish_body,
        out_shape=(
            shape((2, 128, 1024)),
            shape((2, 128, 1024)),
            shape((2, 16, 1024)),
            shape((3, 32, 1024), F32),
            shape((32, 1024), F32),
            shape((3, 32, 1024), F32),
            shape((32, 1024), F32),
            shape((32, 4096), F32),
            shape((128, 1024), F32),
            shape((3, 32), F32),
            shape((3, 32), F32),
        ),
        in_specs=[VMEM] * 9,
        out_specs=(VMEM,) * 11,
        compiler_params=pltpu.CompilerParams(vmem_limit_bytes=60 * 2**20),
    )(*args)


def on_device_fast(
    hidden_in,
    text_states,
    out_grad,
    self_qkv,
    self_out,
    cross_qkv,
    cross_out,
    ffn_in,
    ffn_out,
    ln_gain,
    ln_bias,
    clip_len,
    frame_mask,
    text_len,
    text_mask,
):
    (
        hid_all, first_low, query, key, value, att_heads, lse, w_a, w_b, params, att, tkv, square,
        second, cross_query, crossed, after_self, after_cross, out_terms, in_terms, third_sum, grad_ffn_out,
    ) = forward(
        clip_len, text_len, frame_mask, text_mask, ln_gain, ln_bias, jnp.moveaxis(self_qkv, 1, 0),
        jnp.moveaxis(cross_qkv, 1, 0), self_out, cross_out, text_states, hidden_in, ffn_in, ffn_out, out_grad.reshape(256, 1024),
    )
    output, grad_ffn_in, grad_hidden, square_sum, qkv_sum, ckv_sum, norm_sum, grad_text = backward(
        clip_len, text_len, frame_mask, text_mask, params,
        third_sum, out_grad, after_cross, after_self, second, cross_query, crossed, att, square, tkv,
        out_terms, in_terms.reshape(8, 4, 32, 1024), query, key, value, att_heads, lse,
        hid_all.reshape(4, 8, 32, 1024), first_low.reshape(4, 8, 32, 1024), w_a, w_b, text_states, hidden_in,
    )
    results = finish(output, grad_hidden, grad_text, qkv_sum, square_sum, ckv_sum, grad_ffn_in, grad_ffn_out, norm_sum)
    output, grad_hidden, grad_text, qkv, g_self_out, cross, g_cross_out, grad_ffn_in, grad_ffn_out, gains, shifts = results
    return (
        output,
        grad_hidden,
        grad_text,
        jnp.moveaxis(qkv, 0, 1),
        g_self_out,
        jnp.moveaxis(cross, 0, 1),
        g_cross_out,
        grad_ffn_in,
        grad_ffn_out,
        gains,
        shifts,
    )


def solution(mesh):
    return jax.shard_map(
        on_device_fast if fits(mesh) else on_device_any,
        mesh=mesh,
        in_specs=(
            P("clip", "frame", None),
            P("clip", None, None),
            P("clip", "frame", None),
            P(("clip", "frame"), None, None),
            P(("clip", "frame"), None),
            P(("clip", "frame"), None, None),
            P(("clip", "frame"), None),
            P(("clip", "frame"), None),
            P(("clip", "frame"), None),
            P(None, ("clip", "frame")),
            P(None, ("clip", "frame")),
            P("clip"),
            P("clip", None),
            P("clip"),
            P("clip", None),
        ),
        out_specs=(
            P("clip", "frame", None),
            P("clip", "frame", None),
            P("clip", "frame", None),
            P(("clip", "frame"), None, None),
            P(("clip", "frame"), None),
            P(("clip", "frame"), None, None),
            P(("clip", "frame"), None),
            P(("clip", "frame"), None),
            P(("clip", "frame"), None),
            P(None, ("clip", "frame")),
            P(None, ("clip", "frame")),
        ),
        check_vma=False,
    )
```
